32 devices in a mesh: seq: 8 (over z, x), exp: 4 (over y, core).
Axes of the slice: x: 2, y: 2, z: 4, core: 2. Of those that a mesh axis runs over, the one named last changes fastest.
Arguments:
- query: bfloat16 [4, 512, 2304], P('exp', 'seq'), may hold values from -40 to 40
- key_value: bfloat16 [4, 512, 2, 2304], P('exp', 'seq'), may hold values from -6 to 6
- residual: bfloat16 [4, 512, 2304], P('exp', 'seq'), may hold values from -6 to 6
- norm_gain: bfloat16 [2304], replicated, may hold values from 0.099609375 to 1.8984375
- segment_ids: int32 [4, 512], P('exp'), may hold values from 0 to 2, as said below
- routes: int32 [4, 512, 2], P('exp', 'seq'), may hold values from 0 to 7, all different within a row; in each aligned block of 64 rows (0 to 63, 64 to 127, ..., all dimensions but the last counted through in order) at most 24 rows name the same one
- gate_weights: float32 [4, 512, 2], P('exp', 'seq'), may hold values from 0.3 to 1
- page_table: int32 [4, 32], P('exp'), may hold values from 0 to 31, each once within a row
- w_gate: bfloat16 [8, 2304, 5760], P('exp', None, 'seq'), may hold values from -0.125 to 0.125
- w_up: bfloat16 [8, 2304, 5760], P('exp', None, 'seq'), may hold values from -0.125 to 0.125
- w_down: bfloat16 [8, 5760, 2304], P('exp', 'seq'), may hold values from -0.078125 to 0.078125
Outputs:
- layer_out: bfloat16 [4, 512, 2304], P('exp', 'seq')
- cache_pages: bfloat16 [4, 32, 16, 4608], P('exp', 'seq')
The draws below stay inside these ranges and needn't reach their ends.
Inputs may be any that keep to these rules, and one draw needn't show every extreme that they name: `segment_ids`: within a pack the ids start at 0 and rise by 0 or 1 from one token to the next, ending at 2. The two experts of a token differ; among the 64 tokens of one device at most 24 routes name one expert, and in some device exactly 24 do. `page_table`: each row is a permutation of the slots.
All inputs are finite; a program needn't handle non-finite values.
Results may differ from the reference program's by a relative error of at most 0.013.
Values may be sent and summed in bfloat16 or wider, within the bound.
No kernel may reach another device: no remote copies, remote signals or barrier semaphores. Data moves between devices by JAX's collectives and lax.ppermute only.
A program may use at most 128 MiB of HBM per device.

```python
import math
import jax
import jax.numpy as jnp
import numpy as np
from jax import lax

HEADS = 36
HEAD_DIM = 64
D = 2304
FF = 5760
EXPERTS = 8
TOK_DEV = 64
PAGE = 16
CAP = 24
GROUPS = 4
GROUP = 512
N_SEQ = 8


def segments_of(key):
    group_keys = jax.random.split(key, GROUPS)

    def one_pack(pack_key):
        order = jax.random.permutation(pack_key, GROUP - 1) + 1
        starts = jnp.zeros((GROUP,), jnp.int32).at[order[:2]].set(1)
        return jnp.cumsum(starts).astype(jnp.int32)
    return jax.vmap(one_pack)(group_keys)


def draw_segment_ids(key, part):
    return segments_of(jax.random.fold_in(key, 11))


def draw_query(key, part):
    inner = jax.random.fold_in(key, 2)
    base = jnp.clip(jax.random.normal(inner, (GROUPS, GROUP, D), jnp.float32), -6.0, 6.0)
    return base.astype(jnp.bfloat16)


def draw_key_value(key, part):
    inner = jax.random.fold_in(key, 3)
    base = jnp.clip(jax.random.normal(inner, (GROUPS, GROUP, 2, D), jnp.float32), -6.0, 6.0)
    return base.astype(jnp.bfloat16)


def block_levels(rng, shape, shards, smallest, top_value):
    def one(dim, blocks):
        draws = jax.random.uniform(jax.random.fold_in(jax.random.fold_in(rng, 6), dim), (blocks,), jnp.float32, smallest / len(shards), top_value / len(shards))
        return jnp.repeat(jnp.exp(draws), shape[dim] // blocks).reshape((-1,) + (1,) * (len(shape) - dim - 1))

    loudness = one(*shards[0])
    for cut in shards[1:]:
        loudness = loudness * one(*cut)
    return loudness


def assign_block(stream_key, own, number, rows, count, top, most, skew):
    order = jax.random.permutation(stream_key, count)
    crowded, usual = shares(count, rows * top, most, skew, True), shares(count, rows * top, most, skew, False)
    places = jnp.arange(count)

    def named(tallies, rotation):
        used = int((tallies > 0).sum())
        fixed = max(1, used // 4)
        moved = fixed + (places - fixed + rotation * (used - fixed)) % max(1, count - fixed)
        return jnp.zeros((count,), jnp.int32).at[order[jnp.where(places < fixed, places, moved)]].set(jnp.asarray(tallies, jnp.int32))

    tallies = jnp.where(number % 4 == 0, named(crowded, number // 4), named(usual, number - number // 4 - 1))
    mixed = jax.random.permutation(jax.random.fold_in(own, 3), count)
    giver, receiver = mixed[0:count // 2 * 2:2], mixed[1:count // 2 * 2:2]
    margin = jnp.minimum(tallies[giver] - 1, most - tallies[receiver]) // 2
    margin = jnp.where((giver == order[0]) | (receiver == order[0]) | (tallies[receiver] == 0), 0, jnp.maximum(margin, 0))
    moved = jax.random.randint(jax.random.fold_in(own, 4), (count // 2,), 0, 1 << 20) % (margin + 1)
    tallies = tallies.at[giver].add(-moved).at[receiver].add(moved)
    labels = jnp.searchsorted(jnp.cumsum(tallies), jnp.arange(rows * top), side="right").astype(jnp.int32)
    listing = labels.reshape(top, rows).T
    listing = listing[jax.random.permutation(jax.random.fold_in(own, 1), rows)]
    rotation = jax.random.randint(jax.random.fold_in(own, 2), (rows, 1), 0, top)
    return jnp.take_along_axis(listing, (jnp.arange(top)[None, :] + rotation) % top, axis=1)


def shares(number_of, total, limit, lean, full):
    loads = [(1 << 20) // math.isqrt(grade ** lean) + 1 for grade in range(1, number_of + 1)]
    largest = limit if full else min(limit, max(-(-total // number_of), total * loads[0] // sum(loads)))
    least = 1 if total - largest >= number_of - 1 else 0
    counts, spare = [largest] + [least] * (number_of - 1), total - largest - least * (number_of - 1)
    while spare > 0:
        free = [i for i in range(1, number_of) if counts[i] < largest] or [i for i in range(1, number_of) if counts[i] < limit]
        whole, budget = sum([loads[i] for i in free]), spare
        for i in free:
            extra = min(limit - counts[i], max(1, budget * loads[i] // whole), spare)
            counts[i] = counts[i] + extra
            spare = spare - extra
    return np.array(counts)


def bell_draw(stream_key, dims, width, reach, cuts=(), kind=jnp.bfloat16):
    values = jax.random.normal(stream_key, dims, jnp.float32) * width
    if len(cuts) > 0:
        values = block_levels(stream_key, dims, cuts, -0.22, 0.18) * values
    return jnp.clip(values, min=-reach, max=reach).astype(kind)


def setup_inputs(seed: int = 0) -> dict:
    streams_of = jax.random.split(jax.random.key(seed), 12)
    query = draw_query(jax.random.fold_in(streams_of[11], 71), 0)
    key_value = draw_key_value(jax.random.fold_in(streams_of[11], 71), 0)
    residual = bell_draw(streams_of[2], (GROUPS, GROUP, D), 1.0, 6.0, ((0, 4), (1, 8)))
    norm_gain = jnp.clip(1.0 + 0.18 * jax.random.normal(streams_of[3], (D,), jnp.float32), 0.099609375, 1.8984375).astype(jnp.bfloat16)
    segment_ids = draw_segment_ids(jax.random.fold_in(streams_of[11], 71), 0)
    routes_keys = jax.random.split(jax.random.fold_in(streams_of[5], 1), GROUPS * GROUP // TOK_DEV)
    routes_turns = jax.random.permutation(jax.random.fold_in(streams_of[5], 3), GROUPS * GROUP // TOK_DEV)
    routes = jax.vmap(lambda own, number: assign_block(jax.random.fold_in(streams_of[5], 2), own, number, TOK_DEV, EXPERTS, 2, CAP, 1))(routes_keys, routes_turns).reshape((GROUPS, GROUP, 2))
    gate_weights = jnp.clip(0.3 + 0.7 * jax.random.uniform(streams_of[6], (GROUPS, GROUP, 2), jnp.float32) ** block_levels(streams_of[6], (GROUPS, GROUP, 2), ((0, 4), (1, 8)), -0.2, 0.2), 0.3, 1.0)
    page_table = jax.vmap(lambda own: jax.random.permutation(own, GROUP // PAGE))(jax.random.split(streams_of[7], GROUPS)).reshape((GROUPS, GROUP // PAGE)).astype(jnp.int32)
    w_gate = bell_draw(streams_of[8], (EXPERTS, D, FF), D ** -0.5, 0.125, ((0, 4), (2, 8)))
    w_up = bell_draw(streams_of[9], (EXPERTS, D, FF), D ** -0.5, 0.125, ((0, 4), (2, 8)))
    w_down = bell_draw(streams_of[10], (EXPERTS, FF, D), FF ** -0.5, 0.078125, ((0, 4), (1, 8)))
    return {"query": query, "key_value": key_value, "residual": residual, "norm_gain": norm_gain, "segment_ids": segment_ids, "routes": routes, "gate_weights": gate_weights, "page_table": page_table, "w_gate": w_gate, "w_up": w_up, "w_down": w_down}


def attend_group(operands):
    queries, pairs, segments = operands
    length = queries.shape[0]
    heads_q = queries.reshape(length, HEADS, HEAD_DIM).astype(jnp.float32)
    heads_k = pairs[:, 0].reshape(length, HEADS, HEAD_DIM).astype(jnp.float32)
    heads_v = pairs[:, 1].reshape(length, HEADS, HEAD_DIM).astype(jnp.float32)
    scores = jnp.einsum('qhd,khd->qhk', heads_q, heads_k) * (1.0 / math.sqrt(HEAD_DIM))
    places = jnp.arange(length, dtype=jnp.int32)
    visible = (segments[:, None] == segments[None, :]) & (places[None, :] <= places[:, None])
    scores = jnp.where(visible[:, None, :], scores, -jnp.inf)
    highest = lax.optimization_barrier(jnp.max(scores, axis=-1, keepdims=True))
    probs = jnp.exp(scores - highest)
    totals = lax.optimization_barrier(jnp.sum(probs, axis=-1))
    weights = lax.optimization_barrier(probs.astype(jnp.bfloat16)).astype(jnp.float32)
    mixed = jnp.einsum('qhk,khd->qhd', weights, heads_v) / totals[..., None]
    return mixed.reshape(length, HEADS * HEAD_DIM)

def fill_pages(operands):
    pairs, table = operands
    pages = pairs.reshape(GROUP // PAGE, PAGE, 2 * D)
    return jnp.zeros_like(pages).at[table].set(pages)

def run_expert(operands):
    rows, gate_w, up_w, down_w = operands
    gate = jnp.dot(rows, gate_w, preferred_element_type=jnp.float32)
    upper = jnp.dot(rows, up_w, preferred_element_type=jnp.float32)
    hidden = (jax.nn.silu(gate) * upper).astype(jnp.bfloat16)
    block_width = FF // N_SEQ

    def add_block(running, index):
        part_h = lax.dynamic_slice_in_dim(hidden, index * block_width, block_width, 1)
        part_w = lax.dynamic_slice_in_dim(down_w, index * block_width, block_width, 0)
        term = jnp.dot(part_h, part_w, preferred_element_type=jnp.float32).astype(jnp.bfloat16)
        term = lax.optimization_barrier(term)
        return (running + term.astype(jnp.float32), None)
    start = jnp.zeros((rows.shape[0], D), jnp.float32)
    running, _ = lax.scan(add_block, start, jnp.arange(N_SEQ, dtype=jnp.int32))
    return running.astype(jnp.bfloat16)

def reference(query, key_value, residual, norm_gain, segment_ids, routes, gate_weights, page_table, w_gate, w_up, w_down):
    context = lax.map(attend_group, (query, key_value, segment_ids))
    stream = residual.astype(jnp.float32) + context
    normed = (stream * lax.rsqrt(lax.optimization_barrier(jnp.mean(stream * stream, axis=-1, keepdims=True)) + 1e-05) * norm_gain.astype(jnp.float32)).astype(jnp.bfloat16)
    cache_pages = lax.map(fill_pages, (key_value, page_table))
    blocks = GROUPS * N_SEQ
    flat_routes = routes.reshape(blocks, TOK_DEV * 2)
    onehot = (flat_routes[..., None] == jnp.arange(EXPERTS, dtype=jnp.int32)).astype(jnp.int32)
    before = jnp.cumsum(onehot, axis=1) - onehot
    slot = lax.optimization_barrier(jnp.sum(before * onehot, axis=-1))
    target = (flat_routes * CAP + slot).astype(jnp.int32)
    source_rows = jnp.repeat(normed.reshape(blocks, TOK_DEV, D), 2, axis=1)
    block_ids = jnp.arange(blocks, dtype=jnp.int32)[:, None]
    buffer = jnp.zeros((blocks, EXPERTS * CAP, D), jnp.bfloat16).at[block_ids, target].set(source_rows)
    per_expert = buffer.reshape(blocks, EXPERTS, CAP, D).transpose(1, 0, 2, 3).reshape(EXPERTS, blocks * CAP, D)
    outputs = lax.map(run_expert, (per_expert, w_gate, w_up, w_down))
    lookup = outputs.reshape(EXPERTS, blocks, CAP, D).transpose(1, 0, 2, 3).reshape(blocks, EXPERTS * CAP, D)
    picked = jnp.take_along_axis(lookup, target[..., None], axis=1).reshape(blocks, TOK_DEV, 2, D)
    gates = gate_weights.reshape(blocks, TOK_DEV, 2)
    mixture = lax.optimization_barrier(jnp.sum(gates[..., None] * picked.astype(jnp.float32), axis=2))
    layer_out = (stream.reshape(blocks, TOK_DEV, D) + mixture).astype(jnp.bfloat16).reshape(GROUPS, GROUP, D)
    return (layer_out, cache_pages)
```

```python
import functools
import math

import jax
import jax.numpy as jnp
from jax import lax
from jax.experimental import pallas as pl
from jax.experimental.pallas import tpu as pltpu
from jax.sharding import PartitionSpec as P

HEADS = 36
HEAD_DIM = 64
EXPERTS = 8
PAGE = 16
CAP = 24
CHUNK_BLOCKS = 8


def head_ranges(width, n_seq):
    share = width // n_seq
    firsts = [j * share // HEAD_DIM for j in range(n_seq)]
    count = max(-(-(j + 1) * share // HEAD_DIM) - firsts[j] for j in range(n_seq))
    firsts = [min(f, HEADS - count) for f in firsts]
    return share, firsts, count


def attention_kernel(heads, q_rows, packed_ref, seg_row_ref, seg_col_ref, out_ref):
    total = packed_ref.shape[0]
    span = heads * HEAD_DIM
    scale = 1.0 / math.sqrt(HEAD_DIM)
    for start in range(0, total, q_rows):
        end = start + q_rows
        q_place = start + lax.broadcasted_iota(jnp.int32, (q_rows, end), 0)
        k_place = lax.broadcasted_iota(jnp.int32, (q_rows, end), 1)
        visible = (seg_col_ref[start:end, :] == seg_row_ref[:, :end]) & (k_place <= q_place)
        parts = []
        for h in range(heads):
            a = h * HEAD_DIM
            q = packed_ref[start:end, a : a + HEAD_DIM]
            k = packed_ref[:end, span + a : span + a + HEAD_DIM]
            v = packed_ref[:end, 2 * span + a : 2 * span + a + HEAD_DIM]
            s = lax.dot_general(q, k, (((1,), (1,)), ((), ())), preferred_element_type=jnp.float32)
            s = jnp.where(visible, s * scale, -1e30)
            top = jnp.max(s, axis=1, keepdims=True)
            p = jnp.exp(s - top)
            denominator = jnp.sum(p, axis=1, keepdims=True)
            o = jnp.dot(p.astype(jnp.bfloat16), v, preferred_element_type=jnp.float32)
            parts.append((o / denominator).astype(jnp.bfloat16))
        out_ref[start:end, :] = jnp.concatenate(parts, axis=1)


def attention(packed, segments, heads):
    total = packed.shape[0]
    span = heads * HEAD_DIM
    return pl.pallas_call(
        functools.partial(attention_kernel, heads, 128),
        out_shape=jax.ShapeDtypeStruct((total, span), jnp.bfloat16),
        compiler_params=pltpu.CompilerParams(vmem_limit_bytes=40 * 1024 * 1024),
        cost_estimate=pl.CostEstimate(
            flops=4 * total * total * span, bytes_accessed=8 * total * span, transcendentals=total * total * heads
        ),
    )(packed, segments[None, :], segments[:, None])


def expert_kernel(
    local, rows, tokens, first_ref, x_ref, tgt_ref, gates_ref, wg_ref, wu_ref, wd_ref, out_ref, kept_ref
):
    le = pl.program_id(0)
    chunk = pl.program_id(1)

    def selection(which):
        base = (first_ref[0] + which) * CAP
        row_id = lax.broadcasted_iota(jnp.int32, (rows, tokens), 0)
        block = lax.broadcasted_iota(jnp.int32, (1, tokens), 1) // 64
        picks, weights = None, None
        for j in range(2):
            slot = tgt_ref[0, j : j + 1, :] - base
            place = jnp.where((slot >= 0) & (slot < CAP), block * CAP + slot, -1)
            hit = row_id == place
            gate = jnp.where(hit, gates_ref[0, j : j + 1, :], 0.0)
            picks = hit if picks is None else picks | hit
            weights = gate if weights is None else weights + gate
        return picks.astype(jnp.float32).astype(jnp.bfloat16), jnp.sum(weights, axis=1, keepdims=True)

    pick, weight = selection(le)
    chosen = jnp.dot(pick, x_ref[...], preferred_element_type=jnp.float32).astype(jnp.bfloat16)
    gate = jnp.dot(chosen, wg_ref[0], preferred_element_type=jnp.float32)
    upper = jnp.dot(chosen, wu_ref[0], preferred_element_type=jnp.float32)
    hidden = (gate / (1.0 + jnp.exp(-gate)) * upper).astype(jnp.bfloat16)
    y = jnp.dot(hidden, wd_ref[0], preferred_element_type=jnp.float32)
    y = (y * weight).astype(jnp.bfloat16)

    if local > 1:

        @pl.when(le < local - 1)
        def _():
            kept_ref[le, chunk] = y

    @pl.when(le == local - 1)
    def _():
        total = lax.dot_general(pick, y, (((0,), (0,)), ((), ())), preferred_element_type=jnp.float32)
        for other in range(local - 1):
            pick_o, _ = selection(other)
            total += lax.dot_general(
                pick_o, kept_ref[other, chunk], (((0,), (0,)), ((), ())), preferred_element_type=jnp.float32
            )
        out_ref[...] = total.astype(jnp.bfloat16)


def experts(x, tgt, gates, w_gate, w_up, w_down, first):
    local, width, hidden = w_gate.shape
    chunks, _, tokens = tgt.shape
    rows = tokens // 64 * CAP
    last = local - 1
    return pl.pallas_call(
        functools.partial(expert_kernel, local, rows, tokens),
        out_shape=jax.ShapeDtypeStruct(x.shape, jnp.bfloat16),
        grid=(local, chunks),
        in_specs=[
            pl.BlockSpec(memory_space=pltpu.SMEM),
            pl.BlockSpec((tokens, width), lambda e, c: (c, 0)),
            pl.BlockSpec((1, 2, tokens), lambda e, c: (c, 0, 0)),
            pl.BlockSpec((1, 2, tokens), lambda e, c: (c, 0, 0)),
            pl.BlockSpec((1, width, hidden), lambda e, c: (e, 0, 0)),
            pl.BlockSpec((1, width, hidden), lambda e, c: (e, 0, 0)),
            pl.BlockSpec((1, hidden, width), lambda e, c: (e, 0, 0)),
        ],
        out_specs=pl.BlockSpec((tokens, width), lambda e, c: (jnp.where(e == last, c, 0), 0)),
        scratch_shapes=[pltpu.VMEM((max(last, 1), chunks if last else 1, rows, width), jnp.bfloat16)],
        compiler_params=pltpu.CompilerParams(vmem_limit_bytes=58 * 1024 * 1024),
        cost_estimate=pl.CostEstimate(
            flops=6 * local * chunks * rows * width * hidden,
            bytes_accessed=6 * local * width * hidden + 6 * chunks * tokens * width,
            transcendentals=local * chunks * rows * hidden,
        ),
    )(first, x, tgt, gates, w_gate, w_up, w_down)


def body(
    n_seq,
    n_exp,
    query,
    key_value,
    residual,
    norm_gain,
    segment_ids,
    routes,
    gate_weights,
    page_table,
    w_gate,
    w_up,
    w_down,
):
    rows_dev, width = query.shape[1:]
    everyone = ("exp", "seq")
    group = segment_ids.shape[1]
    share, firsts, heads = head_ranges(width, n_seq)
    span = heads * HEAD_DIM

    flat = routes[0].reshape(rows_dev * 2)
    onehot = (flat[:, None] == jnp.arange(EXPERTS, dtype=jnp.int32)[None, :]).astype(jnp.int32)
    before = jnp.cumsum(onehot, axis=0) - onehot
    target = (flat * CAP + jnp.sum(before * onehot, axis=1)).reshape(rows_dev, 2)
    facts = jnp.concatenate([target.astype(jnp.float32), gate_weights[0]], axis=1).T
    facts = lax.all_gather(facts, everyone, axis=0, tiled=False)
    blocks = n_seq * n_exp
    facts = facts.reshape(blocks // CHUNK_BLOCKS, CHUNK_BLOCKS, 4, rows_dev).transpose(0, 2, 1, 3)
    facts = facts.reshape(blocks // CHUNK_BLOCKS, 4, CHUNK_BLOCKS * rows_dev)
    tgt = facts[:, :2].astype(jnp.int32)
    gates = facts[:, 2:]

    keys, values = key_value[0, :, 0], key_value[0, :, 1]

    def spans(a):
        return jnp.stack([a[:, f * HEAD_DIM : f * HEAD_DIM + span] for f in firsts])

    packed = jnp.concatenate([spans(query[0]), spans(keys), spans(values)], axis=2)
    packed = lax.all_to_all(packed, "seq", split_axis=0, concat_axis=0, tiled=True)
    packed = packed.reshape(group, 3 * span)
    context = attention(packed, segment_ids[0], heads)
    context = lax.all_to_all(
        context.reshape(n_seq, rows_dev, span), "seq", split_axis=0, concat_axis=0, tiled=True
    )
    offsets = [j * share - firsts[j] * HEAD_DIM for j in range(n_seq)]

    def unspan(a):
        return jnp.concatenate([a[j][..., offsets[j] : offsets[j] + share] for j in range(n_seq)], axis=-1)

    stream = residual[0].astype(jnp.float32) + unspan(context).astype(jnp.float32)
    normed = (
        stream
        * lax.rsqrt(jnp.mean(stream * stream, axis=-1, keepdims=True) + 1e-05)
        * norm_gain.astype(jnp.float32)
    ).astype(jnp.bfloat16)

    pages = packed[:, span:].reshape(group // PAGE, PAGE, 2 * span)
    slots = jnp.arange(group // PAGE, dtype=jnp.int32)
    order = jnp.sum(jnp.where(page_table[0][None, :] == slots[:, None], slots[None, :], 0), axis=1)
    pages = jnp.take(pages, order, axis=0)
    pages = pages.reshape(n_seq, rows_dev, 2 * span)
    pages = lax.all_to_all(pages, "seq", split_axis=0, concat_axis=0, tiled=True)
    cache = jnp.concatenate([unspan(pages[..., :span]), unspan(pages[..., span:])], axis=-1)
    cache = cache.reshape(1, rows_dev // PAGE, PAGE, 2 * width)

    everything = lax.all_gather(normed, everyone, axis=0, tiled=True)
    first = (lax.axis_index("exp") * (EXPERTS // n_exp)).astype(jnp.int32).reshape(1)
    partial = experts(everything, tgt, gates, w_gate, w_up, w_down, first)
    mixture = lax.psum_scatter(partial, everyone, scatter_dimension=0, tiled=True)
    layer_out = (stream + mixture.astype(jnp.float32)).astype(jnp.bfloat16)
    return (layer_out[None], cache)


def solution(mesh):
    in_specs = (
        P("exp", "seq", None),
        P("exp", "seq", None, None),
        P("exp", "seq", None),
        P(),
        P("exp", None),
        P("exp", "seq", None),
        P("exp", "seq", None),
        P("exp", None),
        P("exp", None, "seq"),
        P("exp", None, "seq"),
        P("exp", "seq", None),
    )
    out_specs = (P("exp", "seq", None), P("exp", "seq", None, None))
    run = functools.partial(body, mesh.shape["seq"], mesh.shape["exp"])
    return jax.shard_map(run, mesh=mesh, in_specs=in_specs, out_specs=out_specs, check_vma=False)
```

```python
import functools
import math

import jax
import jax.numpy as jnp
from jax import lax
from jax.experimental import pallas as pl
from jax.experimental.pallas import tpu as pltpu
from jax.sharding import PartitionSpec as P

HEADS = 36
HEAD_DIM = 64
EXPERTS = 8
PAGE = 16
CAP = 24
CHUNK_BLOCKS = 8


def head_ranges(width, n_seq):
    share = width // n_seq
    firsts = [j * share // HEAD_DIM for j in range(n_seq)]
    count = max(-(-(j + 1) * share // HEAD_DIM) - firsts[j] for j in range(n_seq))
    firsts = [min(f, HEADS - count) for f in firsts]
    return share, firsts, count


def attention_kernel(heads, q_rows, packed_ref, seg_row_ref, seg_col_ref, out_ref):
    total = packed_ref.shape[0]
    span = heads * HEAD_DIM
    scale = 1.0 / math.sqrt(HEAD_DIM)
    for start in range(0, total, q_rows):
        end = start + q_rows
        q_place = start + lax.broadcasted_iota(jnp.int32, (q_rows, end), 0)
        k_place = lax.broadcasted_iota(jnp.int32, (q_rows, end), 1)
        visible = (seg_col_ref[start:end, :] == seg_row_ref[:, :end]) & (k_place <= q_place)
        parts = []
        for h in range(heads):
            a = h * HEAD_DIM
            q = packed_ref[start:end, a : a + HEAD_DIM]
            k = packed_ref[:end, span + a : span + a + HEAD_DIM]
            v = packed_ref[:end, 2 * span + a : 2 * span + a + HEAD_DIM]
            s = lax.dot_general(q, k, (((1,), (1,)), ((), ())), preferred_element_type=jnp.float32)
            s = jnp.where(visible, s * scale, -1e30)
            top = jnp.max(s, axis=1, keepdims=True)
            p = jnp.exp(s - top)
            denominator = jnp.sum(p, axis=1, keepdims=True)
            o = jnp.dot(p.astype(jnp.bfloat16), v, preferred_element_type=jnp.float32)
            parts.append((o / denominator).astype(jnp.bfloat16))
        out_ref[start:end, :] = jnp.concatenate(parts, axis=1)


def attention(packed, segments, heads):
    total = packed.shape[0]
    span = heads * HEAD_DIM
    return pl.pallas_call(
        functools.partial(attention_kernel, heads, 128),
        out_shape=jax.ShapeDtypeStruct((total, span), jnp.bfloat16),
        compiler_params=pltpu.CompilerParams(vmem_limit_bytes=40 * 1024 * 1024),
        cost_estimate=pl.CostEstimate(
            flops=4 * total * total * span, bytes_accessed=8 * total * span, transcendentals=total * total * heads
        ),
    )(packed, segments[None, :], segments[:, None])


def dot_t(a, b):
    return lax.dot_general(a, b, (((1,), (1,)), ((), ())), preferred_element_type=jnp.float32)


def expert_kernel(
    local, rows, tokens, first_ref, x_ref, tgt_ref, gates_ref, wg_ref, wu_ref, wd_ref, out_ref, kept_ref
):
    le = pl.program_id(0)
    chunk = pl.program_id(1)

    def selection(which):
        base = (first_ref[0] + which) * CAP
        row_id = lax.broadcasted_iota(jnp.int32, (rows, tokens), 0)
        block = lax.broadcasted_iota(jnp.int32, (1, tokens), 1) // 64
        picks, weights = None, None
        for j in range(2):
            slot = tgt_ref[0, j : j + 1, :] - base
            place = jnp.where((slot >= 0) & (slot < CAP), block * CAP + slot, -1)
            hit = row_id == place
            gate = jnp.where(hit, gates_ref[0, j : j + 1, :], 0.0)
            picks = hit if picks is None else picks | hit
            weights = gate if weights is None else weights + gate
        return picks.astype(jnp.float32).astype(jnp.bfloat16), jnp.sum(weights, axis=1, keepdims=True)

    pick, weight = selection(le)
    chosen = jnp.dot(pick, x_ref[...], preferred_element_type=jnp.float32).astype(jnp.bfloat16)
    gate = dot_t(chosen, wg_ref[0])
    upper = dot_t(chosen, wu_ref[0])
    hidden = (gate / (1.0 + jnp.exp(-gate)) * upper).astype(jnp.bfloat16)
    y = jnp.dot(hidden, wd_ref[0], preferred_element_type=jnp.float32)
    y = (y * weight).astype(jnp.bfloat16)

    if local > 1:

        @pl.when(le < local - 1)
        def _():
            kept_ref[le, chunk] = y

    @pl.when(le == local - 1)
    def _():
        total = lax.dot_general(pick, y, (((0,), (0,)), ((), ())), preferred_element_type=jnp.float32)
        for other in range(local - 1):
            pick_o, _ = selection(other)
            total += lax.dot_general(
                pick_o, kept_ref[other, chunk], (((0,), (0,)), ((), ())), preferred_element_type=jnp.float32
            )
        out_ref[...] = total.astype(jnp.bfloat16)


def experts(x, tgt, gates, w_gate, w_up, w_down, first):
    local, hidden, width = w_gate.shape
    chunks, _, tokens = tgt.shape
    rows = tokens // 64 * CAP
    last = local - 1
    return pl.pallas_call(
        functools.partial(expert_kernel, local, rows, tokens),
        out_shape=jax.ShapeDtypeStruct(x.shape, jnp.bfloat16),
        grid=(local, chunks),
        in_specs=[
            pl.BlockSpec(memory_space=pltpu.SMEM),
            pl.BlockSpec((tokens, width), lambda e, c: (c, 0)),
            pl.BlockSpec((1, 2, tokens), lambda e, c: (c, 0, 0)),
            pl.BlockSpec((1, 2, tokens), lambda e, c: (c, 0, 0)),
            pl.BlockSpec((1, hidden, width), lambda e, c: (e, 0, 0)),
            pl.BlockSpec((1, hidden, width), lambda e, c: (e, 0, 0)),
            pl.BlockSpec((1, hidden, width), lambda e, c: (e, 0, 0)),
        ],
        out_specs=pl.BlockSpec((tokens, width), lambda e, c: (jnp.where(e == last, c, 0), 0)),
        scratch_shapes=[pltpu.VMEM((max(last, 1), chunks if last else 1, rows, width), jnp.bfloat16)],
        compiler_params=pltpu.CompilerParams(vmem_limit_bytes=58 * 1024 * 1024),
        cost_estimate=pl.CostEstimate(
            flops=6 * local * chunks * rows * width * hidden,
            bytes_accessed=6 * local * width * hidden + 6 * chunks * tokens * width,
            transcendentals=local * chunks * rows * hidden,
        ),
    )(first, x, tgt, gates, w_gate, w_up, w_down)


def chunk_kernel(
    local, pieces, rows, tokens, parts, first_ref, row_ref, col_ref, wg_ref, wu_ref, wd_ref, *rest
):
    piece_refs = rest[:pieces]
    keep_ref, send_ref, chosen_ref, sum_ref, y_ref = rest[pieces:]
    le = pl.program_id(0)
    part = pl.program_id(1)
    rows_dev = tokens // pieces

    @pl.when(part == 0)
    def _():
        base = (first_ref[0] + le) * CAP
        row_id = lax.broadcasted_iota(jnp.int32, (rows, tokens), 0)
        shift = lax.broadcasted_iota(jnp.int32, (1, tokens), 1) // rows_dev * CAP
        pick = None
        for j in range(2):
            slot = row_ref[j : j + 1, :].astype(jnp.int32) - base
            hit = row_id == jnp.where((slot >= 0) & (slot < CAP), shift + slot, -1)
            pick = hit if pick is None else pick | hit
        x = jnp.concatenate([p[...] for p in piece_refs], axis=0)
        pick = pick.astype(jnp.float32).astype(jnp.bfloat16)
        chosen_ref[...] = jnp.dot(pick, x, preferred_element_type=jnp.float32).astype(jnp.bfloat16)

    chosen = chosen_ref[...]
    gate = dot_t(chosen, wg_ref[0])
    upper = dot_t(chosen, wu_ref[0])
    hidden = (gate / (1.0 + jnp.exp(-gate)) * upper).astype(jnp.bfloat16)
    y = jnp.dot(hidden, wd_ref[0], preferred_element_type=jnp.float32)

    @pl.when(part == 0)
    def _():
        sum_ref[...] = y

    @pl.when((part > 0) & (part < parts - 1))
    def _():
        sum_ref[...] += y

    @pl.when(part == parts - 1)
    def _():
        base = (first_ref[0] + le) * CAP
        row_id = lax.broadcasted_iota(jnp.int32, (rows, tokens), 0)
        shift = lax.broadcasted_iota(jnp.int32, (1, tokens), 1) // rows_dev * CAP
        weights = jnp.zeros((rows, tokens), jnp.float32)
        for j in range(2):
            slot = row_ref[j : j + 1, :].astype(jnp.int32) - base
            hit = row_id == jnp.where((slot >= 0) & (slot < CAP), shift + slot, -1)
            weights = weights + jnp.where(hit, row_ref[2 + j : 3 + j, :], 0.0)
        weight = jnp.sum(weights, axis=1, keepdims=True)
        y_ref[pl.ds(pl.multiple_of(le * rows, rows), rows), :] = ((sum_ref[...] + y) * weight).astype(jnp.bfloat16)

    @pl.when((part == parts - 1) & (le == local - 1))
    def _():
        lane = lax.broadcasted_iota(jnp.int32, (tokens, local * rows), 1)
        shift = lax.broadcasted_iota(jnp.int32, (tokens, 1), 0) // rows_dev * CAP
        place = None
        for e in range(local):
            base = (first_ref[0] + e) * CAP
            for j in range(2):
                slot = col_ref[:, j : j + 1].astype(jnp.int32) - base
                hit = lane == jnp.where((slot >= 0) & (slot < CAP), e * rows + shift + slot, -1)
                place = hit if place is None else place | hit
        place = place.astype(jnp.float32).astype(jnp.bfloat16)
        half = tokens // 2
        keep_ref[...] = jnp.dot(place[:half], y_ref[...], preferred_element_type=jnp.float32).astype(jnp.bfloat16)
        send_ref[...] = jnp.dot(place[half:], y_ref[...], preferred_element_type=jnp.float32).astype(jnp.bfloat16)


def chunk_experts(pieces, facts, w_gate, w_up, w_down, first):
    local, hidden, width = w_gate.shape
    tokens = facts.shape[1]
    rows = len(pieces) * CAP
    parts = 3
    step = hidden // parts
    whole = lambda e, f: (0, 0)
    weights = pl.BlockSpec((1, step, width), lambda e, f: (e, f, 0))
    piece = pl.BlockSpec(pieces[0].shape, whole)
    half = jax.ShapeDtypeStruct((tokens // 2, width), jnp.bfloat16)
    return pl.pallas_call(
        functools.partial(chunk_kernel, local, len(pieces), rows, tokens, parts),
        out_shape=(half, half),
        grid=(local, parts),
        in_specs=[
            pl.BlockSpec(memory_space=pltpu.SMEM),
            pl.BlockSpec((4, tokens), whole),
            pl.BlockSpec((tokens, 4), whole),
            weights,
            weights,
            weights,
        ]
        + [piece] * len(pieces),
        out_specs=(pl.BlockSpec(half.shape, whole), pl.BlockSpec(half.shape, whole)),
        scratch_shapes=[
            pltpu.VMEM((rows, width), jnp.bfloat16),
            pltpu.VMEM((rows, width), jnp.float32),
            pltpu.VMEM((local * rows, width), jnp.bfloat16),
        ],
        compiler_params=pltpu.CompilerParams(vmem_limit_bytes=48 * 1024 * 1024),
        cost_estimate=pl.CostEstimate(
            flops=6 * local * rows * width * hidden,
            bytes_accessed=6 * local * width * hidden + 4 * tokens * width,
            transcendentals=local * rows * hidden,
        ),
    )(first, facts, facts.T, w_gate, w_up, w_down, *pieces)


def swap(a, axis, size, distance):
    return lax.ppermute(a, axis, [(i, i ^ distance) for i in range(size)])


def add(a, b):
    return (a.astype(jnp.float32) + b.astype(jnp.float32)).astype(jnp.bfloat16)


def exchange_experts(normed, facts, w_gate, w_up, w_down, first, n_seq, n_exp):
    rows_dev, width = normed.shape
    over = {
        "x": lambda a: swap(a, "seq", n_seq, 1),
        "y": lambda a: swap(a, "exp", n_exp, 2),
        "c": lambda a: swap(a, "exp", n_exp, 1),
    }
    distance = {"x": (0, 1), "y": (2, 0), "c": (1, 0)}
    me_seq, me_exp = lax.axis_index("seq"), lax.axis_index("exp")
    depth = n_seq // 2
    mixture = None
    starts = [normed] + [swap(normed, "seq", n_seq, 2 * k) for k in range(1, depth)]
    chunks = []
    for k in range(depth):
        f, g = ("x", "y") if k % 2 == 0 else ("y", "x")
        by_f, by_g = over[f](starts[k]), over[g](starts[k])
        pieces = [starts[k], by_g, by_f, over[g](by_f)]
        pieces = pieces + [over["c"](p) for p in pieces]
        hops = [(0, 0), distance[g], distance[f], tuple(i + j for i, j in zip(distance[f], distance[g]))]
        hops = hops + [(i + 1, j) for i, j in hops]
        ids = jnp.stack([(me_exp ^ i) * n_seq + (me_seq ^ (j + 2 * k)) for i, j in hops])
        here = jnp.take(facts, ids, axis=0).transpose(1, 0, 2).reshape(4, len(pieces) * rows_dev)
        chunks.append((f, g, pieces, here))
    for k, (f, g, pieces, here) in enumerate(chunks):
        keep, send = chunk_experts(pieces, here, w_gate, w_up, w_down, first)
        two = 2 * rows_dev
        got = over["c"](send)
        keep, send = add(keep[:two], got[:two]), add(keep[two:], got[two:])
        got = over[f](send)
        keep, send = add(keep[:rows_dev], got[:rows_dev]), add(keep[rows_dev:], got[rows_dev:])
        done = add(keep, over[g](send))
        if k > 0:
            done = swap(done, "seq", n_seq, 2 * k)
        mixture = done.astype(jnp.float32) if mixture is None else mixture + done.astype(jnp.float32)
    return mixture


def body(
    n_seq,
    n_exp,
    query,
    key_value,
    residual,
    norm_gain,
    segment_ids,
    routes,
    gate_weights,
    page_table,
    w_gate,
    w_up,
    w_down,
):
    rows_dev, width = query.shape[1:]
    everyone = ("exp", "seq")
    group = segment_ids.shape[1]
    share, firsts, heads = head_ranges(width, n_seq)
    span = heads * HEAD_DIM

    flat = routes[0].reshape(rows_dev * 2)
    onehot = (flat[:, None] == jnp.arange(EXPERTS, dtype=jnp.int32)[None, :]).astype(jnp.int32)
    before = jnp.cumsum(onehot, axis=0) - onehot
    target = (flat * CAP + jnp.sum(before * onehot, axis=1)).reshape(rows_dev, 2)
    facts = jnp.concatenate([target.astype(jnp.float32), gate_weights[0]], axis=1).T
    facts = lax.all_gather(facts, everyone, axis=0, tiled=False)
    blocks = n_seq * n_exp

    keys, values = key_value[0, :, 0], key_value[0, :, 1]

    def spans(a):
        return jnp.stack([a[:, f * HEAD_DIM : f * HEAD_DIM + span] for f in firsts])

    packed = jnp.concatenate([spans(query[0]), spans(keys), spans(values)], axis=2)
    packed = lax.all_to_all(packed, "seq", split_axis=0, concat_axis=0, tiled=True)
    packed = packed.reshape(group, 3 * span)
    context = attention(packed, segment_ids[0], heads)
    context = lax.all_to_all(
        context.reshape(n_seq, rows_dev, span), "seq", split_axis=0, concat_axis=0, tiled=True
    )
    offsets = [j * share - firsts[j] * HEAD_DIM for j in range(n_seq)]

    def unspan(a):
        return jnp.concatenate([a[j][..., offsets[j] : offsets[j] + share] for j in range(n_seq)], axis=-1)

    stream = residual[0].astype(jnp.float32) + unspan(context).astype(jnp.float32)
    normed = (
        stream
        * lax.rsqrt(jnp.mean(stream * stream, axis=-1, keepdims=True) + 1e-05)
        * norm_gain.astype(jnp.float32)
    ).astype(jnp.bfloat16)

    pages = packed[:, span:].reshape(group // PAGE, PAGE, 2 * span)
    slots = jnp.arange(group // PAGE, dtype=jnp.int32)
    order = jnp.sum(jnp.where(page_table[0][None, :] == slots[:, None], slots[None, :], 0), axis=1)
    pages = jnp.take(pages, order, axis=0)
    pages = pages.reshape(n_seq, rows_dev, 2 * span)
    if n_seq == 8:
        others = lax.axis_index("seq") ^ jnp.arange(n_seq, dtype=jnp.int32)
        pages = jnp.take(pages, others, axis=0)
        pages = jnp.stack([pages[0]] + [swap(pages[j], "seq", n_seq, j) for j in range(1, n_seq)])
        pages = jnp.take(pages, others, axis=0)
    else:
        pages = lax.all_to_all(pages, "seq", split_axis=0, concat_axis=0, tiled=True)
    cache = jnp.concatenate([unspan(pages[..., :span]), unspan(pages[..., span:])], axis=-1)
    cache = cache.reshape(1, rows_dev // PAGE, PAGE, 2 * width)

    first = (lax.axis_index("exp") * (EXPERTS // n_exp)).astype(jnp.int32).reshape(1)
    w_gate, w_up = jnp.swapaxes(w_gate, 1, 2), jnp.swapaxes(w_up, 1, 2)
    if (n_seq, n_exp) == (8, 4):
        mixture = exchange_experts(normed, facts, w_gate, w_up, w_down, first, n_seq, n_exp)
    else:
        everything = lax.all_gather(normed, everyone, axis=0, tiled=True)
        facts = facts.reshape(blocks // CHUNK_BLOCKS, CHUNK_BLOCKS, 4, rows_dev).transpose(0, 2, 1, 3)
        facts = facts.reshape(blocks // CHUNK_BLOCKS, 4, CHUNK_BLOCKS * rows_dev)
        partial = experts(
            everything, facts[:, :2].astype(jnp.int32), facts[:, 2:], w_gate, w_up, w_down, first
        )
        mixture = lax.psum_scatter(partial, everyone, scatter_dimension=0, tiled=True).astype(jnp.float32)
    layer_out = (stream + mixture).astype(jnp.bfloat16)
    return (layer_out[None], cache)


def solution(mesh):
    in_specs = (
        P("exp", "seq", None),
        P("exp", "seq", None, None),
        P("exp", "seq", None),
        P(),
        P("exp", None),
        P("exp", "seq", None),
        P("exp", "seq", None),
        P("exp", None),
        P("exp", None, "seq"),
        P("exp", None, "seq"),
        P("exp", "seq", None),
    )
    out_specs = (P("exp", "seq", None), P("exp", "seq", None, None))
    run = functools.partial(body, mesh.shape["seq"], mesh.shape["exp"])
    return jax.shard_map(run, mesh=mesh, in_specs=in_specs, out_specs=out_specs, check_vma=False)
```

```python
import functools
import math

import jax
import jax.numpy as jnp
from jax import lax
from jax.experimental import pallas as pl
from jax.experimental.pallas import tpu as pltpu
from jax.sharding import PartitionSpec as P

HEADS = 36
HEAD_DIM = 64
EXPERTS = 8
PAGE = 16
CAP = 24
CHUNK_BLOCKS = 8


def head_ranges(width, n_seq):
    share = width // n_seq
    firsts = [j * share // HEAD_DIM for j in range(n_seq)]
    count = max(-(-(j + 1) * share // HEAD_DIM) - firsts[j] for j in range(n_seq))
    firsts = [min(f, HEADS - count) for f in firsts]
    return share, firsts, count


def attention_kernel(heads, q_rows, packed_ref, seg_row_ref, seg_col_ref, out_ref):
    total = packed_ref.shape[0]
    span = heads * HEAD_DIM
    scale = 1.0 / math.sqrt(HEAD_DIM)
    for start in range(0, total, q_rows):
        end = start + q_rows
        q_place = start + lax.broadcasted_iota(jnp.int32, (q_rows, end), 0)
        k_place = lax.broadcasted_iota(jnp.int32, (q_rows, end), 1)
        visible = (seg_col_ref[start:end, :] == seg_row_ref[:, :end]) & (k_place <= q_place)
        parts = []
        for h in range(heads):
            a = h * HEAD_DIM
            q = packed_ref[start:end, a : a + HEAD_DIM]
            k = packed_ref[:end, span + a : span + a + HEAD_DIM]
            v = packed_ref[:end, 2 * span + a : 2 * span + a + HEAD_DIM]
            s = lax.dot_general(q, k, (((1,), (1,)), ((), ())), preferred_element_type=jnp.float32)
            s = jnp.where(visible, s * scale, -1e30)
            top = jnp.max(s, axis=1, keepdims=True)
            p = jnp.exp(s - top)
            denominator = jnp.sum(p, axis=1, keepdims=True)
            o = jnp.dot(p.astype(jnp.bfloat16), v, preferred_element_type=jnp.float32)
            parts.append((o / denominator).astype(jnp.bfloat16))
        out_ref[start:end, :] = jnp.concatenate(parts, axis=1)


def attention(packed, segments, heads):
    total = packed.shape[0]
    span = heads * HEAD_DIM
    return pl.pallas_call(
        functools.partial(attention_kernel, heads, 128),
        out_shape=jax.ShapeDtypeStruct((total, span), jnp.bfloat16),
        compiler_params=pltpu.CompilerParams(vmem_limit_bytes=40 * 1024 * 1024),
        cost_estimate=pl.CostEstimate(
            flops=4 * total * total * span, bytes_accessed=8 * total * span, transcendentals=total * total * heads
        ),
    )(packed, segments[None, :], segments[:, None])


def dot_t(a, b):
    return lax.dot_general(a, b, (((1,), (1,)), ((), ())), preferred_element_type=jnp.float32)


def expert_kernel(
    local, rows, tokens, first_ref, x_ref, tgt_ref, gates_ref, wg_ref, wu_ref, wd_ref, out_ref, kept_ref
):
    le = pl.program_id(0)
    chunk = pl.program_id(1)

    def selection(which):
        base = (first_ref[0] + which) * CAP
        row_id = lax.broadcasted_iota(jnp.int32, (rows, tokens), 0)
        block = lax.broadcasted_iota(jnp.int32, (1, tokens), 1) // 64
        picks, weights = None, None
        for j in range(2):
            slot = tgt_ref[0, j : j + 1, :] - base
            place = jnp.where((slot >= 0) & (slot < CAP), block * CAP + slot, -1)
            hit = row_id == place
            gate = jnp.where(hit, gates_ref[0, j : j + 1, :], 0.0)
            picks = hit if picks is None else picks | hit
            weights = gate if weights is None else weights + gate
        return picks.astype(jnp.float32).astype(jnp.bfloat16), jnp.sum(weights, axis=1, keepdims=True)

    pick, weight = selection(le)
    chosen = jnp.dot(pick, x_ref[...], preferred_element_type=jnp.float32).astype(jnp.bfloat16)
    gate = dot_t(chosen, wg_ref[0])
    upper = dot_t(chosen, wu_ref[0])
    hidden = (gate / (1.0 + jnp.exp(-gate)) * upper).astype(jnp.bfloat16)
    y = jnp.dot(hidden, wd_ref[0], preferred_element_type=jnp.float32)
    y = (y * weight).astype(jnp.bfloat16)

    if local > 1:

        @pl.when(le < local - 1)
        def _():
            kept_ref[le, chunk] = y

    @pl.when(le == local - 1)
    def _():
        total = lax.dot_general(pick, y, (((0,), (0,)), ((), ())), preferred_element_type=jnp.float32)
        for other in range(local - 1):
            pick_o, _ = selection(other)
            total += lax.dot_general(
                pick_o, kept_ref[other, chunk], (((0,), (0,)), ((), ())), preferred_element_type=jnp.float32
            )
        out_ref[...] = total.astype(jnp.bfloat16)


def experts(x, tgt, gates, w_gate, w_up, w_down, first):
    local, hidden, width = w_gate.shape
    chunks, _, tokens = tgt.shape
    rows = tokens // 64 * CAP
    last = local - 1
    return pl.pallas_call(
        functools.partial(expert_kernel, local, rows, tokens),
        out_shape=jax.ShapeDtypeStruct(x.shape, jnp.bfloat16),
        grid=(local, chunks),
        in_specs=[
            pl.BlockSpec(memory_space=pltpu.SMEM),
            pl.BlockSpec((tokens, width), lambda e, c: (c, 0)),
            pl.BlockSpec((1, 2, tokens), lambda e, c: (c, 0, 0)),
            pl.BlockSpec((1, 2, tokens), lambda e, c: (c, 0, 0)),
            pl.BlockSpec((1, hidden, width), lambda e, c: (e, 0, 0)),
            pl.BlockSpec((1, hidden, width), lambda e, c: (e, 0, 0)),
            pl.BlockSpec((1, hidden, width), lambda e, c: (e, 0, 0)),
        ],
        out_specs=pl.BlockSpec((tokens, width), lambda e, c: (jnp.where(e == last, c, 0), 0)),
        scratch_shapes=[pltpu.VMEM((max(last, 1), chunks if last else 1, rows, width), jnp.bfloat16)],
        compiler_params=pltpu.CompilerParams(vmem_limit_bytes=58 * 1024 * 1024),
        cost_estimate=pl.CostEstimate(
            flops=6 * local * chunks * rows * width * hidden,
            bytes_accessed=6 * local * width * hidden + 6 * chunks * tokens * width,
            transcendentals=local * chunks * rows * hidden,
        ),
    )(first, x, tgt, gates, w_gate, w_up, w_down)


def norm_kernel(share, offsets, context_ref, residual_ref, gain_ref, facts_ref, stream_ref, piece_ref):
    n_seq, _, _ = context_ref.shape
    width = residual_ref.shape[1]
    parts = [context_ref[j][:, offsets[j] : offsets[j] + share] for j in range(n_seq)]
    context = jnp.concatenate(parts, axis=1).astype(jnp.float32)
    stream = residual_ref[...].astype(jnp.float32) + context
    stream_ref[...] = stream
    mean = jnp.mean(stream * stream, axis=1, keepdims=True)
    normed = stream * lax.rsqrt(mean + 1e-05) * gain_ref[...].astype(jnp.float32)
    piece_ref[:, :width] = normed.astype(jnp.bfloat16)
    facts = facts_ref[...]
    lane = lax.broadcasted_iota(jnp.int32, facts.shape, 1)
    high = facts.astype(jnp.bfloat16).astype(jnp.float32)
    middle = (facts - high).astype(jnp.bfloat16).astype(jnp.float32)
    low = facts - high - middle
    own = jnp.where(lane < 4, high, jnp.where(lane < 6, middle, low))
    piece_ref[:, width:] = own.astype(jnp.bfloat16)


def norm_tokens(context, residual, gain, facts, share, offsets):
    rows_dev, width = residual.shape
    return pl.pallas_call(
        functools.partial(norm_kernel, share, offsets),
        out_shape=(
            jax.ShapeDtypeStruct((rows_dev, width), jnp.float32),
            jax.ShapeDtypeStruct((rows_dev, width + facts.shape[1]), jnp.bfloat16),
        ),
        cost_estimate=pl.CostEstimate(
            flops=10 * rows_dev * width, bytes_accessed=10 * rows_dev * width, transcendentals=rows_dev
        ),
    )(context, residual, gain[None, :], facts)


def pick_pages_kernel(per_device, first_lane, order_ref, me_ref, packed_ref, late_ref, *out_refs):
    del late_ref
    for j, out_ref in enumerate(out_refs):
        peer = jnp.bitwise_xor(me_ref[0], j)
        for i in range(per_device):
            page = order_ref[peer * per_device + i]
            rows = pl.ds(pl.multiple_of(page * PAGE, PAGE), PAGE)
            out_ref[i * PAGE : (i + 1) * PAGE, :] = packed_ref[rows, first_lane:]


def pick_pages(packed, order, me, late, n_seq, span):
    rows = packed.shape[0] // n_seq
    smem = pl.BlockSpec(memory_space=pltpu.SMEM)
    vmem = pl.BlockSpec(memory_space=pltpu.VMEM)
    out = jax.ShapeDtypeStruct((rows, 2 * span), jnp.bfloat16)
    return pl.pallas_call(
        functools.partial(pick_pages_kernel, rows // PAGE, span),
        out_shape=(out,) * n_seq,
        in_specs=[smem, smem, vmem, pl.BlockSpec(memory_space=pl.ANY)],
        cost_estimate=pl.CostEstimate(flops=0, bytes_accessed=10 * packed.shape[0] * span, transcendentals=0),
    )(order, me, packed, late)


def join_pages_kernel(share, offsets, span, me_ref, *refs):
    piece_refs, out_ref, all_ref = refs[:-2], refs[-2], refs[-1]
    for j, ref in enumerate(piece_refs):
        all_ref[jnp.bitwise_xor(me_ref[0], j)] = ref[...]
    for part in range(2):
        parts = [
            all_ref[j][:, part * span + offsets[j] : part * span + offsets[j] + share]
            for j in range(len(piece_refs))
        ]
        width = share * len(piece_refs)
        out_ref[:, part * width : (part + 1) * width] = jnp.concatenate(parts, axis=1)


def join_pages(pieces, me, share, offsets, span):
    rows = pieces[0].shape[0]
    n_seq = len(pieces)
    return pl.pallas_call(
        functools.partial(join_pages_kernel, share, offsets, span),
        out_shape=jax.ShapeDtypeStruct((rows, 2 * share * n_seq), jnp.bfloat16),
        in_specs=[pl.BlockSpec(memory_space=pltpu.SMEM)] + [pl.BlockSpec(memory_space=pltpu.VMEM)] * n_seq,
        scratch_shapes=[pltpu.VMEM((n_seq,) + pieces[0].shape, jnp.bfloat16)],
        cost_estimate=pl.CostEstimate(flops=0, bytes_accessed=8 * rows * n_seq * span, transcendentals=0),
    )(me, *pieces)


def places_of(slots, base, shift):
    place = -1
    for slot in slots:
        slot = slot.astype(jnp.int32) - base
        place = jnp.where((slot >= 0) & (slot < CAP), shift + slot, place)
    return place


def chunk_kernel(local, pieces, rows, tokens, parts, waits, first_ref, wg_ref, wu_ref, wd_ref, *rest):
    piece_refs = rest[:pieces]
    keep_ref, send_ref, chosen_ref, weight_ref, sum_ref, y_ref = rest[pieces + waits :]
    le = pl.program_id(0)
    part = pl.program_id(1)
    rows_dev = tokens // pieces
    width = wd_ref.shape[2]

    @pl.when(part == 0)
    def _():
        base = (first_ref[0] + le) * CAP
        facts = jnp.concatenate([p[:, width:] for p in piece_refs], axis=0)
        unit = lax.broadcasted_iota(jnp.int32, (8, 128), 0) == lax.broadcasted_iota(jnp.int32, (8, 128), 1)
        facts = dot_t(unit.astype(jnp.float32).astype(jnp.bfloat16), facts)
        shift = lax.broadcasted_iota(jnp.int32, (1, tokens), 1) // rows_dev * CAP
        row_id = lax.broadcasted_iota(jnp.int32, (rows, tokens), 0)
        pick, weights = None, None
        for j in range(2):
            hit = row_id == places_of([facts[j : j + 1]], base, shift)
            gate = facts[2 + j : 3 + j] + facts[4 + j : 5 + j] + facts[6 + j : 7 + j]
            weight = jnp.where(hit, gate, 0.0)
            pick = hit if pick is None else pick | hit
            weights = weight if weights is None else weights + weight
        weight_ref[...] = jnp.sum(weights, axis=1, keepdims=True)
        pick = pick.astype(jnp.float32).astype(jnp.bfloat16)
        x = jnp.concatenate([p[:, :width] for p in piece_refs], axis=0)
        chosen = jnp.dot(pick, x, preferred_element_type=jnp.float32)
        chosen_ref[...] = chosen.T.astype(jnp.bfloat16)

    chosen = chosen_ref[...]
    gate = jnp.dot(wg_ref[0], chosen, preferred_element_type=jnp.float32)
    upper = jnp.dot(wu_ref[0], chosen, preferred_element_type=jnp.float32)
    hidden = (gate / (1.0 + jnp.exp(-gate)) * upper).T.astype(jnp.bfloat16)
    y = jnp.dot(hidden, wd_ref[0], preferred_element_type=jnp.float32)

    @pl.when(part == 0)
    def _():
        sum_ref[...] = y

    @pl.when((part > 0) & (part < parts - 1))
    def _():
        sum_ref[...] += y

    @pl.when(part == parts - 1)
    def _():
        here = pl.ds(pl.multiple_of(le * rows, rows), rows)
        y_ref[here, :] = ((sum_ref[...] + y) * weight_ref[...]).astype(jnp.bfloat16)

    @pl.when((part == parts - 1) & (le == local - 1))
    def _():
        facts = jnp.concatenate([p[:, width:] for p in piece_refs], axis=0).astype(jnp.float32)
        shift = lax.broadcasted_iota(jnp.int32, (tokens, 1), 0) // rows_dev * CAP
        lane = lax.broadcasted_iota(jnp.int32, (tokens, local * rows), 1)
        put = None
        for e in range(local):
            base = (first_ref[0] + e) * CAP
            hit = lane == places_of([facts[:, j : j + 1] for j in range(2)], base, shift + e * rows)
            put = hit if put is None else put | hit
        put = put.astype(jnp.float32).astype(jnp.bfloat16)
        half = tokens // 2
        keep_ref[...] = jnp.dot(put[:half], y_ref[...], preferred_element_type=jnp.float32).astype(jnp.bfloat16)
        send_ref[...] = jnp.dot(put[half:], y_ref[...], preferred_element_type=jnp.float32).astype(jnp.bfloat16)


def chunk_experts(pieces, w_gate, w_up, w_down, first, waits):
    local, hidden, width = w_gate.shape
    rows_dev = pieces[0].shape[0]
    tokens = rows_dev * len(pieces)
    rows = len(pieces) * CAP
    parts = 3
    step = hidden // parts
    whole = lambda e, f: (0, 0)
    weights = pl.BlockSpec((1, step, width), lambda e, f: (e, f, 0))
    piece = pl.BlockSpec(pieces[0].shape, whole)
    half = jax.ShapeDtypeStruct((tokens // 2, width), jnp.bfloat16)
    return pl.pallas_call(
        functools.partial(chunk_kernel, local, len(pieces), rows, tokens, parts, len(waits)),
        out_shape=(half, half),
        grid=(local, parts),
        in_specs=[pl.BlockSpec(memory_space=pltpu.SMEM), weights, weights, weights]
        + [piece] * len(pieces)
        + [pl.BlockSpec(memory_space=pl.ANY)] * len(waits),
        out_specs=(pl.BlockSpec(half.shape, whole), pl.BlockSpec(half.shape, whole)),
        scratch_shapes=[
            pltpu.VMEM((width, rows), jnp.bfloat16),
            pltpu.VMEM((rows, 1), jnp.float32),
            pltpu.VMEM((rows, width), jnp.float32),
            pltpu.VMEM((local * rows, width), jnp.bfloat16),
        ],
        compiler_params=pltpu.CompilerParams(vmem_limit_bytes=32 * 1024 * 1024),
        cost_estimate=pl.CostEstimate(
            flops=6 * local * rows * width * hidden,
            bytes_accessed=6 * local * width * hidden + 4 * tokens * width,
            transcendentals=local * rows * hidden,
        ),
    )(first, w_gate, w_up, w_down, *pieces, *waits)


def swap(a, axis, size, distance):
    return lax.ppermute(a, axis, [(i, i ^ distance) for i in range(size)])


def add(a, b):
    return (a.astype(jnp.float32) + b.astype(jnp.float32)).astype(jnp.bfloat16)


def exchange_experts(piece, w_gate, w_up, w_down, first, n_seq, n_exp, late_work):
    one = piece.shape[0]
    two = 2 * one
    over = {
        "x": lambda a: swap(a, "seq", n_seq, 1),
        "y": lambda a: swap(a, "exp", n_exp, 2),
        "c": lambda a: swap(a, "exp", n_exp, 1),
    }
    depth = n_seq // 2
    axes = [("x", "y") if k % 2 == 0 else ("y", "x") for k in range(depth)]
    starts = [piece] + [swap(piece, "seq", n_seq, 2 * k) for k in range(1, depth)]
    gathered = []
    for k, (f, g) in enumerate(axes):
        by_f, by_g = over[f](starts[k]), over[g](starts[k])
        near = [starts[k], by_g, by_f, over[g](by_f)]
        gathered.append(near + [over["c"](p) for p in near])

    kept, sent, lag = [None] * depth, [None] * depth, [None] * depth

    def after_core(k):
        got = over["c"](sent[k])
        kept[k], sent[k] = add(kept[k][:two], got[:two]), add(kept[k][two:], got[two:])

    def after_first(k):
        got = over[axes[k][0]](sent[k])
        kept[k], sent[k] = add(kept[k][:one], got[:one]), add(kept[k][one:], got[one:])

    def after_second(k):
        done = add(kept[k], over[axes[k][1]](sent[k]))
        kept[k] = swap(done, "seq", n_seq, 2 * k) if k else done

    steps = [after_core, after_first, after_second]
    other = None
    for turn in range(depth + len(steps)):
        for late, stage in enumerate(steps):
            k = turn - 2 - late
            if 0 <= k < depth:
                stage(k)
        if turn < depth:
            waits = [sent[k] for k in range(max(turn - 3, 0), turn - 1)]
            kept[turn], sent[turn] = chunk_experts(gathered[turn], w_gate, w_up, w_down, first, waits)
        if turn == 1:
            other = late_work(sent[0])
    for late, stage in enumerate(steps):
        for k in range(depth):
            if depth + len(steps) - 1 - 2 - late < k:
                stage(k)
    mixture = sum(k.astype(jnp.float32) for k in kept)
    return mixture, other


def body(
    n_seq,
    n_exp,
    query,
    key_value,
    residual,
    norm_gain,
    segment_ids,
    routes,
    gate_weights,
    page_table,
    w_gate,
    w_up,
    w_down,
):
    rows_dev, width = query.shape[1:]
    everyone = ("exp", "seq")
    group = segment_ids.shape[1]
    share, firsts, heads = head_ranges(width, n_seq)
    span = heads * HEAD_DIM

    flat = routes[0].reshape(rows_dev * 2)
    onehot = (flat[:, None] == jnp.arange(EXPERTS, dtype=jnp.int32)[None, :]).astype(jnp.int32)
    before = jnp.cumsum(onehot, axis=0) - onehot
    target = (flat * CAP + jnp.sum(before * onehot, axis=1)).reshape(rows_dev, 2).astype(jnp.float32)

    keys, values = key_value[0, :, 0], key_value[0, :, 1]

    def spans(a):
        return jnp.stack([a[:, f * HEAD_DIM : f * HEAD_DIM + span] for f in firsts])

    packed = jnp.concatenate([spans(query[0]), spans(keys), spans(values)], axis=2)
    packed = lax.all_to_all(packed, "seq", split_axis=0, concat_axis=0, tiled=True)
    packed = packed.reshape(group, 3 * span)
    context = attention(packed, segment_ids[0], heads)
    context = lax.all_to_all(
        context.reshape(n_seq, rows_dev, span), "seq", split_axis=0, concat_axis=0, tiled=True
    )
    offsets = [j * share - firsts[j] * HEAD_DIM for j in range(n_seq)]

    first = (lax.axis_index("exp") * (EXPERTS // n_exp)).astype(jnp.int32).reshape(1)
    me = lax.axis_index("seq").astype(jnp.int32).reshape(1)
    w_gate, w_up = jnp.swapaxes(w_gate, 1, 2), jnp.swapaxes(w_up, 1, 2)
    gates = gate_weights[0]
    facts = jnp.concatenate([target, gates, gates, gates], axis=1)
    facts = jnp.pad(facts, ((0, 0), (0, 128 - facts.shape[1])))
    stream, piece = norm_tokens(context, residual[0], norm_gain, facts, share, offsets)

    slots = jnp.arange(group // PAGE, dtype=jnp.int32)
    order = jnp.sum(jnp.where(page_table[0][None, :] == slots[:, None], slots[None, :], 0), axis=1)

    def fill_cache(late):
        if n_seq & (n_seq - 1) == 0:
            pages = pick_pages(packed, order, me, late, n_seq, span)
            pages = [pages[0]] + [swap(pages[j], "seq", n_seq, j) for j in range(1, n_seq)]
            return join_pages(pages, me, share, offsets, span)
        pages = jnp.take(packed[:, span:].reshape(group // PAGE, PAGE, 2 * span), order, axis=0)
        pages = pages.reshape(n_seq, rows_dev, 2 * span)
        pages = lax.all_to_all(pages, "seq", split_axis=0, concat_axis=0, tiled=True)
        parts = [
            pages[j][:, at + offsets[j] : at + offsets[j] + share] for at in (0, span) for j in range(n_seq)
        ]
        return jnp.concatenate(parts, axis=1)

    if (n_seq, n_exp) == (8, 4):
        mixture, cache = exchange_experts(piece, w_gate, w_up, w_down, first, n_seq, n_exp, fill_cache)
    else:
        cache = fill_cache(piece)
        blocks = n_seq * n_exp
        everything = lax.all_gather(piece, everyone, axis=0, tiled=True)
        facts = everything[:, width : width + 8].astype(jnp.float32)
        facts = facts.reshape(blocks // CHUNK_BLOCKS, CHUNK_BLOCKS * rows_dev, 8).transpose(0, 2, 1)
        gates = facts[:, 2:4] + facts[:, 4:6] + facts[:, 6:8]
        partial = experts(
            everything[:, :width], facts[:, :2].astype(jnp.int32), gates, w_gate, w_up, w_down, first
        )
        mixture = lax.psum_scatter(partial, everyone, scatter_dimension=0, tiled=True).astype(jnp.float32)
    layer_out = (stream + mixture).astype(jnp.bfloat16)
    return (layer_out[None], cache.reshape(1, rows_dev // PAGE, PAGE, 2 * width))


def solution(mesh):
    in_specs = (
        P("exp", "seq", None),
        P("exp", "seq", None, None),
        P("exp", "seq", None),
        P(),
        P("exp", None),
        P("exp", "seq", None),
        P("exp", "seq", None),
        P("exp", None),
        P("exp", None, "seq"),
        P("exp", None, "seq"),
        P("exp", "seq", None),
    )
    out_specs = (P("exp", "seq", None), P("exp", "seq", None, None))
    run = functools.partial(body, mesh.shape["seq"], mesh.shape["exp"])
    return jax.shard_map(run, mesh=mesh, in_specs=in_specs, out_specs=out_specs, check_vma=False)
```

```python
import functools
import math

import jax
import jax.numpy as jnp
from jax import lax
from jax.experimental import pallas as pl
from jax.experimental.pallas import tpu as pltpu
from jax.sharding import PartitionSpec as P

HEADS = 36
HEAD_DIM = 64
EXPERTS = 8
PAGE = 16
CAP = 24
CHUNK_BLOCKS = 8


def head_ranges(width, n_seq):
    share = width // n_seq
    firsts = [j * share // HEAD_DIM for j in range(n_seq)]
    count = max(-(-(j + 1) * share // HEAD_DIM) - firsts[j] for j in range(n_seq))
    firsts = [min(f, HEADS - count) for f in firsts]
    return share, firsts, count


def attention_kernel(heads, q_rows, packed_ref, seg_row_ref, seg_col_ref, out_ref):
    total = packed_ref.shape[0]
    span = heads * HEAD_DIM
    scale = 1.0 / math.sqrt(HEAD_DIM)
    for start in range(0, total, q_rows):
        end = start + q_rows
        q_place = start + lax.broadcasted_iota(jnp.int32, (q_rows, end), 0)
        k_place = lax.broadcasted_iota(jnp.int32, (q_rows, end), 1)
        visible = (seg_col_ref[start:end, :] == seg_row_ref[:, :end]) & (k_place <= q_place)
        parts = []
        for h in range(heads):
            a = h * HEAD_DIM
            q = packed_ref[start:end, a : a + HEAD_DIM]
            k = packed_ref[:end, span + a : span + a + HEAD_DIM]
            v = packed_ref[:end, 2 * span + a : 2 * span + a + HEAD_DIM]
            s = lax.dot_general(q, k, (((1,), (1,)), ((), ())), preferred_element_type=jnp.float32)
            s = jnp.where(visible, s * scale, -1e30)
            top = jnp.max(s, axis=1, keepdims=True)
            p = jnp.exp(s - top)
            denominator = jnp.sum(p, axis=1, keepdims=True)
            o = jnp.dot(p.astype(jnp.bfloat16), v, preferred_element_type=jnp.float32)
            parts.append((o / denominator).astype(jnp.bfloat16))
        out_ref[start:end, :] = jnp.concatenate(parts, axis=1)


def attention(packed, segments, heads):
    total = packed.shape[0]
    span = heads * HEAD_DIM
    return pl.pallas_call(
        functools.partial(attention_kernel, heads, 128),
        out_shape=jax.ShapeDtypeStruct((total, span), jnp.bfloat16),
        compiler_params=pltpu.CompilerParams(vmem_limit_bytes=40 * 1024 * 1024),
        cost_estimate=pl.CostEstimate(
            flops=4 * total * total * span, bytes_accessed=8 * total * span, transcendentals=total * total * heads
        ),
    )(packed, segments[None, :], segments[:, None])


def dot_t(a, b):
    return lax.dot_general(a, b, (((1,), (1,)), ((), ())), preferred_element_type=jnp.float32)


def expert_kernel(
    local, rows, tokens, first_ref, x_ref, tgt_ref, gates_ref, wg_ref, wu_ref, wd_ref, out_ref, kept_ref
):
    le = pl.program_id(0)
    chunk = pl.program_id(1)

    def selection(which):
        base = (first_ref[0] + which) * CAP
        row_id = lax.broadcasted_iota(jnp.int32, (rows, tokens), 0)
        block = lax.broadcasted_iota(jnp.int32, (1, tokens), 1) // 64
        picks, weights = None, None
        for j in range(2):
            slot = tgt_ref[0, j : j + 1, :] - base
            place = jnp.where((slot >= 0) & (slot < CAP), block * CAP + slot, -1)
            hit = row_id == place
            gate = jnp.where(hit, gates_ref[0, j : j + 1, :], 0.0)
            picks = hit if picks is None else picks | hit
            weights = gate if weights is None else weights + gate
        return picks.astype(jnp.float32).astype(jnp.bfloat16), jnp.sum(weights, axis=1, keepdims=True)

    pick, weight = selection(le)
    chosen = jnp.dot(pick, x_ref[...], preferred_element_type=jnp.float32).astype(jnp.bfloat16)
    gate = dot_t(chosen, wg_ref[0])
    upper = dot_t(chosen, wu_ref[0])
    hidden = (gate / (1.0 + jnp.exp(-gate)) * upper).astype(jnp.bfloat16)
    y = jnp.dot(hidden, wd_ref[0], preferred_element_type=jnp.float32)
    y = (y * weight).astype(jnp.bfloat16)

    if local > 1:

        @pl.when(le < local - 1)
        def _():
            kept_ref[le, chunk] = y

    @pl.when(le == local - 1)
    def _():
        total = lax.dot_general(pick, y, (((0,), (0,)), ((), ())), preferred_element_type=jnp.float32)
        for other in range(local - 1):
            pick_o, _ = selection(other)
            total += lax.dot_general(
                pick_o, kept_ref[other, chunk], (((0,), (0,)), ((), ())), preferred_element_type=jnp.float32
            )
        out_ref[...] = total.astype(jnp.bfloat16)


def experts(x, tgt, gates, w_gate, w_up, w_down, first):
    local, hidden, width = w_gate.shape
    chunks, _, tokens = tgt.shape
    rows = tokens // 64 * CAP
    last = local - 1
    return pl.pallas_call(
        functools.partial(expert_kernel, local, rows, tokens),
        out_shape=jax.ShapeDtypeStruct(x.shape, jnp.bfloat16),
        grid=(local, chunks),
        in_specs=[
            pl.BlockSpec(memory_space=pltpu.SMEM),
            pl.BlockSpec((tokens, width), lambda e, c: (c, 0)),
            pl.BlockSpec((1, 2, tokens), lambda e, c: (c, 0, 0)),
            pl.BlockSpec((1, 2, tokens), lambda e, c: (c, 0, 0)),
            pl.BlockSpec((1, hidden, width), lambda e, c: (e, 0, 0)),
            pl.BlockSpec((1, hidden, width), lambda e, c: (e, 0, 0)),
            pl.BlockSpec((1, hidden, width), lambda e, c: (e, 0, 0)),
        ],
        out_specs=pl.BlockSpec((tokens, width), lambda e, c: (jnp.where(e == last, c, 0), 0)),
        scratch_shapes=[pltpu.VMEM((max(last, 1), chunks if last else 1, rows, width), jnp.bfloat16)],
        compiler_params=pltpu.CompilerParams(vmem_limit_bytes=58 * 1024 * 1024),
        cost_estimate=pl.CostEstimate(
            flops=6 * local * chunks * rows * width * hidden,
            bytes_accessed=6 * local * width * hidden + 6 * chunks * tokens * width,
            transcendentals=local * chunks * rows * hidden,
        ),
    )(first, x, tgt, gates, w_gate, w_up, w_down)


def norm_kernel(share, offsets, context_ref, residual_ref, gain_ref, facts_ref, stream_ref, piece_ref):
    n_seq, _, _ = context_ref.shape
    width = residual_ref.shape[1]
    parts = [context_ref[j][:, offsets[j] : offsets[j] + share] for j in range(n_seq)]
    context = jnp.concatenate(parts, axis=1).astype(jnp.float32)
    stream = residual_ref[...].astype(jnp.float32) + context
    stream_ref[...] = stream
    mean = jnp.mean(stream * stream, axis=1, keepdims=True)
    normed = stream * lax.rsqrt(mean + 1e-05) * gain_ref[...].astype(jnp.float32)
    piece_ref[:, :width] = normed.astype(jnp.bfloat16)
    facts = facts_ref[...]
    lane = lax.broadcasted_iota(jnp.int32, facts.shape, 1)
    high = facts.astype(jnp.bfloat16).astype(jnp.float32)
    middle = (facts - high).astype(jnp.bfloat16).astype(jnp.float32)
    low = facts - high - middle
    own = jnp.where(lane < 4, high, jnp.where(lane < 6, middle, low))
    piece_ref[:, width:] = own.astype(jnp.bfloat16)


def norm_tokens(context, residual, gain, facts, share, offsets):
    rows_dev, width = residual.shape
    return pl.pallas_call(
        functools.partial(norm_kernel, share, offsets),
        out_shape=(
            jax.ShapeDtypeStruct((rows_dev, width), jnp.float32),
            jax.ShapeDtypeStruct((rows_dev, width + facts.shape[1]), jnp.bfloat16),
        ),
        cost_estimate=pl.CostEstimate(
            flops=10 * rows_dev * width, bytes_accessed=10 * rows_dev * width, transcendentals=rows_dev
        ),
    )(context, residual, gain[None, :], facts)


def pick_pages_kernel(per_device, first_lane, order_ref, me_ref, packed_ref, late_ref, *out_refs):
    del late_ref
    for j, out_ref in enumerate(out_refs):
        peer = jnp.bitwise_xor(me_ref[0], j)
        for i in range(per_device):
            page = order_ref[peer * per_device + i]
            rows = pl.ds(pl.multiple_of(page * PAGE, PAGE), PAGE)
            out_ref[i * PAGE : (i + 1) * PAGE, :] = packed_ref[rows, first_lane:]


def pick_pages(packed, order, me, late, n_seq, span):
    rows = packed.shape[0] // n_seq
    smem = pl.BlockSpec(memory_space=pltpu.SMEM)
    vmem = pl.BlockSpec(memory_space=pltpu.VMEM)
    out = jax.ShapeDtypeStruct((rows, 2 * span), jnp.bfloat16)
    return pl.pallas_call(
        functools.partial(pick_pages_kernel, rows // PAGE, span),
        out_shape=(out,) * n_seq,
        in_specs=[smem, smem, vmem, pl.BlockSpec(memory_space=pl.ANY)],
        cost_estimate=pl.CostEstimate(flops=0, bytes_accessed=10 * packed.shape[0] * span, transcendentals=0),
    )(order, me, packed, late)


def join_pages_kernel(share, offsets, span, me_ref, *refs):
    piece_refs, out_ref, all_ref = refs[:-2], refs[-2], refs[-1]
    for j, ref in enumerate(piece_refs):
        all_ref[jnp.bitwise_xor(me_ref[0], j)] = ref[...]
    for part in range(2):
        parts = [
            all_ref[j][:, part * span + offsets[j] : part * span + offsets[j] + share]
            for j in range(len(piece_refs))
        ]
        width = share * len(piece_refs)
        out_ref[:, part * width : (part + 1) * width] = jnp.concatenate(parts, axis=1)


def join_pages(pieces, me, share, offsets, span):
    rows = pieces[0].shape[0]
    n_seq = len(pieces)
    return pl.pallas_call(
        functools.partial(join_pages_kernel, share, offsets, span),
        out_shape=jax.ShapeDtypeStruct((rows, 2 * share * n_seq), jnp.bfloat16),
        in_specs=[pl.BlockSpec(memory_space=pltpu.SMEM)] + [pl.BlockSpec(memory_space=pltpu.VMEM)] * n_seq,
        scratch_shapes=[pltpu.VMEM((n_seq,) + pieces[0].shape, jnp.bfloat16)],
        cost_estimate=pl.CostEstimate(flops=0, bytes_accessed=8 * rows * n_seq * span, transcendentals=0),
    )(me, *pieces)


def places_of(slots, base, shift):
    place = -1
    for slot in slots:
        slot = slot.astype(jnp.int32) - base
        place = jnp.where((slot >= 0) & (slot < CAP), shift + slot, place)
    return place


def chunk_kernel(local, pieces, waits, first_ref, wg_hbm, wu_hbm, wd_hbm, *rest):
    piece_refs = rest[:pieces]
    keep_hbm, send_hbm, x, wg, wu, wd, rows_of, y, out, piece_sem, weight_sem, out_sem = rest[pieces + waits :]
    rows_dev = piece_refs[0].shape[0]
    width = wd.shape[2]
    groups = pieces // 4
    tokens = 4 * rows_dev
    rows = 4 * CAP
    piece_copies = [
        pltpu.make_async_copy(ref, x.at[pl.ds(i * rows_dev, rows_dev), :], piece_sem.at[i])
        for i, ref in enumerate(piece_refs)
    ]
    weight_copies = [
        [
            pltpu.make_async_copy(source.at[e], target.at[e], weight_sem.at[3 * e + i])
            for i, (source, target) in enumerate(((wg_hbm, wg), (wu_hbm, wu), (wd_hbm, wd)))
        ]
        for e in range(local)
    ]
    for copy in piece_copies:
        copy.start()
    for copies in weight_copies:
        for copy in copies:
            copy.start()

    unit = lax.broadcasted_iota(jnp.int32, (8, 128), 0) == lax.broadcasted_iota(jnp.int32, (8, 128), 1)
    unit = unit.astype(jnp.float32).astype(jnp.bfloat16)
    shift = lax.broadcasted_iota(jnp.int32, (1, tokens), 1) // rows_dev * CAP
    row_id = lax.broadcasted_iota(jnp.int32, (rows, tokens), 0)
    weights = [[] for _ in range(local)]
    for g in range(groups):
        for copy in piece_copies[4 * g : 4 * g + 4]:
            copy.wait()
        here = slice(g * tokens, (g + 1) * tokens)
        facts = dot_t(unit, x[here, width:])
        picks = []
        for e in range(local):
            base = (first_ref[0] + e) * CAP
            pick, weight = None, None
            for j in range(2):
                hit = row_id == places_of([facts[j : j + 1]], base, shift)
                gate = facts[2 + j : 3 + j] + facts[4 + j : 5 + j] + facts[6 + j : 7 + j]
                gate = jnp.where(hit, gate, 0.0)
                pick = hit if pick is None else pick | hit
                weight = gate if weight is None else weight + gate
            picks.append(pick.astype(jnp.float32))
            weights[e].append(jnp.sum(weight, axis=1, keepdims=True))
        picks = jnp.concatenate(picks, axis=0).astype(jnp.bfloat16)
        chosen = jnp.dot(picks, x[here, :width], preferred_element_type=jnp.float32)
        for e in range(local):
            rows_of[e, g * rows : (g + 1) * rows, :] = chosen[e * rows : (e + 1) * rows].astype(jnp.bfloat16)

    for e in range(local):
        chosen = rows_of[e].T
        weight_copies[e][0].wait()
        gate = jnp.dot(wg[e], chosen, preferred_element_type=jnp.float32)
        weight_copies[e][1].wait()
        upper = jnp.dot(wu[e], chosen, preferred_element_type=jnp.float32)
        hidden = (gate / (1.0 + jnp.exp(-gate)) * upper).T.astype(jnp.bfloat16)
        weight_copies[e][2].wait()
        result = jnp.dot(hidden, wd[e], preferred_element_type=jnp.float32)
        result = (result * jnp.concatenate(weights[e], axis=0)).astype(jnp.bfloat16)
        for g in range(groups):
            y[g, e * rows : (e + 1) * rows, :] = result[g * rows : (g + 1) * rows]

    shift = lax.broadcasted_iota(jnp.int32, (tokens, 1), 0) // rows_dev * CAP
    lane = lax.broadcasted_iota(jnp.int32, (tokens, local * rows), 1)
    out_copies = []
    for g in reversed(range(groups)):
        here = slice(g * tokens, (g + 1) * tokens)
        facts = x[here, width:].astype(jnp.float32)
        put = None
        for e in range(local):
            base = (first_ref[0] + e) * CAP
            hit = lane == places_of([facts[:, j : j + 1] for j in range(2)], base, shift + e * rows)
            put = hit if put is None else put | hit
        put = put.astype(jnp.float32).astype(jnp.bfloat16)
        out[here, :] = jnp.dot(put, y[g], preferred_element_type=jnp.float32).astype(jnp.bfloat16)
        target, at = (keep_hbm, g) if g < groups // 2 else (send_hbm, g - groups // 2)
        copy = pltpu.make_async_copy(
            out.at[pl.ds(g * tokens, tokens), :], target.at[pl.ds(at * tokens, tokens), :], out_sem.at[g]
        )
        copy.start()
        out_copies.append(copy)
    for copy in out_copies:
        copy.wait()


def chunk_experts(pieces, w_gate, w_up, w_down, first, waits):
    local, hidden, width = w_gate.shape
    rows_dev, wide = pieces[0].shape
    tokens = rows_dev * len(pieces)
    rows = len(pieces) * CAP
    groups = len(pieces) // 4
    half = jax.ShapeDtypeStruct((tokens // 2, width), jnp.bfloat16)
    anywhere = pl.BlockSpec(memory_space=pl.ANY)
    weights = pltpu.VMEM((local, hidden, width), jnp.bfloat16)
    return pl.pallas_call(
        functools.partial(chunk_kernel, local, len(pieces), len(waits)),
        out_shape=(half, half),
        in_specs=[pl.BlockSpec(memory_space=pltpu.SMEM)] + [anywhere] * (3 + len(pieces) + len(waits)),
        out_specs=(anywhere, anywhere),
        scratch_shapes=[
            pltpu.VMEM((tokens, wide), jnp.bfloat16),
            weights,
            weights,
            weights,
            pltpu.VMEM((local, rows, width), jnp.bfloat16),
            pltpu.VMEM((groups, local * rows // groups, width), jnp.bfloat16),
            pltpu.VMEM((tokens, width), jnp.bfloat16),
            pltpu.SemaphoreType.DMA((len(pieces),)),
            pltpu.SemaphoreType.DMA((3 * local,)),
            pltpu.SemaphoreType.DMA((groups,)),
        ],
        compiler_params=pltpu.CompilerParams(vmem_limit_bytes=58 * 1024 * 1024),
        cost_estimate=pl.CostEstimate(
            flops=6 * local * rows * width * hidden,
            bytes_accessed=6 * local * width * hidden + 4 * tokens * width,
            transcendentals=local * rows * hidden,
        ),
    )(first, w_gate, w_up, w_down, *pieces, *waits)


def swap(a, axis, size, distance):
    return lax.ppermute(a, axis, [(i, i ^ distance) for i in range(size)])


def fold_kernel(groups, count, waits, keep_ref, *rest):
    got_refs, (kept_ref, *send_refs) = rest[:count], rest[count + waits :]
    got = jnp.concatenate([r[...] for r in got_refs], axis=0) if count > 1 else got_refs[0][...]
    total = (keep_ref[...].astype(jnp.float32) + got.astype(jnp.float32)).astype(jnp.bfloat16)
    part = total.shape[0] // (2 * groups)
    for i in range(groups):
        kept_ref[i * part : (i + 1) * part, :] = total[2 * i * part : (2 * i + 1) * part]
        send_refs[i][...] = total[(2 * i + 1) * part : (2 * i + 2) * part]


def fold(keep, gots, groups, waits=()):
    rows, width = keep.shape
    part = rows // (2 * groups)
    steps = 3 if width % (3 * 128) == 0 else 1
    block = lambda n: pl.BlockSpec((n, width // steps), lambda i: (0, i))
    shape = lambda n: jax.ShapeDtypeStruct((n, width), jnp.bfloat16)
    out = pl.pallas_call(
        functools.partial(fold_kernel, groups, len(gots), len(waits)),
        out_shape=(shape(groups * part),) + (shape(part),) * groups,
        grid=(steps,),
        in_specs=[block(rows)]
        + [block(g.shape[0]) for g in gots]
        + [pl.BlockSpec(memory_space=pl.ANY)] * len(waits),
        out_specs=(block(groups * part),) + (block(part),) * groups,
        compiler_params=pltpu.CompilerParams(vmem_limit_bytes=58 * 1024 * 1024),
        cost_estimate=pl.CostEstimate(flops=rows * width, bytes_accessed=6 * rows * width, transcendentals=0),
    )(keep, *gots, *waits)
    return out[0], out[1:]


def exchange_experts(piece, w_gate, w_up, w_down, first, n_seq, n_exp, late_work):
    x = lambda a: swap(a, "seq", n_seq, 1)
    y = lambda a: swap(a, "exp", n_exp, 2)
    core = lambda a: swap(a, "exp", n_exp, 1)
    z = lambda a, k: swap(a, "seq", n_seq, 2 * k)
    starts = [piece] + [z(piece, k) for k in range(1, 4)]

    def gather(k):
        near = []
        for start, (f, g) in ((starts[k], (x, y)), (starts[k + 1], (y, x))):
            by_f = f(start)
            near += [start, g(start), by_f, g(by_f)]
        return near + [core(p) for p in near]

    experts_of = lambda pieces, waits: chunk_experts(pieces, w_gate, w_up, w_down, first, waits)
    keep_a, send_a = experts_of(gather(0), [])
    keep_a, (fx_a, fy_a) = fold(keep_a, [core(send_a)], 2)
    keep_b, send_b = experts_of(gather(2), [fx_a])
    got_b = core(send_b)
    other = late_work(send_b)
    keep_a, (gy_a, gx_a) = fold(keep_a, [x(fx_a), y(fy_a)], 2)
    keep_b, (fx_b, fy_b) = fold(keep_b, [got_b], 2, [gy_a])
    keep_a, (z_a,) = fold(keep_a, [y(gy_a), x(gx_a)], 1)
    keep_b, (gy_b, gx_b) = fold(keep_b, [x(fx_b), y(fy_b)], 2, [z_a, other])
    got_a = z(z_a, 1)
    keep_b, (z_b,) = fold(keep_b, [y(gy_b), x(gx_b)], 1)
    mine = keep_a.astype(jnp.float32) + got_a.astype(jnp.float32)
    over_z = (keep_b.astype(jnp.float32) + z(z_b, 1).astype(jnp.float32)).astype(jnp.bfloat16)
    return mine + z(over_z, 2).astype(jnp.float32), other


def body(
    n_seq,
    n_exp,
    query,
    key_value,
    residual,
    norm_gain,
    segment_ids,
    routes,
    gate_weights,
    page_table,
    w_gate,
    w_up,
    w_down,
):
    rows_dev, width = query.shape[1:]
    everyone = ("exp", "seq")
    group = segment_ids.shape[1]
    share, firsts, heads = head_ranges(width, n_seq)
    span = heads * HEAD_DIM

    flat = routes[0].reshape(rows_dev * 2)
    onehot = (flat[:, None] == jnp.arange(EXPERTS, dtype=jnp.int32)[None, :]).astype(jnp.int32)
    before = jnp.cumsum(onehot, axis=0) - onehot
    target = (flat * CAP + jnp.sum(before * onehot, axis=1)).reshape(rows_dev, 2).astype(jnp.float32)

    keys, values = key_value[0, :, 0], key_value[0, :, 1]

    def spans(a):
        return jnp.stack([a[:, f * HEAD_DIM : f * HEAD_DIM + span] for f in firsts])

    packed = jnp.concatenate([spans(query[0]), spans(keys), spans(values)], axis=2)
    packed = lax.all_to_all(packed, "seq", split_axis=0, concat_axis=0, tiled=True)
    packed = packed.reshape(group, 3 * span)
    context = attention(packed, segment_ids[0], heads)
    context = lax.all_to_all(
        context.reshape(n_seq, rows_dev, span), "seq", split_axis=0, concat_axis=0, tiled=True
    )
    offsets = [j * share - firsts[j] * HEAD_DIM for j in range(n_seq)]

    first = (lax.axis_index("exp") * (EXPERTS // n_exp)).astype(jnp.int32).reshape(1)
    me = lax.axis_index("seq").astype(jnp.int32).reshape(1)
    w_gate, w_up = jnp.swapaxes(w_gate, 1, 2), jnp.swapaxes(w_up, 1, 2)
    gates = gate_weights[0]
    facts = jnp.concatenate([target, gates, gates, gates], axis=1)
    facts = jnp.pad(facts, ((0, 0), (0, 128 - facts.shape[1])))
    stream, piece = norm_tokens(context, residual[0], norm_gain, facts, share, offsets)

    slots = jnp.arange(group // PAGE, dtype=jnp.int32)
    order = jnp.sum(jnp.where(page_table[0][None, :] == slots[:, None], slots[None, :], 0), axis=1)

    def fill_cache(late):
        if n_seq & (n_seq - 1) == 0:
            pages = pick_pages(packed, order, me, late, n_seq, span)
            pages = [pages[0]] + [swap(pages[j], "seq", n_seq, j) for j in range(1, n_seq)]
            return join_pages(pages, me, share, offsets, span)
        pages = jnp.take(packed[:, span:].reshape(group // PAGE, PAGE, 2 * span), order, axis=0)
        pages = pages.reshape(n_seq, rows_dev, 2 * span)
        pages = lax.all_to_all(pages, "seq", split_axis=0, concat_axis=0, tiled=True)
        parts = [
            pages[j][:, at + offsets[j] : at + offsets[j] + share] for at in (0, span) for j in range(n_seq)
        ]
        return jnp.concatenate(parts, axis=1)

    if (n_seq, n_exp) == (8, 4):
        mixture, cache = exchange_experts(piece, w_gate, w_up, w_down, first, n_seq, n_exp, fill_cache)
    else:
        cache = fill_cache(piece)
        blocks = n_seq * n_exp
        everything = lax.all_gather(piece, everyone, axis=0, tiled=True)
        facts = everything[:, width : width + 8].astype(jnp.float32)
        facts = facts.reshape(blocks // CHUNK_BLOCKS, CHUNK_BLOCKS * rows_dev, 8).transpose(0, 2, 1)
        gates = facts[:, 2:4] + facts[:, 4:6] + facts[:, 6:8]
        partial = experts(
            everything[:, :width], facts[:, :2].astype(jnp.int32), gates, w_gate, w_up, w_down, first
        )
        mixture = lax.psum_scatter(partial, everyone, scatter_dimension=0, tiled=True).astype(jnp.float32)
    layer_out = (stream + mixture).astype(jnp.bfloat16)
    return (layer_out[None], cache.reshape(1, rows_dev // PAGE, PAGE, 2 * width))


def solution(mesh):
    in_specs = (
        P("exp", "seq", None),
        P("exp", "seq", None, None),
        P("exp", "seq", None),
        P(),
        P("exp", None),
        P("exp", "seq", None),
        P("exp", "seq", None),
        P("exp", None),
        P("exp", None, "seq"),
        P("exp", None, "seq"),
        P("exp", "seq", None),
    )
    out_specs = (P("exp", "seq", None), P("exp", "seq", None, None))
    run = functools.partial(body, mesh.shape["seq"], mesh.shape["exp"])
    return jax.shard_map(run, mesh=mesh, in_specs=in_specs, out_specs=out_specs, check_vma=False)
```

```python
import functools
import math

import jax
import jax.numpy as jnp
from jax import lax
from jax.experimental import pallas as pl
from jax.experimental.pallas import tpu as pltpu
from jax.sharding import PartitionSpec as P

HEADS = 36
HEAD_DIM = 64
EXPERTS = 8
PAGE = 16
CAP = 24
CHUNK_BLOCKS = 8


def head_ranges(width, n_seq):
    share = width // n_seq
    firsts = [j * share // HEAD_DIM for j in range(n_seq)]
    count = max(-(-(j + 1) * share // HEAD_DIM) - firsts[j] for j in range(n_seq))
    firsts = [min(f, HEADS - count) for f in firsts]
    return share, firsts, count


def attention_kernel(heads, q_rows, packed_ref, seg_row_ref, seg_col_ref, out_ref):
    total = packed_ref.shape[0]
    span = heads * HEAD_DIM
    scale = 1.0 / math.sqrt(HEAD_DIM)
    for start in range(0, total, q_rows):
        end = start + q_rows
        q_place = start + lax.broadcasted_iota(jnp.int32, (q_rows, end), 0)
        k_place = lax.broadcasted_iota(jnp.int32, (q_rows, end), 1)
        visible = (seg_col_ref[start:end, :] == seg_row_ref[:, :end]) & (k_place <= q_place)
        parts = []
        for h in range(heads):
            a = h * HEAD_DIM
            q = packed_ref[start:end, a : a + HEAD_DIM]
            k = packed_ref[:end, span + a : span + a + HEAD_DIM]
            v = packed_ref[:end, 2 * span + a : 2 * span + a + HEAD_DIM]
            s = lax.dot_general(q, k, (((1,), (1,)), ((), ())), preferred_element_type=jnp.float32)
            s = jnp.where(visible, s * scale, -1e30)
            top = jnp.max(s, axis=1, keepdims=True)
            p = jnp.exp(s - top)
            denominator = jnp.sum(p, axis=1, keepdims=True)
            o = jnp.dot(p.astype(jnp.bfloat16), v, preferred_element_type=jnp.float32)
            parts.append((o / denominator).astype(jnp.bfloat16))
        out_ref[start:end, :] = jnp.concatenate(parts, axis=1)


def attention(packed, segments, heads):
    total = packed.shape[0]
    span = heads * HEAD_DIM
    return pl.pallas_call(
        functools.partial(attention_kernel, heads, 128),
        out_shape=jax.ShapeDtypeStruct((total, span), jnp.bfloat16),
        compiler_params=pltpu.CompilerParams(vmem_limit_bytes=40 * 1024 * 1024),
        cost_estimate=pl.CostEstimate(
            flops=4 * total * total * span, bytes_accessed=8 * total * span, transcendentals=total * total * heads
        ),
    )(packed, segments[None, :], segments[:, None])


def dot_t(a, b):
    return lax.dot_general(a, b, (((1,), (1,)), ((), ())), preferred_element_type=jnp.float32)


def expert_kernel(
    local, rows, tokens, first_ref, x_ref, tgt_ref, gates_ref, wg_ref, wu_ref, wd_ref, out_ref, kept_ref
):
    le = pl.program_id(0)
    chunk = pl.program_id(1)

    def selection(which):
        base = (first_ref[0] + which) * CAP
        row_id = lax.broadcasted_iota(jnp.int32, (rows, tokens), 0)
        block = lax.broadcasted_iota(jnp.int32, (1, tokens), 1) // 64
        picks, weights = None, None
        for j in range(2):
            slot = tgt_ref[0, j : j + 1, :] - base
            place = jnp.where((slot >= 0) & (slot < CAP), block * CAP + slot, -1)
            hit = row_id == place
            gate = jnp.where(hit, gates_ref[0, j : j + 1, :], 0.0)
            picks = hit if picks is None else picks | hit
            weights = gate if weights is None else weights + gate
        return picks.astype(jnp.float32).astype(jnp.bfloat16), jnp.sum(weights, axis=1, keepdims=True)

    pick, weight = selection(le)
    chosen = jnp.dot(pick, x_ref[...], preferred_element_type=jnp.float32).astype(jnp.bfloat16)
    gate = dot_t(chosen, wg_ref[0])
    upper = dot_t(chosen, wu_ref[0])
    hidden = (gate / (1.0 + jnp.exp(-gate)) * upper).astype(jnp.bfloat16)
    y = jnp.dot(hidden, wd_ref[0], preferred_element_type=jnp.float32)
    y = (y * weight).astype(jnp.bfloat16)

    if local > 1:

        @pl.when(le < local - 1)
        def _():
            kept_ref[le, chunk] = y

    @pl.when(le == local - 1)
    def _():
        total = lax.dot_general(pick, y, (((0,), (0,)), ((), ())), preferred_element_type=jnp.float32)
        for other in range(local - 1):
            pick_o, _ = selection(other)
            total += lax.dot_general(
                pick_o, kept_ref[other, chunk], (((0,), (0,)), ((), ())), preferred_element_type=jnp.float32
            )
        out_ref[...] = total.astype(jnp.bfloat16)


def experts(x, tgt, gates, w_gate, w_up, w_down, first):
    local, hidden, width = w_gate.shape
    chunks, _, tokens = tgt.shape
    rows = tokens // 64 * CAP
    last = local - 1
    return pl.pallas_call(
        functools.partial(expert_kernel, local, rows, tokens),
        out_shape=jax.ShapeDtypeStruct(x.shape, jnp.bfloat16),
        grid=(local, chunks),
        in_specs=[
            pl.BlockSpec(memory_space=pltpu.SMEM),
            pl.BlockSpec((tokens, width), lambda e, c: (c, 0)),
            pl.BlockSpec((1, 2, tokens), lambda e, c: (c, 0, 0)),
            pl.BlockSpec((1, 2, tokens), lambda e, c: (c, 0, 0)),
            pl.BlockSpec((1, hidden, width), lambda e, c: (e, 0, 0)),
            pl.BlockSpec((1, hidden, width), lambda e, c: (e, 0, 0)),
            pl.BlockSpec((1, hidden, width), lambda e, c: (e, 0, 0)),
        ],
        out_specs=pl.BlockSpec((tokens, width), lambda e, c: (jnp.where(e == last, c, 0), 0)),
        scratch_shapes=[pltpu.VMEM((max(last, 1), chunks if last else 1, rows, width), jnp.bfloat16)],
        compiler_params=pltpu.CompilerParams(vmem_limit_bytes=58 * 1024 * 1024),
        cost_estimate=pl.CostEstimate(
            flops=6 * local * chunks * rows * width * hidden,
            bytes_accessed=6 * local * width * hidden + 6 * chunks * tokens * width,
            transcendentals=local * chunks * rows * hidden,
        ),
    )(first, x, tgt, gates, w_gate, w_up, w_down)


def norm_kernel(share, offsets, context_ref, residual_ref, gain_ref, facts_ref, stream_ref, piece_ref):
    n_seq, _, _ = context_ref.shape
    width = residual_ref.shape[1]
    parts = [context_ref[j][:, offsets[j] : offsets[j] + share] for j in range(n_seq)]
    context = jnp.concatenate(parts, axis=1).astype(jnp.float32)
    stream = residual_ref[...].astype(jnp.float32) + context
    stream_ref[...] = stream
    mean = jnp.mean(stream * stream, axis=1, keepdims=True)
    normed = stream * lax.rsqrt(mean + 1e-05) * gain_ref[...].astype(jnp.float32)
    piece_ref[:, :width] = normed.astype(jnp.bfloat16)
    facts = facts_ref[...]
    lane = lax.broadcasted_iota(jnp.int32, facts.shape, 1)
    high = facts.astype(jnp.bfloat16).astype(jnp.float32)
    middle = (facts - high).astype(jnp.bfloat16).astype(jnp.float32)
    low = facts - high - middle
    own = jnp.where(lane < 4, high, jnp.where(lane < 6, middle, low))
    piece_ref[:, width:] = own.astype(jnp.bfloat16)


def norm_tokens(context, residual, gain, facts, share, offsets):
    rows_dev, width = residual.shape
    return pl.pallas_call(
        functools.partial(norm_kernel, share, offsets),
        out_shape=(
            jax.ShapeDtypeStruct((rows_dev, width), jnp.float32),
            jax.ShapeDtypeStruct((rows_dev, width + facts.shape[1]), jnp.bfloat16),
        ),
        cost_estimate=pl.CostEstimate(
            flops=10 * rows_dev * width, bytes_accessed=10 * rows_dev * width, transcendentals=rows_dev
        ),
    )(context, residual, gain[None, :], facts)


def pick_pages_kernel(per_device, first_lane, order_ref, packed_ref, late_ref, out_ref):
    del late_ref
    for j in range(out_ref.shape[0]):
        for i in range(per_device):
            rows = pl.ds(pl.multiple_of(order_ref[j * per_device + i] * PAGE, PAGE), PAGE)
            out_ref[j, i * PAGE : (i + 1) * PAGE, :] = packed_ref[rows, first_lane:]


def pick_pages(packed, order, late, n_seq, span):
    rows = packed.shape[0] // n_seq
    vmem = pl.BlockSpec(memory_space=pltpu.VMEM)
    return pl.pallas_call(
        functools.partial(pick_pages_kernel, rows // PAGE, span),
        out_shape=jax.ShapeDtypeStruct((n_seq, rows, 2 * span), jnp.bfloat16),
        in_specs=[pl.BlockSpec(memory_space=pltpu.SMEM), vmem, pl.BlockSpec(memory_space=pl.ANY)],
        cost_estimate=pl.CostEstimate(flops=0, bytes_accessed=10 * packed.shape[0] * span, transcendentals=0),
    )(order, packed, late)


def join_pages_kernel(share, offsets, span, pages_ref, out_ref):
    width = share * len(offsets)
    for part in range(2):
        parts = [
            pages_ref[j][:, part * span + offsets[j] : part * span + offsets[j] + share]
            for j in range(len(offsets))
        ]
        out_ref[:, part * width : (part + 1) * width] = jnp.concatenate(parts, axis=1)


def join_pages(pages, share, offsets, span):
    n_seq, rows, _ = pages.shape
    return pl.pallas_call(
        functools.partial(join_pages_kernel, share, offsets, span),
        out_shape=jax.ShapeDtypeStruct((rows, 2 * share * n_seq), jnp.bfloat16),
        cost_estimate=pl.CostEstimate(flops=0, bytes_accessed=8 * rows * n_seq * span, transcendentals=0),
    )(pages)


def places_of(slots, base, shift):
    place = -1
    for slot in slots:
        slot = slot.astype(jnp.int32) - base
        place = jnp.where((slot >= 0) & (slot < CAP), shift + slot, place)
    return place


def chunk_kernel(local, pieces, waits, first_ref, wg_hbm, wu_hbm, wd_hbm, *rest):
    piece_refs = rest[:pieces]
    keep_hbm, send_hbm, x, wg, wu, wd, rows_of, y, out, piece_sem, weight_sem, out_sem = rest[pieces + waits :]
    rows_dev = piece_refs[0].shape[0]
    width = wd.shape[2]
    groups = pieces // 4
    tokens = 4 * rows_dev
    rows = 4 * CAP
    piece_copies = [
        pltpu.make_async_copy(ref, x.at[pl.ds(i * rows_dev, rows_dev), :], piece_sem.at[i])
        for i, ref in enumerate(piece_refs)
    ]
    weight_copies = [
        [
            pltpu.make_async_copy(source.at[e], target.at[e], weight_sem.at[3 * e + i])
            for i, (source, target) in enumerate(((wg_hbm, wg), (wu_hbm, wu), (wd_hbm, wd)))
        ]
        for e in range(local)
    ]
    for copy in piece_copies:
        copy.start()
    for copies in weight_copies:
        for copy in copies:
            copy.start()

    unit = lax.broadcasted_iota(jnp.int32, (8, 128), 0) == lax.broadcasted_iota(jnp.int32, (8, 128), 1)
    unit = unit.astype(jnp.float32).astype(jnp.bfloat16)
    shift = lax.broadcasted_iota(jnp.int32, (1, tokens), 1) // rows_dev * CAP
    row_id = lax.broadcasted_iota(jnp.int32, (rows, tokens), 0)
    weights = [[] for _ in range(local)]
    for g in range(groups):
        for copy in piece_copies[4 * g : 4 * g + 4]:
            copy.wait()
        here = slice(g * tokens, (g + 1) * tokens)
        facts = dot_t(unit, x[here, width:])
        picks = []
        for e in range(local):
            base = (first_ref[0] + e) * CAP
            pick, weight = None, None
            for j in range(2):
                hit = row_id == places_of([facts[j : j + 1]], base, shift)
                gate = facts[2 + j : 3 + j] + facts[4 + j : 5 + j] + facts[6 + j : 7 + j]
                gate = jnp.where(hit, gate, 0.0)
                pick = hit if pick is None else pick | hit
                weight = gate if weight is None else weight + gate
            picks.append(pick.astype(jnp.float32))
            weights[e].append(jnp.sum(weight, axis=1, keepdims=True))
        picks = jnp.concatenate(picks, axis=0).astype(jnp.bfloat16)
        chosen = jnp.dot(picks, x[here, :width], preferred_element_type=jnp.float32)
        for e in range(local):
            rows_of[e, g * rows : (g + 1) * rows, :] = chosen[e * rows : (e + 1) * rows].astype(jnp.bfloat16)

    for e in range(local):
        chosen = rows_of[e]
        weight_copies[e][0].wait()
        gate = dot_t(chosen, wg[e])
        weight_copies[e][1].wait()
        upper = dot_t(chosen, wu[e])
        hidden = (gate / (1.0 + jnp.exp(-gate)) * upper).astype(jnp.bfloat16)
        weight_copies[e][2].wait()
        result = jnp.dot(hidden, wd[e], preferred_element_type=jnp.float32)
        result = (result * jnp.concatenate(weights[e], axis=0)).astype(jnp.bfloat16)
        for g in range(groups):
            y[g, e * rows : (e + 1) * rows, :] = result[g * rows : (g + 1) * rows]

    shift = lax.broadcasted_iota(jnp.int32, (tokens, 1), 0) // rows_dev * CAP
    lane = lax.broadcasted_iota(jnp.int32, (tokens, local * rows), 1)
    out_copies = []
    for g in reversed(range(groups)):
        here = slice(g * tokens, (g + 1) * tokens)
        facts = x[here, width:].astype(jnp.float32)
        put = None
        for e in range(local):
            base = (first_ref[0] + e) * CAP
            hit = lane == places_of([facts[:, j : j + 1] for j in range(2)], base, shift + e * rows)
            put = hit if put is None else put | hit
        put = put.astype(jnp.float32).astype(jnp.bfloat16)
        out[here, :] = jnp.dot(put, y[g], preferred_element_type=jnp.float32).astype(jnp.bfloat16)
        target, at = (keep_hbm, g) if g < groups // 2 else (send_hbm, g - groups // 2)
        copy = pltpu.make_async_copy(
            out.at[pl.ds(g * tokens, tokens), :], target.at[pl.ds(at * tokens, tokens), :], out_sem.at[g]
        )
        copy.start()
        out_copies.append(copy)
    for copy in out_copies:
        copy.wait()


def chunk_experts(pieces, w_gate, w_up, w_down, first, waits):
    local, hidden, width = w_gate.shape
    rows_dev, wide = pieces[0].shape
    tokens = rows_dev * len(pieces)
    rows = len(pieces) * CAP
    groups = len(pieces) // 4
    half = jax.ShapeDtypeStruct((tokens // 2, width), jnp.bfloat16)
    anywhere = pl.BlockSpec(memory_space=pl.ANY)
    weights = pltpu.VMEM((local, hidden, width), jnp.bfloat16)
    return pl.pallas_call(
        functools.partial(chunk_kernel, local, len(pieces), len(waits)),
        out_shape=(half, half),
        in_specs=[pl.BlockSpec(memory_space=pltpu.SMEM)] + [anywhere] * (3 + len(pieces) + len(waits)),
        out_specs=(anywhere, anywhere),
        scratch_shapes=[
            pltpu.VMEM((tokens, wide), jnp.bfloat16),
            weights,
            weights,
            weights,
            pltpu.VMEM((local, rows, width), jnp.bfloat16),
            pltpu.VMEM((groups, local * rows // groups, width), jnp.bfloat16),
            pltpu.VMEM((tokens, width), jnp.bfloat16),
            pltpu.SemaphoreType.DMA((len(pieces),)),
            pltpu.SemaphoreType.DMA((3 * local,)),
            pltpu.SemaphoreType.DMA((groups,)),
        ],
        compiler_params=pltpu.CompilerParams(vmem_limit_bytes=58 * 1024 * 1024),
        cost_estimate=pl.CostEstimate(
            flops=6 * local * rows * width * hidden,
            bytes_accessed=6 * local * width * hidden + 4 * tokens * width,
            transcendentals=local * rows * hidden,
        ),
    )(first, w_gate, w_up, w_down, *pieces, *waits)


def swap(a, axis, size, distance):
    return lax.ppermute(a, axis, [(i, i ^ distance) for i in range(size)])


def fold_kernel(groups, count, waits, keep_ref, *rest):
    got_refs, (kept_ref, *send_refs) = rest[:count], rest[count + waits :]
    part = keep_ref.shape[0] // (2 * groups)
    span = got_refs[0].shape[0]
    for i in range(2 * groups):
        start = i * part
        got = got_refs[start // span][start % span : start % span + part, :]
        total = keep_ref[start : start + part, :].astype(jnp.float32) + got.astype(jnp.float32)
        total = total.astype(jnp.bfloat16)
        if i % 2 == 0:
            kept_ref[i // 2 * part : (i // 2 + 1) * part, :] = total
        else:
            send_refs[i // 2][...] = total


def fold(keep, gots, groups, waits=()):
    rows, width = keep.shape
    part = rows // (2 * groups)
    vmem = pl.BlockSpec(memory_space=pltpu.VMEM)
    shape = lambda n: jax.ShapeDtypeStruct((n, width), jnp.bfloat16)
    out = pl.pallas_call(
        functools.partial(fold_kernel, groups, len(gots), len(waits)),
        out_shape=(shape(groups * part),) + (shape(part),) * groups,
        in_specs=[vmem] * (1 + len(gots)) + [pl.BlockSpec(memory_space=pl.ANY)] * len(waits),
        out_specs=(vmem,) * (1 + groups),
        compiler_params=pltpu.CompilerParams(vmem_limit_bytes=24 * 1024 * 1024),
        cost_estimate=pl.CostEstimate(flops=rows * width, bytes_accessed=6 * rows * width, transcendentals=0),
    )(keep, *gots, *waits)
    return out[0], out[1:]


def exchange_experts(piece, w_gate, w_up, w_down, first, n_seq, n_exp, late_work):
    x = lambda a: swap(a, "seq", n_seq, 1)
    y = lambda a: swap(a, "exp", n_exp, 2)
    core = lambda a: swap(a, "exp", n_exp, 1)
    z = lambda a, k: swap(a, "seq", n_seq, 2 * k)
    starts = [piece] + [z(piece, k) for k in range(1, 4)]

    def gather(k):
        near = []
        for start, (f, g) in ((starts[k], (x, y)), (starts[k + 1], (y, x))):
            by_f = f(start)
            near += [start, g(start), by_f, g(by_f)]
        return near + [core(p) for p in near]

    experts_of = lambda pieces, waits: chunk_experts(pieces, w_gate, w_up, w_down, first, waits)
    chunk_a, chunk_b = gather(0), gather(2)
    keep_a, send_a = experts_of(chunk_a, chunk_b)
    pages, other = late_work(send_a)
    keep_b, send_b = experts_of(chunk_b, [pages, send_a])
    keep_a, (fx_a, fy_a) = fold(keep_a, [core(send_a)], 2)
    got_b = core(send_b)
    keep_a, (gy_a, gx_a) = fold(keep_a, [x(fx_a), y(fy_a)], 2)
    keep_b, (fx_b, fy_b) = fold(keep_b, [got_b], 2, [gy_a, other])
    keep_a, (z_a,) = fold(keep_a, [y(gy_a), x(gx_a)], 1)
    keep_b, (gy_b, gx_b) = fold(keep_b, [x(fx_b), y(fy_b)], 2, [z_a])
    got_a = z(z_a, 1)
    keep_b, (z_b,) = fold(keep_b, [y(gy_b), x(gx_b)], 1)
    mine = keep_a.astype(jnp.float32) + got_a.astype(jnp.float32)
    over_z = (keep_b.astype(jnp.float32) + z(z_b, 1).astype(jnp.float32)).astype(jnp.bfloat16)
    return mine + z(over_z, 2).astype(jnp.float32), other


def body(
    n_seq,
    n_exp,
    query,
    key_value,
    residual,
    norm_gain,
    segment_ids,
    routes,
    gate_weights,
    page_table,
    w_gate,
    w_up,
    w_down,
):
    rows_dev, width = query.shape[1:]
    everyone = ("exp", "seq")
    group = segment_ids.shape[1]
    share, firsts, heads = head_ranges(width, n_seq)
    span = heads * HEAD_DIM

    flat = routes[0].reshape(rows_dev * 2)
    onehot = (flat[:, None] == jnp.arange(EXPERTS, dtype=jnp.int32)[None, :]).astype(jnp.int32)
    before = jnp.cumsum(onehot, axis=0) - onehot
    target = (flat * CAP + jnp.sum(before * onehot, axis=1)).reshape(rows_dev, 2).astype(jnp.float32)

    keys, values = key_value[0, :, 0], key_value[0, :, 1]

    def spans(a):
        return jnp.stack([a[:, f * HEAD_DIM : f * HEAD_DIM + span] for f in firsts])

    packed = jnp.concatenate([spans(query[0]), spans(keys), spans(values)], axis=2)
    packed = lax.all_to_all(packed, "seq", split_axis=0, concat_axis=0, tiled=True)
    packed = packed.reshape(group, 3 * span)
    context = attention(packed, segment_ids[0], heads)
    context = lax.all_to_all(
        context.reshape(n_seq, rows_dev, span), "seq", split_axis=0, concat_axis=0, tiled=True
    )
    offsets = [j * share - firsts[j] * HEAD_DIM for j in range(n_seq)]

    first = (lax.axis_index("exp") * (EXPERTS // n_exp)).astype(jnp.int32).reshape(1)
    w_gate, w_up = jnp.swapaxes(w_gate, 1, 2), jnp.swapaxes(w_up, 1, 2)
    gates = gate_weights[0]
    facts = jnp.concatenate([target, gates, gates, gates], axis=1)
    facts = jnp.pad(facts, ((0, 0), (0, 128 - facts.shape[1])))
    stream, piece = norm_tokens(context, residual[0], norm_gain, facts, share, offsets)

    slots = jnp.arange(group // PAGE, dtype=jnp.int32)
    order = jnp.sum(jnp.where(page_table[0][None, :] == slots[:, None], slots[None, :], 0), axis=1)

    def fill_cache(late):
        pages = pick_pages(packed, order, late, n_seq, span)
        sent = lax.all_to_all(pages, "seq", split_axis=0, concat_axis=0, tiled=True)
        return pages, join_pages(sent, share, offsets, span)

    if (n_seq, n_exp) == (8, 4):
        mixture, cache = exchange_experts(piece, w_gate, w_up, w_down, first, n_seq, n_exp, fill_cache)
    else:
        _, cache = fill_cache(piece)
        blocks = n_seq * n_exp
        everything = lax.all_gather(piece, everyone, axis=0, tiled=True)
        facts = everything[:, width : width + 8].astype(jnp.float32)
        facts = facts.reshape(blocks // CHUNK_BLOCKS, CHUNK_BLOCKS * rows_dev, 8).transpose(0, 2, 1)
        gates = facts[:, 2:4] + facts[:, 4:6] + facts[:, 6:8]
        partial = experts(
            everything[:, :width], facts[:, :2].astype(jnp.int32), gates, w_gate, w_up, w_down, first
        )
        mixture = lax.psum_scatter(partial, everyone, scatter_dimension=0, tiled=True).astype(jnp.float32)
    layer_out = (stream + mixture).astype(jnp.bfloat16)
    return (layer_out[None], cache.reshape(1, rows_dev // PAGE, PAGE, 2 * width))


def solution(mesh):
    in_specs = (
        P("exp", "seq", None),
        P("exp", "seq", None, None),
        P("exp", "seq", None),
        P(),
        P("exp", None),
        P("exp", "seq", None),
        P("exp", "seq", None),
        P("exp", None),
        P("exp", None, "seq"),
        P("exp", None, "seq"),
        P("exp", "seq", None),
    )
    out_specs = (P("exp", "seq", None), P("exp", "seq", None, None))
    run = functools.partial(body, mesh.shape["seq"], mesh.shape["exp"])
    return jax.shard_map(run, mesh=mesh, in_specs=in_specs, out_specs=out_specs, check_vma=False)
```

```python
import functools
import math

import jax
import jax.numpy as jnp
from jax import lax
from jax.experimental import pallas as pl
from jax.experimental.pallas import tpu as pltpu
from jax.sharding import PartitionSpec as P

HEADS = 36
HEAD_DIM = 64
EXPERTS = 8
PAGE = 16
CAP = 24
CHUNK_BLOCKS = 8


def head_ranges(width, n_seq):
    share = width // n_seq
    firsts = [j * share // HEAD_DIM for j in range(n_seq)]
    count = max(-(-(j + 1) * share // HEAD_DIM) - firsts[j] for j in range(n_seq))
    firsts = [min(f, HEADS - count) for f in firsts]
    return share, firsts, count


def attention_kernel(heads, q_rows, packed_ref, seg_row_ref, seg_col_ref, out_ref):
    total = packed_ref.shape[0]
    span = heads * HEAD_DIM
    scale = 1.0 / math.sqrt(HEAD_DIM)
    for start in range(0, total, q_rows):
        end = start + q_rows
        q_place = start + lax.broadcasted_iota(jnp.int32, (q_rows, end), 0)
        k_place = lax.broadcasted_iota(jnp.int32, (q_rows, end), 1)
        visible = (seg_col_ref[start:end, :] == seg_row_ref[:, :end]) & (k_place <= q_place)
        parts = []
        for h in range(heads):
            a = h * HEAD_DIM
            q = packed_ref[start:end, a : a + HEAD_DIM]
            k = packed_ref[:end, span + a : span + a + HEAD_DIM]
            v = packed_ref[:end, 2 * span + a : 2 * span + a + HEAD_DIM]
            s = lax.dot_general(q, k, (((1,), (1,)), ((), ())), preferred_element_type=jnp.float32)
            s = jnp.where(visible, s * scale, -1e30)
            top = jnp.max(s, axis=1, keepdims=True)
            p = jnp.exp(s - top)
            denominator = jnp.sum(p, axis=1, keepdims=True)
            o = jnp.dot(p.astype(jnp.bfloat16), v, preferred_element_type=jnp.float32)
            parts.append((o / denominator).astype(jnp.bfloat16))
        out_ref[start:end, :] = jnp.concatenate(parts, axis=1)


def attention(packed, segments, heads):
    total = packed.shape[0]
    span = heads * HEAD_DIM
    return pl.pallas_call(
        functools.partial(attention_kernel, heads, 128),
        out_shape=jax.ShapeDtypeStruct((total, span), jnp.bfloat16),
        compiler_params=pltpu.CompilerParams(vmem_limit_bytes=40 * 1024 * 1024),
        cost_estimate=pl.CostEstimate(
            flops=4 * total * total * span, bytes_accessed=8 * total * span, transcendentals=total * total * heads
        ),
    )(packed, segments[None, :], segments[:, None])


def dot_t(a, b):
    return lax.dot_general(a, b, (((1,), (1,)), ((), ())), preferred_element_type=jnp.float32)


def expert_kernel(
    local, rows, tokens, first_ref, x_ref, tgt_ref, gates_ref, wg_ref, wu_ref, wd_ref, out_ref, kept_ref
):
    le = pl.program_id(0)
    chunk = pl.program_id(1)

    def selection(which):
        base = (first_ref[0] + which) * CAP
        row_id = lax.broadcasted_iota(jnp.int32, (rows, tokens), 0)
        block = lax.broadcasted_iota(jnp.int32, (1, tokens), 1) // 64
        picks, weights = None, None
        for j in range(2):
            slot = tgt_ref[0, j : j + 1, :] - base
            place = jnp.where((slot >= 0) & (slot < CAP), block * CAP + slot, -1)
            hit = row_id == place
            gate = jnp.where(hit, gates_ref[0, j : j + 1, :], 0.0)
            picks = hit if picks is None else picks | hit
            weights = gate if weights is None else weights + gate
        return picks.astype(jnp.float32).astype(jnp.bfloat16), jnp.sum(weights, axis=1, keepdims=True)

    pick, weight = selection(le)
    chosen = jnp.dot(pick, x_ref[...], preferred_element_type=jnp.float32).astype(jnp.bfloat16)
    gate = dot_t(chosen, wg_ref[0])
    upper = dot_t(chosen, wu_ref[0])
    hidden = (gate / (1.0 + jnp.exp(-gate)) * upper).astype(jnp.bfloat16)
    y = jnp.dot(hidden, wd_ref[0], preferred_element_type=jnp.float32)
    y = (y * weight).astype(jnp.bfloat16)

    if local > 1:

        @pl.when(le < local - 1)
        def _():
            kept_ref[le, chunk] = y

    @pl.when(le == local - 1)
    def _():
        total = lax.dot_general(pick, y, (((0,), (0,)), ((), ())), preferred_element_type=jnp.float32)
        for other in range(local - 1):
            pick_o, _ = selection(other)
            total += lax.dot_general(
                pick_o, kept_ref[other, chunk], (((0,), (0,)), ((), ())), preferred_element_type=jnp.float32
            )
        out_ref[...] = total.astype(jnp.bfloat16)


def experts(x, tgt, gates, w_gate, w_up, w_down, first):
    local, hidden, width = w_gate.shape
    chunks, _, tokens = tgt.shape
    rows = tokens // 64 * CAP
    last = local - 1
    return pl.pallas_call(
        functools.partial(expert_kernel, local, rows, tokens),
        out_shape=jax.ShapeDtypeStruct(x.shape, jnp.bfloat16),
        grid=(local, chunks),
        in_specs=[
            pl.BlockSpec(memory_space=pltpu.SMEM),
            pl.BlockSpec((tokens, width), lambda e, c: (c, 0)),
            pl.BlockSpec((1, 2, tokens), lambda e, c: (c, 0, 0)),
            pl.BlockSpec((1, 2, tokens), lambda e, c: (c, 0, 0)),
            pl.BlockSpec((1, hidden, width), lambda e, c: (e, 0, 0)),
            pl.BlockSpec((1, hidden, width), lambda e, c: (e, 0, 0)),
            pl.BlockSpec((1, hidden, width), lambda e, c: (e, 0, 0)),
        ],
        out_specs=pl.BlockSpec((tokens, width), lambda e, c: (jnp.where(e == last, c, 0), 0)),
        scratch_shapes=[pltpu.VMEM((max(last, 1), chunks if last else 1, rows, width), jnp.bfloat16)],
        compiler_params=pltpu.CompilerParams(vmem_limit_bytes=58 * 1024 * 1024),
        cost_estimate=pl.CostEstimate(
            flops=6 * local * chunks * rows * width * hidden,
            bytes_accessed=6 * local * width * hidden + 6 * chunks * tokens * width,
            transcendentals=local * chunks * rows * hidden,
        ),
    )(first, x, tgt, gates, w_gate, w_up, w_down)


def norm_kernel(share, offsets, context_ref, residual_ref, gain_ref, facts_ref, stream_ref, piece_ref):
    n_seq, _, _ = context_ref.shape
    width = residual_ref.shape[1]
    parts = [context_ref[j][:, offsets[j] : offsets[j] + share] for j in range(n_seq)]
    context = jnp.concatenate(parts, axis=1).astype(jnp.float32)
    stream = residual_ref[...].astype(jnp.float32) + context
    stream_ref[...] = stream
    mean = jnp.mean(stream * stream, axis=1, keepdims=True)
    normed = stream * lax.rsqrt(mean + 1e-05) * gain_ref[...].astype(jnp.float32)
    piece_ref[:, :width] = normed.astype(jnp.bfloat16)
    facts = facts_ref[...]
    lane = lax.broadcasted_iota(jnp.int32, facts.shape, 1)
    high = facts.astype(jnp.bfloat16).astype(jnp.float32)
    middle = (facts - high).astype(jnp.bfloat16).astype(jnp.float32)
    low = facts - high - middle
    own = jnp.where(lane < 4, high, jnp.where(lane < 6, middle, low))
    piece_ref[:, width:] = own.astype(jnp.bfloat16)


def norm_tokens(context, residual, gain, facts, share, offsets):
    rows_dev, width = residual.shape
    return pl.pallas_call(
        functools.partial(norm_kernel, share, offsets),
        out_shape=(
            jax.ShapeDtypeStruct((rows_dev, width), jnp.float32),
            jax.ShapeDtypeStruct((rows_dev, width + facts.shape[1]), jnp.bfloat16),
        ),
        cost_estimate=pl.CostEstimate(
            flops=10 * rows_dev * width, bytes_accessed=10 * rows_dev * width, transcendentals=rows_dev
        ),
    )(context, residual, gain[None, :], facts)


def pick_pages_kernel(per_device, first_lane, order_ref, packed_ref, late_ref, out_ref):
    del late_ref
    for j in range(out_ref.shape[0]):
        for i in range(per_device):
            rows = pl.ds(pl.multiple_of(order_ref[j * per_device + i] * PAGE, PAGE), PAGE)
            out_ref[j, i * PAGE : (i + 1) * PAGE, :] = packed_ref[rows, first_lane:]


def pick_pages(packed, order, late, n_seq, span):
    rows = packed.shape[0] // n_seq
    vmem = pl.BlockSpec(memory_space=pltpu.VMEM)
    return pl.pallas_call(
        functools.partial(pick_pages_kernel, rows // PAGE, span),
        out_shape=jax.ShapeDtypeStruct((n_seq, rows, 2 * span), jnp.bfloat16),
        in_specs=[pl.BlockSpec(memory_space=pltpu.SMEM), vmem, pl.BlockSpec(memory_space=pl.ANY)],
        cost_estimate=pl.CostEstimate(flops=0, bytes_accessed=10 * packed.shape[0] * span, transcendentals=0),
    )(order, packed, late)


def join_pages_kernel(share, offsets, span, pages_ref, out_ref):
    width = share * len(offsets)
    for part in range(2):
        parts = [
            pages_ref[j][:, part * span + offsets[j] : part * span + offsets[j] + share]
            for j in range(len(offsets))
        ]
        out_ref[:, part * width : (part + 1) * width] = jnp.concatenate(parts, axis=1)


def join_pages(pages, share, offsets, span):
    n_seq, rows, _ = pages.shape
    return pl.pallas_call(
        functools.partial(join_pages_kernel, share, offsets, span),
        out_shape=jax.ShapeDtypeStruct((rows, 2 * share * n_seq), jnp.bfloat16),
        cost_estimate=pl.CostEstimate(flops=0, bytes_accessed=8 * rows * n_seq * span, transcendentals=0),
    )(pages)


def places_of(slots, base, shift):
    place = -1
    for slot in slots:
        slot = slot.astype(jnp.int32) - base
        place = jnp.where((slot >= 0) & (slot < CAP), shift + slot, place)
    return place


def facts_by_lane(x):
    unit = lax.broadcasted_iota(jnp.int32, (8, 128), 0) == lax.broadcasted_iota(jnp.int32, (8, 128), 1)
    return dot_t(unit.astype(jnp.float32).astype(jnp.bfloat16), x)


def select_kernel(local, rows_dev, count, bases_ref, *refs):
    piece_refs, own_ref, sib_ref = refs[:count], refs[-2], refs[-1]
    width = own_ref.shape[2]
    tokens, rows = 4 * rows_dev, 4 * CAP
    shift = lax.broadcasted_iota(jnp.int32, (1, tokens), 1) // rows_dev * CAP
    row_id = lax.broadcasted_iota(jnp.int32, (rows, tokens), 0)
    for g in range(len(piece_refs) // 4):
        x = jnp.concatenate([p[...] for p in piece_refs[4 * g : 4 * g + 4]], axis=0)
        facts = facts_by_lane(x[:, width:])
        picks = []
        for core in range(2):
            for e in range(local):
                base = (bases_ref[core] + e) * CAP
                hit = row_id == places_of([facts[j : j + 1] for j in range(2)], base, shift)
                picks.append(hit.astype(jnp.float32))
        picks = jnp.concatenate(picks, axis=0).astype(jnp.bfloat16)
        chosen = jnp.dot(picks, x[:, :width], preferred_element_type=jnp.float32).astype(jnp.bfloat16)
        for e in range(local):
            own_ref[e, g * rows : (g + 1) * rows, :] = chosen[e * rows : (e + 1) * rows]
            sib_ref[e, g * rows : (g + 1) * rows, :] = chosen[(local + e) * rows : (local + e + 1) * rows]


def select_rows(pieces, bases, local, waits=()):
    rows_dev, wide = pieces[0].shape
    width = wide - 128
    rows = len(pieces) * CAP
    out = jax.ShapeDtypeStruct((local, rows, width), jnp.bfloat16)
    vmem = pl.BlockSpec(memory_space=pltpu.VMEM)
    return pl.pallas_call(
        functools.partial(select_kernel, local, rows_dev, len(pieces)),
        out_shape=(out, out),
        in_specs=[pl.BlockSpec(memory_space=pltpu.SMEM)]
        + [vmem] * len(pieces)
        + [pl.BlockSpec(memory_space=pl.ANY)] * len(waits),
        out_specs=(vmem, vmem),
        compiler_params=pltpu.CompilerParams(vmem_limit_bytes=28 * 1024 * 1024),
        cost_estimate=pl.CostEstimate(
            flops=16 * local * CAP * rows_dev * len(pieces) * width,
            bytes_accessed=2 * len(pieces) * rows_dev * wide + 4 * local * rows * width,
            transcendentals=0,
        ),
    )(bases, *pieces, *waits)


def rows_kernel(local, waits, own_ref, got_ref, wg_hbm, wu_hbm, wd_hbm, *rest):
    y_own_ref, y_sib_ref, wg, wu, wd, weight_sem = rest[waits:]
    half = own_ref.shape[1]
    copies = [
        [
            pltpu.make_async_copy(source.at[e], target.at[e], weight_sem.at[3 * e + i])
            for i, (source, target) in enumerate(((wg_hbm, wg), (wu_hbm, wu), (wd_hbm, wd)))
        ]
        for e in range(local)
    ]
    for group in copies:
        for copy in group:
            copy.start()
    for e in range(local):
        rows = jnp.concatenate([own_ref[e], got_ref[e]], axis=0)
        copies[e][0].wait()
        gate = dot_t(rows, wg[e])
        copies[e][1].wait()
        upper = dot_t(rows, wu[e])
        hidden = (gate / (1.0 + jnp.exp(-gate)) * upper).astype(jnp.bfloat16)
        copies[e][2].wait()
        y = jnp.dot(hidden, wd[e], preferred_element_type=jnp.float32).astype(jnp.bfloat16)
        y_own_ref[e] = y[:half]
        y_sib_ref[e] = y[half:]


def expert_rows(own, got, w_gate, w_up, w_down, waits):
    local, hidden, width = w_gate.shape
    rows = 2 * own.shape[1]
    out = jax.ShapeDtypeStruct(own.shape, jnp.bfloat16)
    vmem = pl.BlockSpec(memory_space=pltpu.VMEM)
    weights = pltpu.VMEM((local, hidden, width), jnp.bfloat16)
    return pl.pallas_call(
        functools.partial(rows_kernel, local, len(waits)),
        out_shape=(out, out),
        in_specs=[vmem, vmem] + [pl.BlockSpec(memory_space=pl.ANY)] * (3 + len(waits)),
        out_specs=(vmem, vmem),
        scratch_shapes=[weights, weights, weights, pltpu.SemaphoreType.DMA((3 * local,))],
        compiler_params=pltpu.CompilerParams(vmem_limit_bytes=44 * 1024 * 1024),
        cost_estimate=pl.CostEstimate(
            flops=6 * local * rows * width * hidden,
            bytes_accessed=6 * local * width * hidden + 4 * local * rows * width,
            transcendentals=local * rows * hidden,
        ),
    )(own, got, w_gate, w_up, w_down, *waits)


def put_kernel(local, rows_dev, count, waits, bases_ref, y_own_ref, y_got_ref, *rest):
    fact_refs = rest[:count]
    kept_ref, *send_refs = rest[count + waits :]
    tokens, rows = 4 * rows_dev, 4 * CAP
    total = 2 * local * rows
    shift_lane = lax.broadcasted_iota(jnp.int32, (1, tokens), 1) // rows_dev * CAP
    shift_row = lax.broadcasted_iota(jnp.int32, (tokens, 1), 0) // rows_dev * CAP
    row_id = lax.broadcasted_iota(jnp.int32, (rows, tokens), 0)
    lane = lax.broadcasted_iota(jnp.int32, (tokens, total), 1)
    for g in range(count // 4):
        facts = jnp.concatenate([f[...] for f in fact_refs[4 * g : 4 * g + 4]], axis=0)
        by_lane = facts_by_lane(facts)
        by_row = facts.astype(jnp.float32)
        here = slice(g * rows, (g + 1) * rows)
        weighed, put = [], None
        for core, y_ref in enumerate((y_own_ref, y_got_ref)):
            for e in range(local):
                base = (bases_ref[core] + e) * CAP
                weight = jnp.zeros((rows, tokens), jnp.float32)
                for j in range(2):
                    hit = row_id == places_of([by_lane[j : j + 1]], base, shift_lane)
                    gate = by_lane[2 + j : 3 + j] + by_lane[4 + j : 5 + j] + by_lane[6 + j : 7 + j]
                    weight = weight + jnp.where(hit, gate, 0.0)
                weight = jnp.sum(weight, axis=1, keepdims=True)
                weighed.append((y_ref[e, here, :].astype(jnp.float32) * weight).astype(jnp.bfloat16))
                first = (core * local + e) * rows
                hit = lane == places_of([by_row[:, j : j + 1] for j in range(2)], base, shift_row + first)
                put = hit if put is None else put | hit
        put = put.astype(jnp.float32).astype(jnp.bfloat16)
        out = jnp.dot(put, jnp.concatenate(weighed, axis=0), preferred_element_type=jnp.float32)
        out = out.astype(jnp.bfloat16)
        kept_ref[g * tokens // 2 : (g + 1) * tokens // 2, :] = out[: tokens // 2]
        send_refs[g][...] = out[tokens // 2 :]


def put_rows(y_own, y_got, pieces, bases, waits):
    local, _, width = y_own.shape
    rows_dev = pieces[0].shape[0]
    planes = len(pieces) // 4
    vmem = pl.BlockSpec(memory_space=pltpu.VMEM)
    shape = lambda n: jax.ShapeDtypeStruct((n, width), jnp.bfloat16)
    out = pl.pallas_call(
        functools.partial(put_kernel, local, rows_dev, len(pieces), len(waits)),
        out_shape=(shape(2 * planes * rows_dev),) + (shape(2 * rows_dev),) * planes,
        in_specs=[pl.BlockSpec(memory_space=pltpu.SMEM), vmem, vmem]
        + [vmem] * len(pieces)
        + [pl.BlockSpec(memory_space=pl.ANY)] * len(waits),
        out_specs=(vmem,) * (1 + planes),
        compiler_params=pltpu.CompilerParams(vmem_limit_bytes=28 * 1024 * 1024),
        cost_estimate=pl.CostEstimate(
            flops=16 * local * CAP * rows_dev * len(pieces) * width,
            bytes_accessed=8 * local * len(pieces) * CAP * width,
            transcendentals=0,
        ),
    )(bases, y_own, y_got, *[p[:, width:] for p in pieces], *waits)
    return out[0], out[1:]


def swap(a, axis, size, distance):
    return lax.ppermute(a, axis, [(i, i ^ distance) for i in range(size)])


def fold_kernel(groups, count, waits, keep_ref, *rest):
    got_refs, (kept_ref, *send_refs) = rest[:count], rest[count + waits :]
    part = keep_ref.shape[0] // (2 * groups)
    span = got_refs[0].shape[0]
    for i in range(2 * groups):
        start = i * part
        got = got_refs[start // span][start % span : start % span + part, :]
        total = keep_ref[start : start + part, :].astype(jnp.float32) + got.astype(jnp.float32)
        total = total.astype(jnp.bfloat16)
        if i % 2 == 0:
            kept_ref[i // 2 * part : (i // 2 + 1) * part, :] = total
        else:
            send_refs[i // 2][...] = total


def fold(keep, gots, groups, waits=()):
    rows, width = keep.shape
    part = rows // (2 * groups)
    vmem = pl.BlockSpec(memory_space=pltpu.VMEM)
    shape = lambda n: jax.ShapeDtypeStruct((n, width), jnp.bfloat16)
    out = pl.pallas_call(
        functools.partial(fold_kernel, groups, len(gots), len(waits)),
        out_shape=(shape(groups * part),) + (shape(part),) * groups,
        in_specs=[vmem] * (1 + len(gots)) + [pl.BlockSpec(memory_space=pl.ANY)] * len(waits),
        out_specs=(vmem,) * (1 + groups),
        compiler_params=pltpu.CompilerParams(vmem_limit_bytes=24 * 1024 * 1024),
        cost_estimate=pl.CostEstimate(flops=rows * width, bytes_accessed=6 * rows * width, transcendentals=0),
    )(keep, *gots, *waits)
    return out[0], out[1:]


def exchange_experts(piece, w_gate, w_up, w_down, n_seq, n_exp, late_work):
    x = lambda a: swap(a, "seq", n_seq, 1)
    y = lambda a: swap(a, "exp", n_exp, 2)
    core = lambda a: swap(a, "exp", n_exp, 1)
    z = lambda a, k: swap(a, "seq", n_seq, 2 * k)
    local = w_gate.shape[0]
    me = lax.axis_index("exp").astype(jnp.int32)
    bases = jnp.stack([me, me ^ 1]) * local
    starts = [piece, z(piece, 1), z(piece, 2)]
    starts.append(z(starts[2], 1))

    def gather(k):
        near = []
        for start, (f, g) in ((starts[k], (x, y)), (starts[k + 1], (y, x))):
            by_f = f(start)
            near += [start, g(start), by_f, g(by_f)]
        return near

    near_a, near_b = gather(0), gather(2)
    own_a, sib_a = select_rows(near_a, bases, local, starts[2:])
    got_a = core(sib_a)
    own_b, sib_b = select_rows(near_b, bases, local)
    got_b = core(sib_b)
    own_a, sib_a = expert_rows(own_a, got_a, w_gate, w_up, w_down, [sib_b])
    pages, other = late_work(sib_a)
    got_a = core(sib_a)
    own_b, sib_b = expert_rows(own_b, got_b, w_gate, w_up, w_down, [pages, sib_a])
    got_b = core(sib_b)
    keep_a, (fx_a, fy_a) = put_rows(own_a, got_a, near_a, bases, [sib_b])
    keep_a, (gy_a, gx_a) = fold(keep_a, [x(fx_a), y(fy_a)], 2)
    keep_b, (fx_b, fy_b) = put_rows(own_b, got_b, near_b, bases, [other])
    keep_a, (z_a,) = fold(keep_a, [y(gy_a), x(gx_a)], 1)
    keep_b, (gy_b, gx_b) = fold(keep_b, [x(fx_b), y(fy_b)], 2, [z_a])
    back_a = z(z_a, 1)
    keep_b, (z_b,) = fold(keep_b, [y(gy_b), x(gx_b)], 1)
    mine = keep_a.astype(jnp.float32) + back_a.astype(jnp.float32)
    over_z = (keep_b.astype(jnp.float32) + z(z_b, 1).astype(jnp.float32)).astype(jnp.bfloat16)
    return mine + z(over_z, 2).astype(jnp.float32), other


def body(
    n_seq,
    n_exp,
    query,
    key_value,
    residual,
    norm_gain,
    segment_ids,
    routes,
    gate_weights,
    page_table,
    w_gate,
    w_up,
    w_down,
):
    rows_dev, width = query.shape[1:]
    everyone = ("exp", "seq")
    group = segment_ids.shape[1]
    share, firsts, heads = head_ranges(width, n_seq)
    span = heads * HEAD_DIM

    flat = routes[0].reshape(rows_dev * 2)
    onehot = (flat[:, None] == jnp.arange(EXPERTS, dtype=jnp.int32)[None, :]).astype(jnp.int32)
    before = jnp.cumsum(onehot, axis=0) - onehot
    target = (flat * CAP + jnp.sum(before * onehot, axis=1)).reshape(rows_dev, 2).astype(jnp.float32)

    keys, values = key_value[0, :, 0], key_value[0, :, 1]

    def spans(a):
        return jnp.stack([a[:, f * HEAD_DIM : f * HEAD_DIM + span] for f in firsts])

    packed = jnp.concatenate([spans(query[0]), spans(keys), spans(values)], axis=2)
    packed = lax.all_to_all(packed, "seq", split_axis=0, concat_axis=0, tiled=True)
    packed = packed.reshape(group, 3 * span)
    context = attention(packed, segment_ids[0], heads)
    context = lax.all_to_all(
        context.reshape(n_seq, rows_dev, span), "seq", split_axis=0, concat_axis=0, tiled=True
    )
    offsets = [j * share - firsts[j] * HEAD_DIM for j in range(n_seq)]

    first = (lax.axis_index("exp") * (EXPERTS // n_exp)).astype(jnp.int32).reshape(1)
    w_gate, w_up = jnp.swapaxes(w_gate, 1, 2), jnp.swapaxes(w_up, 1, 2)
    gates = gate_weights[0]
    facts = jnp.concatenate([target, gates, gates, gates], axis=1)
    facts = jnp.pad(facts, ((0, 0), (0, 128 - facts.shape[1])))
    stream, piece = norm_tokens(context, residual[0], norm_gain, facts, share, offsets)

    slots = jnp.arange(group // PAGE, dtype=jnp.int32)
    order = jnp.sum(jnp.where(page_table[0][None, :] == slots[:, None], slots[None, :], 0), axis=1)

    def fill_cache(late):
        pages = pick_pages(packed, order, late, n_seq, span)
        sent = lax.all_to_all(pages, "seq", split_axis=0, concat_axis=0, tiled=True)
        return pages, join_pages(sent, share, offsets, span)

    if (n_seq, n_exp) == (8, 4):
        mixture, cache = exchange_experts(piece, w_gate, w_up, w_down, n_seq, n_exp, fill_cache)
    else:
        _, cache = fill_cache(piece)
        blocks = n_seq * n_exp
        everything = lax.all_gather(piece, everyone, axis=0, tiled=True)
        facts = everything[:, width : width + 8].astype(jnp.float32)
        facts = facts.reshape(blocks // CHUNK_BLOCKS, CHUNK_BLOCKS * rows_dev, 8).transpose(0, 2, 1)
        gates = facts[:, 2:4] + facts[:, 4:6] + facts[:, 6:8]
        partial = experts(
            everything[:, :width], facts[:, :2].astype(jnp.int32), gates, w_gate, w_up, w_down, first
        )
        mixture = lax.psum_scatter(partial, everyone, scatter_dimension=0, tiled=True).astype(jnp.float32)
    layer_out = (stream + mixture).astype(jnp.bfloat16)
    return (layer_out[None], cache.reshape(1, rows_dev // PAGE, PAGE, 2 * width))


def solution(mesh):
    in_specs = (
        P("exp", "seq", None),
        P("exp", "seq", None, None),
        P("exp", "seq", None),
        P(),
        P("exp", None),
        P("exp", "seq", None),
        P("exp", "seq", None),
        P("exp", None),
        P("exp", None, "seq"),
        P("exp", None, "seq"),
        P("exp", "seq", None),
    )
    out_specs = (P("exp", "seq", None), P("exp", "seq", None, None))
    run = functools.partial(body, mesh.shape["seq"], mesh.shape["exp"])
    return jax.shard_map(run, mesh=mesh, in_specs=in_specs, out_specs=out_specs, check_vma=False)
```

```python
import functools
import math

import jax
import jax.numpy as jnp
from jax import lax
from jax.experimental import pallas as pl
from jax.experimental.pallas import tpu as pltpu
from jax.sharding import PartitionSpec as P

HEADS = 36
HEAD_DIM = 64
EXPERTS = 8
PAGE = 16
CAP = 24
CHUNK_BLOCKS = 8


def head_ranges(width, n_seq):
    share = width // n_seq
    firsts = [j * share // HEAD_DIM for j in range(n_seq)]
    count = max(-(-(j + 1) * share // HEAD_DIM) - firsts[j] for j in range(n_seq))
    firsts = [min(f, HEADS - count) for f in firsts]
    return share, firsts, count


def attention_kernel(heads, q_rows, packed_ref, seg_row_ref, seg_col_ref, out_ref):
    total = packed_ref.shape[0]
    span = heads * HEAD_DIM
    scale = 1.0 / math.sqrt(HEAD_DIM)
    for start in range(0, total, q_rows):
        end = start + q_rows
        q_place = start + lax.broadcasted_iota(jnp.int32, (q_rows, end), 0)
        k_place = lax.broadcasted_iota(jnp.int32, (q_rows, end), 1)
        visible = (seg_col_ref[start:end, :] == seg_row_ref[:, :end]) & (k_place <= q_place)
        parts = []
        for h in range(heads):
            a = h * HEAD_DIM
            q = packed_ref[start:end, a : a + HEAD_DIM]
            k = packed_ref[:end, span + a : span + a + HEAD_DIM]
            v = packed_ref[:end, 2 * span + a : 2 * span + a + HEAD_DIM]
            s = lax.dot_general(q, k, (((1,), (1,)), ((), ())), preferred_element_type=jnp.float32)
            s = jnp.where(visible, s * scale, -1e30)
            top = jnp.max(s, axis=1, keepdims=True)
            p = jnp.exp(s - top)
            denominator = jnp.sum(p, axis=1, keepdims=True)
            o = jnp.dot(p.astype(jnp.bfloat16), v, preferred_element_type=jnp.float32)
            parts.append((o / denominator).astype(jnp.bfloat16))
        out_ref[start:end, :] = jnp.concatenate(parts, axis=1)


def attention(packed, segments, heads):
    total = packed.shape[0]
    span = heads * HEAD_DIM
    return pl.pallas_call(
        functools.partial(attention_kernel, heads, 128),
        out_shape=jax.ShapeDtypeStruct((total, span), jnp.bfloat16),
        compiler_params=pltpu.CompilerParams(vmem_limit_bytes=40 * 1024 * 1024),
        cost_estimate=pl.CostEstimate(
            flops=4 * total * total * span, bytes_accessed=8 * total * span, transcendentals=total * total * heads
        ),
    )(packed, segments[None, :], segments[:, None])


def dot_t(a, b):
    return lax.dot_general(a, b, (((1,), (1,)), ((), ())), preferred_element_type=jnp.float32)


def expert_kernel(
    local, rows, tokens, first_ref, x_ref, tgt_ref, gates_ref, wg_ref, wu_ref, wd_ref, out_ref, kept_ref
):
    le = pl.program_id(0)
    chunk = pl.program_id(1)

    def selection(which):
        base = (first_ref[0] + which) * CAP
        row_id = lax.broadcasted_iota(jnp.int32, (rows, tokens), 0)
        block = lax.broadcasted_iota(jnp.int32, (1, tokens), 1) // 64
        picks, weights = None, None
        for j in range(2):
            slot = tgt_ref[0, j : j + 1, :] - base
            place = jnp.where((slot >= 0) & (slot < CAP), block * CAP + slot, -1)
            hit = row_id == place
            gate = jnp.where(hit, gates_ref[0, j : j + 1, :], 0.0)
            picks = hit if picks is None else picks | hit
            weights = gate if weights is None else weights + gate
        return picks.astype(jnp.float32).astype(jnp.bfloat16), jnp.sum(weights, axis=1, keepdims=True)

    pick, weight = selection(le)
    chosen = jnp.dot(pick, x_ref[...], preferred_element_type=jnp.float32).astype(jnp.bfloat16)
    gate = dot_t(chosen, wg_ref[0])
    upper = dot_t(chosen, wu_ref[0])
    hidden = (gate / (1.0 + jnp.exp(-gate)) * upper).astype(jnp.bfloat16)
    y = jnp.dot(hidden, wd_ref[0], preferred_element_type=jnp.float32)
    y = (y * weight).astype(jnp.bfloat16)

    if local > 1:

        @pl.when(le < local - 1)
        def _():
            kept_ref[le, chunk] = y

    @pl.when(le == local - 1)
    def _():
        total = lax.dot_general(pick, y, (((0,), (0,)), ((), ())), preferred_element_type=jnp.float32)
        for other in range(local - 1):
            pick_o, _ = selection(other)
            total += lax.dot_general(
                pick_o, kept_ref[other, chunk], (((0,), (0,)), ((), ())), preferred_element_type=jnp.float32
            )
        out_ref[...] = total.astype(jnp.bfloat16)


def experts(x, tgt, gates, w_gate, w_up, w_down, first):
    local, hidden, width = w_gate.shape
    chunks, _, tokens = tgt.shape
    rows = tokens // 64 * CAP
    last = local - 1
    return pl.pallas_call(
        functools.partial(expert_kernel, local, rows, tokens),
        out_shape=jax.ShapeDtypeStruct(x.shape, jnp.bfloat16),
        grid=(local, chunks),
        in_specs=[
            pl.BlockSpec(memory_space=pltpu.SMEM),
            pl.BlockSpec((tokens, width), lambda e, c: (c, 0)),
            pl.BlockSpec((1, 2, tokens), lambda e, c: (c, 0, 0)),
            pl.BlockSpec((1, 2, tokens), lambda e, c: (c, 0, 0)),
            pl.BlockSpec((1, hidden, width), lambda e, c: (e, 0, 0)),
            pl.BlockSpec((1, hidden, width), lambda e, c: (e, 0, 0)),
            pl.BlockSpec((1, hidden, width), lambda e, c: (e, 0, 0)),
        ],
        out_specs=pl.BlockSpec((tokens, width), lambda e, c: (jnp.where(e == last, c, 0), 0)),
        scratch_shapes=[pltpu.VMEM((max(last, 1), chunks if last else 1, rows, width), jnp.bfloat16)],
        compiler_params=pltpu.CompilerParams(vmem_limit_bytes=58 * 1024 * 1024),
        cost_estimate=pl.CostEstimate(
            flops=6 * local * chunks * rows * width * hidden,
            bytes_accessed=6 * local * width * hidden + 6 * chunks * tokens * width,
            transcendentals=local * chunks * rows * hidden,
        ),
    )(first, x, tgt, gates, w_gate, w_up, w_down)


def pack_kernel(firsts, span, q_ref, k_ref, v_ref, out_ref):
    for j, first in enumerate(firsts):
        lanes = slice(first * HEAD_DIM, first * HEAD_DIM + span)
        out_ref[j] = jnp.concatenate([r[:, lanes] for r in (q_ref, k_ref, v_ref)], axis=1)


def pack_heads(query, keys, values, firsts, span):
    rows_dev = query.shape[0]
    n_seq = len(firsts)
    return pl.pallas_call(
        functools.partial(pack_kernel, firsts, span),
        out_shape=jax.ShapeDtypeStruct((n_seq, rows_dev, 3 * span), jnp.bfloat16),
        cost_estimate=pl.CostEstimate(flops=0, bytes_accessed=12 * n_seq * rows_dev * span, transcendentals=0),
    )(query, keys, values)


def norm_kernel(share, offsets, context_ref, residual_ref, gain_ref, facts_ref, stream_ref, piece_ref):
    n_seq, _, _ = context_ref.shape
    width = residual_ref.shape[1]
    parts = [context_ref[j][:, offsets[j] : offsets[j] + share] for j in range(n_seq)]
    context = jnp.concatenate(parts, axis=1).astype(jnp.float32)
    stream = residual_ref[...].astype(jnp.float32) + context
    stream_ref[...] = stream
    mean = jnp.mean(stream * stream, axis=1, keepdims=True)
    normed = stream * lax.rsqrt(mean + 1e-05) * gain_ref[...].astype(jnp.float32)
    piece_ref[:, :width] = normed.astype(jnp.bfloat16)
    facts = facts_ref[...]
    lane = lax.broadcasted_iota(jnp.int32, facts.shape, 1)
    high = facts.astype(jnp.bfloat16).astype(jnp.float32)
    middle = (facts - high).astype(jnp.bfloat16).astype(jnp.float32)
    low = facts - high - middle
    own = jnp.where(lane < 4, high, jnp.where(lane < 6, middle, low))
    piece_ref[:, width:] = own.astype(jnp.bfloat16)


def norm_tokens(context, residual, gain, facts, share, offsets):
    rows_dev, width = residual.shape
    return pl.pallas_call(
        functools.partial(norm_kernel, share, offsets),
        out_shape=(
            jax.ShapeDtypeStruct((rows_dev, width), jnp.float32),
            jax.ShapeDtypeStruct((rows_dev, width + facts.shape[1]), jnp.bfloat16),
        ),
        cost_estimate=pl.CostEstimate(
            flops=10 * rows_dev * width, bytes_accessed=10 * rows_dev * width, transcendentals=rows_dev
        ),
    )(context, residual, gain[None, :], facts)


def pick_pages_kernel(per_device, first_lane, order_ref, packed_ref, late_ref, out_ref):
    del late_ref
    for j in range(out_ref.shape[0]):
        for i in range(per_device):
            rows = pl.ds(pl.multiple_of(order_ref[j * per_device + i] * PAGE, PAGE), PAGE)
            out_ref[j, i * PAGE : (i + 1) * PAGE, :] = packed_ref[rows, first_lane:]


def pick_pages(packed, order, late, n_seq, span):
    rows = packed.shape[0] // n_seq
    vmem = pl.BlockSpec(memory_space=pltpu.VMEM)
    return pl.pallas_call(
        functools.partial(pick_pages_kernel, rows // PAGE, span),
        out_shape=jax.ShapeDtypeStruct((n_seq, rows, 2 * span), jnp.bfloat16),
        in_specs=[pl.BlockSpec(memory_space=pltpu.SMEM), vmem, pl.BlockSpec(memory_space=pl.ANY)],
        cost_estimate=pl.CostEstimate(flops=0, bytes_accessed=10 * packed.shape[0] * span, transcendentals=0),
    )(order, packed, late)


def join_pages_kernel(share, offsets, span, pages_ref, out_ref):
    width = share * len(offsets)
    for part in range(2):
        parts = [
            pages_ref[j][:, part * span + offsets[j] : part * span + offsets[j] + share]
            for j in range(len(offsets))
        ]
        out_ref[:, part * width : (part + 1) * width] = jnp.concatenate(parts, axis=1)


def join_pages(pages, share, offsets, span):
    n_seq, rows, _ = pages.shape
    return pl.pallas_call(
        functools.partial(join_pages_kernel, share, offsets, span),
        out_shape=jax.ShapeDtypeStruct((rows, 2 * share * n_seq), jnp.bfloat16),
        cost_estimate=pl.CostEstimate(flops=0, bytes_accessed=8 * rows * n_seq * span, transcendentals=0),
    )(pages)


def places_of(slots, base, shift):
    place = -1
    for slot in slots:
        slot = slot.astype(jnp.int32) - base
        place = jnp.where((slot >= 0) & (slot < CAP), shift + slot, place)
    return place


def facts_by_lane(x):
    unit = lax.broadcasted_iota(jnp.int32, (8, 128), 0) == lax.broadcasted_iota(jnp.int32, (8, 128), 1)
    return dot_t(unit.astype(jnp.float32).astype(jnp.bfloat16), x)


def select_kernel(local, rows_dev, count, bases_ref, *refs):
    piece_refs, (own_ref, sib_ref, facts_ref) = refs[:count], refs[-3:]
    width = own_ref.shape[2]
    tokens, rows = 4 * rows_dev, 4 * CAP
    shift = lax.broadcasted_iota(jnp.int32, (1, tokens), 1) // rows_dev * CAP
    row_id = lax.broadcasted_iota(jnp.int32, (rows, tokens), 0)
    for g in range(len(piece_refs) // 4):
        x = jnp.concatenate([p[...] for p in piece_refs[4 * g : 4 * g + 4]], axis=0)
        facts_ref[g * tokens : (g + 1) * tokens, :] = x[:, width:]
        facts = facts_by_lane(x[:, width:])
        picks = []
        for core in range(2):
            for e in range(local):
                base = (bases_ref[core] + e) * CAP
                hit = row_id == places_of([facts[j : j + 1] for j in range(2)], base, shift)
                picks.append(hit.astype(jnp.float32))
        picks = jnp.concatenate(picks, axis=0).astype(jnp.bfloat16)
        chosen = jnp.dot(picks, x[:, :width], preferred_element_type=jnp.float32).astype(jnp.bfloat16)
        for e in range(local):
            own_ref[e, g * rows : (g + 1) * rows, :] = chosen[e * rows : (e + 1) * rows]
            sib_ref[e, g * rows : (g + 1) * rows, :] = chosen[(local + e) * rows : (local + e + 1) * rows]


def select_rows(pieces, bases, local, waits=()):
    rows_dev, wide = pieces[0].shape
    width = wide - 128
    rows = len(pieces) * CAP
    out = jax.ShapeDtypeStruct((local, rows, width), jnp.bfloat16)
    vmem = pl.BlockSpec(memory_space=pltpu.VMEM)
    return pl.pallas_call(
        functools.partial(select_kernel, local, rows_dev, len(pieces)),
        out_shape=(out, out, jax.ShapeDtypeStruct((len(pieces) * rows_dev, 128), jnp.bfloat16)),
        in_specs=[pl.BlockSpec(memory_space=pltpu.SMEM)]
        + [vmem] * len(pieces)
        + [pl.BlockSpec(memory_space=pl.ANY)] * len(waits),
        out_specs=(vmem, vmem, vmem),
        compiler_params=pltpu.CompilerParams(vmem_limit_bytes=28 * 1024 * 1024),
        cost_estimate=pl.CostEstimate(
            flops=16 * local * CAP * rows_dev * len(pieces) * width,
            bytes_accessed=2 * len(pieces) * rows_dev * wide + 4 * local * rows * width,
            transcendentals=0,
        ),
    )(bases, *pieces, *waits)


def rows_kernel(local, waits, own_ref, got_ref, wg_hbm, wu_hbm, wd_hbm, *rest):
    y_own_ref, y_sib_ref, wg, wu, wd, weight_sem = rest[waits:]
    half = own_ref.shape[1]
    copies = [
        [
            pltpu.make_async_copy(source.at[e], target.at[e], weight_sem.at[3 * e + i])
            for i, (source, target) in enumerate(((wg_hbm, wg), (wu_hbm, wu), (wd_hbm, wd)))
        ]
        for e in range(local)
    ]
    for group in copies:
        for copy in group:
            copy.start()
    for e in range(local):
        rows = jnp.concatenate([own_ref[e], got_ref[e]], axis=0)
        copies[e][0].wait()
        gate = dot_t(rows, wg[e])
        copies[e][1].wait()
        upper = dot_t(rows, wu[e])
        hidden = (gate / (1.0 + jnp.exp(-gate)) * upper).astype(jnp.bfloat16)
        copies[e][2].wait()
        y = jnp.dot(hidden, wd[e], preferred_element_type=jnp.float32).astype(jnp.bfloat16)
        y_own_ref[e] = y[:half]
        y_sib_ref[e] = y[half:]


def expert_rows(own, got, w_gate, w_up, w_down, waits):
    local, hidden, width = w_gate.shape
    rows = 2 * own.shape[1]
    out = jax.ShapeDtypeStruct(own.shape, jnp.bfloat16)
    vmem = pl.BlockSpec(memory_space=pltpu.VMEM)
    weights = pltpu.VMEM((local, hidden, width), jnp.bfloat16)
    return pl.pallas_call(
        functools.partial(rows_kernel, local, len(waits)),
        out_shape=(out, out),
        in_specs=[vmem, vmem] + [pl.BlockSpec(memory_space=pl.ANY)] * (3 + len(waits)),
        out_specs=(vmem, vmem),
        scratch_shapes=[weights, weights, weights, pltpu.SemaphoreType.DMA((3 * local,))],
        compiler_params=pltpu.CompilerParams(vmem_limit_bytes=44 * 1024 * 1024),
        cost_estimate=pl.CostEstimate(
            flops=6 * local * rows * width * hidden,
            bytes_accessed=6 * local * width * hidden + 4 * local * rows * width,
            transcendentals=local * rows * hidden,
        ),
    )(own, got, w_gate, w_up, w_down, *waits)


def put_kernel(local, rows_dev, planes, waits, bases_ref, y_own_ref, y_got_ref, facts_ref, *rest):
    kept_ref, *send_refs = rest[waits:]
    tokens, rows = 4 * rows_dev, 4 * CAP
    total = 2 * local * rows
    shift_lane = lax.broadcasted_iota(jnp.int32, (1, tokens), 1) // rows_dev * CAP
    shift_row = lax.broadcasted_iota(jnp.int32, (tokens, 1), 0) // rows_dev * CAP
    row_id = lax.broadcasted_iota(jnp.int32, (rows, tokens), 0)
    lane = lax.broadcasted_iota(jnp.int32, (tokens, total), 1)
    for g in range(planes):
        facts = facts_ref[g * tokens : (g + 1) * tokens, :]
        by_lane = facts_by_lane(facts)
        by_row = facts.astype(jnp.float32)
        here = slice(g * rows, (g + 1) * rows)
        weighed, put = [], None
        for core, y_ref in enumerate((y_own_ref, y_got_ref)):
            for e in range(local):
                base = (bases_ref[core] + e) * CAP
                weight = jnp.zeros((rows, tokens), jnp.float32)
                for j in range(2):
                    hit = row_id == places_of([by_lane[j : j + 1]], base, shift_lane)
                    gate = by_lane[2 + j : 3 + j] + by_lane[4 + j : 5 + j] + by_lane[6 + j : 7 + j]
                    weight = weight + jnp.where(hit, gate, 0.0)
                weight = jnp.sum(weight, axis=1, keepdims=True)
                weighed.append((y_ref[e, here, :].astype(jnp.float32) * weight).astype(jnp.bfloat16))
                first = (core * local + e) * rows
                hit = lane == places_of([by_row[:, j : j + 1] for j in range(2)], base, shift_row + first)
                put = hit if put is None else put | hit
        put = put.astype(jnp.float32).astype(jnp.bfloat16)
        out = jnp.dot(put, jnp.concatenate(weighed, axis=0), preferred_element_type=jnp.float32)
        out = out.astype(jnp.bfloat16)
        kept_ref[g * tokens // 2 : (g + 1) * tokens // 2, :] = out[: tokens // 2]
        send_refs[g][...] = out[tokens // 2 :]


def put_rows(y_own, y_got, facts, bases, rows_dev, waits):
    local, _, width = y_own.shape
    tokens = facts.shape[0]
    planes = tokens // (4 * rows_dev)
    vmem = pl.BlockSpec(memory_space=pltpu.VMEM)
    shape = lambda n: jax.ShapeDtypeStruct((n, width), jnp.bfloat16)
    out = pl.pallas_call(
        functools.partial(put_kernel, local, rows_dev, planes, len(waits)),
        out_shape=(shape(2 * planes * rows_dev),) + (shape(2 * rows_dev),) * planes,
        in_specs=[pl.BlockSpec(memory_space=pltpu.SMEM), vmem, vmem, vmem]
        + [pl.BlockSpec(memory_space=pl.ANY)] * len(waits),
        out_specs=(vmem,) * (1 + planes),
        compiler_params=pltpu.CompilerParams(vmem_limit_bytes=28 * 1024 * 1024),
        cost_estimate=pl.CostEstimate(
            flops=16 * local * CAP * tokens * width,
            bytes_accessed=8 * local * tokens * width,
            transcendentals=0,
        ),
    )(bases, y_own, y_got, facts, *waits)
    return out[0], out[1:]


def swap(a, axis, size, distance):
    return lax.ppermute(a, axis, [(i, i ^ distance) for i in range(size)])


def fold_kernel(groups, count, waits, keep_ref, *rest):
    got_refs, (kept_ref, *send_refs) = rest[:count], rest[count + waits :]
    part = keep_ref.shape[0] // (2 * groups)
    span = got_refs[0].shape[0]
    for i in range(2 * groups):
        start = i * part
        got = got_refs[start // span][start % span : start % span + part, :]
        total = keep_ref[start : start + part, :].astype(jnp.float32) + got.astype(jnp.float32)
        total = total.astype(jnp.bfloat16)
        if i % 2 == 0:
            kept_ref[i // 2 * part : (i // 2 + 1) * part, :] = total
        else:
            send_refs[i // 2][...] = total


def fold(keep, gots, groups, waits=()):
    rows, width = keep.shape
    part = rows // (2 * groups)
    vmem = pl.BlockSpec(memory_space=pltpu.VMEM)
    shape = lambda n: jax.ShapeDtypeStruct((n, width), jnp.bfloat16)
    out = pl.pallas_call(
        functools.partial(fold_kernel, groups, len(gots), len(waits)),
        out_shape=(shape(groups * part),) + (shape(part),) * groups,
        in_specs=[vmem] * (1 + len(gots)) + [pl.BlockSpec(memory_space=pl.ANY)] * len(waits),
        out_specs=(vmem,) * (1 + groups),
        compiler_params=pltpu.CompilerParams(vmem_limit_bytes=24 * 1024 * 1024),
        cost_estimate=pl.CostEstimate(flops=rows * width, bytes_accessed=6 * rows * width, transcendentals=0),
    )(keep, *gots, *waits)
    return out[0], out[1:]


def exchange_experts(piece, w_gate, w_up, w_down, n_seq, n_exp, late_work):
    x = lambda a: swap(a, "seq", n_seq, 1)
    y = lambda a: swap(a, "exp", n_exp, 2)
    core = lambda a: swap(a, "exp", n_exp, 1)
    z = lambda a, k: swap(a, "seq", n_seq, 2 * k)
    local = w_gate.shape[0]
    me = lax.axis_index("exp").astype(jnp.int32)
    bases = jnp.stack([me, me ^ 1]) * local
    starts = [piece, z(piece, 1), z(piece, 2)]
    starts.append(z(starts[2], 1))

    def gather(k):
        near = []
        for start, (f, g) in ((starts[k], (x, y)), (starts[k + 1], (y, x))):
            by_f = f(start)
            near += [start, g(start), by_f, g(by_f)]
        return near

    near_a, near_b = gather(0), gather(2)
    first_b = [near_b[1], near_b[2], near_b[5], near_b[6]]
    own_a, sib_a, facts_a = select_rows(near_a, bases, local, first_b)
    got_a = core(sib_a)
    own_b, sib_b, facts_b = select_rows(near_b, bases, local)
    got_b = core(sib_b)
    own_a, sib_a = expert_rows(own_a, got_a, w_gate, w_up, w_down, [sib_b])
    pages, other = late_work(sib_a)
    got_a = core(sib_a)
    own_b, sib_b = expert_rows(own_b, got_b, w_gate, w_up, w_down, [pages, sib_a])
    got_b = core(sib_b)
    keep_a, (fx_a, fy_a) = put_rows(own_a, got_a, facts_a, bases, piece.shape[0], [sib_b])
    keep_a, (gy_a, gx_a) = fold(keep_a, [x(fx_a), y(fy_a)], 2)
    keep_b, (fx_b, fy_b) = put_rows(own_b, got_b, facts_b, bases, piece.shape[0], [other])
    keep_a, (z_a,) = fold(keep_a, [y(gy_a), x(gx_a)], 1)
    keep_b, (gy_b, gx_b) = fold(keep_b, [x(fx_b), y(fy_b)], 2, [z_a])
    back_a = z(z_a, 1)
    keep_b, (z_b,) = fold(keep_b, [y(gy_b), x(gx_b)], 1, [back_a])
    mine = keep_a.astype(jnp.float32) + back_a.astype(jnp.float32)
    over_z = (keep_b.astype(jnp.float32) + z(z_b, 1).astype(jnp.float32)).astype(jnp.bfloat16)
    return mine + z(over_z, 2).astype(jnp.float32), other


def body(
    n_seq,
    n_exp,
    query,
    key_value,
    residual,
    norm_gain,
    segment_ids,
    routes,
    gate_weights,
    page_table,
    w_gate,
    w_up,
    w_down,
):
    rows_dev, width = query.shape[1:]
    everyone = ("exp", "seq")
    group = segment_ids.shape[1]
    share, firsts, heads = head_ranges(width, n_seq)
    span = heads * HEAD_DIM

    flat = routes[0].reshape(rows_dev * 2)
    onehot = (flat[:, None] == jnp.arange(EXPERTS, dtype=jnp.int32)[None, :]).astype(jnp.int32)
    before = jnp.cumsum(onehot, axis=0) - onehot
    target = (flat * CAP + jnp.sum(before * onehot, axis=1)).reshape(rows_dev, 2).astype(jnp.float32)

    keys, values = key_value[0, :, 0], key_value[0, :, 1]

    packed = pack_heads(query[0], keys, values, firsts, span)
    packed = lax.all_to_all(packed, "seq", split_axis=0, concat_axis=0, tiled=True)
    packed = packed.reshape(group, 3 * span)
    context = attention(packed, segment_ids[0], heads)
    context = lax.all_to_all(
        context.reshape(n_seq, rows_dev, span), "seq", split_axis=0, concat_axis=0, tiled=True
    )
    offsets = [j * share - firsts[j] * HEAD_DIM for j in range(n_seq)]

    first = (lax.axis_index("exp") * (EXPERTS // n_exp)).astype(jnp.int32).reshape(1)
    w_gate, w_up = jnp.swapaxes(w_gate, 1, 2), jnp.swapaxes(w_up, 1, 2)
    gates = gate_weights[0]
    facts = jnp.concatenate([target, gates, gates, gates], axis=1)
    facts = jnp.pad(facts, ((0, 0), (0, 128 - facts.shape[1])))
    stream, piece = norm_tokens(context, residual[0], norm_gain, facts, share, offsets)

    slots = jnp.arange(group // PAGE, dtype=jnp.int32)
    order = jnp.sum(jnp.where(page_table[0][None, :] == slots[:, None], slots[None, :], 0), axis=1)

    def fill_cache(late):
        pages = pick_pages(packed, order, late, n_seq, span)
        sent = lax.all_to_all(pages, "seq", split_axis=0, concat_axis=0, tiled=True)
        return pages, join_pages(sent, share, offsets, span)

    if (n_seq, n_exp) == (8, 4):
        mixture, cache = exchange_experts(piece, w_gate, w_up, w_down, n_seq, n_exp, fill_cache)
    else:
        _, cache = fill_cache(piece)
        blocks = n_seq * n_exp
        everything = lax.all_gather(piece, everyone, axis=0, tiled=True)
        facts = everything[:, width : width + 8].astype(jnp.float32)
        facts = facts.reshape(blocks // CHUNK_BLOCKS, CHUNK_BLOCKS * rows_dev, 8).transpose(0, 2, 1)
        gates = facts[:, 2:4] + facts[:, 4:6] + facts[:, 6:8]
        partial = experts(
            everything[:, :width], facts[:, :2].astype(jnp.int32), gates, w_gate, w_up, w_down, first
        )
        mixture = lax.psum_scatter(partial, everyone, scatter_dimension=0, tiled=True).astype(jnp.float32)
    layer_out = (stream + mixture).astype(jnp.bfloat16)
    return (layer_out[None], cache.reshape(1, rows_dev // PAGE, PAGE, 2 * width))


def solution(mesh):
    in_specs = (
        P("exp", "seq", None),
        P("exp", "seq", None, None),
        P("exp", "seq", None),
        P(),
        P("exp", None),
        P("exp", "seq", None),
        P("exp", "seq", None),
        P("exp", None),
        P("exp", None, "seq"),
        P("exp", None, "seq"),
        P("exp", "seq", None),
    )
    out_specs = (P("exp", "seq", None), P("exp", "seq", None, None))
    run = functools.partial(body, mesh.shape["seq"], mesh.shape["exp"])
    return jax.shard_map(run, mesh=mesh, in_specs=in_specs, out_specs=out_specs, check_vma=False)
```

```python
import functools
import math

import jax
import jax.numpy as jnp
from jax import lax
from jax.experimental import pallas as pl
from jax.experimental.pallas import tpu as pltpu
from jax.sharding import PartitionSpec as P

HEADS = 36
HEAD_DIM = 64
EXPERTS = 8
PAGE = 16
CAP = 24
CHUNK_BLOCKS = 8


def head_ranges(width, n_seq):
    share = width // n_seq
    firsts = [j * share // HEAD_DIM for j in range(n_seq)]
    count = max(-(-(j + 1) * share // HEAD_DIM) - firsts[j] for j in range(n_seq))
    firsts = [min(f, HEADS - count) for f in firsts]
    return share, firsts, count


def attention_kernel(heads, q_rows, packed_ref, seg_row_ref, seg_col_ref, out_ref):
    total = packed_ref.shape[0]
    span = heads * HEAD_DIM
    scale = 1.0 / math.sqrt(HEAD_DIM)
    for start in range(0, total, q_rows):
        end = start + q_rows
        q_place = start + lax.broadcasted_iota(jnp.int32, (q_rows, end), 0)
        k_place = lax.broadcasted_iota(jnp.int32, (q_rows, end), 1)
        visible = (seg_col_ref[start:end, :] == seg_row_ref[:, :end]) & (k_place <= q_place)
        parts = []
        for h in range(heads):
            a = h * HEAD_DIM
            q = packed_ref[start:end, a : a + HEAD_DIM]
            k = packed_ref[:end, span + a : span + a + HEAD_DIM]
            v = packed_ref[:end, 2 * span + a : 2 * span + a + HEAD_DIM]
            s = lax.dot_general(q, k, (((1,), (1,)), ((), ())), preferred_element_type=jnp.float32)
            s = jnp.where(visible, s * scale, -1e30)
            top = jnp.max(s, axis=1, keepdims=True)
            p = jnp.exp(s - top)
            denominator = jnp.sum(p, axis=1, keepdims=True)
            o = jnp.dot(p.astype(jnp.bfloat16), v, preferred_element_type=jnp.float32)
            parts.append((o / denominator).astype(jnp.bfloat16))
        out_ref[start:end, :] = jnp.concatenate(parts, axis=1)


def attention(packed, segments, heads):
    total = packed.shape[0]
    span = heads * HEAD_DIM
    return pl.pallas_call(
        functools.partial(attention_kernel, heads, 128),
        out_shape=jax.ShapeDtypeStruct((total, span), jnp.bfloat16),
        compiler_params=pltpu.CompilerParams(vmem_limit_bytes=40 * 1024 * 1024),
        cost_estimate=pl.CostEstimate(
            flops=4 * total * total * span, bytes_accessed=8 * total * span, transcendentals=total * total * heads
        ),
    )(packed, segments[None, :], segments[:, None])


def dot_t(a, b):
    return lax.dot_general(a, b, (((1,), (1,)), ((), ())), preferred_element_type=jnp.float32)


def expert_kernel(
    local, rows, tokens, first_ref, x_ref, tgt_ref, gates_ref, wg_ref, wu_ref, wd_ref, out_ref, kept_ref
):
    le = pl.program_id(0)
    chunk = pl.program_id(1)

    def selection(which):
        base = (first_ref[0] + which) * CAP
        row_id = lax.broadcasted_iota(jnp.int32, (rows, tokens), 0)
        block = lax.broadcasted_iota(jnp.int32, (1, tokens), 1) // 64
        picks, weights = None, None
        for j in range(2):
            slot = tgt_ref[0, j : j + 1, :] - base
            place = jnp.where((slot >= 0) & (slot < CAP), block * CAP + slot, -1)
            hit = row_id == place
            gate = jnp.where(hit, gates_ref[0, j : j + 1, :], 0.0)
            picks = hit if picks is None else picks | hit
            weights = gate if weights is None else weights + gate
        return picks.astype(jnp.float32).astype(jnp.bfloat16), jnp.sum(weights, axis=1, keepdims=True)

    pick, weight = selection(le)
    chosen = jnp.dot(pick, x_ref[...], preferred_element_type=jnp.float32).astype(jnp.bfloat16)
    gate = dot_t(chosen, wg_ref[0])
    upper = dot_t(chosen, wu_ref[0])
    hidden = (gate / (1.0 + jnp.exp(-gate)) * upper).astype(jnp.bfloat16)
    y = jnp.dot(hidden, wd_ref[0], preferred_element_type=jnp.float32)
    y = (y * weight).astype(jnp.bfloat16)

    if local > 1:

        @pl.when(le < local - 1)
        def _():
            kept_ref[le, chunk] = y

    @pl.when(le == local - 1)
    def _():
        total = lax.dot_general(pick, y, (((0,), (0,)), ((), ())), preferred_element_type=jnp.float32)
        for other in range(local - 1):
            pick_o, _ = selection(other)
            total += lax.dot_general(
                pick_o, kept_ref[other, chunk], (((0,), (0,)), ((), ())), preferred_element_type=jnp.float32
            )
        out_ref[...] = total.astype(jnp.bfloat16)


def experts(x, tgt, gates, w_gate, w_up, w_down, first):
    local, hidden, width = w_gate.shape
    chunks, _, tokens = tgt.shape
    rows = tokens // 64 * CAP
    last = local - 1
    return pl.pallas_call(
        functools.partial(expert_kernel, local, rows, tokens),
        out_shape=jax.ShapeDtypeStruct(x.shape, jnp.bfloat16),
        grid=(local, chunks),
        in_specs=[
            pl.BlockSpec(memory_space=pltpu.SMEM),
            pl.BlockSpec((tokens, width), lambda e, c: (c, 0)),
            pl.BlockSpec((1, 2, tokens), lambda e, c: (c, 0, 0)),
            pl.BlockSpec((1, 2, tokens), lambda e, c: (c, 0, 0)),
            pl.BlockSpec((1, hidden, width), lambda e, c: (e, 0, 0)),
            pl.BlockSpec((1, hidden, width), lambda e, c: (e, 0, 0)),
            pl.BlockSpec((1, hidden, width), lambda e, c: (e, 0, 0)),
        ],
        out_specs=pl.BlockSpec((tokens, width), lambda e, c: (jnp.where(e == last, c, 0), 0)),
        scratch_shapes=[pltpu.VMEM((max(last, 1), chunks if last else 1, rows, width), jnp.bfloat16)],
        compiler_params=pltpu.CompilerParams(vmem_limit_bytes=58 * 1024 * 1024),
        cost_estimate=pl.CostEstimate(
            flops=6 * local * chunks * rows * width * hidden,
            bytes_accessed=6 * local * width * hidden + 6 * chunks * tokens * width,
            transcendentals=local * chunks * rows * hidden,
        ),
    )(first, x, tgt, gates, w_gate, w_up, w_down)


def pack_kernel(firsts, span, q_ref, k_ref, v_ref, out_ref):
    for j, first in enumerate(firsts):
        lanes = slice(first * HEAD_DIM, first * HEAD_DIM + span)
        out_ref[j] = jnp.concatenate([r[:, lanes] for r in (q_ref, k_ref, v_ref)], axis=1)


def pack_heads(query, keys, values, firsts, span):
    rows_dev = query.shape[0]
    n_seq = len(firsts)
    return pl.pallas_call(
        functools.partial(pack_kernel, firsts, span),
        out_shape=jax.ShapeDtypeStruct((n_seq, rows_dev, 3 * span), jnp.bfloat16),
        cost_estimate=pl.CostEstimate(flops=0, bytes_accessed=12 * n_seq * rows_dev * span, transcendentals=0),
    )(query, keys, values)


def norm_kernel(share, offsets, context_ref, residual_ref, gain_ref, facts_ref, stream_ref, piece_ref):
    n_seq, _, _ = context_ref.shape
    width = residual_ref.shape[1]
    parts = [context_ref[j][:, offsets[j] : offsets[j] + share] for j in range(n_seq)]
    context = jnp.concatenate(parts, axis=1).astype(jnp.float32)
    stream = residual_ref[...].astype(jnp.float32) + context
    stream_ref[...] = stream
    mean = jnp.mean(stream * stream, axis=1, keepdims=True)
    normed = stream * lax.rsqrt(mean + 1e-05) * gain_ref[...].astype(jnp.float32)
    piece_ref[:, :width] = normed.astype(jnp.bfloat16)
    facts = facts_ref[...]
    lane = lax.broadcasted_iota(jnp.int32, facts.shape, 1)
    high = facts.astype(jnp.bfloat16).astype(jnp.float32)
    middle = (facts - high).astype(jnp.bfloat16).astype(jnp.float32)
    low = facts - high - middle
    own = jnp.where(lane < 4, high, jnp.where(lane < 6, middle, low))
    piece_ref[:, width:] = own.astype(jnp.bfloat16)


def norm_tokens(context, residual, gain, facts, share, offsets):
    rows_dev, width = residual.shape
    return pl.pallas_call(
        functools.partial(norm_kernel, share, offsets),
        out_shape=(
            jax.ShapeDtypeStruct((rows_dev, width), jnp.float32),
            jax.ShapeDtypeStruct((rows_dev, width + facts.shape[1]), jnp.bfloat16),
        ),
        cost_estimate=pl.CostEstimate(
            flops=10 * rows_dev * width, bytes_accessed=10 * rows_dev * width, transcendentals=rows_dev
        ),
    )(context, residual, gain[None, :], facts)


def pick_pages_kernel(per_device, first_lane, order_ref, packed_ref, late_ref, out_ref):
    del late_ref
    for j in range(out_ref.shape[0]):
        for i in range(per_device):
            rows = pl.ds(pl.multiple_of(order_ref[j * per_device + i] * PAGE, PAGE), PAGE)
            out_ref[j, i * PAGE : (i + 1) * PAGE, :] = packed_ref[rows, first_lane:]


def pick_pages(packed, order, late, n_seq, span):
    rows = packed.shape[0] // n_seq
    vmem = pl.BlockSpec(memory_space=pltpu.VMEM)
    return pl.pallas_call(
        functools.partial(pick_pages_kernel, rows // PAGE, span),
        out_shape=jax.ShapeDtypeStruct((n_seq, rows, 2 * span), jnp.bfloat16),
        in_specs=[pl.BlockSpec(memory_space=pltpu.SMEM), vmem, pl.BlockSpec(memory_space=pl.ANY)],
        cost_estimate=pl.CostEstimate(flops=0, bytes_accessed=10 * packed.shape[0] * span, transcendentals=0),
    )(order, packed, late)


def join_pages_kernel(share, offsets, span, pages_ref, behind_ref, out_ref):
    del behind_ref
    width = share * len(offsets)
    for part in range(2):
        parts = [
            pages_ref[j][:, part * span + offsets[j] : part * span + offsets[j] + share]
            for j in range(len(offsets))
        ]
        out_ref[:, part * width : (part + 1) * width] = jnp.concatenate(parts, axis=1)


def join_pages(pages, share, offsets, span, behind):
    n_seq, rows, _ = pages.shape
    return pl.pallas_call(
        functools.partial(join_pages_kernel, share, offsets, span),
        out_shape=jax.ShapeDtypeStruct((rows, 2 * share * n_seq), jnp.bfloat16),
        in_specs=[pl.BlockSpec(memory_space=pltpu.VMEM), pl.BlockSpec(memory_space=pl.ANY)],
        cost_estimate=pl.CostEstimate(flops=0, bytes_accessed=8 * rows * n_seq * span, transcendentals=0),
    )(pages, behind)


def places_of(slots, base, shift):
    place = -1
    for slot in slots:
        slot = slot.astype(jnp.int32) - base
        place = jnp.where((slot >= 0) & (slot < CAP), shift + slot, place)
    return place


def hold_kernel(a_ref, *rest):
    rest[-1][...] = a_ref[...]


def hold(a, waits):
    return pl.pallas_call(
        hold_kernel,
        out_shape=jax.ShapeDtypeStruct(a.shape, a.dtype),
        in_specs=[pl.BlockSpec(memory_space=pltpu.VMEM)] + [pl.BlockSpec(memory_space=pl.ANY)] * len(waits),
        cost_estimate=pl.CostEstimate(flops=0, bytes_accessed=4 * a.size, transcendentals=0),
    )(a, *waits)


def facts_by_lane(x):
    unit = lax.broadcasted_iota(jnp.int32, (8, 128), 0) == lax.broadcasted_iota(jnp.int32, (8, 128), 1)
    return dot_t(unit.astype(jnp.float32).astype(jnp.bfloat16), x)


def select_kernel(local, rows_dev, count, bases_ref, *refs):
    piece_refs, (own_ref, sib_ref, facts_ref) = refs[:count], refs[-3:]
    width = own_ref.shape[2]
    tokens, rows = 4 * rows_dev, 4 * CAP
    shift = lax.broadcasted_iota(jnp.int32, (1, tokens), 1) // rows_dev * CAP
    row_id = lax.broadcasted_iota(jnp.int32, (rows, tokens), 0)
    for g in range(len(piece_refs) // 4):
        x = jnp.concatenate([p[...] for p in piece_refs[4 * g : 4 * g + 4]], axis=0)
        facts_ref[g * tokens : (g + 1) * tokens, :] = x[:, width:]
        facts = facts_by_lane(x[:, width:])
        picks = []
        for core in range(2):
            for e in range(local):
                base = (bases_ref[core] + e) * CAP
                hit = row_id == places_of([facts[j : j + 1] for j in range(2)], base, shift)
                picks.append(hit.astype(jnp.float32))
        picks = jnp.concatenate(picks, axis=0).astype(jnp.bfloat16)
        chosen = jnp.dot(picks, x[:, :width], preferred_element_type=jnp.float32).astype(jnp.bfloat16)
        for e in range(local):
            own_ref[e, g * rows : (g + 1) * rows, :] = chosen[e * rows : (e + 1) * rows]
            sib_ref[e, g * rows : (g + 1) * rows, :] = chosen[(local + e) * rows : (local + e + 1) * rows]


def select_rows(pieces, bases, local, waits=()):
    rows_dev, wide = pieces[0].shape
    width = wide - 128
    rows = len(pieces) * CAP
    out = jax.ShapeDtypeStruct((local, rows, width), jnp.bfloat16)
    vmem = pl.BlockSpec(memory_space=pltpu.VMEM)
    return pl.pallas_call(
        functools.partial(select_kernel, local, rows_dev, len(pieces)),
        out_shape=(out, out, jax.ShapeDtypeStruct((len(pieces) * rows_dev, 128), jnp.bfloat16)),
        in_specs=[pl.BlockSpec(memory_space=pltpu.SMEM)]
        + [vmem] * len(pieces)
        + [pl.BlockSpec(memory_space=pl.ANY)] * len(waits),
        out_specs=(vmem, vmem, vmem),
        compiler_params=pltpu.CompilerParams(vmem_limit_bytes=28 * 1024 * 1024),
        cost_estimate=pl.CostEstimate(
            flops=16 * local * CAP * rows_dev * len(pieces) * width,
            bytes_accessed=2 * len(pieces) * rows_dev * wide + 4 * local * rows * width,
            transcendentals=0,
        ),
    )(bases, *pieces, *waits)


def rows_kernel(local, waits, own_ref, got_ref, wg_hbm, wu_hbm, wd_hbm, *rest):
    y_own_ref, y_sib_ref, wg, wu, wd, weight_sem = rest[waits:]
    half = own_ref.shape[1]
    copies = [
        [
            pltpu.make_async_copy(source.at[e], target.at[e], weight_sem.at[3 * e + i])
            for i, (source, target) in enumerate(((wg_hbm, wg), (wu_hbm, wu), (wd_hbm, wd)))
        ]
        for e in range(local)
    ]
    for group in copies:
        for copy in group:
            copy.start()
    for e in range(local):
        rows = jnp.concatenate([own_ref[e], got_ref[e]], axis=0)
        copies[e][0].wait()
        gate = dot_t(rows, wg[e])
        copies[e][1].wait()
        upper = dot_t(rows, wu[e])
        hidden = (gate / (1.0 + jnp.exp(-gate)) * upper).astype(jnp.bfloat16)
        copies[e][2].wait()
        y = jnp.dot(hidden, wd[e], preferred_element_type=jnp.float32).astype(jnp.bfloat16)
        y_own_ref[e] = y[:half]
        y_sib_ref[e] = y[half:]


def expert_rows(own, got, w_gate, w_up, w_down, waits):
    local, hidden, width = w_gate.shape
    rows = 2 * own.shape[1]
    out = jax.ShapeDtypeStruct(own.shape, jnp.bfloat16)
    vmem = pl.BlockSpec(memory_space=pltpu.VMEM)
    weights = pltpu.VMEM((local, hidden, width), jnp.bfloat16)
    return pl.pallas_call(
        functools.partial(rows_kernel, local, len(waits)),
        out_shape=(out, out),
        in_specs=[vmem, vmem] + [pl.BlockSpec(memory_space=pl.ANY)] * (3 + len(waits)),
        out_specs=(vmem, vmem),
        scratch_shapes=[weights, weights, weights, pltpu.SemaphoreType.DMA((3 * local,))],
        compiler_params=pltpu.CompilerParams(vmem_limit_bytes=44 * 1024 * 1024),
        cost_estimate=pl.CostEstimate(
            flops=6 * local * rows * width * hidden,
            bytes_accessed=6 * local * width * hidden + 4 * local * rows * width,
            transcendentals=local * rows * hidden,
        ),
    )(own, got, w_gate, w_up, w_down, *waits)


def put_kernel(local, rows_dev, planes, waits, bases_ref, y_own_ref, y_got_ref, facts_ref, *rest):
    kept_ref, *send_refs = rest[waits:]
    tokens, rows = 4 * rows_dev, 4 * CAP
    total = 2 * local * rows
    shift_lane = lax.broadcasted_iota(jnp.int32, (1, tokens), 1) // rows_dev * CAP
    shift_row = lax.broadcasted_iota(jnp.int32, (tokens, 1), 0) // rows_dev * CAP
    row_id = lax.broadcasted_iota(jnp.int32, (rows, tokens), 0)
    lane = lax.broadcasted_iota(jnp.int32, (tokens, total), 1)
    for g in range(planes):
        facts = facts_ref[g * tokens : (g + 1) * tokens, :]
        by_lane = facts_by_lane(facts)
        by_row = facts.astype(jnp.float32)
        here = slice(g * rows, (g + 1) * rows)
        weighed, put = [], None
        for core, y_ref in enumerate((y_own_ref, y_got_ref)):
            for e in range(local):
                base = (bases_ref[core] + e) * CAP
                weight = jnp.zeros((rows, tokens), jnp.float32)
                for j in range(2):
                    hit = row_id == places_of([by_lane[j : j + 1]], base, shift_lane)
                    gate = by_lane[2 + j : 3 + j] + by_lane[4 + j : 5 + j] + by_lane[6 + j : 7 + j]
                    weight = weight + jnp.where(hit, gate, 0.0)
                weight = jnp.sum(weight, axis=1, keepdims=True)
                weighed.append((y_ref[e, here, :].astype(jnp.float32) * weight).astype(jnp.bfloat16))
                first = (core * local + e) * rows
                hit = lane == places_of([by_row[:, j : j + 1] for j in range(2)], base, shift_row + first)
                put = hit if put is None else put | hit
        put = put.astype(jnp.float32).astype(jnp.bfloat16)
        out = jnp.dot(put, jnp.concatenate(weighed, axis=0), preferred_element_type=jnp.float32)
        out = out.astype(jnp.bfloat16)
        kept_ref[g * tokens // 2 : (g + 1) * tokens // 2, :] = out[: tokens // 2]
        send_refs[g][...] = out[tokens // 2 :]


def put_rows(y_own, y_got, facts, bases, rows_dev, waits):
    local, _, width = y_own.shape
    tokens = facts.shape[0]
    planes = tokens // (4 * rows_dev)
    vmem = pl.BlockSpec(memory_space=pltpu.VMEM)
    shape = lambda n: jax.ShapeDtypeStruct((n, width), jnp.bfloat16)
    out = pl.pallas_call(
        functools.partial(put_kernel, local, rows_dev, planes, len(waits)),
        out_shape=(shape(2 * planes * rows_dev),) + (shape(2 * rows_dev),) * planes,
        in_specs=[pl.BlockSpec(memory_space=pltpu.SMEM), vmem, vmem, vmem]
        + [pl.BlockSpec(memory_space=pl.ANY)] * len(waits),
        out_specs=(vmem,) * (1 + planes),
        compiler_params=pltpu.CompilerParams(vmem_limit_bytes=28 * 1024 * 1024),
        cost_estimate=pl.CostEstimate(
            flops=16 * local * CAP * tokens * width,
            bytes_accessed=8 * local * tokens * width,
            transcendentals=0,
        ),
    )(bases, y_own, y_got, facts, *waits)
    return out[0], out[1:]


def swap(a, axis, size, distance):
    return lax.ppermute(a, axis, [(i, i ^ distance) for i in range(size)])


def fold_kernel(groups, count, waits, keep_ref, *rest):
    got_refs, (kept_ref, *send_refs) = rest[:count], rest[count + waits :]
    part = keep_ref.shape[0] // (2 * groups)
    span = got_refs[0].shape[0]
    for i in range(2 * groups):
        start = i * part
        got = got_refs[start // span][start % span : start % span + part, :]
        total = keep_ref[start : start + part, :].astype(jnp.float32) + got.astype(jnp.float32)
        total = total.astype(jnp.bfloat16)
        if i % 2 == 0:
            kept_ref[i // 2 * part : (i // 2 + 1) * part, :] = total
        else:
            send_refs[i // 2][...] = total


def fold(keep, gots, groups, waits=()):
    rows, width = keep.shape
    part = rows // (2 * groups)
    vmem = pl.BlockSpec(memory_space=pltpu.VMEM)
    shape = lambda n: jax.ShapeDtypeStruct((n, width), jnp.bfloat16)
    out = pl.pallas_call(
        functools.partial(fold_kernel, groups, len(gots), len(waits)),
        out_shape=(shape(groups * part),) + (shape(part),) * groups,
        in_specs=[vmem] * (1 + len(gots)) + [pl.BlockSpec(memory_space=pl.ANY)] * len(waits),
        out_specs=(vmem,) * (1 + groups),
        compiler_params=pltpu.CompilerParams(vmem_limit_bytes=24 * 1024 * 1024),
        cost_estimate=pl.CostEstimate(flops=rows * width, bytes_accessed=6 * rows * width, transcendentals=0),
    )(keep, *gots, *waits)
    return out[0], out[1:]


def exchange_experts(piece, w_gate, w_up, w_down, n_seq, n_exp, late_work):
    x = lambda a: swap(a, "seq", n_seq, 1)
    y = lambda a: swap(a, "exp", n_exp, 2)
    core = lambda a: swap(a, "exp", n_exp, 1)
    z = lambda a, k: swap(a, "seq", n_seq, 2 * k)
    local = w_gate.shape[0]
    me = lax.axis_index("exp").astype(jnp.int32)
    bases = jnp.stack([me, me ^ 1]) * local
    starts = [piece, z(piece, 1), z(piece, 2)]
    ways = [("xy", "yx")[k % 2] for k in range(4)]
    over = {"x": x, "y": y}
    single = [[over[way](starts[k]) for way in ways[k]] for k in range(2)]
    starts[2] = hold(starts[2], single[0] + single[1])
    starts.append(z(starts[2], 1))
    single += [[over[way](starts[k]) for way in ways[k]] for k in range(2, 4)]

    def gather(k):
        near = []
        for i in (k, k + 1):
            by_f, by_g = single[i]
            near += [starts[i], by_g, by_f, over[ways[i][1]](by_f)]
        return near

    near_b, near_a = gather(0), gather(2)
    own_a, sib_a, facts_a = select_rows(near_a, bases, local)
    got_a = core(sib_a)
    own_b, sib_b, facts_b = select_rows(near_b, bases, local)
    got_b = core(sib_b)
    pages, fill = late_work(sib_b)
    own_a, sib_a = expert_rows(own_a, got_a, w_gate, w_up, w_down, [sib_b, pages])
    other = fill(sib_a)
    got_a = core(sib_a)
    own_b, sib_b = expert_rows(own_b, got_b, w_gate, w_up, w_down, [other, sib_a])
    got_b = core(sib_b)
    keep_a, (fx_a, fy_a) = put_rows(own_a, got_a, facts_a, bases, piece.shape[0], [sib_b])
    keep_a, (gy_a, gx_a) = fold(keep_a, [x(fx_a), y(fy_a)], 2)
    keep_b, (fx_b, fy_b) = put_rows(own_b, got_b, facts_b, bases, piece.shape[0], [gy_a])
    keep_a, (z_a,) = fold(keep_a, [y(gy_a), x(gx_a)], 1)
    keep_b, (gy_b, gx_b) = fold(keep_b, [x(fx_b), y(fy_b)], 2, [z_a])
    over_z = (keep_a.astype(jnp.float32) + z(z_a, 1).astype(jnp.float32)).astype(jnp.bfloat16)
    keep_b, (z_b,) = fold(keep_b, [y(gy_b), x(gx_b)], 1, [over_z])
    mine = keep_b.astype(jnp.float32) + z(z_b, 1).astype(jnp.float32)
    return mine + z(over_z, 2).astype(jnp.float32), other


def body(
    n_seq,
    n_exp,
    query,
    key_value,
    residual,
    norm_gain,
    segment_ids,
    routes,
    gate_weights,
    page_table,
    w_gate,
    w_up,
    w_down,
):
    rows_dev, width = query.shape[1:]
    everyone = ("exp", "seq")
    group = segment_ids.shape[1]
    share, firsts, heads = head_ranges(width, n_seq)
    span = heads * HEAD_DIM

    flat = routes[0].reshape(rows_dev * 2)
    onehot = (flat[:, None] == jnp.arange(EXPERTS, dtype=jnp.int32)[None, :]).astype(jnp.int32)
    before = jnp.cumsum(onehot, axis=0) - onehot
    target = (flat * CAP + jnp.sum(before * onehot, axis=1)).reshape(rows_dev, 2).astype(jnp.float32)

    keys, values = key_value[0, :, 0], key_value[0, :, 1]

    packed = pack_heads(query[0], keys, values, firsts, span)
    packed = lax.all_to_all(packed, "seq", split_axis=0, concat_axis=0, tiled=True)
    packed = packed.reshape(group, 3 * span)
    context = attention(packed, segment_ids[0], heads)
    context = lax.all_to_all(
        context.reshape(n_seq, rows_dev, span), "seq", split_axis=0, concat_axis=0, tiled=True
    )
    offsets = [j * share - firsts[j] * HEAD_DIM for j in range(n_seq)]

    first = (lax.axis_index("exp") * (EXPERTS // n_exp)).astype(jnp.int32).reshape(1)
    w_gate, w_up = jnp.swapaxes(w_gate, 1, 2), jnp.swapaxes(w_up, 1, 2)
    gates = gate_weights[0]
    facts = jnp.concatenate([target, gates, gates, gates], axis=1)
    facts = jnp.pad(facts, ((0, 0), (0, 128 - facts.shape[1])))
    stream, piece = norm_tokens(context, residual[0], norm_gain, facts, share, offsets)

    slots = jnp.arange(group // PAGE, dtype=jnp.int32)
    order = jnp.sum(jnp.where(page_table[0][None, :] == slots[:, None], slots[None, :], 0), axis=1)

    def fill_cache(late):
        pages = pick_pages(packed, order, late, n_seq, span)
        sent = lax.all_to_all(pages, "seq", split_axis=0, concat_axis=0, tiled=True)
        return pages, lambda behind: join_pages(sent, share, offsets, span, behind)

    if (n_seq, n_exp) == (8, 4):
        mixture, cache = exchange_experts(piece, w_gate, w_up, w_down, n_seq, n_exp, fill_cache)
    else:
        cache = fill_cache(piece)[1](piece)
        blocks = n_seq * n_exp
        everything = lax.all_gather(piece, everyone, axis=0, tiled=True)
        facts = everything[:, width : width + 8].astype(jnp.float32)
        facts = facts.reshape(blocks // CHUNK_BLOCKS, CHUNK_BLOCKS * rows_dev, 8).transpose(0, 2, 1)
        gates = facts[:, 2:4] + facts[:, 4:6] + facts[:, 6:8]
        partial = experts(
            everything[:, :width], facts[:, :2].astype(jnp.int32), gates, w_gate, w_up, w_down, first
        )
        mixture = lax.psum_scatter(partial, everyone, scatter_dimension=0, tiled=True).astype(jnp.float32)
    layer_out = (stream + mixture).astype(jnp.bfloat16)
    return (layer_out[None], cache.reshape(1, rows_dev // PAGE, PAGE, 2 * width))


def solution(mesh):
    in_specs = (
        P("exp", "seq", None),
        P("exp", "seq", None, None),
        P("exp", "seq", None),
        P(),
        P("exp", None),
        P("exp", "seq", None),
        P("exp", "seq", None),
        P("exp", None),
        P("exp", None, "seq"),
        P("exp", None, "seq"),
        P("exp", "seq", None),
    )
    out_specs = (P("exp", "seq", None), P("exp", "seq", None, None))
    run = functools.partial(body, mesh.shape["seq"], mesh.shape["exp"])
    return jax.shard_map(run, mesh=mesh, in_specs=in_specs, out_specs=out_specs, check_vma=False)
```

```python
import functools
import math

import jax
import jax.numpy as jnp
from jax import lax
from jax.experimental import pallas as pl
from jax.experimental.pallas import tpu as pltpu
from jax.sharding import PartitionSpec as P

HEADS = 36
HEAD_DIM = 64
EXPERTS = 8
PAGE = 16
CAP = 24
MIB = 1024 * 1024
CHUNK_BLOCKS = 8


def head_ranges(width, n_seq):
    share = width // n_seq
    firsts = [j * share // HEAD_DIM for j in range(n_seq)]
    count = max(-(-(j + 1) * share // HEAD_DIM) - firsts[j] for j in range(n_seq))
    firsts = [min(f, HEADS - count) for f in firsts]
    return share, firsts, count


def attention_kernel(heads, q_rows, packed_ref, seg_row_ref, seg_col_ref, out_ref):
    total = packed_ref.shape[0]
    span = heads * HEAD_DIM
    scale = 1.0 / math.sqrt(HEAD_DIM)
    for start in range(0, total, q_rows):
        end = start + q_rows
        q_place = start + lax.broadcasted_iota(jnp.int32, (q_rows, end), 0)
        k_place = lax.broadcasted_iota(jnp.int32, (q_rows, end), 1)
        visible = (seg_col_ref[start:end, :] == seg_row_ref[:, :end]) & (k_place <= q_place)
        parts = []
        for h in range(heads):
            a = h * HEAD_DIM
            q = packed_ref[start:end, a : a + HEAD_DIM]
            k = packed_ref[:end, span + a : span + a + HEAD_DIM]
            v = packed_ref[:end, 2 * span + a : 2 * span + a + HEAD_DIM]
            s = lax.dot_general(q, k, (((1,), (1,)), ((), ())), preferred_element_type=jnp.float32)
            s = jnp.where(visible, s * scale, -1e30)
            top = jnp.max(s, axis=1, keepdims=True)
            p = jnp.exp(s - top)
            denominator = jnp.sum(p, axis=1, keepdims=True)
            o = jnp.dot(p.astype(jnp.bfloat16), v, preferred_element_type=jnp.float32)
            parts.append((o / denominator).astype(jnp.bfloat16))
        out_ref[start:end, :] = jnp.concatenate(parts, axis=1)


def attention(packed, segments, heads):
    total = packed.shape[0]
    span = heads * HEAD_DIM
    return pl.pallas_call(
        functools.partial(attention_kernel, heads, 128),
        out_shape=jax.ShapeDtypeStruct((total, span), jnp.bfloat16),
        compiler_params=pltpu.CompilerParams(vmem_limit_bytes=24 * MIB),
        cost_estimate=pl.CostEstimate(
            flops=4 * total * total * span, bytes_accessed=8 * total * span, transcendentals=total * total * heads
        ),
    )(packed, segments[None, :], segments[:, None])


def dot_t(a, b):
    return lax.dot_general(a, b, (((1,), (1,)), ((), ())), preferred_element_type=jnp.float32)


def expert_kernel(
    local, rows, tokens, first_ref, x_ref, tgt_ref, gates_ref, wg_ref, wu_ref, wd_ref, out_ref, kept_ref
):
    le = pl.program_id(0)
    chunk = pl.program_id(1)

    def selection(which):
        base = (first_ref[0] + which) * CAP
        row_id = lax.broadcasted_iota(jnp.int32, (rows, tokens), 0)
        block = lax.broadcasted_iota(jnp.int32, (1, tokens), 1) // 64
        picks, weights = None, None
        for j in range(2):
            slot = tgt_ref[0, j : j + 1, :] - base
            place = jnp.where((slot >= 0) & (slot < CAP), block * CAP + slot, -1)
            hit = row_id == place
            gate = jnp.where(hit, gates_ref[0, j : j + 1, :], 0.0)
            picks = hit if picks is None else picks | hit
            weights = gate if weights is None else weights + gate
        return picks.astype(jnp.float32).astype(jnp.bfloat16), jnp.sum(weights, axis=1, keepdims=True)

    pick, weight = selection(le)
    chosen = jnp.dot(pick, x_ref[...], preferred_element_type=jnp.float32).astype(jnp.bfloat16)
    gate = dot_t(chosen, wg_ref[0])
    upper = dot_t(chosen, wu_ref[0])
    hidden = (gate / (1.0 + jnp.exp(-gate)) * upper).astype(jnp.bfloat16)
    y = jnp.dot(hidden, wd_ref[0], preferred_element_type=jnp.float32)
    y = (y * weight).astype(jnp.bfloat16)

    if local > 1:

        @pl.when(le < local - 1)
        def _():
            kept_ref[le, chunk] = y

    @pl.when(le == local - 1)
    def _():
        total = lax.dot_general(pick, y, (((0,), (0,)), ((), ())), preferred_element_type=jnp.float32)
        for other in range(local - 1):
            pick_o, _ = selection(other)
            total += lax.dot_general(
                pick_o, kept_ref[other, chunk], (((0,), (0,)), ((), ())), preferred_element_type=jnp.float32
            )
        out_ref[...] = total.astype(jnp.bfloat16)


def experts(x, tgt, gates, w_gate, w_up, w_down, first):
    local, hidden, width = w_gate.shape
    chunks, _, tokens = tgt.shape
    rows = tokens // 64 * CAP
    last = local - 1
    return pl.pallas_call(
        functools.partial(expert_kernel, local, rows, tokens),
        out_shape=jax.ShapeDtypeStruct(x.shape, jnp.bfloat16),
        grid=(local, chunks),
        in_specs=[
            pl.BlockSpec(memory_space=pltpu.SMEM),
            pl.BlockSpec((tokens, width), lambda e, c: (c, 0)),
            pl.BlockSpec((1, 2, tokens), lambda e, c: (c, 0, 0)),
            pl.BlockSpec((1, 2, tokens), lambda e, c: (c, 0, 0)),
            pl.BlockSpec((1, hidden, width), lambda e, c: (e, 0, 0)),
            pl.BlockSpec((1, hidden, width), lambda e, c: (e, 0, 0)),
            pl.BlockSpec((1, hidden, width), lambda e, c: (e, 0, 0)),
        ],
        out_specs=pl.BlockSpec((tokens, width), lambda e, c: (jnp.where(e == last, c, 0), 0)),
        scratch_shapes=[pltpu.VMEM((max(last, 1), chunks if last else 1, rows, width), jnp.bfloat16)],
        compiler_params=pltpu.CompilerParams(vmem_limit_bytes=58 * MIB),
        cost_estimate=pl.CostEstimate(
            flops=6 * local * chunks * rows * width * hidden,
            bytes_accessed=6 * local * width * hidden + 6 * chunks * tokens * width,
            transcendentals=local * chunks * rows * hidden,
        ),
    )(first, x, tgt, gates, w_gate, w_up, w_down)


def pack_kernel(firsts, span, q_ref, k_ref, v_ref, out_ref):
    for j, first in enumerate(firsts):
        lanes = slice(first * HEAD_DIM, first * HEAD_DIM + span)
        out_ref[j] = jnp.concatenate([r[:, lanes] for r in (q_ref, k_ref, v_ref)], axis=1)


def pack_heads(query, keys, values, firsts, span):
    rows_dev = query.shape[0]
    n_seq = len(firsts)
    return pl.pallas_call(
        functools.partial(pack_kernel, firsts, span),
        out_shape=jax.ShapeDtypeStruct((n_seq, rows_dev, 3 * span), jnp.bfloat16),
        compiler_params=pltpu.CompilerParams(vmem_limit_bytes=12 * MIB),
        cost_estimate=pl.CostEstimate(flops=0, bytes_accessed=12 * n_seq * rows_dev * span, transcendentals=0),
    )(query, keys, values)


def norm_kernel(share, offsets, context_ref, residual_ref, gain_ref, facts_ref, stream_ref, piece_ref):
    n_seq, _, _ = context_ref.shape
    width = residual_ref.shape[1]
    parts = [context_ref[j][:, offsets[j] : offsets[j] + share] for j in range(n_seq)]
    context = jnp.concatenate(parts, axis=1).astype(jnp.float32)
    stream = residual_ref[...].astype(jnp.float32) + context
    stream_ref[...] = stream
    mean = jnp.mean(stream * stream, axis=1, keepdims=True)
    normed = stream * lax.rsqrt(mean + 1e-05) * gain_ref[...].astype(jnp.float32)
    piece_ref[:, :width] = normed.astype(jnp.bfloat16)
    facts = facts_ref[...]
    lane = lax.broadcasted_iota(jnp.int32, facts.shape, 1)
    high = facts.astype(jnp.bfloat16).astype(jnp.float32)
    middle = (facts - high).astype(jnp.bfloat16).astype(jnp.float32)
    low = facts - high - middle
    own = jnp.where(lane < 4, high, jnp.where(lane < 6, middle, low))
    piece_ref[:, width:] = own.astype(jnp.bfloat16)


def norm_tokens(context, residual, gain, facts, share, offsets):
    rows_dev, width = residual.shape
    return pl.pallas_call(
        functools.partial(norm_kernel, share, offsets),
        out_shape=(
            jax.ShapeDtypeStruct((rows_dev, width), jnp.float32),
            jax.ShapeDtypeStruct((rows_dev, width + facts.shape[1]), jnp.bfloat16),
        ),
        compiler_params=pltpu.CompilerParams(vmem_limit_bytes=12 * MIB),
        cost_estimate=pl.CostEstimate(
            flops=10 * rows_dev * width, bytes_accessed=10 * rows_dev * width, transcendentals=rows_dev
        ),
    )(context, residual, gain[None, :], facts)


def pick_pages_kernel(per_device, first_lane, order_ref, packed_ref, late_ref, out_ref):
    del late_ref
    for j in range(out_ref.shape[0]):
        for i in range(per_device):
            rows = pl.ds(pl.multiple_of(order_ref[j * per_device + i] * PAGE, PAGE), PAGE)
            out_ref[j, i * PAGE : (i + 1) * PAGE, :] = packed_ref[rows, first_lane:]


def pick_pages(packed, order, late, n_seq, span):
    rows = packed.shape[0] // n_seq
    vmem = pl.BlockSpec(memory_space=pltpu.VMEM)
    return pl.pallas_call(
        functools.partial(pick_pages_kernel, rows // PAGE, span),
        out_shape=jax.ShapeDtypeStruct((n_seq, rows, 2 * span), jnp.bfloat16),
        in_specs=[pl.BlockSpec(memory_space=pltpu.SMEM), vmem, pl.BlockSpec(memory_space=pl.ANY)],
        compiler_params=pltpu.CompilerParams(vmem_limit_bytes=8 * MIB),
        cost_estimate=pl.CostEstimate(flops=0, bytes_accessed=10 * packed.shape[0] * span, transcendentals=0),
    )(order, packed, late)


def join_pages_kernel(share, offsets, span, pages_ref, behind_ref, out_ref):
    del behind_ref
    width = share * len(offsets)
    for part in range(2):
        parts = [
            pages_ref[j][:, part * span + offsets[j] : part * span + offsets[j] + share]
            for j in range(len(offsets))
        ]
        out_ref[:, part * width : (part + 1) * width] = jnp.concatenate(parts, axis=1)


def join_pages(pages, share, offsets, span, behind):
    n_seq, rows, _ = pages.shape
    return pl.pallas_call(
        functools.partial(join_pages_kernel, share, offsets, span),
        out_shape=jax.ShapeDtypeStruct((rows, 2 * share * n_seq), jnp.bfloat16),
        in_specs=[pl.BlockSpec(memory_space=pltpu.VMEM), pl.BlockSpec(memory_space=pl.ANY)],
        compiler_params=pltpu.CompilerParams(vmem_limit_bytes=12 * MIB),
        cost_estimate=pl.CostEstimate(flops=0, bytes_accessed=8 * rows * n_seq * span, transcendentals=0),
    )(pages, behind)


def places_of(slots, base, shift):
    place = -1
    for slot in slots:
        slot = slot.astype(jnp.int32) - base
        place = jnp.where((slot >= 0) & (slot < CAP), shift + slot, place)
    return place


def hold_kernel(*refs):
    del refs


def hold(a, waits):
    anywhere = pl.BlockSpec(memory_space=pl.ANY)
    return pl.pallas_call(
        hold_kernel,
        out_shape=jax.ShapeDtypeStruct(a.shape, a.dtype),
        in_specs=[anywhere] * (1 + len(waits)),
        out_specs=anywhere,
        input_output_aliases={0: 0},
        compiler_params=pltpu.CompilerParams(vmem_limit_bytes=MIB),
        cost_estimate=pl.CostEstimate(flops=0, bytes_accessed=0, transcendentals=0),
    )(a, *waits)


def facts_by_lane(x):
    unit = lax.broadcasted_iota(jnp.int32, (8, 128), 0) == lax.broadcasted_iota(jnp.int32, (8, 128), 1)
    return dot_t(unit.astype(jnp.float32).astype(jnp.bfloat16), x)


def select_kernel(local, rows_dev, count, bases_ref, *refs):
    piece_refs, (own_ref, sib_ref, facts_ref) = refs[:count], refs[-3:]
    width = own_ref.shape[2]
    tokens, rows = 4 * rows_dev, 4 * CAP
    shift = lax.broadcasted_iota(jnp.int32, (1, tokens), 1) // rows_dev * CAP
    row_id = lax.broadcasted_iota(jnp.int32, (rows, tokens), 0)
    for g in range(len(piece_refs) // 4):
        x = jnp.concatenate([p[...] for p in piece_refs[4 * g : 4 * g + 4]], axis=0)
        facts_ref[g * tokens : (g + 1) * tokens, :] = x[:, width:]
        facts = facts_by_lane(x[:, width:])
        picks = []
        for core in range(2):
            for e in range(local):
                base = (bases_ref[core] + e) * CAP
                hit = row_id == places_of([facts[j : j + 1] for j in range(2)], base, shift)
                picks.append(hit.astype(jnp.float32))
        picks = jnp.concatenate(picks, axis=0).astype(jnp.bfloat16)
        chosen = jnp.dot(picks, x[:, :width], preferred_element_type=jnp.float32).astype(jnp.bfloat16)
        for e in range(local):
            own_ref[e, g * rows : (g + 1) * rows, :] = chosen[e * rows : (e + 1) * rows]
            sib_ref[e, g * rows : (g + 1) * rows, :] = chosen[(local + e) * rows : (local + e + 1) * rows]


def select_rows(pieces, bases, local, waits=()):
    rows_dev, wide = pieces[0].shape
    width = wide - 128
    rows = len(pieces) * CAP
    out = jax.ShapeDtypeStruct((local, rows, width), jnp.bfloat16)
    vmem = pl.BlockSpec(memory_space=pltpu.VMEM)
    return pl.pallas_call(
        functools.partial(select_kernel, local, rows_dev, len(pieces)),
        out_shape=(out, out, jax.ShapeDtypeStruct((len(pieces) * rows_dev, 128), jnp.bfloat16)),
        in_specs=[pl.BlockSpec(memory_space=pltpu.SMEM)]
        + [vmem] * len(pieces)
        + [pl.BlockSpec(memory_space=pl.ANY)] * len(waits),
        out_specs=(vmem, vmem, vmem),
        compiler_params=pltpu.CompilerParams(vmem_limit_bytes=20 * MIB),
        cost_estimate=pl.CostEstimate(
            flops=16 * local * CAP * rows_dev * len(pieces) * width,
            bytes_accessed=2 * len(pieces) * rows_dev * wide + 4 * local * rows * width,
            transcendentals=0,
        ),
    )(bases, *pieces, *waits)


def rows_kernel(local, waits, own_ref, got_ref, wg_hbm, wu_hbm, wd_hbm, *rest):
    y_own_ref, y_sib_ref, wg, wu, wd, weight_sem = rest[waits:]
    half = own_ref.shape[1]
    copies = [
        [
            pltpu.make_async_copy(source.at[e], target.at[e], weight_sem.at[3 * e + i])
            for i, (source, target) in enumerate(((wg_hbm, wg), (wu_hbm, wu), (wd_hbm, wd)))
        ]
        for e in range(local)
    ]
    for group in copies:
        for copy in group:
            copy.start()
    for e in range(local):
        rows = jnp.concatenate([own_ref[e], got_ref[e]], axis=0)
        copies[e][0].wait()
        gate = dot_t(rows, wg[e])
        copies[e][1].wait()
        upper = dot_t(rows, wu[e])
        hidden = (gate / (1.0 + jnp.exp(-gate)) * upper).astype(jnp.bfloat16)
        copies[e][2].wait()
        y = jnp.dot(hidden, wd[e], preferred_element_type=jnp.float32).astype(jnp.bfloat16)
        y_own_ref[e] = y[:half]
        y_sib_ref[e] = y[half:]


def expert_rows(own, got, w_gate, w_up, w_down, waits):
    local, hidden, width = w_gate.shape
    rows = 2 * own.shape[1]
    out = jax.ShapeDtypeStruct(own.shape, jnp.bfloat16)
    vmem = pl.BlockSpec(memory_space=pltpu.VMEM)
    weights = pltpu.VMEM((local, hidden, width), jnp.bfloat16)
    return pl.pallas_call(
        functools.partial(rows_kernel, local, len(waits)),
        out_shape=(out, out),
        in_specs=[vmem, vmem] + [pl.BlockSpec(memory_space=pl.ANY)] * (3 + len(waits)),
        out_specs=(vmem, vmem),
        scratch_shapes=[weights, weights, weights, pltpu.SemaphoreType.DMA((3 * local,))],
        compiler_params=pltpu.CompilerParams(vmem_limit_bytes=36 * MIB),
        cost_estimate=pl.CostEstimate(
            flops=6 * local * rows * width * hidden,
            bytes_accessed=6 * local * width * hidden + 4 * local * rows * width,
            transcendentals=local * rows * hidden,
        ),
    )(own, got, w_gate, w_up, w_down, *waits)


def put_kernel(local, rows_dev, planes, waits, bases_ref, y_own_ref, y_got_ref, facts_ref, *rest):
    kept_ref, *send_refs = rest[waits:]
    tokens, rows = 4 * rows_dev, 4 * CAP
    total = 2 * local * rows
    shift_lane = lax.broadcasted_iota(jnp.int32, (1, tokens), 1) // rows_dev * CAP
    shift_row = lax.broadcasted_iota(jnp.int32, (tokens, 1), 0) // rows_dev * CAP
    row_id = lax.broadcasted_iota(jnp.int32, (rows, tokens), 0)
    lane = lax.broadcasted_iota(jnp.int32, (tokens, total), 1)
    for g in range(planes):
        facts = facts_ref[g * tokens : (g + 1) * tokens, :]
        by_lane = facts_by_lane(facts)
        by_row = facts.astype(jnp.float32)
        here = slice(g * rows, (g + 1) * rows)
        weighed, put = [], None
        for core, y_ref in enumerate((y_own_ref, y_got_ref)):
            for e in range(local):
                base = (bases_ref[core] + e) * CAP
                weight = jnp.zeros((rows, tokens), jnp.float32)
                for j in range(2):
                    hit = row_id == places_of([by_lane[j : j + 1]], base, shift_lane)
                    gate = by_lane[2 + j : 3 + j] + by_lane[4 + j : 5 + j] + by_lane[6 + j : 7 + j]
                    weight = weight + jnp.where(hit, gate, 0.0)
                weight = jnp.sum(weight, axis=1, keepdims=True)
                weighed.append((y_ref[e, here, :].astype(jnp.float32) * weight).astype(jnp.bfloat16))
                first = (core * local + e) * rows
                hit = lane == places_of([by_row[:, j : j + 1] for j in range(2)], base, shift_row + first)
                put = hit if put is None else put | hit
        put = put.astype(jnp.float32).astype(jnp.bfloat16)
        out = jnp.dot(put, jnp.concatenate(weighed, axis=0), preferred_element_type=jnp.float32)
        out = out.astype(jnp.bfloat16)
        kept_ref[g * tokens // 2 : (g + 1) * tokens // 2, :] = out[: tokens // 2]
        send_refs[g][...] = out[tokens // 2 :]


def put_rows(y_own, y_got, facts, bases, rows_dev, waits):
    local, _, width = y_own.shape
    tokens = facts.shape[0]
    planes = tokens // (4 * rows_dev)
    vmem = pl.BlockSpec(memory_space=pltpu.VMEM)
    shape = lambda n: jax.ShapeDtypeStruct((n, width), jnp.bfloat16)
    out = pl.pallas_call(
        functools.partial(put_kernel, local, rows_dev, planes, len(waits)),
        out_shape=(shape(2 * planes * rows_dev),) + (shape(2 * rows_dev),) * planes,
        in_specs=[pl.BlockSpec(memory_space=pltpu.SMEM), vmem, vmem, vmem]
        + [pl.BlockSpec(memory_space=pl.ANY)] * len(waits),
        out_specs=(vmem,) * (1 + planes),
        compiler_params=pltpu.CompilerParams(vmem_limit_bytes=20 * MIB),
        cost_estimate=pl.CostEstimate(
            flops=16 * local * CAP * tokens * width,
            bytes_accessed=8 * local * tokens * width,
            transcendentals=0,
        ),
    )(bases, y_own, y_got, facts, *waits)
    return out[0], out[1:]


def swap(a, axis, size, distance):
    return lax.ppermute(a, axis, [(i, i ^ distance) for i in range(size)])


def fold_kernel(groups, count, waits, keep_ref, *rest):
    got_refs, (kept_ref, *send_refs) = rest[:count], rest[count + waits :]
    part = keep_ref.shape[0] // (2 * groups)
    span = got_refs[0].shape[0]
    for i in range(2 * groups):
        start = i * part
        got = got_refs[start // span][start % span : start % span + part, :]
        total = keep_ref[start : start + part, :].astype(jnp.float32) + got.astype(jnp.float32)
        total = total.astype(jnp.bfloat16)
        if i % 2 == 0:
            kept_ref[i // 2 * part : (i // 2 + 1) * part, :] = total
        else:
            send_refs[i // 2][...] = total


def fold(keep, gots, groups, waits=()):
    rows, width = keep.shape
    part = rows // (2 * groups)
    vmem = pl.BlockSpec(memory_space=pltpu.VMEM)
    shape = lambda n: jax.ShapeDtypeStruct((n, width), jnp.bfloat16)
    out = pl.pallas_call(
        functools.partial(fold_kernel, groups, len(gots), len(waits)),
        out_shape=(shape(groups * part),) + (shape(part),) * groups,
        in_specs=[vmem] * (1 + len(gots)) + [pl.BlockSpec(memory_space=pl.ANY)] * len(waits),
        out_specs=(vmem,) * (1 + groups),
        compiler_params=pltpu.CompilerParams(vmem_limit_bytes=10 * MIB),
        cost_estimate=pl.CostEstimate(flops=rows * width, bytes_accessed=6 * rows * width, transcendentals=0),
    )(keep, *gots, *waits)
    return out[0], out[1:]


def exchange_experts(piece, w_gate, w_up, w_down, n_seq, n_exp, late_work):
    x = lambda a: swap(a, "seq", n_seq, 1)
    y = lambda a: swap(a, "exp", n_exp, 2)
    core = lambda a: swap(a, "exp", n_exp, 1)
    z = lambda a, k: swap(a, "seq", n_seq, 2 * k)
    local = w_gate.shape[0]
    me = lax.axis_index("exp").astype(jnp.int32)
    bases = jnp.stack([me, me ^ 1]) * local
    starts = [piece, z(piece, 1), z(piece, 2)]
    ways = [("xy", "yx")[k % 2] for k in range(4)]
    over = {"x": x, "y": y}
    single = [[over[way](starts[k]) for way in ways[k]] for k in range(2)]
    starts[2] = hold(starts[2], single[0] + single[1])
    single.append([over[way](starts[2]) for way in ways[2]])
    starts.append(hold(z(starts[2], 1), single[2]))
    single.append([over[way](starts[3]) for way in ways[3]])

    def gather(k):
        near = []
        for i in (k, k + 1):
            by_f, by_g = single[i]
            near += [starts[i], by_g, by_f, over[ways[i][1]](by_f)]
        return near

    near_b, near_a = gather(0), gather(2)
    own_a, sib_a, facts_a = select_rows(near_a, bases, local)
    got_a = core(sib_a)
    own_b, sib_b, facts_b = select_rows(near_b, bases, local)
    got_b = core(sib_b)
    pages, fill = late_work(sib_b)
    own_a, sib_a = expert_rows(own_a, got_a, w_gate, w_up, w_down, [sib_b, pages])
    other = fill(sib_a)
    got_a = core(sib_a)
    own_b, sib_b = expert_rows(own_b, got_b, w_gate, w_up, w_down, [other, sib_a])
    got_b = core(sib_b)
    keep_a, (fx_a, fy_a) = put_rows(own_a, got_a, facts_a, bases, piece.shape[0], [sib_b])
    keep_a, (gy_a, gx_a) = fold(keep_a, [x(fx_a), y(fy_a)], 2)
    keep_b, (fx_b, fy_b) = put_rows(own_b, got_b, facts_b, bases, piece.shape[0], [gy_a])
    gy_a, gx_a = y(gy_a), x(gx_a)
    fx_b, fy_b = hold(fx_b, [gy_a, gx_a]), hold(fy_b, [gy_a, gx_a])
    keep_a, (z_a,) = fold(keep_a, [gy_a, gx_a], 1)
    keep_b, (gy_b, gx_b) = fold(keep_b, [x(fx_b), y(fy_b)], 2, [z_a])
    over_z = (keep_a.astype(jnp.float32) + z(z_a, 1).astype(jnp.float32)).astype(jnp.bfloat16)
    keep_b, (z_b,) = fold(keep_b, [y(gy_b), x(gx_b)], 1, [over_z])
    mine = keep_b.astype(jnp.float32) + z(z_b, 1).astype(jnp.float32)
    return mine + z(over_z, 2).astype(jnp.float32), other


def body(
    n_seq,
    n_exp,
    query,
    key_value,
    residual,
    norm_gain,
    segment_ids,
    routes,
    gate_weights,
    page_table,
    w_gate,
    w_up,
    w_down,
):
    rows_dev, width = query.shape[1:]
    everyone = ("exp", "seq")
    group = segment_ids.shape[1]
    share, firsts, heads = head_ranges(width, n_seq)
    span = heads * HEAD_DIM

    flat = routes[0].reshape(rows_dev * 2)
    onehot = (flat[:, None] == jnp.arange(EXPERTS, dtype=jnp.int32)[None, :]).astype(jnp.int32)
    before = jnp.cumsum(onehot, axis=0) - onehot
    target = (flat * CAP + jnp.sum(before * onehot, axis=1)).reshape(rows_dev, 2).astype(jnp.float32)

    keys, values = key_value[0, :, 0], key_value[0, :, 1]

    packed = pack_heads(query[0], keys, values, firsts, span)
    packed = lax.all_to_all(packed, "seq", split_axis=0, concat_axis=0, tiled=True)
    packed = packed.reshape(group, 3 * span)
    context = attention(packed, segment_ids[0], heads)
    context = lax.all_to_all(
        context.reshape(n_seq, rows_dev, span), "seq", split_axis=0, concat_axis=0, tiled=True
    )
    offsets = [j * share - firsts[j] * HEAD_DIM for j in range(n_seq)]

    first = (lax.axis_index("exp") * (EXPERTS // n_exp)).astype(jnp.int32).reshape(1)
    w_gate, w_up = jnp.swapaxes(w_gate, 1, 2), jnp.swapaxes(w_up, 1, 2)
    gates = gate_weights[0]
    facts = jnp.concatenate([target, gates, gates, gates], axis=1)
    facts = jnp.pad(facts, ((0, 0), (0, 128 - facts.shape[1])))
    stream, piece = norm_tokens(context, residual[0], norm_gain, facts, share, offsets)

    slots = jnp.arange(group // PAGE, dtype=jnp.int32)
    order = jnp.sum(jnp.where(page_table[0][None, :] == slots[:, None], slots[None, :], 0), axis=1)

    def fill_cache(late):
        pages = pick_pages(packed, order, late, n_seq, span)
        sent = lax.all_to_all(pages, "seq", split_axis=0, concat_axis=0, tiled=True)
        return pages, lambda behind: join_pages(sent, share, offsets, span, behind)

    if (n_seq, n_exp) == (8, 4):
        mixture, cache = exchange_experts(piece, w_gate, w_up, w_down, n_seq, n_exp, fill_cache)
    else:
        cache = fill_cache(piece)[1](piece)
        blocks = n_seq * n_exp
        everything = lax.all_gather(piece, everyone, axis=0, tiled=True)
        facts = everything[:, width : width + 8].astype(jnp.float32)
        facts = facts.reshape(blocks // CHUNK_BLOCKS, CHUNK_BLOCKS * rows_dev, 8).transpose(0, 2, 1)
        gates = facts[:, 2:4] + facts[:, 4:6] + facts[:, 6:8]
        partial = experts(
            everything[:, :width], facts[:, :2].astype(jnp.int32), gates, w_gate, w_up, w_down, first
        )
        mixture = lax.psum_scatter(partial, everyone, scatter_dimension=0, tiled=True).astype(jnp.float32)
    layer_out = (stream + mixture).astype(jnp.bfloat16)
    return (layer_out[None], cache.reshape(1, rows_dev // PAGE, PAGE, 2 * width))


def solution(mesh):
    in_specs = (
        P("exp", "seq", None),
        P("exp", "seq", None, None),
        P("exp", "seq", None),
        P(),
        P("exp", None),
        P("exp", "seq", None),
        P("exp", "seq", None),
        P("exp", None),
        P("exp", None, "seq"),
        P("exp", None, "seq"),
        P("exp", "seq", None),
    )
    out_specs = (P("exp", "seq", None), P("exp", "seq", None, None))
    run = functools.partial(body, mesh.shape["seq"], mesh.shape["exp"])
    return jax.shard_map(run, mesh=mesh, in_specs=in_specs, out_specs=out_specs, check_vma=False)
```

```python
import functools
import math

import jax
import jax.numpy as jnp
from jax import lax
from jax.experimental import pallas as pl
from jax.experimental.pallas import tpu as pltpu
from jax.sharding import PartitionSpec as P

HEADS = 36
HEAD_DIM = 64
EXPERTS = 8
PAGE = 16
CAP = 24
MIB = 1024 * 1024
CHUNK_BLOCKS = 8


def head_ranges(width, n_seq):
    share = width // n_seq
    firsts = [j * share // HEAD_DIM for j in range(n_seq)]
    count = max(-(-(j + 1) * share // HEAD_DIM) - firsts[j] for j in range(n_seq))
    firsts = [min(f, HEADS - count) for f in firsts]
    return share, firsts, count


def attention_kernel(heads, q_rows, packed_ref, seg_row_ref, seg_col_ref, out_ref):
    total = packed_ref.shape[0]
    span = heads * HEAD_DIM
    scale = 1.0 / math.sqrt(HEAD_DIM)
    for start in range(0, total, q_rows):
        end = start + q_rows
        q_place = start + lax.broadcasted_iota(jnp.int32, (q_rows, end), 0)
        k_place = lax.broadcasted_iota(jnp.int32, (q_rows, end), 1)
        visible = (seg_col_ref[start:end, :] == seg_row_ref[:, :end]) & (k_place <= q_place)
        parts = []
        for h in range(heads):
            a = h * HEAD_DIM
            q = packed_ref[start:end, a : a + HEAD_DIM]
            k = packed_ref[:end, span + a : span + a + HEAD_DIM]
            v = packed_ref[:end, 2 * span + a : 2 * span + a + HEAD_DIM]
            s = lax.dot_general(q, k, (((1,), (1,)), ((), ())), preferred_element_type=jnp.float32)
            s = jnp.where(visible, s * scale, -1e30)
            top = jnp.max(s, axis=1, keepdims=True)
            p = jnp.exp(s - top)
            denominator = jnp.sum(p, axis=1, keepdims=True)
            o = jnp.dot(p.astype(jnp.bfloat16), v, preferred_element_type=jnp.float32)
            parts.append((o / denominator).astype(jnp.bfloat16))
        out_ref[start:end, :] = jnp.concatenate(parts, axis=1)


def attention(packed, segments, heads):
    total = packed.shape[0]
    span = heads * HEAD_DIM
    return pl.pallas_call(
        functools.partial(attention_kernel, heads, 128),
        out_shape=jax.ShapeDtypeStruct((total, span), jnp.bfloat16),
        compiler_params=pltpu.CompilerParams(vmem_limit_bytes=24 * MIB),
        cost_estimate=pl.CostEstimate(
            flops=4 * total * total * span, bytes_accessed=8 * total * span, transcendentals=total * total * heads
        ),
    )(packed, segments[None, :], segments[:, None])


def dot_t(a, b):
    return lax.dot_general(a, b, (((1,), (1,)), ((), ())), preferred_element_type=jnp.float32)


def expert_kernel(
    local, rows, tokens, first_ref, x_ref, tgt_ref, gates_ref, wg_ref, wu_ref, wd_ref, out_ref, kept_ref
):
    le = pl.program_id(0)
    chunk = pl.program_id(1)

    def selection(which):
        base = (first_ref[0] + which) * CAP
        row_id = lax.broadcasted_iota(jnp.int32, (rows, tokens), 0)
        block = lax.broadcasted_iota(jnp.int32, (1, tokens), 1) // 64
        picks, weights = None, None
        for j in range(2):
            slot = tgt_ref[0, j : j + 1, :] - base
            place = jnp.where((slot >= 0) & (slot < CAP), block * CAP + slot, -1)
            hit = row_id == place
            gate = jnp.where(hit, gates_ref[0, j : j + 1, :], 0.0)
            picks = hit if picks is None else picks | hit
            weights = gate if weights is None else weights + gate
        return picks.astype(jnp.float32).astype(jnp.bfloat16), jnp.sum(weights, axis=1, keepdims=True)

    pick, weight = selection(le)
    chosen = jnp.dot(pick, x_ref[...], preferred_element_type=jnp.float32).astype(jnp.bfloat16)
    gate = dot_t(chosen, wg_ref[0])
    upper = dot_t(chosen, wu_ref[0])
    hidden = (gate / (1.0 + jnp.exp(-gate)) * upper).astype(jnp.bfloat16)
    y = jnp.dot(hidden, wd_ref[0], preferred_element_type=jnp.float32)
    y = (y * weight).astype(jnp.bfloat16)

    if local > 1:

        @pl.when(le < local - 1)
        def _():
            kept_ref[le, chunk] = y

    @pl.when(le == local - 1)
    def _():
        total = lax.dot_general(pick, y, (((0,), (0,)), ((), ())), preferred_element_type=jnp.float32)
        for other in range(local - 1):
            pick_o, _ = selection(other)
            total += lax.dot_general(
                pick_o, kept_ref[other, chunk], (((0,), (0,)), ((), ())), preferred_element_type=jnp.float32
            )
        out_ref[...] = total.astype(jnp.bfloat16)


def experts(x, tgt, gates, w_gate, w_up, w_down, first):
    local, hidden, width = w_gate.shape
    chunks, _, tokens = tgt.shape
    rows = tokens // 64 * CAP
    last = local - 1
    return pl.pallas_call(
        functools.partial(expert_kernel, local, rows, tokens),
        out_shape=jax.ShapeDtypeStruct(x.shape, jnp.bfloat16),
        grid=(local, chunks),
        in_specs=[
            pl.BlockSpec(memory_space=pltpu.SMEM),
            pl.BlockSpec((tokens, width), lambda e, c: (c, 0)),
            pl.BlockSpec((1, 2, tokens), lambda e, c: (c, 0, 0)),
            pl.BlockSpec((1, 2, tokens), lambda e, c: (c, 0, 0)),
            pl.BlockSpec((1, hidden, width), lambda e, c: (e, 0, 0)),
            pl.BlockSpec((1, hidden, width), lambda e, c: (e, 0, 0)),
            pl.BlockSpec((1, hidden, width), lambda e, c: (e, 0, 0)),
        ],
        out_specs=pl.BlockSpec((tokens, width), lambda e, c: (jnp.where(e == last, c, 0), 0)),
        scratch_shapes=[pltpu.VMEM((max(last, 1), chunks if last else 1, rows, width), jnp.bfloat16)],
        compiler_params=pltpu.CompilerParams(vmem_limit_bytes=58 * MIB),
        cost_estimate=pl.CostEstimate(
            flops=6 * local * chunks * rows * width * hidden,
            bytes_accessed=6 * local * width * hidden + 6 * chunks * tokens * width,
            transcendentals=local * chunks * rows * hidden,
        ),
    )(first, x, tgt, gates, w_gate, w_up, w_down)


def pack_kernel(firsts, span, q_ref, k_ref, v_ref, out_ref):
    for j, first in enumerate(firsts):
        lanes = slice(first * HEAD_DIM, first * HEAD_DIM + span)
        out_ref[j] = jnp.concatenate([r[:, lanes] for r in (q_ref, k_ref, v_ref)], axis=1)


def pack_heads(query, keys, values, firsts, span):
    rows_dev = query.shape[0]
    n_seq = len(firsts)
    return pl.pallas_call(
        functools.partial(pack_kernel, firsts, span),
        out_shape=jax.ShapeDtypeStruct((n_seq, rows_dev, 3 * span), jnp.bfloat16),
        compiler_params=pltpu.CompilerParams(vmem_limit_bytes=12 * MIB),
        cost_estimate=pl.CostEstimate(flops=0, bytes_accessed=12 * n_seq * rows_dev * span, transcendentals=0),
    )(query, keys, values)


def norm_kernel(share, offsets, context_ref, residual_ref, gain_ref, facts_ref, stream_ref, piece_ref):
    n_seq, _, _ = context_ref.shape
    width = residual_ref.shape[1]
    parts = [context_ref[j][:, offsets[j] : offsets[j] + share] for j in range(n_seq)]
    context = jnp.concatenate(parts, axis=1).astype(jnp.float32)
    stream = residual_ref[...].astype(jnp.float32) + context
    stream_ref[...] = stream
    mean = jnp.mean(stream * stream, axis=1, keepdims=True)
    normed = stream * lax.rsqrt(mean + 1e-05) * gain_ref[...].astype(jnp.float32)
    piece_ref[:, :width] = normed.astype(jnp.bfloat16)
    facts = facts_ref[...]
    lane = lax.broadcasted_iota(jnp.int32, facts.shape, 1)
    high = facts.astype(jnp.bfloat16).astype(jnp.float32)
    middle = (facts - high).astype(jnp.bfloat16).astype(jnp.float32)
    low = facts - high - middle
    own = jnp.where(lane < 4, high, jnp.where(lane < 6, middle, low))
    piece_ref[:, width:] = own.astype(jnp.bfloat16)


def norm_tokens(context, residual, gain, facts, share, offsets):
    rows_dev, width = residual.shape
    return pl.pallas_call(
        functools.partial(norm_kernel, share, offsets),
        out_shape=(
            jax.ShapeDtypeStruct((rows_dev, width), jnp.float32),
            jax.ShapeDtypeStruct((rows_dev, width + facts.shape[1]), jnp.bfloat16),
        ),
        compiler_params=pltpu.CompilerParams(vmem_limit_bytes=12 * MIB),
        cost_estimate=pl.CostEstimate(
            flops=10 * rows_dev * width, bytes_accessed=10 * rows_dev * width, transcendentals=rows_dev
        ),
    )(context, residual, gain[None, :], facts)


def pick_pages_kernel(per_device, first_lane, order_ref, packed_ref, late_ref, out_ref):
    del late_ref
    for j in range(out_ref.shape[0]):
        for i in range(per_device):
            rows = pl.ds(pl.multiple_of(order_ref[j * per_device + i] * PAGE, PAGE), PAGE)
            out_ref[j, i * PAGE : (i + 1) * PAGE, :] = packed_ref[rows, first_lane:]


def pick_pages(packed, order, late, n_seq, span):
    rows = packed.shape[0] // n_seq
    vmem = pl.BlockSpec(memory_space=pltpu.VMEM)
    return pl.pallas_call(
        functools.partial(pick_pages_kernel, rows // PAGE, span),
        out_shape=jax.ShapeDtypeStruct((n_seq, rows, 2 * span), jnp.bfloat16),
        in_specs=[pl.BlockSpec(memory_space=pltpu.SMEM), vmem, pl.BlockSpec(memory_space=pl.ANY)],
        compiler_params=pltpu.CompilerParams(vmem_limit_bytes=8 * MIB),
        cost_estimate=pl.CostEstimate(flops=0, bytes_accessed=10 * packed.shape[0] * span, transcendentals=0),
    )(order, packed, late)


def join_pages_kernel(share, offsets, span, pages_ref, behind_ref, out_ref, ended_ref):
    del behind_ref
    ended_ref[...] = jnp.zeros_like(ended_ref)
    width = share * len(offsets)
    for part in range(2):
        parts = [
            pages_ref[j][:, part * span + offsets[j] : part * span + offsets[j] + share]
            for j in range(len(offsets))
        ]
        out_ref[:, part * width : (part + 1) * width] = jnp.concatenate(parts, axis=1)


def join_pages(pages, share, offsets, span, behind):
    n_seq, rows, _ = pages.shape
    return pl.pallas_call(
        functools.partial(join_pages_kernel, share, offsets, span),
        out_shape=(
            jax.ShapeDtypeStruct((rows, 2 * share * n_seq), jnp.bfloat16),
            jax.ShapeDtypeStruct((8, 128), jnp.float32),
        ),
        in_specs=[pl.BlockSpec(memory_space=pltpu.VMEM), pl.BlockSpec(memory_space=pl.ANY)],
        compiler_params=pltpu.CompilerParams(vmem_limit_bytes=12 * MIB),
        cost_estimate=pl.CostEstimate(flops=0, bytes_accessed=8 * rows * n_seq * span, transcendentals=0),
    )(pages, behind)


def places_of(slots, base, shift):
    place = -1
    for slot in slots:
        slot = slot.astype(jnp.int32) - base
        place = jnp.where((slot >= 0) & (slot < CAP), shift + slot, place)
    return place


def hold_kernel(*refs):
    del refs


def hold(a, waits):
    anywhere = pl.BlockSpec(memory_space=pl.ANY)
    return pl.pallas_call(
        hold_kernel,
        out_shape=jax.ShapeDtypeStruct(a.shape, a.dtype),
        in_specs=[anywhere] * (1 + len(waits)),
        out_specs=anywhere,
        input_output_aliases={0: 0},
        compiler_params=pltpu.CompilerParams(vmem_limit_bytes=MIB),
        cost_estimate=pl.CostEstimate(flops=0, bytes_accessed=0, transcendentals=0),
    )(a, *waits)


def facts_by_lane(x):
    unit = lax.broadcasted_iota(jnp.int32, (8, 128), 0) == lax.broadcasted_iota(jnp.int32, (8, 128), 1)
    return dot_t(unit.astype(jnp.float32).astype(jnp.bfloat16), x)


def select_kernel(local, rows_dev, count, bases_ref, *refs):
    piece_refs, (own_ref, sib_ref, facts_ref) = refs[:count], refs[-3:]
    width = own_ref.shape[2]
    tokens, rows = 4 * rows_dev, 4 * CAP
    shift = lax.broadcasted_iota(jnp.int32, (1, tokens), 1) // rows_dev * CAP
    row_id = lax.broadcasted_iota(jnp.int32, (rows, tokens), 0)
    for g in range(len(piece_refs) // 4):
        x = jnp.concatenate([p[...] for p in piece_refs[4 * g : 4 * g + 4]], axis=0)
        facts_ref[g * tokens : (g + 1) * tokens, :] = x[:, width:]
        facts = facts_by_lane(x[:, width:])
        picks = []
        for core in range(2):
            for e in range(local):
                base = (bases_ref[core] + e) * CAP
                hit = row_id == places_of([facts[j : j + 1] for j in range(2)], base, shift)
                picks.append(hit.astype(jnp.float32))
        picks = jnp.concatenate(picks, axis=0).astype(jnp.bfloat16)
        chosen = jnp.dot(picks, x[:, :width], preferred_element_type=jnp.float32).astype(jnp.bfloat16)
        for e in range(local):
            own_ref[e, g * rows : (g + 1) * rows, :] = chosen[e * rows : (e + 1) * rows]
            sib_ref[e, g * rows : (g + 1) * rows, :] = chosen[(local + e) * rows : (local + e + 1) * rows]


def select_rows(pieces, bases, local, waits=()):
    rows_dev, wide = pieces[0].shape
    width = wide - 128
    rows = len(pieces) * CAP
    out = jax.ShapeDtypeStruct((local, rows, width), jnp.bfloat16)
    vmem = pl.BlockSpec(memory_space=pltpu.VMEM)
    return pl.pallas_call(
        functools.partial(select_kernel, local, rows_dev, len(pieces)),
        out_shape=(out, out, jax.ShapeDtypeStruct((len(pieces) * rows_dev, 128), jnp.bfloat16)),
        in_specs=[pl.BlockSpec(memory_space=pltpu.SMEM)]
        + [vmem] * len(pieces)
        + [pl.BlockSpec(memory_space=pl.ANY)] * len(waits),
        out_specs=(vmem, vmem, vmem),
        compiler_params=pltpu.CompilerParams(vmem_limit_bytes=20 * MIB),
        cost_estimate=pl.CostEstimate(
            flops=16 * local * CAP * rows_dev * len(pieces) * width,
            bytes_accessed=2 * len(pieces) * rows_dev * wide + 4 * local * rows * width,
            transcendentals=0,
        ),
    )(bases, *pieces, *waits)


def rows_kernel(local, waits, own_hbm, got_ref, wg_hbm, wu_hbm, wd_hbm, *rest):
    y_own_ref, y_sib_ref, ended_ref, own_ref, wg, wu, wd, own_sem, weight_sem = rest[waits:]
    ended_ref[...] = jnp.zeros_like(ended_ref)
    half = got_ref.shape[1]
    own_copy = pltpu.make_async_copy(own_hbm, own_ref, own_sem)
    own_copy.start()
    copies = [
        [
            pltpu.make_async_copy(source.at[e], target.at[e], weight_sem.at[3 * e + i])
            for i, (source, target) in enumerate(((wg_hbm, wg), (wu_hbm, wu), (wd_hbm, wd)))
        ]
        for e in range(local)
    ]
    for group in copies:
        for copy in group:
            copy.start()
    own_copy.wait()
    for e in range(local):
        rows = jnp.concatenate([own_ref[e], got_ref[e]], axis=0)
        copies[e][0].wait()
        gate = dot_t(rows, wg[e])
        copies[e][1].wait()
        upper = dot_t(rows, wu[e])
        hidden = (gate / (1.0 + jnp.exp(-gate)) * upper).astype(jnp.bfloat16)
        copies[e][2].wait()
        y = jnp.dot(hidden, wd[e], preferred_element_type=jnp.float32).astype(jnp.bfloat16)
        y_own_ref[e] = y[:half]
        y_sib_ref[e] = y[half:]


def expert_rows(own, got, w_gate, w_up, w_down, waits):
    local, hidden, width = w_gate.shape
    rows = 2 * own.shape[1]
    out = jax.ShapeDtypeStruct(own.shape, jnp.bfloat16)
    vmem = pl.BlockSpec(memory_space=pltpu.VMEM)
    weights = pltpu.VMEM((local, hidden, width), jnp.bfloat16)
    return pl.pallas_call(
        functools.partial(rows_kernel, local, len(waits)),
        out_shape=(out, out, jax.ShapeDtypeStruct((8, 128), jnp.float32)),
        in_specs=[pl.BlockSpec(memory_space=pl.ANY), vmem]
        + [pl.BlockSpec(memory_space=pl.ANY)] * (3 + len(waits)),
        out_specs=(vmem, vmem, vmem),
        scratch_shapes=[
            pltpu.VMEM(own.shape, jnp.bfloat16),
            weights,
            weights,
            weights,
            pltpu.SemaphoreType.DMA,
            pltpu.SemaphoreType.DMA((3 * local,)),
        ],
        compiler_params=pltpu.CompilerParams(vmem_limit_bytes=46 * MIB),
        cost_estimate=pl.CostEstimate(
            flops=6 * local * rows * width * hidden,
            bytes_accessed=6 * local * width * hidden + 4 * local * rows * width,
            transcendentals=local * rows * hidden,
        ),
    )(own, got, w_gate, w_up, w_down, *waits)


def put_kernel(local, rows_dev, planes, waits, bases_ref, y_own_ref, y_got_ref, facts_ref, *rest):
    kept_ref, *send_refs = rest[waits:]
    tokens, rows = 4 * rows_dev, 4 * CAP
    total = 2 * local * rows
    shift_lane = lax.broadcasted_iota(jnp.int32, (1, tokens), 1) // rows_dev * CAP
    shift_row = lax.broadcasted_iota(jnp.int32, (tokens, 1), 0) // rows_dev * CAP
    row_id = lax.broadcasted_iota(jnp.int32, (rows, tokens), 0)
    lane = lax.broadcasted_iota(jnp.int32, (tokens, total), 1)
    for g in range(planes):
        facts = facts_ref[g * tokens : (g + 1) * tokens, :]
        by_lane = facts_by_lane(facts)
        by_row = facts.astype(jnp.float32)
        here = slice(g * rows, (g + 1) * rows)
        weighed, put = [], None
        for core, y_ref in enumerate((y_own_ref, y_got_ref)):
            for e in range(local):
                base = (bases_ref[core] + e) * CAP
                weight = jnp.zeros((rows, tokens), jnp.float32)
                for j in range(2):
                    hit = row_id == places_of([by_lane[j : j + 1]], base, shift_lane)
                    gate = by_lane[2 + j : 3 + j] + by_lane[4 + j : 5 + j] + by_lane[6 + j : 7 + j]
                    weight = weight + jnp.where(hit, gate, 0.0)
                weight = jnp.sum(weight, axis=1, keepdims=True)
                weighed.append((y_ref[e, here, :].astype(jnp.float32) * weight).astype(jnp.bfloat16))
                first = (core * local + e) * rows
                hit = lane == places_of([by_row[:, j : j + 1] for j in range(2)], base, shift_row + first)
                put = hit if put is None else put | hit
        put = put.astype(jnp.float32).astype(jnp.bfloat16)
        out = jnp.dot(put, jnp.concatenate(weighed, axis=0), preferred_element_type=jnp.float32)
        out = out.astype(jnp.bfloat16)
        kept_ref[g * tokens // 2 : (g + 1) * tokens // 2, :] = out[: tokens // 2]
        send_refs[g][...] = out[tokens // 2 :]


def put_rows(y_own, y_got, facts, bases, rows_dev, waits):
    local, _, width = y_own.shape
    tokens = facts.shape[0]
    planes = tokens // (4 * rows_dev)
    vmem = pl.BlockSpec(memory_space=pltpu.VMEM)
    shape = lambda n: jax.ShapeDtypeStruct((n, width), jnp.bfloat16)
    out = pl.pallas_call(
        functools.partial(put_kernel, local, rows_dev, planes, len(waits)),
        out_shape=(shape(2 * planes * rows_dev),) + (shape(2 * rows_dev),) * planes,
        in_specs=[pl.BlockSpec(memory_space=pltpu.SMEM), vmem, vmem, vmem]
        + [pl.BlockSpec(memory_space=pl.ANY)] * len(waits),
        out_specs=(vmem,) * (1 + planes),
        compiler_params=pltpu.CompilerParams(vmem_limit_bytes=20 * MIB),
        cost_estimate=pl.CostEstimate(
            flops=16 * local * CAP * tokens * width,
            bytes_accessed=8 * local * tokens * width,
            transcendentals=0,
        ),
    )(bases, y_own, y_got, facts, *waits)
    return out[0], out[1:]


def swap(a, axis, size, distance):
    return lax.ppermute(a, axis, [(i, i ^ distance) for i in range(size)])


def fold_kernel(groups, count, waits, keep_ref, *rest):
    got_refs, (kept_ref, *send_refs) = rest[:count], rest[count + waits :]
    part = keep_ref.shape[0] // (2 * groups)
    span = got_refs[0].shape[0]
    for i in range(2 * groups):
        start = i * part
        got = got_refs[start // span][start % span : start % span + part, :]
        total = keep_ref[start : start + part, :].astype(jnp.float32) + got.astype(jnp.float32)
        total = total.astype(jnp.bfloat16)
        if i % 2 == 0:
            kept_ref[i // 2 * part : (i // 2 + 1) * part, :] = total
        else:
            send_refs[i // 2][...] = total


def fold(keep, gots, groups, waits=()):
    rows, width = keep.shape
    part = rows // (2 * groups)
    vmem = pl.BlockSpec(memory_space=pltpu.VMEM)
    shape = lambda n: jax.ShapeDtypeStruct((n, width), jnp.bfloat16)
    out = pl.pallas_call(
        functools.partial(fold_kernel, groups, len(gots), len(waits)),
        out_shape=(shape(groups * part),) + (shape(part),) * groups,
        in_specs=[vmem] * (1 + len(gots)) + [pl.BlockSpec(memory_space=pl.ANY)] * len(waits),
        out_specs=(vmem,) * (1 + groups),
        compiler_params=pltpu.CompilerParams(vmem_limit_bytes=10 * MIB),
        cost_estimate=pl.CostEstimate(flops=rows * width, bytes_accessed=6 * rows * width, transcendentals=0),
    )(keep, *gots, *waits)
    return out[0], out[1:]


def exchange_experts(piece, w_gate, w_up, w_down, n_seq, n_exp, late_work):
    x = lambda a: swap(a, "seq", n_seq, 1)
    y = lambda a: swap(a, "exp", n_exp, 2)
    core = lambda a: swap(a, "exp", n_exp, 1)
    z = lambda a, k: swap(a, "seq", n_seq, 2 * k)
    local = w_gate.shape[0]
    me = lax.axis_index("exp").astype(jnp.int32)
    bases = jnp.stack([me, me ^ 1]) * local
    starts = [piece, z(piece, 1), z(piece, 2)]
    ways = [("xy", "yx")[k % 2] for k in range(4)]
    over = {"x": x, "y": y}
    single = [[over[way](starts[k]) for way in ways[k]] for k in range(2)]
    starts[2] = hold(starts[2], single[0] + single[1])
    single.append([over[way](starts[2]) for way in ways[2]])
    starts.append(hold(z(starts[2], 1), single[2]))
    single.append([over[way](starts[3]) for way in ways[3]])

    def gather(k):
        near = []
        for i in (k, k + 1):
            by_f, by_g = single[i]
            near += [starts[i], by_g, by_f, over[ways[i][1]](by_f)]
        return near

    near_b, near_a = gather(0), gather(2)
    own_a, sib_a, facts_a = select_rows(near_a, bases, local)
    got_a = core(sib_a)
    own_b, sib_b, facts_b = select_rows(near_b, bases, local)
    got_b = core(sib_b)
    pages, fill = late_work(facts_b)
    own_a, sib_a, ended = expert_rows(own_a, got_a, w_gate, w_up, w_down, [facts_b, pages])
    cache, filled = fill(ended)
    got_a = core(sib_a)
    own_b, sib_b, ended = expert_rows(own_b, got_b, w_gate, w_up, w_down, [filled])
    got_b = core(sib_b)
    keep_a, (fx_a, fy_a) = put_rows(own_a, got_a, facts_a, bases, piece.shape[0], [ended])
    keep_a, (gy_a, gx_a) = fold(keep_a, [x(fx_a), y(fy_a)], 2)
    keep_b, (fx_b, fy_b) = put_rows(own_b, got_b, facts_b, bases, piece.shape[0], [gy_a])
    gy_a, gx_a = y(gy_a), x(gx_a)
    fx_b, fy_b = hold(fx_b, [gy_a, gx_a]), hold(fy_b, [gy_a, gx_a])
    keep_a, (z_a,) = fold(keep_a, [gy_a, gx_a], 1)
    over_z = (keep_a.astype(jnp.float32) + z(z_a, 1).astype(jnp.float32)).astype(jnp.bfloat16)
    keep_b, (gy_b, gx_b) = fold(keep_b, [x(fx_b), y(fy_b)], 2, [over_z])
    keep_b, (z_b,) = fold(keep_b, [y(gy_b), x(gx_b)], 1)
    mine = keep_b.astype(jnp.float32) + z(z_b, 1).astype(jnp.float32)
    return mine + z(over_z, 2).astype(jnp.float32), cache


def body(
    n_seq,
    n_exp,
    query,
    key_value,
    residual,
    norm_gain,
    segment_ids,
    routes,
    gate_weights,
    page_table,
    w_gate,
    w_up,
    w_down,
):
    rows_dev, width = query.shape[1:]
    everyone = ("exp", "seq")
    group = segment_ids.shape[1]
    share, firsts, heads = head_ranges(width, n_seq)
    span = heads * HEAD_DIM

    flat = routes[0].reshape(rows_dev * 2)
    onehot = (flat[:, None] == jnp.arange(EXPERTS, dtype=jnp.int32)[None, :]).astype(jnp.int32)
    before = jnp.cumsum(onehot, axis=0) - onehot
    target = (flat * CAP + jnp.sum(before * onehot, axis=1)).reshape(rows_dev, 2).astype(jnp.float32)

    keys, values = key_value[0, :, 0], key_value[0, :, 1]

    packed = pack_heads(query[0], keys, values, firsts, span)
    packed = lax.all_to_all(packed, "seq", split_axis=0, concat_axis=0, tiled=True)
    packed = packed.reshape(group, 3 * span)
    context = attention(packed, segment_ids[0], heads)
    context = lax.all_to_all(
        context.reshape(n_seq, rows_dev, span), "seq", split_axis=0, concat_axis=0, tiled=True
    )
    offsets = [j * share - firsts[j] * HEAD_DIM for j in range(n_seq)]

    first = (lax.axis_index("exp") * (EXPERTS // n_exp)).astype(jnp.int32).reshape(1)
    w_gate, w_up = jnp.swapaxes(w_gate, 1, 2), jnp.swapaxes(w_up, 1, 2)
    gates = gate_weights[0]
    facts = jnp.concatenate([target, gates, gates, gates], axis=1)
    facts = jnp.pad(facts, ((0, 0), (0, 128 - facts.shape[1])))
    stream, piece = norm_tokens(context, residual[0], norm_gain, facts, share, offsets)

    slots = jnp.arange(group // PAGE, dtype=jnp.int32)
    order = jnp.sum(jnp.where(page_table[0][None, :] == slots[:, None], slots[None, :], 0), axis=1)

    def fill_cache(late):
        pages = pick_pages(packed, order, late, n_seq, span)
        sent = lax.all_to_all(pages, "seq", split_axis=0, concat_axis=0, tiled=True)
        return pages, lambda behind: join_pages(sent, share, offsets, span, behind)

    if (n_seq, n_exp) == (8, 4):
        mixture, cache = exchange_experts(piece, w_gate, w_up, w_down, n_seq, n_exp, fill_cache)
    else:
        cache, _ = fill_cache(piece)[1](piece)
        blocks = n_seq * n_exp
        everything = lax.all_gather(piece, everyone, axis=0, tiled=True)
        facts = everything[:, width : width + 8].astype(jnp.float32)
        facts = facts.reshape(blocks // CHUNK_BLOCKS, CHUNK_BLOCKS * rows_dev, 8).transpose(0, 2, 1)
        gates = facts[:, 2:4] + facts[:, 4:6] + facts[:, 6:8]
        partial = experts(
            everything[:, :width], facts[:, :2].astype(jnp.int32), gates, w_gate, w_up, w_down, first
        )
        mixture = lax.psum_scatter(partial, everyone, scatter_dimension=0, tiled=True).astype(jnp.float32)
    layer_out = (stream + mixture).astype(jnp.bfloat16)
    return (layer_out[None], cache.reshape(1, rows_dev // PAGE, PAGE, 2 * width))


def solution(mesh):
    in_specs = (
        P("exp", "seq", None),
        P("exp", "seq", None, None),
        P("exp", "seq", None),
        P(),
        P("exp", None),
        P("exp", "seq", None),
        P("exp", "seq", None),
        P("exp", None),
        P("exp", None, "seq"),
        P("exp", None, "seq"),
        P("exp", "seq", None),
    )
    out_specs = (P("exp", "seq", None), P("exp", "seq", None, None))
    run = functools.partial(body, mesh.shape["seq"], mesh.shape["exp"])
    return jax.shard_map(run, mesh=mesh, in_specs=in_specs, out_specs=out_specs, check_vma=False)
```

```python
import functools
import math

import jax
import jax.numpy as jnp
from jax import lax
from jax.experimental import pallas as pl
from jax.experimental.pallas import tpu as pltpu
from jax.sharding import PartitionSpec as P

HEADS = 36
HEAD_DIM = 64
EXPERTS = 8
PAGE = 16
CAP = 24
MIB = 1024 * 1024
CHUNK_BLOCKS = 8


def head_ranges(width, n_seq):
    share = width // n_seq
    firsts = [j * share // HEAD_DIM for j in range(n_seq)]
    count = max(-(-(j + 1) * share // HEAD_DIM) - firsts[j] for j in range(n_seq))
    firsts = [min(f, HEADS - count) for f in firsts]
    return share, firsts, count


def attention_kernel(heads, q_rows, packed_ref, seg_row_ref, seg_col_ref, out_ref):
    total = packed_ref.shape[0]
    span = heads * HEAD_DIM
    scale = 1.0 / math.sqrt(HEAD_DIM)
    for start in range(0, total, q_rows):
        end = start + q_rows
        q_place = start + lax.broadcasted_iota(jnp.int32, (q_rows, end), 0)
        k_place = lax.broadcasted_iota(jnp.int32, (q_rows, end), 1)
        visible = (seg_col_ref[start:end, :] == seg_row_ref[:, :end]) & (k_place <= q_place)
        parts = []
        for h in range(heads):
            a = h * HEAD_DIM
            q = packed_ref[start:end, a : a + HEAD_DIM]
            k = packed_ref[:end, span + a : span + a + HEAD_DIM]
            v = packed_ref[:end, 2 * span + a : 2 * span + a + HEAD_DIM]
            s = lax.dot_general(q, k, (((1,), (1,)), ((), ())), preferred_element_type=jnp.float32)
            s = jnp.where(visible, s * scale, -1e30)
            top = jnp.max(s, axis=1, keepdims=True)
            p = jnp.exp(s - top)
            denominator = jnp.sum(p, axis=1, keepdims=True)
            o = jnp.dot(p.astype(jnp.bfloat16), v, preferred_element_type=jnp.float32)
            parts.append((o / denominator).astype(jnp.bfloat16))
        out_ref[start:end, :] = jnp.concatenate(parts, axis=1)


def attention(packed, segments, heads):
    total = packed.shape[0]
    span = heads * HEAD_DIM
    return pl.pallas_call(
        functools.partial(attention_kernel, heads, 128),
        out_shape=jax.ShapeDtypeStruct((total, span), jnp.bfloat16),
        compiler_params=pltpu.CompilerParams(vmem_limit_bytes=24 * MIB),
        cost_estimate=pl.CostEstimate(
            flops=4 * total * total * span, bytes_accessed=8 * total * span, transcendentals=total * total * heads
        ),
    )(packed, segments[None, :], segments[:, None])


def dot_t(a, b):
    return lax.dot_general(a, b, (((1,), (1,)), ((), ())), preferred_element_type=jnp.float32)


def expert_kernel(
    local, rows, tokens, first_ref, x_ref, tgt_ref, gates_ref, wg_ref, wu_ref, wd_ref, out_ref, kept_ref
):
    le = pl.program_id(0)
    chunk = pl.program_id(1)

    def selection(which):
        base = (first_ref[0] + which) * CAP
        row_id = lax.broadcasted_iota(jnp.int32, (rows, tokens), 0)
        block = lax.broadcasted_iota(jnp.int32, (1, tokens), 1) // 64
        picks, weights = None, None
        for j in range(2):
            slot = tgt_ref[0, j : j + 1, :] - base
            place = jnp.where((slot >= 0) & (slot < CAP), block * CAP + slot, -1)
            hit = row_id == place
            gate = jnp.where(hit, gates_ref[0, j : j + 1, :], 0.0)
            picks = hit if picks is None else picks | hit
            weights = gate if weights is None else weights + gate
        return picks.astype(jnp.float32).astype(jnp.bfloat16), jnp.sum(weights, axis=1, keepdims=True)

    pick, weight = selection(le)
    chosen = jnp.dot(pick, x_ref[...], preferred_element_type=jnp.float32).astype(jnp.bfloat16)
    gate = dot_t(chosen, wg_ref[0])
    upper = dot_t(chosen, wu_ref[0])
    hidden = (gate / (1.0 + jnp.exp(-gate)) * upper).astype(jnp.bfloat16)
    y = jnp.dot(hidden, wd_ref[0], preferred_element_type=jnp.float32)
    y = (y * weight).astype(jnp.bfloat16)

    if local > 1:

        @pl.when(le < local - 1)
        def _():
            kept_ref[le, chunk] = y

    @pl.when(le == local - 1)
    def _():
        total = lax.dot_general(pick, y, (((0,), (0,)), ((), ())), preferred_element_type=jnp.float32)
        for other in range(local - 1):
            pick_o, _ = selection(other)
            total += lax.dot_general(
                pick_o, kept_ref[other, chunk], (((0,), (0,)), ((), ())), preferred_element_type=jnp.float32
            )
        out_ref[...] = total.astype(jnp.bfloat16)


def experts(x, tgt, gates, w_gate, w_up, w_down, first):
    local, hidden, width = w_gate.shape
    chunks, _, tokens = tgt.shape
    rows = tokens // 64 * CAP
    last = local - 1
    return pl.pallas_call(
        functools.partial(expert_kernel, local, rows, tokens),
        out_shape=jax.ShapeDtypeStruct(x.shape, jnp.bfloat16),
        grid=(local, chunks),
        in_specs=[
            pl.BlockSpec(memory_space=pltpu.SMEM),
            pl.BlockSpec((tokens, width), lambda e, c: (c, 0)),
            pl.BlockSpec((1, 2, tokens), lambda e, c: (c, 0, 0)),
            pl.BlockSpec((1, 2, tokens), lambda e, c: (c, 0, 0)),
            pl.BlockSpec((1, hidden, width), lambda e, c: (e, 0, 0)),
            pl.BlockSpec((1, hidden, width), lambda e, c: (e, 0, 0)),
            pl.BlockSpec((1, hidden, width), lambda e, c: (e, 0, 0)),
        ],
        out_specs=pl.BlockSpec((tokens, width), lambda e, c: (jnp.where(e == last, c, 0), 0)),
        scratch_shapes=[pltpu.VMEM((max(last, 1), chunks if last else 1, rows, width), jnp.bfloat16)],
        compiler_params=pltpu.CompilerParams(vmem_limit_bytes=58 * MIB),
        cost_estimate=pl.CostEstimate(
            flops=6 * local * chunks * rows * width * hidden,
            bytes_accessed=6 * local * width * hidden + 6 * chunks * tokens * width,
            transcendentals=local * chunks * rows * hidden,
        ),
    )(first, x, tgt, gates, w_gate, w_up, w_down)


def pack_kernel(firsts, span, q_ref, k_ref, v_ref, out_ref):
    for j, first in enumerate(firsts):
        lanes = slice(first * HEAD_DIM, first * HEAD_DIM + span)
        out_ref[j] = jnp.concatenate([r[:, lanes] for r in (q_ref, k_ref, v_ref)], axis=1)


def pack_heads(query, keys, values, firsts, span):
    rows_dev = query.shape[0]
    n_seq = len(firsts)
    return pl.pallas_call(
        functools.partial(pack_kernel, firsts, span),
        out_shape=jax.ShapeDtypeStruct((n_seq, rows_dev, 3 * span), jnp.bfloat16),
        compiler_params=pltpu.CompilerParams(vmem_limit_bytes=12 * MIB),
        cost_estimate=pl.CostEstimate(flops=0, bytes_accessed=12 * n_seq * rows_dev * span, transcendentals=0),
    )(query, keys, values)


def norm_kernel(share, offsets, context_ref, residual_ref, gain_ref, facts_ref, stream_ref, piece_ref):
    n_seq, _, _ = context_ref.shape
    width = residual_ref.shape[1]
    parts = [context_ref[j][:, offsets[j] : offsets[j] + share] for j in range(n_seq)]
    context = jnp.concatenate(parts, axis=1).astype(jnp.float32)
    stream = residual_ref[...].astype(jnp.float32) + context
    stream_ref[...] = stream
    mean = jnp.mean(stream * stream, axis=1, keepdims=True)
    normed = stream * lax.rsqrt(mean + 1e-05) * gain_ref[...].astype(jnp.float32)
    piece_ref[:, :width] = normed.astype(jnp.bfloat16)
    facts = facts_ref[...]
    lane = lax.broadcasted_iota(jnp.int32, facts.shape, 1)
    high = facts.astype(jnp.bfloat16).astype(jnp.float32)
    middle = (facts - high).astype(jnp.bfloat16).astype(jnp.float32)
    low = facts - high - middle
    own = jnp.where(lane < 4, high, jnp.where(lane < 6, middle, low))
    piece_ref[:, width:] = own.astype(jnp.bfloat16)


def norm_tokens(context, residual, gain, facts, share, offsets):
    rows_dev, width = residual.shape
    return pl.pallas_call(
        functools.partial(norm_kernel, share, offsets),
        out_shape=(
            jax.ShapeDtypeStruct((rows_dev, width), jnp.float32),
            jax.ShapeDtypeStruct((rows_dev, width + facts.shape[1]), jnp.bfloat16),
        ),
        compiler_params=pltpu.CompilerParams(vmem_limit_bytes=12 * MIB),
        cost_estimate=pl.CostEstimate(
            flops=10 * rows_dev * width, bytes_accessed=10 * rows_dev * width, transcendentals=rows_dev
        ),
    )(context, residual, gain[None, :], facts)


def pick_pages_kernel(per_device, first_lane, order_ref, packed_ref, late_ref, out_ref):
    del late_ref
    for j in range(out_ref.shape[0]):
        for i in range(per_device):
            rows = pl.ds(pl.multiple_of(order_ref[j * per_device + i] * PAGE, PAGE), PAGE)
            out_ref[j, i * PAGE : (i + 1) * PAGE, :] = packed_ref[rows, first_lane:]


def pick_pages(packed, order, late, n_seq, span):
    rows = packed.shape[0] // n_seq
    vmem = pl.BlockSpec(memory_space=pltpu.VMEM)
    return pl.pallas_call(
        functools.partial(pick_pages_kernel, rows // PAGE, span),
        out_shape=jax.ShapeDtypeStruct((n_seq, rows, 2 * span), jnp.bfloat16),
        in_specs=[pl.BlockSpec(memory_space=pltpu.SMEM), vmem, pl.BlockSpec(memory_space=pl.ANY)],
        compiler_params=pltpu.CompilerParams(vmem_limit_bytes=8 * MIB),
        cost_estimate=pl.CostEstimate(flops=0, bytes_accessed=10 * packed.shape[0] * span, transcendentals=0),
    )(order, packed, late)


def join_pages_kernel(share, offsets, span, pages_ref, behind_ref, out_ref, ended_ref):
    del behind_ref
    ended_ref[...] = jnp.zeros_like(ended_ref)
    width = share * len(offsets)
    for part in range(2):
        parts = [
            pages_ref[j][:, part * span + offsets[j] : part * span + offsets[j] + share]
            for j in range(len(offsets))
        ]
        out_ref[:, part * width : (part + 1) * width] = jnp.concatenate(parts, axis=1)


def join_pages(pages, share, offsets, span, behind):
    n_seq, rows, _ = pages.shape
    return pl.pallas_call(
        functools.partial(join_pages_kernel, share, offsets, span),
        out_shape=(
            jax.ShapeDtypeStruct((rows, 2 * share * n_seq), jnp.bfloat16),
            jax.ShapeDtypeStruct((8, 128), jnp.float32),
        ),
        in_specs=[pl.BlockSpec(memory_space=pltpu.VMEM), pl.BlockSpec(memory_space=pl.ANY)],
        compiler_params=pltpu.CompilerParams(vmem_limit_bytes=12 * MIB),
        cost_estimate=pl.CostEstimate(flops=0, bytes_accessed=8 * rows * n_seq * span, transcendentals=0),
    )(pages, behind)


def places_of(slots, base, shift):
    place = -1
    for slot in slots:
        slot = slot.astype(jnp.int32) - base
        place = jnp.where((slot >= 0) & (slot < CAP), shift + slot, place)
    return place


def hold_kernel(*refs):
    del refs


def hold(a, waits):
    anywhere = pl.BlockSpec(memory_space=pl.ANY)
    return pl.pallas_call(
        hold_kernel,
        out_shape=jax.ShapeDtypeStruct(a.shape, a.dtype),
        in_specs=[anywhere] * (1 + len(waits)),
        out_specs=anywhere,
        input_output_aliases={0: 0},
        compiler_params=pltpu.CompilerParams(vmem_limit_bytes=MIB),
        cost_estimate=pl.CostEstimate(flops=0, bytes_accessed=0, transcendentals=0),
    )(a, *waits)


def facts_by_lane(x):
    unit = lax.broadcasted_iota(jnp.int32, (8, 128), 0) == lax.broadcasted_iota(jnp.int32, (8, 128), 1)
    return dot_t(unit.astype(jnp.float32).astype(jnp.bfloat16), x)


def select_kernel(local, rows_dev, count, bases_ref, *refs):
    piece_refs, (own_hbm, sib_ref, facts_ref, own_ref, own_sem) = refs[:count], refs[-5:]
    width = own_ref.shape[2]
    own_copies = []
    tokens, rows = 4 * rows_dev, 4 * CAP
    shift = lax.broadcasted_iota(jnp.int32, (1, tokens), 1) // rows_dev * CAP
    row_id = lax.broadcasted_iota(jnp.int32, (rows, tokens), 0)
    for g in range(len(piece_refs) // 4):
        x = jnp.concatenate([p[...] for p in piece_refs[4 * g : 4 * g + 4]], axis=0)
        facts_ref[g * tokens : (g + 1) * tokens, :] = x[:, width:]
        facts = facts_by_lane(x[:, width:])
        picks = []
        for core in range(2):
            for e in range(local):
                base = (bases_ref[core] + e) * CAP
                hit = row_id == places_of([facts[j : j + 1] for j in range(2)], base, shift)
                picks.append(hit.astype(jnp.float32))
        picks = jnp.concatenate(picks, axis=0).astype(jnp.bfloat16)
        chosen = jnp.dot(picks, x[:, :width], preferred_element_type=jnp.float32).astype(jnp.bfloat16)
        for e in range(local):
            own_ref[e, g * rows : (g + 1) * rows, :] = chosen[e * rows : (e + 1) * rows]
            sib_ref[e, g * rows : (g + 1) * rows, :] = chosen[(local + e) * rows : (local + e + 1) * rows]
        for e in range(local):
            here = (e, pl.ds(g * rows, rows), slice(None))
            copy = pltpu.make_async_copy(own_ref.at[here], own_hbm.at[here], own_sem.at[g * local + e])
            copy.start()
            own_copies.append(copy)
    for copy in own_copies:
        copy.wait()


def select_rows(pieces, bases, local, waits=()):
    rows_dev, wide = pieces[0].shape
    width = wide - 128
    rows = len(pieces) * CAP
    out = jax.ShapeDtypeStruct((local, rows, width), jnp.bfloat16)
    vmem = pl.BlockSpec(memory_space=pltpu.VMEM)
    return pl.pallas_call(
        functools.partial(select_kernel, local, rows_dev, len(pieces)),
        out_shape=(out, out, jax.ShapeDtypeStruct((len(pieces) * rows_dev, 128), jnp.bfloat16)),
        in_specs=[pl.BlockSpec(memory_space=pltpu.SMEM)]
        + [vmem] * len(pieces)
        + [pl.BlockSpec(memory_space=pl.ANY)] * len(waits),
        out_specs=(pl.BlockSpec(memory_space=pl.ANY), vmem, vmem),
        scratch_shapes=[
            pltpu.VMEM(out.shape, jnp.bfloat16),
            pltpu.SemaphoreType.DMA((len(pieces) // 4 * local,)),
        ],
        compiler_params=pltpu.CompilerParams(vmem_limit_bytes=20 * MIB),
        cost_estimate=pl.CostEstimate(
            flops=16 * local * CAP * rows_dev * len(pieces) * width,
            bytes_accessed=2 * len(pieces) * rows_dev * wide + 4 * local * rows * width,
            transcendentals=0,
        ),
    )(bases, *pieces, *waits)


def rows_kernel(local, waits, own_hbm, got_ref, wg_hbm, wu_hbm, wd_hbm, *rest):
    y_own_ref, y_sib_ref, ended_ref, own_ref, wg, wu, wd, own_sem, weight_sem = rest[waits:]
    ended_ref[...] = jnp.zeros_like(ended_ref)
    half = got_ref.shape[1]
    own_copy = pltpu.make_async_copy(own_hbm, own_ref, own_sem)
    own_copy.start()
    copies = [
        [
            pltpu.make_async_copy(source.at[e], target.at[e], weight_sem.at[3 * e + i])
            for i, (source, target) in enumerate(((wg_hbm, wg), (wu_hbm, wu), (wd_hbm, wd)))
        ]
        for e in range(local)
    ]
    for group in copies:
        for copy in group:
            copy.start()
    own_copy.wait()
    for e in range(local):
        rows = jnp.concatenate([own_ref[e], got_ref[e]], axis=0)
        copies[e][0].wait()
        gate = dot_t(rows, wg[e])
        copies[e][1].wait()
        upper = dot_t(rows, wu[e])
        hidden = (gate / (1.0 + jnp.exp(-gate)) * upper).astype(jnp.bfloat16)
        copies[e][2].wait()
        y = jnp.dot(hidden, wd[e], preferred_element_type=jnp.float32).astype(jnp.bfloat16)
        y_own_ref[e] = y[:half]
        y_sib_ref[e] = y[half:]


def expert_rows(own, got, w_gate, w_up, w_down, waits):
    local, hidden, width = w_gate.shape
    rows = 2 * own.shape[1]
    out = jax.ShapeDtypeStruct(own.shape, jnp.bfloat16)
    vmem = pl.BlockSpec(memory_space=pltpu.VMEM)
    weights = pltpu.VMEM((local, hidden, width), jnp.bfloat16)
    return pl.pallas_call(
        functools.partial(rows_kernel, local, len(waits)),
        out_shape=(out, out, jax.ShapeDtypeStruct((8, 128), jnp.float32)),
        in_specs=[pl.BlockSpec(memory_space=pl.ANY), vmem]
        + [pl.BlockSpec(memory_space=pl.ANY)] * (3 + len(waits)),
        out_specs=(vmem, vmem, vmem),
        scratch_shapes=[
            pltpu.VMEM(own.shape, jnp.bfloat16),
            weights,
            weights,
            weights,
            pltpu.SemaphoreType.DMA,
            pltpu.SemaphoreType.DMA((3 * local,)),
        ],
        compiler_params=pltpu.CompilerParams(vmem_limit_bytes=46 * MIB),
        cost_estimate=pl.CostEstimate(
            flops=6 * local * rows * width * hidden,
            bytes_accessed=6 * local * width * hidden + 4 * local * rows * width,
            transcendentals=local * rows * hidden,
        ),
    )(own, got, w_gate, w_up, w_down, *waits)


def put_kernel(local, rows_dev, planes, waits, bases_ref, y_own_ref, y_got_ref, facts_ref, *rest):
    kept_ref, *send_refs, ended_ref = rest[waits:]
    ended_ref[...] = jnp.zeros_like(ended_ref)
    tokens, rows = 4 * rows_dev, 4 * CAP
    total = 2 * local * rows
    shift_lane = lax.broadcasted_iota(jnp.int32, (1, tokens), 1) // rows_dev * CAP
    shift_row = lax.broadcasted_iota(jnp.int32, (tokens, 1), 0) // rows_dev * CAP
    row_id = lax.broadcasted_iota(jnp.int32, (rows, tokens), 0)
    lane = lax.broadcasted_iota(jnp.int32, (tokens, total), 1)
    for g in range(planes):
        facts = facts_ref[g * tokens : (g + 1) * tokens, :]
        by_lane = facts_by_lane(facts)
        by_row = facts.astype(jnp.float32)
        here = slice(g * rows, (g + 1) * rows)
        weighed, put = [], None
        for core, y_ref in enumerate((y_own_ref, y_got_ref)):
            for e in range(local):
                base = (bases_ref[core] + e) * CAP
                weight = jnp.zeros((rows, tokens), jnp.float32)
                for j in range(2):
                    hit = row_id == places_of([by_lane[j : j + 1]], base, shift_lane)
                    gate = by_lane[2 + j : 3 + j] + by_lane[4 + j : 5 + j] + by_lane[6 + j : 7 + j]
                    weight = weight + jnp.where(hit, gate, 0.0)
                weight = jnp.sum(weight, axis=1, keepdims=True)
                weighed.append((y_ref[e, here, :].astype(jnp.float32) * weight).astype(jnp.bfloat16))
                first = (core * local + e) * rows
                hit = lane == places_of([by_row[:, j : j + 1] for j in range(2)], base, shift_row + first)
                put = hit if put is None else put | hit
        put = put.astype(jnp.float32).astype(jnp.bfloat16)
        out = jnp.dot(put, jnp.concatenate(weighed, axis=0), preferred_element_type=jnp.float32)
        out = out.astype(jnp.bfloat16)
        kept_ref[g * tokens // 2 : (g + 1) * tokens // 2, :] = out[: tokens // 2]
        send_refs[g][...] = out[tokens // 2 :]


def put_rows(y_own, y_got, facts, bases, rows_dev, waits):
    local, _, width = y_own.shape
    tokens = facts.shape[0]
    planes = tokens // (4 * rows_dev)
    vmem = pl.BlockSpec(memory_space=pltpu.VMEM)
    shape = lambda n: jax.ShapeDtypeStruct((n, width), jnp.bfloat16)
    out = pl.pallas_call(
        functools.partial(put_kernel, local, rows_dev, planes, len(waits)),
        out_shape=(shape(2 * planes * rows_dev),)
        + (shape(2 * rows_dev),) * planes
        + (jax.ShapeDtypeStruct((8, 128), jnp.float32),),
        in_specs=[pl.BlockSpec(memory_space=pltpu.SMEM), vmem, vmem, vmem]
        + [pl.BlockSpec(memory_space=pl.ANY)] * len(waits),
        out_specs=(vmem,) * (2 + planes),
        compiler_params=pltpu.CompilerParams(vmem_limit_bytes=20 * MIB),
        cost_estimate=pl.CostEstimate(
            flops=16 * local * CAP * tokens * width,
            bytes_accessed=8 * local * tokens * width,
            transcendentals=0,
        ),
    )(bases, y_own, y_got, facts, *waits)
    return out[0], out[1:-1], out[-1]


def swap(a, axis, size, distance):
    return lax.ppermute(a, axis, [(i, i ^ distance) for i in range(size)])


def fold_kernel(groups, count, waits, keep_ref, *rest):
    got_refs, (kept_ref, *send_refs) = rest[:count], rest[count + waits :]
    part = keep_ref.shape[0] // (2 * groups)
    span = got_refs[0].shape[0]
    for i in range(2 * groups):
        start = i * part
        got = got_refs[start // span][start % span : start % span + part, :]
        total = keep_ref[start : start + part, :].astype(jnp.float32) + got.astype(jnp.float32)
        total = total.astype(jnp.bfloat16)
        if i % 2 == 0:
            kept_ref[i // 2 * part : (i // 2 + 1) * part, :] = total
        else:
            send_refs[i // 2][...] = total


def fold(keep, gots, groups, waits=()):
    rows, width = keep.shape
    part = rows // (2 * groups)
    vmem = pl.BlockSpec(memory_space=pltpu.VMEM)
    shape = lambda n: jax.ShapeDtypeStruct((n, width), jnp.bfloat16)
    out = pl.pallas_call(
        functools.partial(fold_kernel, groups, len(gots), len(waits)),
        out_shape=(shape(groups * part),) + (shape(part),) * groups,
        in_specs=[vmem] * (1 + len(gots)) + [pl.BlockSpec(memory_space=pl.ANY)] * len(waits),
        out_specs=(vmem,) * (1 + groups),
        compiler_params=pltpu.CompilerParams(vmem_limit_bytes=10 * MIB),
        cost_estimate=pl.CostEstimate(flops=rows * width, bytes_accessed=6 * rows * width, transcendentals=0),
    )(keep, *gots, *waits)
    return out[0], out[1:]


def exchange_experts(piece, w_gate, w_up, w_down, n_seq, n_exp, late_work):
    x = lambda a: swap(a, "seq", n_seq, 1)
    y = lambda a: swap(a, "exp", n_exp, 2)
    core = lambda a: swap(a, "exp", n_exp, 1)
    z = lambda a, k: swap(a, "seq", n_seq, 2 * k)
    local = w_gate.shape[0]
    me = lax.axis_index("exp").astype(jnp.int32)
    bases = jnp.stack([me, me ^ 1]) * local
    starts = [piece, z(piece, 1), z(piece, 2)]
    ways = [("xy", "yx")[k % 2] for k in range(4)]
    over = {"x": x, "y": y}
    single = [[over[way](starts[k]) for way in ways[k]] for k in range(2)]
    starts[2] = hold(starts[2], single[0] + single[1])
    single.append([over[way](starts[2]) for way in ways[2]])
    starts.append(hold(z(starts[2], 1), single[2]))
    single.append([over[way](starts[3]) for way in ways[3]])

    def gather(k):
        near = []
        for i in (k, k + 1):
            by_f, by_g = single[i]
            near += [starts[i], by_g, by_f, over[ways[i][1]](by_f)]
        return near

    near_b, near_a = gather(0), gather(2)
    own_a, sib_a, facts_a = select_rows(near_a, bases, local)
    got_a = core(sib_a)
    pages, fill = late_work(facts_a)
    own_b, sib_b, facts_b = select_rows(near_b, bases, local, [pages])
    got_b = core(sib_b)
    own_a, sib_a, ended = expert_rows(own_a, got_a, w_gate, w_up, w_down, [facts_b, pages])
    cache, filled = fill(ended)
    got_a = core(sib_a)
    own_b, sib_b, ended = expert_rows(own_b, got_b, w_gate, w_up, w_down, [filled])
    got_b = core(sib_b)
    keep_a, (fx_a, fy_a), _ = put_rows(own_a, got_a, facts_a, bases, piece.shape[0], [ended])
    keep_a, (gy_a, gx_a) = fold(keep_a, [x(fx_a), y(fy_a)], 2)
    keep_b, (fx_b, fy_b), put_b = put_rows(own_b, got_b, facts_b, bases, piece.shape[0], [gy_a])
    gy_a, gx_a = y(gy_a), x(gx_a)
    fx_b, fy_b = hold(fx_b, [gy_a, gx_a]), hold(fy_b, [gy_a, gx_a])
    keep_a, (z_a,) = fold(keep_a, [gy_a, gx_a], 1, [put_b])
    over_z = (keep_a.astype(jnp.float32) + z(z_a, 1).astype(jnp.float32)).astype(jnp.bfloat16)
    keep_b, (gy_b, gx_b) = fold(keep_b, [x(fx_b), y(fy_b)], 2, [over_z])
    back_a = z(over_z, 2)
    keep_b, (z_b,) = fold(keep_b, [y(gy_b), x(gx_b)], 1, [back_a])
    mine = keep_b.astype(jnp.float32) + z(z_b, 1).astype(jnp.float32)
    return mine + back_a.astype(jnp.float32), cache


def body(
    n_seq,
    n_exp,
    query,
    key_value,
    residual,
    norm_gain,
    segment_ids,
    routes,
    gate_weights,
    page_table,
    w_gate,
    w_up,
    w_down,
):
    rows_dev, width = query.shape[1:]
    everyone = ("exp", "seq")
    group = segment_ids.shape[1]
    share, firsts, heads = head_ranges(width, n_seq)
    span = heads * HEAD_DIM

    flat = routes[0].reshape(rows_dev * 2)
    onehot = (flat[:, None] == jnp.arange(EXPERTS, dtype=jnp.int32)[None, :]).astype(jnp.int32)
    before = jnp.cumsum(onehot, axis=0) - onehot
    target = (flat * CAP + jnp.sum(before * onehot, axis=1)).reshape(rows_dev, 2).astype(jnp.float32)

    keys, values = key_value[0, :, 0], key_value[0, :, 1]

    packed = pack_heads(query[0], keys, values, firsts, span)
    packed = lax.all_to_all(packed, "seq", split_axis=0, concat_axis=0, tiled=True)
    packed = packed.reshape(group, 3 * span)
    context = attention(packed, segment_ids[0], heads)
    context = lax.all_to_all(
        context.reshape(n_seq, rows_dev, span), "seq", split_axis=0, concat_axis=0, tiled=True
    )
    offsets = [j * share - firsts[j] * HEAD_DIM for j in range(n_seq)]

    first = (lax.axis_index("exp") * (EXPERTS // n_exp)).astype(jnp.int32).reshape(1)
    w_gate, w_up = jnp.swapaxes(w_gate, 1, 2), jnp.swapaxes(w_up, 1, 2)
    gates = gate_weights[0]
    facts = jnp.concatenate([target, gates, gates, gates], axis=1)
    facts = jnp.pad(facts, ((0, 0), (0, 128 - facts.shape[1])))
    stream, piece = norm_tokens(context, residual[0], norm_gain, facts, share, offsets)

    slots = jnp.arange(group // PAGE, dtype=jnp.int32)
    order = jnp.sum(jnp.where(page_table[0][None, :] == slots[:, None], slots[None, :], 0), axis=1)

    def fill_cache(late):
        pages = pick_pages(packed, order, late, n_seq, span)
        sent = lax.all_to_all(pages, "seq", split_axis=0, concat_axis=0, tiled=True)
        return pages, lambda behind: join_pages(sent, share, offsets, span, behind)

    if (n_seq, n_exp) == (8, 4):
        mixture, cache = exchange_experts(piece, w_gate, w_up, w_down, n_seq, n_exp, fill_cache)
    else:
        cache, _ = fill_cache(piece)[1](piece)
        blocks = n_seq * n_exp
        everything = lax.all_gather(piece, everyone, axis=0, tiled=True)
        facts = everything[:, width : width + 8].astype(jnp.float32)
        facts = facts.reshape(blocks // CHUNK_BLOCKS, CHUNK_BLOCKS * rows_dev, 8).transpose(0, 2, 1)
        gates = facts[:, 2:4] + facts[:, 4:6] + facts[:, 6:8]
        partial = experts(
            everything[:, :width], facts[:, :2].astype(jnp.int32), gates, w_gate, w_up, w_down, first
        )
        mixture = lax.psum_scatter(partial, everyone, scatter_dimension=0, tiled=True).astype(jnp.float32)
    layer_out = (stream + mixture).astype(jnp.bfloat16)
    return (layer_out[None], cache.reshape(1, rows_dev // PAGE, PAGE, 2 * width))


def solution(mesh):
    in_specs = (
        P("exp", "seq", None),
        P("exp", "seq", None, None),
        P("exp", "seq", None),
        P(),
        P("exp", None),
        P("exp", "seq", None),
        P("exp", "seq", None),
        P("exp", None),
        P("exp", None, "seq"),
        P("exp", None, "seq"),
        P("exp", "seq", None),
    )
    out_specs = (P("exp", "seq", None), P("exp", "seq", None, None))
    run = functools.partial(body, mesh.shape["seq"], mesh.shape["exp"])
    return jax.shard_map(run, mesh=mesh, in_specs=in_specs, out_specs=out_specs, check_vma=False)
```

```python
import functools
import math

import jax
import jax.numpy as jnp
from jax import lax
from jax.experimental import pallas as pl
from jax.experimental.pallas import tpu as pltpu
from jax.sharding import PartitionSpec as P

HEADS = 36
HEAD_DIM = 64
EXPERTS = 8
PAGE = 16
CAP = 24
MIB = 1024 * 1024
CHUNK_BLOCKS = 8


def head_ranges(width, n_seq):
    share = width // n_seq
    firsts = [j * share // HEAD_DIM for j in range(n_seq)]
    count = max(-(-(j + 1) * share // HEAD_DIM) - firsts[j] for j in range(n_seq))
    firsts = [min(f, HEADS - count) for f in firsts]
    return share, firsts, count


def attention_kernel(heads, q_rows, packed_ref, seg_row_ref, seg_col_ref, out_ref):
    total = packed_ref.shape[0]
    span = heads * HEAD_DIM
    scale = 1.0 / math.sqrt(HEAD_DIM)
    for start in range(0, total, q_rows):
        end = start + q_rows
        q_place = start + lax.broadcasted_iota(jnp.int32, (q_rows, end), 0)
        k_place = lax.broadcasted_iota(jnp.int32, (q_rows, end), 1)
        visible = (seg_col_ref[start:end, :] == seg_row_ref[:, :end]) & (k_place <= q_place)
        parts = []
        for h in range(heads):
            a = h * HEAD_DIM
            q = packed_ref[start:end, a : a + HEAD_DIM]
            k = packed_ref[:end, span + a : span + a + HEAD_DIM]
            v = packed_ref[:end, 2 * span + a : 2 * span + a + HEAD_DIM]
            s = lax.dot_general(q, k, (((1,), (1,)), ((), ())), preferred_element_type=jnp.float32)
            s = jnp.where(visible, s * scale, -1e30)
            top = jnp.max(s, axis=1, keepdims=True)
            p = jnp.exp(s - top)
            denominator = jnp.sum(p, axis=1, keepdims=True)
            o = jnp.dot(p.astype(jnp.bfloat16), v, preferred_element_type=jnp.float32)
            parts.append((o / denominator).astype(jnp.bfloat16))
        out_ref[start:end, :] = jnp.concatenate(parts, axis=1)


def attention(packed, segments, heads):
    total = packed.shape[0]
    span = heads * HEAD_DIM
    return pl.pallas_call(
        functools.partial(attention_kernel, heads, 128),
        out_shape=jax.ShapeDtypeStruct((total, span), jnp.bfloat16),
        compiler_params=pltpu.CompilerParams(vmem_limit_bytes=24 * MIB),
        cost_estimate=pl.CostEstimate(
            flops=4 * total * total * span, bytes_accessed=8 * total * span, transcendentals=total * total * heads
        ),
    )(packed, segments[None, :], segments[:, None])


def dot_t(a, b):
    return lax.dot_general(a, b, (((1,), (1,)), ((), ())), preferred_element_type=jnp.float32)


def expert_kernel(
    local, rows, tokens, first_ref, x_ref, tgt_ref, gates_ref, wg_ref, wu_ref, wd_ref, out_ref, kept_ref
):
    le = pl.program_id(0)
    chunk = pl.program_id(1)

    def selection(which):
        base = (first_ref[0] + which) * CAP
        row_id = lax.broadcasted_iota(jnp.int32, (rows, tokens), 0)
        block = lax.broadcasted_iota(jnp.int32, (1, tokens), 1) // 64
        picks, weights = None, None
        for j in range(2):
            slot = tgt_ref[0, j : j + 1, :] - base
            place = jnp.where((slot >= 0) & (slot < CAP), block * CAP + slot, -1)
            hit = row_id == place
            gate = jnp.where(hit, gates_ref[0, j : j + 1, :], 0.0)
            picks = hit if picks is None else picks | hit
            weights = gate if weights is None else weights + gate
        return picks.astype(jnp.float32).astype(jnp.bfloat16), jnp.sum(weights, axis=1, keepdims=True)

    pick, weight = selection(le)
    chosen = jnp.dot(pick, x_ref[...], preferred_element_type=jnp.float32).astype(jnp.bfloat16)
    gate = dot_t(chosen, wg_ref[0])
    upper = dot_t(chosen, wu_ref[0])
    hidden = (gate / (1.0 + jnp.exp(-gate)) * upper).astype(jnp.bfloat16)
    y = jnp.dot(hidden, wd_ref[0], preferred_element_type=jnp.float32)
    y = (y * weight).astype(jnp.bfloat16)

    if local > 1:

        @pl.when(le < local - 1)
        def _():
            kept_ref[le, chunk] = y

    @pl.when(le == local - 1)
    def _():
        total = lax.dot_general(pick, y, (((0,), (0,)), ((), ())), preferred_element_type=jnp.float32)
        for other in range(local - 1):
            pick_o, _ = selection(other)
            total += lax.dot_general(
                pick_o, kept_ref[other, chunk], (((0,), (0,)), ((), ())), preferred_element_type=jnp.float32
            )
        out_ref[...] = total.astype(jnp.bfloat16)


def experts(x, tgt, gates, w_gate, w_up, w_down, first):
    local, hidden, width = w_gate.shape
    chunks, _, tokens = tgt.shape
    rows = tokens // 64 * CAP
    last = local - 1
    return pl.pallas_call(
        functools.partial(expert_kernel, local, rows, tokens),
        out_shape=jax.ShapeDtypeStruct(x.shape, jnp.bfloat16),
        grid=(local, chunks),
        in_specs=[
            pl.BlockSpec(memory_space=pltpu.SMEM),
            pl.BlockSpec((tokens, width), lambda e, c: (c, 0)),
            pl.BlockSpec((1, 2, tokens), lambda e, c: (c, 0, 0)),
            pl.BlockSpec((1, 2, tokens), lambda e, c: (c, 0, 0)),
            pl.BlockSpec((1, hidden, width), lambda e, c: (e, 0, 0)),
            pl.BlockSpec((1, hidden, width), lambda e, c: (e, 0, 0)),
            pl.BlockSpec((1, hidden, width), lambda e, c: (e, 0, 0)),
        ],
        out_specs=pl.BlockSpec((tokens, width), lambda e, c: (jnp.where(e == last, c, 0), 0)),
        scratch_shapes=[pltpu.VMEM((max(last, 1), chunks if last else 1, rows, width), jnp.bfloat16)],
        compiler_params=pltpu.CompilerParams(vmem_limit_bytes=58 * MIB),
        cost_estimate=pl.CostEstimate(
            flops=6 * local * chunks * rows * width * hidden,
            bytes_accessed=6 * local * width * hidden + 6 * chunks * tokens * width,
            transcendentals=local * chunks * rows * hidden,
        ),
    )(first, x, tgt, gates, w_gate, w_up, w_down)


def pack_kernel(firsts, span, q_ref, k_ref, v_ref, out_ref):
    for j, first in enumerate(firsts):
        lanes = slice(first * HEAD_DIM, first * HEAD_DIM + span)
        out_ref[j] = jnp.concatenate([r[:, lanes] for r in (q_ref, k_ref, v_ref)], axis=1)


def pack_heads(query, keys, values, firsts, span):
    rows_dev = query.shape[0]
    n_seq = len(firsts)
    return pl.pallas_call(
        functools.partial(pack_kernel, firsts, span),
        out_shape=jax.ShapeDtypeStruct((n_seq, rows_dev, 3 * span), jnp.bfloat16),
        compiler_params=pltpu.CompilerParams(vmem_limit_bytes=12 * MIB),
        cost_estimate=pl.CostEstimate(flops=0, bytes_accessed=12 * n_seq * rows_dev * span, transcendentals=0),
    )(query, keys, values)


def norm_kernel(share, offsets, context_ref, residual_ref, gain_ref, facts_ref, stream_ref, piece_ref):
    n_seq, _, _ = context_ref.shape
    width = residual_ref.shape[1]
    parts = [context_ref[j][:, offsets[j] : offsets[j] + share] for j in range(n_seq)]
    context = jnp.concatenate(parts, axis=1).astype(jnp.float32)
    stream = residual_ref[...].astype(jnp.float32) + context
    stream_ref[...] = stream
    mean = jnp.mean(stream * stream, axis=1, keepdims=True)
    normed = stream * lax.rsqrt(mean + 1e-05) * gain_ref[...].astype(jnp.float32)
    piece_ref[:, :width] = normed.astype(jnp.bfloat16)
    facts = facts_ref[...]
    lane = lax.broadcasted_iota(jnp.int32, facts.shape, 1)
    high = facts.astype(jnp.bfloat16).astype(jnp.float32)
    middle = (facts - high).astype(jnp.bfloat16).astype(jnp.float32)
    low = facts - high - middle
    own = jnp.where(lane < 4, high, jnp.where(lane < 6, middle, low))
    piece_ref[:, width:] = own.astype(jnp.bfloat16)


def norm_tokens(context, residual, gain, facts, share, offsets):
    rows_dev, width = residual.shape
    return pl.pallas_call(
        functools.partial(norm_kernel, share, offsets),
        out_shape=(
            jax.ShapeDtypeStruct((rows_dev, width), jnp.float32),
            jax.ShapeDtypeStruct((rows_dev, width + facts.shape[1]), jnp.bfloat16),
        ),
        compiler_params=pltpu.CompilerParams(vmem_limit_bytes=12 * MIB),
        cost_estimate=pl.CostEstimate(
            flops=10 * rows_dev * width, bytes_accessed=10 * rows_dev * width, transcendentals=rows_dev
        ),
    )(context, residual, gain[None, :], facts)


def pick_pages_kernel(per_device, first_lane, order_ref, packed_ref, late_ref, out_ref):
    del late_ref
    for j in range(out_ref.shape[0]):
        for i in range(per_device):
            rows = pl.ds(pl.multiple_of(order_ref[j * per_device + i] * PAGE, PAGE), PAGE)
            out_ref[j, i * PAGE : (i + 1) * PAGE, :] = packed_ref[rows, first_lane:]


def pick_pages(packed, order, late, n_seq, span):
    rows = packed.shape[0] // n_seq
    vmem = pl.BlockSpec(memory_space=pltpu.VMEM)
    return pl.pallas_call(
        functools.partial(pick_pages_kernel, rows // PAGE, span),
        out_shape=jax.ShapeDtypeStruct((n_seq, rows, 2 * span), jnp.bfloat16),
        in_specs=[pl.BlockSpec(memory_space=pltpu.SMEM), vmem, pl.BlockSpec(memory_space=pl.ANY)],
        compiler_params=pltpu.CompilerParams(vmem_limit_bytes=8 * MIB),
        cost_estimate=pl.CostEstimate(flops=0, bytes_accessed=10 * packed.shape[0] * span, transcendentals=0),
    )(order, packed, late)


def join_pages_kernel(share, offsets, span, pages_ref, behind_ref, out_ref, ended_ref):
    del behind_ref
    ended_ref[...] = jnp.zeros_like(ended_ref)
    width = share * len(offsets)
    for part in range(2):
        parts = [
            pages_ref[j][:, part * span + offsets[j] : part * span + offsets[j] + share]
            for j in range(len(offsets))
        ]
        out_ref[:, part * width : (part + 1) * width] = jnp.concatenate(parts, axis=1)


def join_pages(pages, share, offsets, span, behind):
    n_seq, rows, _ = pages.shape
    return pl.pallas_call(
        functools.partial(join_pages_kernel, share, offsets, span),
        out_shape=(
            jax.ShapeDtypeStruct((rows, 2 * share * n_seq), jnp.bfloat16),
            jax.ShapeDtypeStruct((8, 128), jnp.float32),
        ),
        in_specs=[pl.BlockSpec(memory_space=pltpu.VMEM), pl.BlockSpec(memory_space=pl.ANY)],
        compiler_params=pltpu.CompilerParams(vmem_limit_bytes=12 * MIB),
        cost_estimate=pl.CostEstimate(flops=0, bytes_accessed=8 * rows * n_seq * span, transcendentals=0),
    )(pages, behind)


def places_of(slots, base, shift):
    place = -1
    for slot in slots:
        slot = slot.astype(jnp.int32) - base
        place = jnp.where((slot >= 0) & (slot < CAP), shift + slot, place)
    return place


def hold_kernel(*refs):
    del refs


def hold(a, waits):
    anywhere = pl.BlockSpec(memory_space=pl.ANY)
    return pl.pallas_call(
        hold_kernel,
        out_shape=jax.ShapeDtypeStruct(a.shape, a.dtype),
        in_specs=[anywhere] * (1 + len(waits)),
        out_specs=anywhere,
        input_output_aliases={0: 0},
        compiler_params=pltpu.CompilerParams(vmem_limit_bytes=MIB),
        cost_estimate=pl.CostEstimate(flops=0, bytes_accessed=0, transcendentals=0),
    )(a, *waits)


def facts_by_lane(x):
    unit = lax.broadcasted_iota(jnp.int32, (8, 128), 0) == lax.broadcasted_iota(jnp.int32, (8, 128), 1)
    return dot_t(unit.astype(jnp.float32).astype(jnp.bfloat16), x)


def select_kernel(local, rows_dev, count, bases_ref, *refs):
    piece_refs, (own_ref, sib_ref, facts_ref) = refs[:count], refs[-3:]
    width = own_ref.shape[2]
    tokens, rows = 4 * rows_dev, 4 * CAP
    shift = lax.broadcasted_iota(jnp.int32, (1, tokens), 1) // rows_dev * CAP
    row_id = lax.broadcasted_iota(jnp.int32, (rows, tokens), 0)
    for g in range(len(piece_refs) // 4):
        x = jnp.concatenate([p[...] for p in piece_refs[4 * g : 4 * g + 4]], axis=0)
        facts_ref[g * tokens : (g + 1) * tokens, :] = x[:, width:]
        facts = facts_by_lane(x[:, width:])
        picks = []
        for core in range(2):
            for e in range(local):
                base = (bases_ref[core] + e) * CAP
                hit = row_id == places_of([facts[j : j + 1] for j in range(2)], base, shift)
                picks.append(hit.astype(jnp.float32))
        picks = jnp.concatenate(picks, axis=0).astype(jnp.bfloat16)
        chosen = jnp.dot(picks, x[:, :width], preferred_element_type=jnp.float32).astype(jnp.bfloat16)
        for e in range(local):
            own_ref[e, g * rows : (g + 1) * rows, :] = chosen[e * rows : (e + 1) * rows]
            sib_ref[e, g * rows : (g + 1) * rows, :] = chosen[(local + e) * rows : (local + e + 1) * rows]


def select_rows(pieces, bases, local, waits=()):
    rows_dev, wide = pieces[0].shape
    width = wide - 128
    rows = len(pieces) * CAP
    out = jax.ShapeDtypeStruct((local, rows, width), jnp.bfloat16)
    vmem = pl.BlockSpec(memory_space=pltpu.VMEM)
    return pl.pallas_call(
        functools.partial(select_kernel, local, rows_dev, len(pieces)),
        out_shape=(out, out, jax.ShapeDtypeStruct((len(pieces) * rows_dev, 128), jnp.bfloat16)),
        in_specs=[pl.BlockSpec(memory_space=pltpu.SMEM)]
        + [vmem] * len(pieces)
        + [pl.BlockSpec(memory_space=pl.ANY)] * len(waits),
        out_specs=(vmem, vmem, vmem),
        compiler_params=pltpu.CompilerParams(vmem_limit_bytes=20 * MIB),
        cost_estimate=pl.CostEstimate(
            flops=16 * local * CAP * rows_dev * len(pieces) * width,
            bytes_accessed=2 * len(pieces) * rows_dev * wide + 4 * local * rows * width,
            transcendentals=0,
        ),
    )(bases, *pieces, *waits)


def rows_kernel(local, waits, own_ref, got_ref, wg_hbm, wu_hbm, wd_hbm, *rest):
    y_own_ref, y_sib_ref, ended_ref, wg, wu, wd, weight_sem = rest[waits:]
    ended_ref[...] = jnp.zeros_like(ended_ref)
    half = got_ref.shape[1]
    copies = [
        [
            pltpu.make_async_copy(source.at[e], target.at[e], weight_sem.at[3 * e + i])
            for i, (source, target) in enumerate(((wg_hbm, wg), (wu_hbm, wu), (wd_hbm, wd)))
        ]
        for e in range(local)
    ]
    for group in copies:
        for copy in group:
            copy.start()
    for e in range(local):
        rows = jnp.concatenate([own_ref[e], got_ref[e]], axis=0)
        copies[e][0].wait()
        gate = dot_t(rows, wg[e])
        copies[e][1].wait()
        upper = dot_t(rows, wu[e])
        hidden = (gate / (1.0 + jnp.exp(-gate)) * upper).astype(jnp.bfloat16)
        copies[e][2].wait()
        y = jnp.dot(hidden, wd[e], preferred_element_type=jnp.float32).astype(jnp.bfloat16)
        y_own_ref[e] = y[:half]
        y_sib_ref[e] = y[half:]


def expert_rows(own, got, w_gate, w_up, w_down, waits):
    local, hidden, width = w_gate.shape
    rows = 2 * own.shape[1]
    out = jax.ShapeDtypeStruct(own.shape, jnp.bfloat16)
    vmem = pl.BlockSpec(memory_space=pltpu.VMEM)
    weights = pltpu.VMEM((local, hidden, width), jnp.bfloat16)
    return pl.pallas_call(
        functools.partial(rows_kernel, local, len(waits)),
        out_shape=(out, out, jax.ShapeDtypeStruct((8, 128), jnp.float32)),
        in_specs=[vmem, vmem]
        + [pl.BlockSpec(memory_space=pl.ANY)] * (3 + len(waits)),
        out_specs=(vmem, vmem, vmem),
        scratch_shapes=[
            weights,
            weights,
            weights,
            pltpu.SemaphoreType.DMA((3 * local,)),
        ],
        compiler_params=pltpu.CompilerParams(vmem_limit_bytes=44 * MIB),
        cost_estimate=pl.CostEstimate(
            flops=6 * local * rows * width * hidden,
            bytes_accessed=6 * local * width * hidden + 4 * local * rows * width,
            transcendentals=local * rows * hidden,
        ),
    )(own, got, w_gate, w_up, w_down, *waits)


def put_kernel(local, rows_dev, planes, waits, bases_ref, y_own_ref, y_got_ref, facts_ref, *rest):
    kept_ref, *send_refs, ended_ref = rest[waits:]
    ended_ref[...] = jnp.zeros_like(ended_ref)
    tokens, rows = 4 * rows_dev, 4 * CAP
    total = 2 * local * rows
    shift_lane = lax.broadcasted_iota(jnp.int32, (1, tokens), 1) // rows_dev * CAP
    shift_row = lax.broadcasted_iota(jnp.int32, (tokens, 1), 0) // rows_dev * CAP
    row_id = lax.broadcasted_iota(jnp.int32, (rows, tokens), 0)
    lane = lax.broadcasted_iota(jnp.int32, (tokens, total), 1)
    for g in range(planes):
        facts = facts_ref[g * tokens : (g + 1) * tokens, :]
        by_lane = facts_by_lane(facts)
        by_row = facts.astype(jnp.float32)
        here = slice(g * rows, (g + 1) * rows)
        weighed, put = [], None
        for core, y_ref in enumerate((y_own_ref, y_got_ref)):
            for e in range(local):
                base = (bases_ref[core] + e) * CAP
                weight = jnp.zeros((rows, tokens), jnp.float32)
                for j in range(2):
                    hit = row_id == places_of([by_lane[j : j + 1]], base, shift_lane)
                    gate = by_lane[2 + j : 3 + j] + by_lane[4 + j : 5 + j] + by_lane[6 + j : 7 + j]
                    weight = weight + jnp.where(hit, gate, 0.0)
                weight = jnp.sum(weight, axis=1, keepdims=True)
                weighed.append((y_ref[e, here, :].astype(jnp.float32) * weight).astype(jnp.bfloat16))
                first = (core * local + e) * rows
                hit = lane == places_of([by_row[:, j : j + 1] for j in range(2)], base, shift_row + first)
                put = hit if put is None else put | hit
        put = put.astype(jnp.float32).astype(jnp.bfloat16)
        out = jnp.dot(put, jnp.concatenate(weighed, axis=0), preferred_element_type=jnp.float32)
        out = out.astype(jnp.bfloat16)
        kept_ref[g * tokens // 2 : (g + 1) * tokens // 2, :] = out[: tokens // 2]
        send_refs[g][...] = out[tokens // 2 :]


def put_rows(y_own, y_got, facts, bases, rows_dev, waits):
    local, _, width = y_own.shape
    tokens = facts.shape[0]
    planes = tokens // (4 * rows_dev)
    vmem = pl.BlockSpec(memory_space=pltpu.VMEM)
    shape = lambda n: jax.ShapeDtypeStruct((n, width), jnp.bfloat16)
    out = pl.pallas_call(
        functools.partial(put_kernel, local, rows_dev, planes, len(waits)),
        out_shape=(shape(2 * planes * rows_dev),)
        + (shape(2 * rows_dev),) * planes
        + (jax.ShapeDtypeStruct((8, 128), jnp.float32),),
        in_specs=[pl.BlockSpec(memory_space=pltpu.SMEM), vmem, vmem, vmem]
        + [pl.BlockSpec(memory_space=pl.ANY)] * len(waits),
        out_specs=(vmem,) * (2 + planes),
        compiler_params=pltpu.CompilerParams(vmem_limit_bytes=20 * MIB),
        cost_estimate=pl.CostEstimate(
            flops=16 * local * CAP * tokens * width,
            bytes_accessed=8 * local * tokens * width,
            transcendentals=0,
        ),
    )(bases, y_own, y_got, facts, *waits)
    return out[0], out[1:-1], out[-1]


def swap(a, axis, size, distance):
    return lax.ppermute(a, axis, [(i, i ^ distance) for i in range(size)])


def fold_kernel(groups, count, waits, keep_ref, *rest):
    got_refs, (kept_ref, *send_refs) = rest[:count], rest[count + waits :]
    part = keep_ref.shape[0] // (2 * groups)
    span = got_refs[0].shape[0]
    for i in range(2 * groups):
        start = i * part
        got = got_refs[start // span][start % span : start % span + part, :]
        total = keep_ref[start : start + part, :].astype(jnp.float32) + got.astype(jnp.float32)
        total = total.astype(jnp.bfloat16)
        if i % 2 == 0:
            kept_ref[i // 2 * part : (i // 2 + 1) * part, :] = total
        else:
            send_refs[i // 2][...] = total


def fold(keep, gots, groups, waits=()):
    rows, width = keep.shape
    part = rows // (2 * groups)
    vmem = pl.BlockSpec(memory_space=pltpu.VMEM)
    shape = lambda n: jax.ShapeDtypeStruct((n, width), jnp.bfloat16)
    out = pl.pallas_call(
        functools.partial(fold_kernel, groups, len(gots), len(waits)),
        out_shape=(shape(groups * part),) + (shape(part),) * groups,
        in_specs=[vmem] * (1 + len(gots)) + [pl.BlockSpec(memory_space=pl.ANY)] * len(waits),
        out_specs=(vmem,) * (1 + groups),
        compiler_params=pltpu.CompilerParams(vmem_limit_bytes=10 * MIB),
        cost_estimate=pl.CostEstimate(flops=rows * width, bytes_accessed=6 * rows * width, transcendentals=0),
    )(keep, *gots, *waits)
    return out[0], out[1:]


def exchange_experts(piece, w_gate, w_up, w_down, n_seq, n_exp, late_work):
    x = lambda a: swap(a, "seq", n_seq, 1)
    y = lambda a: swap(a, "exp", n_exp, 2)
    core = lambda a: swap(a, "exp", n_exp, 1)
    z = lambda a, k: swap(a, "seq", n_seq, 2 * k)
    local = w_gate.shape[0]
    me = lax.axis_index("exp").astype(jnp.int32)
    bases = jnp.stack([me, me ^ 1]) * local
    starts = [piece, z(piece, 1), z(piece, 2)]
    ways = [("xy", "yx")[k % 2] for k in range(4)]
    over = {"x": x, "y": y}
    single = [[over[way](starts[k]) for way in ways[k]] for k in range(2)]
    starts[2] = hold(starts[2], single[0] + single[1])
    single.append([over[way](starts[2]) for way in ways[2]])

    def both(k):
        return over[ways[k][1]](single[k][0])

    double = [both(0), both(1)]
    starts.append(hold(z(starts[2], 1), double))
    single.append([over[way](starts[3]) for way in ways[3]])
    double += [both(2), both(3)]

    def gather(k):
        near = []
        for i in (k, k + 1):
            by_f, by_g = single[i]
            near += [starts[i], by_g, by_f, double[i]]
        return near

    near_b, near_a = gather(0), gather(2)
    own_a, sib_a, facts_a = select_rows(near_a, bases, local)
    got_a = core(sib_a)
    pages, fill = late_work(facts_a)
    own_b, sib_b, facts_b = select_rows(near_b, bases, local, [pages])
    got_b = core(sib_b)
    own_a, sib_a, ended = expert_rows(own_a, got_a, w_gate, w_up, w_down, [facts_b, pages])
    cache, filled = fill(ended)
    got_a = core(sib_a)
    own_b, sib_b, ended = expert_rows(own_b, got_b, w_gate, w_up, w_down, [filled])
    got_b = core(sib_b)
    keep_a, (fx_a, fy_a), _ = put_rows(own_a, got_a, facts_a, bases, piece.shape[0], [ended])
    keep_a, (gy_a, gx_a) = fold(keep_a, [x(fx_a), y(fy_a)], 2)
    keep_b, (fx_b, fy_b), put_b = put_rows(own_b, got_b, facts_b, bases, piece.shape[0], [gy_a])
    gy_a, gx_a = y(gy_a), x(gx_a)
    fx_b, fy_b = hold(fx_b, [gy_a, gx_a]), hold(fy_b, [gy_a, gx_a])
    keep_a, (z_a,) = fold(keep_a, [gy_a, gx_a], 1, [put_b])
    over_z = (keep_a.astype(jnp.float32) + z(z_a, 1).astype(jnp.float32)).astype(jnp.bfloat16)
    keep_b, (gy_b, gx_b) = fold(keep_b, [x(fx_b), y(fy_b)], 2, [over_z])
    back_a = z(over_z, 2)
    keep_b, (z_b,) = fold(keep_b, [y(gy_b), x(gx_b)], 1, [back_a])
    mine = keep_b.astype(jnp.float32) + z(z_b, 1).astype(jnp.float32)
    return mine + back_a.astype(jnp.float32), cache


def body(
    n_seq,
    n_exp,
    query,
    key_value,
    residual,
    norm_gain,
    segment_ids,
    routes,
    gate_weights,
    page_table,
    w_gate,
    w_up,
    w_down,
):
    rows_dev, width = query.shape[1:]
    everyone = ("exp", "seq")
    group = segment_ids.shape[1]
    share, firsts, heads = head_ranges(width, n_seq)
    span = heads * HEAD_DIM

    flat = routes[0].reshape(rows_dev * 2)
    onehot = (flat[:, None] == jnp.arange(EXPERTS, dtype=jnp.int32)[None, :]).astype(jnp.int32)
    before = jnp.cumsum(onehot, axis=0) - onehot
    target = (flat * CAP + jnp.sum(before * onehot, axis=1)).reshape(rows_dev, 2).astype(jnp.float32)

    keys, values = key_value[0, :, 0], key_value[0, :, 1]

    packed = pack_heads(query[0], keys, values, firsts, span)
    packed = lax.all_to_all(packed, "seq", split_axis=0, concat_axis=0, tiled=True)
    packed = packed.reshape(group, 3 * span)
    context = attention(packed, segment_ids[0], heads)
    context = lax.all_to_all(
        context.reshape(n_seq, rows_dev, span), "seq", split_axis=0, concat_axis=0, tiled=True
    )
    offsets = [j * share - firsts[j] * HEAD_DIM for j in range(n_seq)]

    first = (lax.axis_index("exp") * (EXPERTS // n_exp)).astype(jnp.int32).reshape(1)
    w_gate, w_up = jnp.swapaxes(w_gate, 1, 2), jnp.swapaxes(w_up, 1, 2)
    gates = gate_weights[0]
    facts = jnp.concatenate([target, gates, gates, gates], axis=1)
    facts = jnp.pad(facts, ((0, 0), (0, 128 - facts.shape[1])))
    stream, piece = norm_tokens(context, residual[0], norm_gain, facts, share, offsets)

    slots = jnp.arange(group // PAGE, dtype=jnp.int32)
    order = jnp.sum(jnp.where(page_table[0][None, :] == slots[:, None], slots[None, :], 0), axis=1)

    def fill_cache(late):
        pages = pick_pages(packed, order, late, n_seq, span)
        sent = lax.all_to_all(pages, "seq", split_axis=0, concat_axis=0, tiled=True)
        return pages, lambda behind: join_pages(sent, share, offsets, span, behind)

    if (n_seq, n_exp) == (8, 4):
        mixture, cache = exchange_experts(piece, w_gate, w_up, w_down, n_seq, n_exp, fill_cache)
    else:
        cache, _ = fill_cache(piece)[1](piece)
        blocks = n_seq * n_exp
        everything = lax.all_gather(piece, everyone, axis=0, tiled=True)
        facts = everything[:, width : width + 8].astype(jnp.float32)
        facts = facts.reshape(blocks // CHUNK_BLOCKS, CHUNK_BLOCKS * rows_dev, 8).transpose(0, 2, 1)
        gates = facts[:, 2:4] + facts[:, 4:6] + facts[:, 6:8]
        partial = experts(
            everything[:, :width], facts[:, :2].astype(jnp.int32), gates, w_gate, w_up, w_down, first
        )
        mixture = lax.psum_scatter(partial, everyone, scatter_dimension=0, tiled=True).astype(jnp.float32)
    layer_out = (stream + mixture).astype(jnp.bfloat16)
    return (layer_out[None], cache.reshape(1, rows_dev // PAGE, PAGE, 2 * width))


def solution(mesh):
    in_specs = (
        P("exp", "seq", None),
        P("exp", "seq", None, None),
        P("exp", "seq", None),
        P(),
        P("exp", None),
        P("exp", "seq", None),
        P("exp", "seq", None),
        P("exp", None),
        P("exp", None, "seq"),
        P("exp", None, "seq"),
        P("exp", "seq", None),
    )
    out_specs = (P("exp", "seq", None), P("exp", "seq", None, None))
    run = functools.partial(body, mesh.shape["seq"], mesh.shape["exp"])
    return jax.shard_map(run, mesh=mesh, in_specs=in_specs, out_specs=out_specs, check_vma=False)
```

```python
import functools
import math

import jax
import jax.numpy as jnp
from jax import lax
from jax.experimental import pallas as pl
from jax.experimental.pallas import tpu as pltpu
from jax.sharding import PartitionSpec as P

HEADS = 36
HEAD_DIM = 64
EXPERTS = 8
PAGE = 16
CAP = 24
MIB = 1024 * 1024
CHUNK_BLOCKS = 8


def head_ranges(width, n_seq):
    share = width // n_seq
    firsts = [j * share // HEAD_DIM for j in range(n_seq)]
    count = max(-(-(j + 1) * share // HEAD_DIM) - firsts[j] for j in range(n_seq))
    firsts = [min(f, HEADS - count) for f in firsts]
    return share, firsts, count


def attention_kernel(heads, q_rows, packed_ref, seg_row_ref, seg_col_ref, out_ref):
    total = packed_ref.shape[0]
    span = heads * HEAD_DIM
    scale = 1.0 / math.sqrt(HEAD_DIM)
    for start in range(0, total, q_rows):
        end = start + q_rows
        q_place = start + lax.broadcasted_iota(jnp.int32, (q_rows, end), 0)
        k_place = lax.broadcasted_iota(jnp.int32, (q_rows, end), 1)
        visible = (seg_col_ref[start:end, :] == seg_row_ref[:, :end]) & (k_place <= q_place)
        parts = []
        for h in range(heads):
            a = h * HEAD_DIM
            q = packed_ref[start:end, a : a + HEAD_DIM]
            k = packed_ref[:end, span + a : span + a + HEAD_DIM]
            v = packed_ref[:end, 2 * span + a : 2 * span + a + HEAD_DIM]
            s = lax.dot_general(q, k, (((1,), (1,)), ((), ())), preferred_element_type=jnp.float32)
            s = jnp.where(visible, s * scale, -1e30)
            top = jnp.max(s, axis=1, keepdims=True)
            p = jnp.exp(s - top)
            denominator = jnp.sum(p, axis=1, keepdims=True)
            o = jnp.dot(p.astype(jnp.bfloat16), v, preferred_element_type=jnp.float32)
            parts.append((o / denominator).astype(jnp.bfloat16))
        out_ref[start:end, :] = jnp.concatenate(parts, axis=1)


def attention(packed, segments, heads):
    total = packed.shape[0]
    span = heads * HEAD_DIM
    return pl.pallas_call(
        functools.partial(attention_kernel, heads, 128),
        out_shape=jax.ShapeDtypeStruct((total, span), jnp.bfloat16),
        compiler_params=pltpu.CompilerParams(vmem_limit_bytes=24 * MIB),
        cost_estimate=pl.CostEstimate(
            flops=4 * total * total * span, bytes_accessed=8 * total * span, transcendentals=total * total * heads
        ),
    )(packed, segments[None, :], segments[:, None])


def dot_t(a, b):
    return lax.dot_general(a, b, (((1,), (1,)), ((), ())), preferred_element_type=jnp.float32)


def expert_kernel(
    local, rows, tokens, first_ref, x_ref, tgt_ref, gates_ref, wg_ref, wu_ref, wd_ref, out_ref, kept_ref
):
    le = pl.program_id(0)
    chunk = pl.program_id(1)

    def selection(which):
        base = (first_ref[0] + which) * CAP
        row_id = lax.broadcasted_iota(jnp.int32, (rows, tokens), 0)
        block = lax.broadcasted_iota(jnp.int32, (1, tokens), 1) // 64
        picks, weights = None, None
        for j in range(2):
            slot = tgt_ref[0, j : j + 1, :] - base
            place = jnp.where((slot >= 0) & (slot < CAP), block * CAP + slot, -1)
            hit = row_id == place
            gate = jnp.where(hit, gates_ref[0, j : j + 1, :], 0.0)
            picks = hit if picks is None else picks | hit
            weights = gate if weights is None else weights + gate
        return picks.astype(jnp.float32).astype(jnp.bfloat16), jnp.sum(weights, axis=1, keepdims=True)

    pick, weight = selection(le)
    chosen = jnp.dot(pick, x_ref[...], preferred_element_type=jnp.float32).astype(jnp.bfloat16)
    gate = dot_t(chosen, wg_ref[0])
    upper = dot_t(chosen, wu_ref[0])
    hidden = (gate / (1.0 + jnp.exp(-gate)) * upper).astype(jnp.bfloat16)
    y = jnp.dot(hidden, wd_ref[0], preferred_element_type=jnp.float32)
    y = (y * weight).astype(jnp.bfloat16)

    if local > 1:

        @pl.when(le < local - 1)
        def _():
            kept_ref[le, chunk] = y

    @pl.when(le == local - 1)
    def _():
        total = lax.dot_general(pick, y, (((0,), (0,)), ((), ())), preferred_element_type=jnp.float32)
        for other in range(local - 1):
            pick_o, _ = selection(other)
            total += lax.dot_general(
                pick_o, kept_ref[other, chunk], (((0,), (0,)), ((), ())), preferred_element_type=jnp.float32
            )
        out_ref[...] = total.astype(jnp.bfloat16)


def experts(x, tgt, gates, w_gate, w_up, w_down, first):
    local, hidden, width = w_gate.shape
    chunks, _, tokens = tgt.shape
    rows = tokens // 64 * CAP
    last = local - 1
    return pl.pallas_call(
        functools.partial(expert_kernel, local, rows, tokens),
        out_shape=jax.ShapeDtypeStruct(x.shape, jnp.bfloat16),
        grid=(local, chunks),
        in_specs=[
            pl.BlockSpec(memory_space=pltpu.SMEM),
            pl.BlockSpec((tokens, width), lambda e, c: (c, 0)),
            pl.BlockSpec((1, 2, tokens), lambda e, c: (c, 0, 0)),
            pl.BlockSpec((1, 2, tokens), lambda e, c: (c, 0, 0)),
            pl.BlockSpec((1, hidden, width), lambda e, c: (e, 0, 0)),
            pl.BlockSpec((1, hidden, width), lambda e, c: (e, 0, 0)),
            pl.BlockSpec((1, hidden, width), lambda e, c: (e, 0, 0)),
        ],
        out_specs=pl.BlockSpec((tokens, width), lambda e, c: (jnp.where(e == last, c, 0), 0)),
        scratch_shapes=[pltpu.VMEM((max(last, 1), chunks if last else 1, rows, width), jnp.bfloat16)],
        compiler_params=pltpu.CompilerParams(vmem_limit_bytes=58 * MIB),
        cost_estimate=pl.CostEstimate(
            flops=6 * local * chunks * rows * width * hidden,
            bytes_accessed=6 * local * width * hidden + 6 * chunks * tokens * width,
            transcendentals=local * chunks * rows * hidden,
        ),
    )(first, x, tgt, gates, w_gate, w_up, w_down)


def pack_kernel(firsts, span, q_ref, k_ref, v_ref, out_ref):
    for j, first in enumerate(firsts):
        lanes = slice(first * HEAD_DIM, first * HEAD_DIM + span)
        out_ref[j] = jnp.concatenate([r[:, lanes] for r in (q_ref, k_ref, v_ref)], axis=1)


def pack_heads(query, keys, values, firsts, span):
    rows_dev = query.shape[0]
    n_seq = len(firsts)
    return pl.pallas_call(
        functools.partial(pack_kernel, firsts, span),
        out_shape=jax.ShapeDtypeStruct((n_seq, rows_dev, 3 * span), jnp.bfloat16),
        compiler_params=pltpu.CompilerParams(vmem_limit_bytes=12 * MIB),
        cost_estimate=pl.CostEstimate(flops=0, bytes_accessed=12 * n_seq * rows_dev * span, transcendentals=0),
    )(query, keys, values)


def norm_kernel(share, offsets, context_ref, residual_ref, gain_ref, facts_ref, stream_ref, piece_ref):
    n_seq, _, _ = context_ref.shape
    width = residual_ref.shape[1]
    parts = [context_ref[j][:, offsets[j] : offsets[j] + share] for j in range(n_seq)]
    context = jnp.concatenate(parts, axis=1).astype(jnp.float32)
    stream = residual_ref[...].astype(jnp.float32) + context
    stream_ref[...] = stream
    mean = jnp.mean(stream * stream, axis=1, keepdims=True)
    normed = stream * lax.rsqrt(mean + 1e-05) * gain_ref[...].astype(jnp.float32)
    piece_ref[:, :width] = normed.astype(jnp.bfloat16)
    facts = facts_ref[...]
    lane = lax.broadcasted_iota(jnp.int32, facts.shape, 1)
    high = facts.astype(jnp.bfloat16).astype(jnp.float32)
    middle = (facts - high).astype(jnp.bfloat16).astype(jnp.float32)
    low = facts - high - middle
    own = jnp.where(lane < 4, high, jnp.where(lane < 6, middle, low))
    piece_ref[:, width:] = own.astype(jnp.bfloat16)


def norm_tokens(context, residual, gain, facts, share, offsets):
    rows_dev, width = residual.shape
    return pl.pallas_call(
        functools.partial(norm_kernel, share, offsets),
        out_shape=(
            jax.ShapeDtypeStruct((rows_dev, width), jnp.float32),
            jax.ShapeDtypeStruct((rows_dev, width + facts.shape[1]), jnp.bfloat16),
        ),
        compiler_params=pltpu.CompilerParams(vmem_limit_bytes=12 * MIB),
        cost_estimate=pl.CostEstimate(
            flops=10 * rows_dev * width, bytes_accessed=10 * rows_dev * width, transcendentals=rows_dev
        ),
    )(context, residual, gain[None, :], facts)


def pick_pages_kernel(per_device, first_lane, order_ref, packed_ref, late_ref, out_ref):
    del late_ref
    for j in range(out_ref.shape[0]):
        for i in range(per_device):
            rows = pl.ds(pl.multiple_of(order_ref[j * per_device + i] * PAGE, PAGE), PAGE)
            out_ref[j, i * PAGE : (i + 1) * PAGE, :] = packed_ref[rows, first_lane:]


def pick_pages(packed, order, late, n_seq, span):
    rows = packed.shape[0] // n_seq
    vmem = pl.BlockSpec(memory_space=pltpu.VMEM)
    return pl.pallas_call(
        functools.partial(pick_pages_kernel, rows // PAGE, span),
        out_shape=jax.ShapeDtypeStruct((n_seq, rows, 2 * span), jnp.bfloat16),
        in_specs=[pl.BlockSpec(memory_space=pltpu.SMEM), vmem, pl.BlockSpec(memory_space=pl.ANY)],
        compiler_params=pltpu.CompilerParams(vmem_limit_bytes=8 * MIB),
        cost_estimate=pl.CostEstimate(flops=0, bytes_accessed=10 * packed.shape[0] * span, transcendentals=0),
    )(order, packed, late)


def join_pages_kernel(share, offsets, span, pages_ref, behind_ref, out_ref, ended_ref):
    del behind_ref
    ended_ref[...] = jnp.zeros_like(ended_ref)
    width = share * len(offsets)
    for part in range(2):
        parts = [
            pages_ref[j][:, part * span + offsets[j] : part * span + offsets[j] + share]
            for j in range(len(offsets))
        ]
        out_ref[:, part * width : (part + 1) * width] = jnp.concatenate(parts, axis=1)


def join_pages(pages, share, offsets, span, behind):
    n_seq, rows, _ = pages.shape
    return pl.pallas_call(
        functools.partial(join_pages_kernel, share, offsets, span),
        out_shape=(
            jax.ShapeDtypeStruct((rows, 2 * share * n_seq), jnp.bfloat16),
            jax.ShapeDtypeStruct((8, 128), jnp.float32),
        ),
        in_specs=[pl.BlockSpec(memory_space=pltpu.VMEM), pl.BlockSpec(memory_space=pl.ANY)],
        compiler_params=pltpu.CompilerParams(vmem_limit_bytes=12 * MIB),
        cost_estimate=pl.CostEstimate(flops=0, bytes_accessed=8 * rows * n_seq * span, transcendentals=0),
    )(pages, behind)


def places_of(slots, base, shift):
    place = -1
    for slot in slots:
        slot = slot.astype(jnp.int32) - base
        place = jnp.where((slot >= 0) & (slot < CAP), shift + slot, place)
    return place


def hold_kernel(*refs):
    del refs


def hold(a, waits):
    anywhere = pl.BlockSpec(memory_space=pl.ANY)
    return pl.pallas_call(
        hold_kernel,
        out_shape=jax.ShapeDtypeStruct(a.shape, a.dtype),
        in_specs=[anywhere] * (1 + len(waits)),
        out_specs=anywhere,
        input_output_aliases={0: 0},
        compiler_params=pltpu.CompilerParams(vmem_limit_bytes=MIB),
        cost_estimate=pl.CostEstimate(flops=0, bytes_accessed=0, transcendentals=0),
    )(a, *waits)


def facts_by_lane(x):
    unit = lax.broadcasted_iota(jnp.int32, (8, 128), 0) == lax.broadcasted_iota(jnp.int32, (8, 128), 1)
    return dot_t(unit.astype(jnp.float32).astype(jnp.bfloat16), x)


def select_kernel(local, rows_dev, count, bases_ref, *refs):
    piece_refs, (own_ref, sib_ref, facts_ref) = refs[:count], refs[-3:]
    width = own_ref.shape[2]
    tokens, rows = 4 * rows_dev, 4 * CAP
    shift = lax.broadcasted_iota(jnp.int32, (1, tokens), 1) // rows_dev * CAP
    row_id = lax.broadcasted_iota(jnp.int32, (rows, tokens), 0)
    for g in range(len(piece_refs) // 4):
        x = jnp.concatenate([p[...] for p in piece_refs[4 * g : 4 * g + 4]], axis=0)
        facts_ref[g * tokens : (g + 1) * tokens, :] = x[:, width:]
        facts = facts_by_lane(x[:, width:])
        picks = []
        for core in range(2):
            for e in range(local):
                base = (bases_ref[core] + e) * CAP
                hit = row_id == places_of([facts[j : j + 1] for j in range(2)], base, shift)
                picks.append(hit.astype(jnp.float32))
        picks = jnp.concatenate(picks, axis=0).astype(jnp.bfloat16)
        chosen = jnp.dot(picks, x[:, :width], preferred_element_type=jnp.float32).astype(jnp.bfloat16)
        for e in range(local):
            own_ref[e, g * rows : (g + 1) * rows, :] = chosen[e * rows : (e + 1) * rows]
            sib_ref[e, g * rows : (g + 1) * rows, :] = chosen[(local + e) * rows : (local + e + 1) * rows]


def select_rows(pieces, bases, local, waits=()):
    rows_dev, wide = pieces[0].shape
    width = wide - 128
    rows = len(pieces) * CAP
    out = jax.ShapeDtypeStruct((local, rows, width), jnp.bfloat16)
    vmem = pl.BlockSpec(memory_space=pltpu.VMEM)
    return pl.pallas_call(
        functools.partial(select_kernel, local, rows_dev, len(pieces)),
        out_shape=(out, out, jax.ShapeDtypeStruct((len(pieces) * rows_dev, 128), jnp.bfloat16)),
        in_specs=[pl.BlockSpec(memory_space=pltpu.SMEM)]
        + [vmem] * len(pieces)
        + [pl.BlockSpec(memory_space=pl.ANY)] * len(waits),
        out_specs=(vmem, vmem, vmem),
        compiler_params=pltpu.CompilerParams(vmem_limit_bytes=20 * MIB),
        cost_estimate=pl.CostEstimate(
            flops=16 * local * CAP * rows_dev * len(pieces) * width,
            bytes_accessed=2 * len(pieces) * rows_dev * wide + 4 * local * rows * width,
            transcendentals=0,
        ),
    )(bases, *pieces, *waits)


def rows_kernel(local, waits, own_ref, got_ref, wg_hbm, wu_hbm, wd_hbm, *rest):
    y_own_ref, y_sib_ref, ended_ref, wg, wu, wd, weight_sem = rest[waits:]
    ended_ref[...] = jnp.zeros_like(ended_ref)
    half = got_ref.shape[1]
    copies = [
        pltpu.make_async_copy(source.at[e], target.at[e], weight_sem.at[3 * e + i])
        for e in range(local)
        for i, (source, target) in enumerate(((wg_hbm, wg), (wu_hbm, wu), (wd_hbm, wd)))
    ]
    for copy in copies[:2]:
        copy.start()

    def arrived(number):
        copies[number].wait()
        if number + 2 < len(copies):
            copies[number + 2].start()

    for e in range(local):
        rows = jnp.concatenate([own_ref[e], got_ref[e]], axis=0)
        arrived(3 * e)
        gate = dot_t(rows, wg[e])
        arrived(3 * e + 1)
        upper = dot_t(rows, wu[e])
        hidden = (gate / (1.0 + jnp.exp(-gate)) * upper).astype(jnp.bfloat16)
        arrived(3 * e + 2)
        y = jnp.dot(hidden, wd[e], preferred_element_type=jnp.float32).astype(jnp.bfloat16)
        y_own_ref[e] = y[:half]
        y_sib_ref[e] = y[half:]


def expert_rows(own, got, w_gate, w_up, w_down, waits):
    local, hidden, width = w_gate.shape
    rows = 2 * own.shape[1]
    out = jax.ShapeDtypeStruct(own.shape, jnp.bfloat16)
    vmem = pl.BlockSpec(memory_space=pltpu.VMEM)
    weights = pltpu.VMEM((local, hidden, width), jnp.bfloat16)
    return pl.pallas_call(
        functools.partial(rows_kernel, local, len(waits)),
        out_shape=(out, out, jax.ShapeDtypeStruct((8, 128), jnp.float32)),
        in_specs=[vmem, vmem]
        + [pl.BlockSpec(memory_space=pl.ANY)] * (3 + len(waits)),
        out_specs=(vmem, vmem, vmem),
        scratch_shapes=[
            weights,
            weights,
            weights,
            pltpu.SemaphoreType.DMA((3 * local,)),
        ],
        compiler_params=pltpu.CompilerParams(vmem_limit_bytes=44 * MIB),
        cost_estimate=pl.CostEstimate(
            flops=6 * local * rows * width * hidden,
            bytes_accessed=6 * local * width * hidden + 4 * local * rows * width,
            transcendentals=local * rows * hidden,
        ),
    )(own, got, w_gate, w_up, w_down, *waits)


def put_kernel(local, rows_dev, planes, waits, bases_ref, y_own_ref, y_got_ref, facts_ref, *rest):
    kept_ref, *send_refs, ended_ref = rest[waits:]
    ended_ref[...] = jnp.zeros_like(ended_ref)
    tokens, rows = 4 * rows_dev, 4 * CAP
    total = 2 * local * rows
    shift_lane = lax.broadcasted_iota(jnp.int32, (1, tokens), 1) // rows_dev * CAP
    shift_row = lax.broadcasted_iota(jnp.int32, (tokens, 1), 0) // rows_dev * CAP
    row_id = lax.broadcasted_iota(jnp.int32, (rows, tokens), 0)
    lane = lax.broadcasted_iota(jnp.int32, (tokens, total), 1)
    for g in range(planes):
        facts = facts_ref[g * tokens : (g + 1) * tokens, :]
        by_lane = facts_by_lane(facts)
        by_row = facts.astype(jnp.float32)
        here = slice(g * rows, (g + 1) * rows)
        weighed, put = [], None
        for core, y_ref in enumerate((y_own_ref, y_got_ref)):
            for e in range(local):
                base = (bases_ref[core] + e) * CAP
                weight = jnp.zeros((rows, tokens), jnp.float32)
                for j in range(2):
                    hit = row_id == places_of([by_lane[j : j + 1]], base, shift_lane)
                    gate = by_lane[2 + j : 3 + j] + by_lane[4 + j : 5 + j] + by_lane[6 + j : 7 + j]
                    weight = weight + jnp.where(hit, gate, 0.0)
                weight = jnp.sum(weight, axis=1, keepdims=True)
                weighed.append((y_ref[e, here, :].astype(jnp.float32) * weight).astype(jnp.bfloat16))
                first = (core * local + e) * rows
                hit = lane == places_of([by_row[:, j : j + 1] for j in range(2)], base, shift_row + first)
                put = hit if put is None else put | hit
        put = put.astype(jnp.float32).astype(jnp.bfloat16)
        out = jnp.dot(put, jnp.concatenate(weighed, axis=0), preferred_element_type=jnp.float32)
        out = out.astype(jnp.bfloat16)
        kept_ref[g * tokens // 2 : (g + 1) * tokens // 2, :] = out[: tokens // 2]
        send_refs[g][...] = out[tokens // 2 :]


def put_rows(y_own, y_got, facts, bases, rows_dev, waits):
    local, _, width = y_own.shape
    tokens = facts.shape[0]
    planes = tokens // (4 * rows_dev)
    vmem = pl.BlockSpec(memory_space=pltpu.VMEM)
    shape = lambda n: jax.ShapeDtypeStruct((n, width), jnp.bfloat16)
    out = pl.pallas_call(
        functools.partial(put_kernel, local, rows_dev, planes, len(waits)),
        out_shape=(shape(2 * planes * rows_dev),)
        + (shape(2 * rows_dev),) * planes
        + (jax.ShapeDtypeStruct((8, 128), jnp.float32),),
        in_specs=[pl.BlockSpec(memory_space=pltpu.SMEM), vmem, vmem, vmem]
        + [pl.BlockSpec(memory_space=pl.ANY)] * len(waits),
        out_specs=(vmem,) * (2 + planes),
        compiler_params=pltpu.CompilerParams(vmem_limit_bytes=20 * MIB),
        cost_estimate=pl.CostEstimate(
            flops=16 * local * CAP * tokens * width,
            bytes_accessed=8 * local * tokens * width,
            transcendentals=0,
        ),
    )(bases, y_own, y_got, facts, *waits)
    return out[0], out[1:-1], out[-1]


def swap(a, axis, size, distance):
    return lax.ppermute(a, axis, [(i, i ^ distance) for i in range(size)])


def fold_kernel(groups, count, waits, keep_ref, *rest):
    got_refs, (kept_ref, *send_refs) = rest[:count], rest[count + waits :]
    part = keep_ref.shape[0] // (2 * groups)
    span = got_refs[0].shape[0]
    for i in range(2 * groups):
        start = i * part
        got = got_refs[start // span][start % span : start % span + part, :]
        total = keep_ref[start : start + part, :].astype(jnp.float32) + got.astype(jnp.float32)
        total = total.astype(jnp.bfloat16)
        if i % 2 == 0:
            kept_ref[i // 2 * part : (i // 2 + 1) * part, :] = total
        else:
            send_refs[i // 2][...] = total


def fold(keep, gots, groups, waits=()):
    rows, width = keep.shape
    part = rows // (2 * groups)
    vmem = pl.BlockSpec(memory_space=pltpu.VMEM)
    shape = lambda n: jax.ShapeDtypeStruct((n, width), jnp.bfloat16)
    out = pl.pallas_call(
        functools.partial(fold_kernel, groups, len(gots), len(waits)),
        out_shape=(shape(groups * part),) + (shape(part),) * groups,
        in_specs=[vmem] * (1 + len(gots)) + [pl.BlockSpec(memory_space=pl.ANY)] * len(waits),
        out_specs=(vmem,) * (1 + groups),
        compiler_params=pltpu.CompilerParams(vmem_limit_bytes=10 * MIB),
        cost_estimate=pl.CostEstimate(flops=rows * width, bytes_accessed=6 * rows * width, transcendentals=0),
    )(keep, *gots, *waits)
    return out[0], out[1:]


def exchange_experts(piece, w_gate, w_up, w_down, n_seq, n_exp, late_work):
    x = lambda a: swap(a, "seq", n_seq, 1)
    y = lambda a: swap(a, "exp", n_exp, 2)
    core = lambda a: swap(a, "exp", n_exp, 1)
    z = lambda a, k: swap(a, "seq", n_seq, 2 * k)
    local = w_gate.shape[0]
    me = lax.axis_index("exp").astype(jnp.int32)
    bases = jnp.stack([me, me ^ 1]) * local
    starts = [piece, z(piece, 1), z(piece, 2)]
    ways = [("xy", "yx")[k % 2] for k in range(4)]
    over = {"x": x, "y": y}
    single = [[over[way](starts[k]) for way in ways[k]] for k in range(2)]
    starts[2] = hold(starts[2], single[0] + single[1])
    single.append([over[way](starts[2]) for way in ways[2]])

    def both(k):
        return over[ways[k][1]](single[k][0])

    double = [both(0), both(1)]
    starts.append(hold(z(starts[2], 1), double))
    single.append([over[way](starts[3]) for way in ways[3]])
    double += [both(2), both(3)]

    def gather(k):
        near = []
        for i in (k, k + 1):
            by_f, by_g = single[i]
            near += [starts[i], by_g, by_f, double[i]]
        return near

    near_b, near_a = gather(0), gather(2)
    own_a, sib_a, facts_a = select_rows(near_a, bases, local)
    got_a = core(sib_a)
    pages, fill = late_work(facts_a)
    own_b, sib_b, facts_b = select_rows(near_b, bases, local, [pages])
    got_b = core(sib_b)
    own_a, sib_a, ended = expert_rows(own_a, got_a, w_gate, w_up, w_down, [facts_b, pages])
    cache, filled = fill(ended)
    got_a = core(sib_a)
    own_b, sib_b, ended = expert_rows(own_b, got_b, w_gate, w_up, w_down, [filled])
    got_b = core(sib_b)
    keep_a, (fx_a, fy_a), _ = put_rows(own_a, got_a, facts_a, bases, piece.shape[0], [ended])
    keep_a, (gy_a, gx_a) = fold(keep_a, [x(fx_a), y(fy_a)], 2)
    keep_b, (fx_b, fy_b), put_b = put_rows(own_b, got_b, facts_b, bases, piece.shape[0], [gy_a])
    gy_a, gx_a = y(gy_a), x(gx_a)
    fx_b, fy_b = hold(fx_b, [gy_a, gx_a]), hold(fy_b, [gy_a, gx_a])
    keep_a, (z_a,) = fold(keep_a, [gy_a, gx_a], 1, [put_b])
    over_z = (keep_a.astype(jnp.float32) + z(z_a, 1).astype(jnp.float32)).astype(jnp.bfloat16)
    keep_b, (gy_b, gx_b) = fold(keep_b, [x(fx_b), y(fy_b)], 2, [over_z])
    back_a = z(over_z, 2)
    keep_b, (z_b,) = fold(keep_b, [y(gy_b), x(gx_b)], 1, [back_a])
    mine = keep_b.astype(jnp.float32) + z(z_b, 1).astype(jnp.float32)
    return mine + back_a.astype(jnp.float32), cache


def body(
    n_seq,
    n_exp,
    query,
    key_value,
    residual,
    norm_gain,
    segment_ids,
    routes,
    gate_weights,
    page_table,
    w_gate,
    w_up,
    w_down,
):
    rows_dev, width = query.shape[1:]
    everyone = ("exp", "seq")
    group = segment_ids.shape[1]
    share, firsts, heads = head_ranges(width, n_seq)
    span = heads * HEAD_DIM

    flat = routes[0].reshape(rows_dev * 2)
    onehot = (flat[:, None] == jnp.arange(EXPERTS, dtype=jnp.int32)[None, :]).astype(jnp.int32)
    before = jnp.cumsum(onehot, axis=0) - onehot
    target = (flat * CAP + jnp.sum(before * onehot, axis=1)).reshape(rows_dev, 2).astype(jnp.float32)

    keys, values = key_value[0, :, 0], key_value[0, :, 1]

    packed = pack_heads(query[0], keys, values, firsts, span)
    packed = lax.all_to_all(packed, "seq", split_axis=0, concat_axis=0, tiled=True)
    packed = packed.reshape(group, 3 * span)
    context = attention(packed, segment_ids[0], heads)
    context = lax.all_to_all(
        context.reshape(n_seq, rows_dev, span), "seq", split_axis=0, concat_axis=0, tiled=True
    )
    offsets = [j * share - firsts[j] * HEAD_DIM for j in range(n_seq)]

    first = (lax.axis_index("exp") * (EXPERTS // n_exp)).astype(jnp.int32).reshape(1)
    w_gate, w_up = jnp.swapaxes(w_gate, 1, 2), jnp.swapaxes(w_up, 1, 2)
    gates = gate_weights[0]
    facts = jnp.concatenate([target, gates, gates, gates], axis=1)
    facts = jnp.pad(facts, ((0, 0), (0, 128 - facts.shape[1])))
    stream, piece = norm_tokens(context, residual[0], norm_gain, facts, share, offsets)

    slots = jnp.arange(group // PAGE, dtype=jnp.int32)
    order = jnp.sum(jnp.where(page_table[0][None, :] == slots[:, None], slots[None, :], 0), axis=1)

    def fill_cache(late):
        pages = pick_pages(packed, order, late, n_seq, span)
        sent = lax.all_to_all(pages, "seq", split_axis=0, concat_axis=0, tiled=True)
        return pages, lambda behind: join_pages(sent, share, offsets, span, behind)

    if (n_seq, n_exp) == (8, 4):
        mixture, cache = exchange_experts(piece, w_gate, w_up, w_down, n_seq, n_exp, fill_cache)
    else:
        cache, _ = fill_cache(piece)[1](piece)
        blocks = n_seq * n_exp
        everything = lax.all_gather(piece, everyone, axis=0, tiled=True)
        facts = everything[:, width : width + 8].astype(jnp.float32)
        facts = facts.reshape(blocks // CHUNK_BLOCKS, CHUNK_BLOCKS * rows_dev, 8).transpose(0, 2, 1)
        gates = facts[:, 2:4] + facts[:, 4:6] + facts[:, 6:8]
        partial = experts(
            everything[:, :width], facts[:, :2].astype(jnp.int32), gates, w_gate, w_up, w_down, first
        )
        mixture = lax.psum_scatter(partial, everyone, scatter_dimension=0, tiled=True).astype(jnp.float32)
    layer_out = (stream + mixture).astype(jnp.bfloat16)
    return (layer_out[None], cache.reshape(1, rows_dev // PAGE, PAGE, 2 * width))


def solution(mesh):
    in_specs = (
        P("exp", "seq", None),
        P("exp", "seq", None, None),
        P("exp", "seq", None),
        P(),
        P("exp", None),
        P("exp", "seq", None),
        P("exp", "seq", None),
        P("exp", None),
        P("exp", None, "seq"),
        P("exp", None, "seq"),
        P("exp", "seq", None),
    )
    out_specs = (P("exp", "seq", None), P("exp", "seq", None, None))
    run = functools.partial(body, mesh.shape["seq"], mesh.shape["exp"])
    return jax.shard_map(run, mesh=mesh, in_specs=in_specs, out_specs=out_specs, check_vma=False)
```

```python
import functools
import math

import jax
import jax.numpy as jnp
from jax import lax
from jax.experimental import pallas as pl
from jax.experimental.pallas import tpu as pltpu
from jax.sharding import PartitionSpec as P

HEADS = 36
HEAD_DIM = 64
EXPERTS = 8
PAGE = 16
CAP = 24
MIB = 1024 * 1024
CHUNK_BLOCKS = 8


def head_ranges(width, n_seq):
    share = width // n_seq
    firsts = [j * share // HEAD_DIM for j in range(n_seq)]
    count = max(-(-(j + 1) * share // HEAD_DIM) - firsts[j] for j in range(n_seq))
    firsts = [min(f, HEADS - count) for f in firsts]
    return share, firsts, count


def attention_kernel(heads, q_rows, packed_ref, seg_row_ref, seg_col_ref, out_ref):
    total = packed_ref.shape[0]
    span = heads * HEAD_DIM
    scale = 1.0 / math.sqrt(HEAD_DIM)
    for start in range(0, total, q_rows):
        end = start + q_rows
        q_place = start + lax.broadcasted_iota(jnp.int32, (q_rows, end), 0)
        k_place = lax.broadcasted_iota(jnp.int32, (q_rows, end), 1)
        visible = (seg_col_ref[start:end, :] == seg_row_ref[:, :end]) & (k_place <= q_place)
        parts = []
        for h in range(heads):
            a = h * HEAD_DIM
            q = packed_ref[start:end, a : a + HEAD_DIM]
            k = packed_ref[:end, span + a : span + a + HEAD_DIM]
            v = packed_ref[:end, 2 * span + a : 2 * span + a + HEAD_DIM]
            s = lax.dot_general(q, k, (((1,), (1,)), ((), ())), preferred_element_type=jnp.float32)
            s = jnp.where(visible, s * scale, -1e30)
            top = jnp.max(s, axis=1, keepdims=True)
            p = jnp.exp(s - top)
            denominator = jnp.sum(p, axis=1, keepdims=True)
            o = jnp.dot(p.astype(jnp.bfloat16), v, preferred_element_type=jnp.float32)
            parts.append((o / denominator).astype(jnp.bfloat16))
        out_ref[start:end, :] = jnp.concatenate(parts, axis=1)


def attention(packed, segments, heads):
    total = packed.shape[0]
    span = heads * HEAD_DIM
    return pl.pallas_call(
        functools.partial(attention_kernel, heads, 128),
        out_shape=jax.ShapeDtypeStruct((total, span), jnp.bfloat16),
        compiler_params=pltpu.CompilerParams(vmem_limit_bytes=24 * MIB),
        cost_estimate=pl.CostEstimate(
            flops=4 * total * total * span, bytes_accessed=8 * total * span, transcendentals=total * total * heads
        ),
    )(packed, segments[None, :], segments[:, None])


def dot_t(a, b):
    return lax.dot_general(a, b, (((1,), (1,)), ((), ())), preferred_element_type=jnp.float32)


def expert_kernel(
    local, rows, tokens, first_ref, x_ref, tgt_ref, gates_ref, wg_ref, wu_ref, wd_ref, out_ref, kept_ref
):
    le = pl.program_id(0)
    chunk = pl.program_id(1)

    def selection(which):
        base = (first_ref[0] + which) * CAP
        row_id = lax.broadcasted_iota(jnp.int32, (rows, tokens), 0)
        block = lax.broadcasted_iota(jnp.int32, (1, tokens), 1) // 64
        picks, weights = None, None
        for j in range(2):
            slot = tgt_ref[0, j : j + 1, :] - base
            place = jnp.where((slot >= 0) & (slot < CAP), block * CAP + slot, -1)
            hit = row_id == place
            gate = jnp.where(hit, gates_ref[0, j : j + 1, :], 0.0)
            picks = hit if picks is None else picks | hit
            weights = gate if weights is None else weights + gate
        return picks.astype(jnp.float32).astype(jnp.bfloat16), jnp.sum(weights, axis=1, keepdims=True)

    pick, weight = selection(le)
    chosen = jnp.dot(pick, x_ref[...], preferred_element_type=jnp.float32).astype(jnp.bfloat16)
    gate = dot_t(chosen, wg_ref[0])
    upper = dot_t(chosen, wu_ref[0])
    hidden = (gate / (1.0 + jnp.exp(-gate)) * upper).astype(jnp.bfloat16)
    y = jnp.dot(hidden, wd_ref[0], preferred_element_type=jnp.float32)
    y = (y * weight).astype(jnp.bfloat16)

    if local > 1:

        @pl.when(le < local - 1)
        def _():
            kept_ref[le, chunk] = y

    @pl.when(le == local - 1)
    def _():
        total = lax.dot_general(pick, y, (((0,), (0,)), ((), ())), preferred_element_type=jnp.float32)
        for other in range(local - 1):
            pick_o, _ = selection(other)
            total += lax.dot_general(
                pick_o, kept_ref[other, chunk], (((0,), (0,)), ((), ())), preferred_element_type=jnp.float32
            )
        out_ref[...] = total.astype(jnp.bfloat16)


def experts(x, tgt, gates, w_gate, w_up, w_down, first):
    local, hidden, width = w_gate.shape
    chunks, _, tokens = tgt.shape
    rows = tokens // 64 * CAP
    last = local - 1
    return pl.pallas_call(
        functools.partial(expert_kernel, local, rows, tokens),
        out_shape=jax.ShapeDtypeStruct(x.shape, jnp.bfloat16),
        grid=(local, chunks),
        in_specs=[
            pl.BlockSpec(memory_space=pltpu.SMEM),
            pl.BlockSpec((tokens, width), lambda e, c: (c, 0)),
            pl.BlockSpec((1, 2, tokens), lambda e, c: (c, 0, 0)),
            pl.BlockSpec((1, 2, tokens), lambda e, c: (c, 0, 0)),
            pl.BlockSpec((1, hidden, width), lambda e, c: (e, 0, 0)),
            pl.BlockSpec((1, hidden, width), lambda e, c: (e, 0, 0)),
            pl.BlockSpec((1, hidden, width), lambda e, c: (e, 0, 0)),
        ],
        out_specs=pl.BlockSpec((tokens, width), lambda e, c: (jnp.where(e == last, c, 0), 0)),
        scratch_shapes=[pltpu.VMEM((max(last, 1), chunks if last else 1, rows, width), jnp.bfloat16)],
        compiler_params=pltpu.CompilerParams(vmem_limit_bytes=58 * MIB),
        cost_estimate=pl.CostEstimate(
            flops=6 * local * chunks * rows * width * hidden,
            bytes_accessed=6 * local * width * hidden + 6 * chunks * tokens * width,
            transcendentals=local * chunks * rows * hidden,
        ),
    )(first, x, tgt, gates, w_gate, w_up, w_down)


def pack_kernel(firsts, span, q_ref, k_ref, v_ref, out_ref):
    for j, first in enumerate(firsts):
        lanes = slice(first * HEAD_DIM, first * HEAD_DIM + span)
        out_ref[j] = jnp.concatenate([r[:, lanes] for r in (q_ref, k_ref, v_ref)], axis=1)


def pack_heads(query, keys, values, firsts, span):
    rows_dev = query.shape[0]
    n_seq = len(firsts)
    return pl.pallas_call(
        functools.partial(pack_kernel, firsts, span),
        out_shape=jax.ShapeDtypeStruct((n_seq, rows_dev, 3 * span), jnp.bfloat16),
        compiler_params=pltpu.CompilerParams(vmem_limit_bytes=12 * MIB),
        cost_estimate=pl.CostEstimate(flops=0, bytes_accessed=12 * n_seq * rows_dev * span, transcendentals=0),
    )(query, keys, values)


def norm_kernel(share, offsets, context_ref, residual_ref, gain_ref, facts_ref, stream_ref, piece_ref):
    n_seq, _, _ = context_ref.shape
    width = residual_ref.shape[1]
    parts = [context_ref[j][:, offsets[j] : offsets[j] + share] for j in range(n_seq)]
    context = jnp.concatenate(parts, axis=1).astype(jnp.float32)
    stream = residual_ref[...].astype(jnp.float32) + context
    stream_ref[...] = stream
    mean = jnp.mean(stream * stream, axis=1, keepdims=True)
    normed = stream * lax.rsqrt(mean + 1e-05) * gain_ref[...].astype(jnp.float32)
    piece_ref[:, :width] = normed.astype(jnp.bfloat16)
    facts = facts_ref[...]
    lane = lax.broadcasted_iota(jnp.int32, facts.shape, 1)
    high = facts.astype(jnp.bfloat16).astype(jnp.float32)
    middle = (facts - high).astype(jnp.bfloat16).astype(jnp.float32)
    low = facts - high - middle
    own = jnp.where(lane < 4, high, jnp.where(lane < 6, middle, low))
    piece_ref[:, width:] = own.astype(jnp.bfloat16)


def norm_tokens(context, residual, gain, facts, share, offsets):
    rows_dev, width = residual.shape
    return pl.pallas_call(
        functools.partial(norm_kernel, share, offsets),
        out_shape=(
            jax.ShapeDtypeStruct((rows_dev, width), jnp.float32),
            jax.ShapeDtypeStruct((rows_dev, width + facts.shape[1]), jnp.bfloat16),
        ),
        compiler_params=pltpu.CompilerParams(vmem_limit_bytes=12 * MIB),
        cost_estimate=pl.CostEstimate(
            flops=10 * rows_dev * width, bytes_accessed=10 * rows_dev * width, transcendentals=rows_dev
        ),
    )(context, residual, gain[None, :], facts)


def pick_pages_kernel(per_device, first_lane, order_ref, packed_ref, late_ref, out_ref):
    del late_ref
    for j in range(out_ref.shape[0]):
        for i in range(per_device):
            rows = pl.ds(pl.multiple_of(order_ref[j * per_device + i] * PAGE, PAGE), PAGE)
            out_ref[j, i * PAGE : (i + 1) * PAGE, :] = packed_ref[rows, first_lane:]


def pick_pages(packed, order, late, n_seq, span):
    rows = packed.shape[0] // n_seq
    vmem = pl.BlockSpec(memory_space=pltpu.VMEM)
    return pl.pallas_call(
        functools.partial(pick_pages_kernel, rows // PAGE, span),
        out_shape=jax.ShapeDtypeStruct((n_seq, rows, 2 * span), jnp.bfloat16),
        in_specs=[pl.BlockSpec(memory_space=pltpu.SMEM), vmem, pl.BlockSpec(memory_space=pl.ANY)],
        compiler_params=pltpu.CompilerParams(vmem_limit_bytes=8 * MIB),
        cost_estimate=pl.CostEstimate(flops=0, bytes_accessed=10 * packed.shape[0] * span, transcendentals=0),
    )(order, packed, late)


def join_pages_kernel(share, offsets, span, pages_ref, behind_ref, out_ref, ended_ref):
    del behind_ref
    ended_ref[...] = jnp.zeros_like(ended_ref)
    width = share * len(offsets)
    for part in range(2):
        parts = [
            pages_ref[j][:, part * span + offsets[j] : part * span + offsets[j] + share]
            for j in range(len(offsets))
        ]
        out_ref[:, part * width : (part + 1) * width] = jnp.concatenate(parts, axis=1)


def join_pages(pages, share, offsets, span, behind):
    n_seq, rows, _ = pages.shape
    return pl.pallas_call(
        functools.partial(join_pages_kernel, share, offsets, span),
        out_shape=(
            jax.ShapeDtypeStruct((rows, 2 * share * n_seq), jnp.bfloat16),
            jax.ShapeDtypeStruct((8, 128), jnp.float32),
        ),
        in_specs=[pl.BlockSpec(memory_space=pltpu.VMEM), pl.BlockSpec(memory_space=pl.ANY)],
        compiler_params=pltpu.CompilerParams(vmem_limit_bytes=12 * MIB),
        cost_estimate=pl.CostEstimate(flops=0, bytes_accessed=8 * rows * n_seq * span, transcendentals=0),
    )(pages, behind)


def places_of(slots, base, shift):
    place = -1
    for slot in slots:
        slot = slot.astype(jnp.int32) - base
        place = jnp.where((slot >= 0) & (slot < CAP), shift + slot, place)
    return place


def hold_kernel(*refs):
    del refs


def hold(a, waits):
    anywhere = pl.BlockSpec(memory_space=pl.ANY)
    return pl.pallas_call(
        hold_kernel,
        out_shape=jax.ShapeDtypeStruct(a.shape, a.dtype),
        in_specs=[anywhere] * (1 + len(waits)),
        out_specs=anywhere,
        input_output_aliases={0: 0},
        compiler_params=pltpu.CompilerParams(vmem_limit_bytes=MIB),
        cost_estimate=pl.CostEstimate(flops=0, bytes_accessed=0, transcendentals=0),
    )(a, *waits)


def facts_by_lane(x):
    unit = lax.broadcasted_iota(jnp.int32, (8, 128), 0) == lax.broadcasted_iota(jnp.int32, (8, 128), 1)
    return dot_t(unit.astype(jnp.float32).astype(jnp.bfloat16), x)


def select_kernel(local, rows_dev, count, bases_ref, *refs):
    piece_refs, (own_ref, sib_ref, facts_ref) = refs[:count], refs[-3:]
    width = own_ref.shape[2]
    tokens, rows = 4 * rows_dev, 4 * CAP
    shift = lax.broadcasted_iota(jnp.int32, (1, tokens), 1) // rows_dev * CAP
    row_id = lax.broadcasted_iota(jnp.int32, (rows, tokens), 0)
    for g in range(len(piece_refs) // 4):
        x = jnp.concatenate([p[...] for p in piece_refs[4 * g : 4 * g + 4]], axis=0)
        facts_ref[g * tokens : (g + 1) * tokens, :] = x[:, width:]
        facts = facts_by_lane(x[:, width:])
        picks = []
        for core in range(2):
            for e in range(local):
                base = (bases_ref[core] + e) * CAP
                hit = row_id == places_of([facts[j : j + 1] for j in range(2)], base, shift)
                picks.append(hit.astype(jnp.float32))
        picks = jnp.concatenate(picks, axis=0).astype(jnp.bfloat16)
        chosen = jnp.dot(picks, x[:, :width], preferred_element_type=jnp.float32).astype(jnp.bfloat16)
        for e in range(local):
            own_ref[e, g * rows : (g + 1) * rows, :] = chosen[e * rows : (e + 1) * rows]
            sib_ref[e, g * rows : (g + 1) * rows, :] = chosen[(local + e) * rows : (local + e + 1) * rows]


def select_rows(pieces, bases, local, waits=()):
    rows_dev, wide = pieces[0].shape
    width = wide - 128
    rows = len(pieces) * CAP
    out = jax.ShapeDtypeStruct((local, rows, width), jnp.bfloat16)
    vmem = pl.BlockSpec(memory_space=pltpu.VMEM)
    return pl.pallas_call(
        functools.partial(select_kernel, local, rows_dev, len(pieces)),
        out_shape=(out, out, jax.ShapeDtypeStruct((len(pieces) * rows_dev, 128), jnp.bfloat16)),
        in_specs=[pl.BlockSpec(memory_space=pltpu.SMEM)]
        + [vmem] * len(pieces)
        + [pl.BlockSpec(memory_space=pl.ANY)] * len(waits),
        out_specs=(vmem, vmem, vmem),
        compiler_params=pltpu.CompilerParams(vmem_limit_bytes=20 * MIB),
        cost_estimate=pl.CostEstimate(
            flops=16 * local * CAP * rows_dev * len(pieces) * width,
            bytes_accessed=2 * len(pieces) * rows_dev * wide + 4 * local * rows * width,
            transcendentals=0,
        ),
    )(bases, *pieces, *waits)


def rows_kernel(local, waits, own_ref, got_ref, wg_hbm, wu_hbm, wd_hbm, *rest):
    y_own_ref, y_sib_ref, ended_ref, wg, wu, wd, weight_sem = rest[waits:]
    ended_ref[...] = jnp.zeros_like(ended_ref)
    half = got_ref.shape[1]
    copies = [
        pltpu.make_async_copy(source.at[e], target.at[e], weight_sem.at[3 * e + i])
        for e in range(local)
        for i, (source, target) in enumerate(((wg_hbm, wg), (wu_hbm, wu), (wd_hbm, wd)))
    ]
    for copy in copies[:2]:
        copy.start()

    def arrived(number):
        copies[number].wait()
        if number + 2 < len(copies):
            copies[number + 2].start()

    for e in range(local):
        rows = jnp.concatenate([own_ref[e], got_ref[e]], axis=0).T
        arrived(3 * e)
        gate = jnp.dot(wg[e], rows, preferred_element_type=jnp.float32)
        arrived(3 * e + 1)
        upper = jnp.dot(wu[e], rows, preferred_element_type=jnp.float32)
        hidden = (gate / (1.0 + jnp.exp(-gate)) * upper).T.astype(jnp.bfloat16)
        arrived(3 * e + 2)
        y = jnp.dot(hidden, wd[e], preferred_element_type=jnp.float32).astype(jnp.bfloat16)
        y_own_ref[e] = y[:half]
        y_sib_ref[e] = y[half:]


def expert_rows(own, got, w_gate, w_up, w_down, waits):
    local, hidden, width = w_gate.shape
    rows = 2 * own.shape[1]
    out = jax.ShapeDtypeStruct(own.shape, jnp.bfloat16)
    vmem = pl.BlockSpec(memory_space=pltpu.VMEM)
    weights = pltpu.VMEM((local, hidden, width), jnp.bfloat16)
    return pl.pallas_call(
        functools.partial(rows_kernel, local, len(waits)),
        out_shape=(out, out, jax.ShapeDtypeStruct((8, 128), jnp.float32)),
        in_specs=[vmem, vmem]
        + [pl.BlockSpec(memory_space=pl.ANY)] * (3 + len(waits)),
        out_specs=(vmem, vmem, vmem),
        scratch_shapes=[
            weights,
            weights,
            weights,
            pltpu.SemaphoreType.DMA((3 * local,)),
        ],
        compiler_params=pltpu.CompilerParams(vmem_limit_bytes=44 * MIB),
        cost_estimate=pl.CostEstimate(
            flops=6 * local * rows * width * hidden,
            bytes_accessed=6 * local * width * hidden + 4 * local * rows * width,
            transcendentals=local * rows * hidden,
        ),
    )(own, got, w_gate, w_up, w_down, *waits)


def put_kernel(local, rows_dev, planes, waits, bases_ref, y_own_ref, y_got_ref, facts_ref, *rest):
    kept_ref, *send_refs, ended_ref = rest[waits:]
    ended_ref[...] = jnp.zeros_like(ended_ref)
    tokens, rows = 4 * rows_dev, 4 * CAP
    total = 2 * local * rows
    shift = lax.broadcasted_iota(jnp.int32, (tokens, 1), 0) // rows_dev * CAP
    lane = lax.broadcasted_iota(jnp.int32, (tokens, total), 1)
    for g in range(planes):
        facts = facts_ref[g * tokens : (g + 1) * tokens, :].astype(jnp.float32)
        high, middle = jnp.zeros((tokens, total), jnp.float32), jnp.zeros((tokens, total), jnp.float32)
        for j in range(2):
            slot = facts[:, j : j + 1].astype(jnp.int32)
            place = jnp.full((tokens, 1), -1, jnp.int32)
            for core in range(2):
                for e in range(local):
                    near = slot - (bases_ref[core] + e) * CAP
                    here = shift + near + (core * local + e) * rows
                    place = jnp.where((near >= 0) & (near < CAP), here, place)
            hit = lane == place
            high = jnp.where(hit, facts[:, 2 + j : 3 + j], high)
            middle = jnp.where(hit, facts[:, 4 + j : 5 + j], middle)
        here = slice(g * rows, (g + 1) * rows)
        y = jnp.concatenate([ref[e, here, :] for ref in (y_own_ref, y_got_ref) for e in range(local)], axis=0)
        out = jnp.dot(high.astype(jnp.bfloat16), y, preferred_element_type=jnp.float32)
        out += jnp.dot(middle.astype(jnp.bfloat16), y, preferred_element_type=jnp.float32)
        out = out.astype(jnp.bfloat16)
        kept_ref[g * tokens // 2 : (g + 1) * tokens // 2, :] = out[: tokens // 2]
        send_refs[g][...] = out[tokens // 2 :]


def put_rows(y_own, y_got, facts, bases, rows_dev, waits):
    local, _, width = y_own.shape
    tokens = facts.shape[0]
    planes = tokens // (4 * rows_dev)
    vmem = pl.BlockSpec(memory_space=pltpu.VMEM)
    shape = lambda n: jax.ShapeDtypeStruct((n, width), jnp.bfloat16)
    out = pl.pallas_call(
        functools.partial(put_kernel, local, rows_dev, planes, len(waits)),
        out_shape=(shape(2 * planes * rows_dev),)
        + (shape(2 * rows_dev),) * planes
        + (jax.ShapeDtypeStruct((8, 128), jnp.float32),),
        in_specs=[pl.BlockSpec(memory_space=pltpu.SMEM), vmem, vmem, vmem]
        + [pl.BlockSpec(memory_space=pl.ANY)] * len(waits),
        out_specs=(vmem,) * (2 + planes),
        compiler_params=pltpu.CompilerParams(vmem_limit_bytes=20 * MIB),
        cost_estimate=pl.CostEstimate(
            flops=16 * local * CAP * tokens * width,
            bytes_accessed=8 * local * tokens * width,
            transcendentals=0,
        ),
    )(bases, y_own, y_got, facts, *waits)
    return out[0], out[1:-1], out[-1]


def swap(a, axis, size, distance):
    return lax.ppermute(a, axis, [(i, i ^ distance) for i in range(size)])


def fold_kernel(groups, count, waits, keep_ref, *rest):
    got_refs, (kept_ref, *send_refs) = rest[:count], rest[count + waits :]
    part = keep_ref.shape[0] // (2 * groups)
    span = got_refs[0].shape[0]
    for i in range(2 * groups):
        start = i * part
        got = got_refs[start // span][start % span : start % span + part, :]
        total = keep_ref[start : start + part, :].astype(jnp.float32) + got.astype(jnp.float32)
        total = total.astype(jnp.bfloat16)
        if i % 2 == 0:
            kept_ref[i // 2 * part : (i // 2 + 1) * part, :] = total
        else:
            send_refs[i // 2][...] = total


def fold(keep, gots, groups, waits=()):
    rows, width = keep.shape
    part = rows // (2 * groups)
    vmem = pl.BlockSpec(memory_space=pltpu.VMEM)
    shape = lambda n: jax.ShapeDtypeStruct((n, width), jnp.bfloat16)
    out = pl.pallas_call(
        functools.partial(fold_kernel, groups, len(gots), len(waits)),
        out_shape=(shape(groups * part),) + (shape(part),) * groups,
        in_specs=[vmem] * (1 + len(gots)) + [pl.BlockSpec(memory_space=pl.ANY)] * len(waits),
        out_specs=(vmem,) * (1 + groups),
        compiler_params=pltpu.CompilerParams(vmem_limit_bytes=10 * MIB),
        cost_estimate=pl.CostEstimate(flops=rows * width, bytes_accessed=6 * rows * width, transcendentals=0),
    )(keep, *gots, *waits)
    return out[0], out[1:]


def exchange_experts(piece, w_gate, w_up, w_down, n_seq, n_exp, late_work):
    x = lambda a: swap(a, "seq", n_seq, 1)
    y = lambda a: swap(a, "exp", n_exp, 2)
    core = lambda a: swap(a, "exp", n_exp, 1)
    z = lambda a, k: swap(a, "seq", n_seq, 2 * k)
    local = w_gate.shape[0]
    me = lax.axis_index("exp").astype(jnp.int32)
    bases = jnp.stack([me, me ^ 1]) * local
    starts = [piece, z(piece, 1), z(piece, 2)]
    ways = [("xy", "yx")[k % 2] for k in range(4)]
    over = {"x": x, "y": y}
    single = [[over[way](starts[k]) for way in ways[k]] for k in range(2)]
    starts[2] = hold(starts[2], single[0] + single[1])
    single.append([over[way](starts[2]) for way in ways[2]])

    def both(k):
        return over[ways[k][1]](single[k][0])

    double = [both(0), both(1)]
    starts.append(hold(z(starts[2], 1), double))
    single.append([over[way](starts[3]) for way in ways[3]])
    double += [both(2), both(3)]

    def gather(k):
        near = []
        for i in (k, k + 1):
            by_f, by_g = single[i]
            near += [starts[i], by_g, by_f, double[i]]
        return near

    near_b, near_a = gather(0), gather(2)
    own_a, sib_a, facts_a = select_rows(near_a, bases, local)
    got_a = core(sib_a)
    pages, fill = late_work(facts_a)
    own_b, sib_b, facts_b = select_rows(near_b, bases, local, [pages])
    got_b = core(sib_b)
    own_a, sib_a, ended = expert_rows(own_a, got_a, w_gate, w_up, w_down, [facts_b, pages])
    cache, filled = fill(ended)
    got_a = core(sib_a)
    own_b, sib_b, ended = expert_rows(own_b, got_b, w_gate, w_up, w_down, [filled])
    got_b = core(sib_b)
    keep_a, (fx_a, fy_a), _ = put_rows(own_a, got_a, facts_a, bases, piece.shape[0], [ended])
    keep_a, (gy_a, gx_a) = fold(keep_a, [x(fx_a), y(fy_a)], 2)
    keep_b, (fx_b, fy_b), put_b = put_rows(own_b, got_b, facts_b, bases, piece.shape[0], [gy_a])
    gy_a, gx_a = y(gy_a), x(gx_a)
    fx_b, fy_b = hold(fx_b, [gy_a, gx_a]), hold(fy_b, [gy_a, gx_a])
    keep_a, (z_a,) = fold(keep_a, [gy_a, gx_a], 1, [put_b])
    over_z = (keep_a.astype(jnp.float32) + z(z_a, 1).astype(jnp.float32)).astype(jnp.bfloat16)
    keep_b, (gy_b, gx_b) = fold(keep_b, [x(fx_b), y(fy_b)], 2, [over_z])
    back_a = z(over_z, 2)
    keep_b, (z_b,) = fold(keep_b, [y(gy_b), x(gx_b)], 1, [back_a])
    mine = keep_b.astype(jnp.float32) + z(z_b, 1).astype(jnp.float32)
    return mine + back_a.astype(jnp.float32), cache


def body(
    n_seq,
    n_exp,
    query,
    key_value,
    residual,
    norm_gain,
    segment_ids,
    routes,
    gate_weights,
    page_table,
    w_gate,
    w_up,
    w_down,
):
    rows_dev, width = query.shape[1:]
    everyone = ("exp", "seq")
    group = segment_ids.shape[1]
    share, firsts, heads = head_ranges(width, n_seq)
    span = heads * HEAD_DIM

    flat = routes[0].reshape(rows_dev * 2)
    onehot = (flat[:, None] == jnp.arange(EXPERTS, dtype=jnp.int32)[None, :]).astype(jnp.int32)
    before = jnp.cumsum(onehot, axis=0) - onehot
    target = (flat * CAP + jnp.sum(before * onehot, axis=1)).reshape(rows_dev, 2).astype(jnp.float32)

    keys, values = key_value[0, :, 0], key_value[0, :, 1]

    packed = pack_heads(query[0], keys, values, firsts, span)
    packed = lax.all_to_all(packed, "seq", split_axis=0, concat_axis=0, tiled=True)
    packed = packed.reshape(group, 3 * span)
    context = attention(packed, segment_ids[0], heads)
    context = lax.all_to_all(
        context.reshape(n_seq, rows_dev, span), "seq", split_axis=0, concat_axis=0, tiled=True
    )
    offsets = [j * share - firsts[j] * HEAD_DIM for j in range(n_seq)]

    first = (lax.axis_index("exp") * (EXPERTS // n_exp)).astype(jnp.int32).reshape(1)
    w_gate, w_up = jnp.swapaxes(w_gate, 1, 2), jnp.swapaxes(w_up, 1, 2)
    gates = gate_weights[0]
    facts = jnp.concatenate([target, gates, gates, gates], axis=1)
    facts = jnp.pad(facts, ((0, 0), (0, 128 - facts.shape[1])))
    stream, piece = norm_tokens(context, residual[0], norm_gain, facts, share, offsets)

    slots = jnp.arange(group // PAGE, dtype=jnp.int32)
    order = jnp.sum(jnp.where(page_table[0][None, :] == slots[:, None], slots[None, :], 0), axis=1)

    def fill_cache(late):
        pages = pick_pages(packed, order, late, n_seq, span)
        sent = lax.all_to_all(pages, "seq", split_axis=0, concat_axis=0, tiled=True)
        return pages, lambda behind: join_pages(sent, share, offsets, span, behind)

    if (n_seq, n_exp) == (8, 4):
        mixture, cache = exchange_experts(piece, w_gate, w_up, w_down, n_seq, n_exp, fill_cache)
    else:
        cache, _ = fill_cache(piece)[1](piece)
        blocks = n_seq * n_exp
        everything = lax.all_gather(piece, everyone, axis=0, tiled=True)
        facts = everything[:, width : width + 8].astype(jnp.float32)
        facts = facts.reshape(blocks // CHUNK_BLOCKS, CHUNK_BLOCKS * rows_dev, 8).transpose(0, 2, 1)
        gates = facts[:, 2:4] + facts[:, 4:6] + facts[:, 6:8]
        partial = experts(
            everything[:, :width], facts[:, :2].astype(jnp.int32), gates, w_gate, w_up, w_down, first
        )
        mixture = lax.psum_scatter(partial, everyone, scatter_dimension=0, tiled=True).astype(jnp.float32)
    layer_out = (stream + mixture).astype(jnp.bfloat16)
    return (layer_out[None], cache.reshape(1, rows_dev // PAGE, PAGE, 2 * width))


def solution(mesh):
    in_specs = (
        P("exp", "seq", None),
        P("exp", "seq", None, None),
        P("exp", "seq", None),
        P(),
        P("exp", None),
        P("exp", "seq", None),
        P("exp", "seq", None),
        P("exp", None),
        P("exp", None, "seq"),
        P("exp", None, "seq"),
        P("exp", "seq", None),
    )
    out_specs = (P("exp", "seq", None), P("exp", "seq", None, None))
    run = functools.partial(body, mesh.shape["seq"], mesh.shape["exp"])
    return jax.shard_map(run, mesh=mesh, in_specs=in_specs, out_specs=out_specs, check_vma=False)
```

```python
import functools
import math

import jax
import jax.numpy as jnp
from jax import lax
from jax.experimental import pallas as pl
from jax.experimental.pallas import tpu as pltpu
from jax.sharding import PartitionSpec as P

HEADS = 36
HEAD_DIM = 64
EXPERTS = 8
PAGE = 16
CAP = 24
MIB = 1024 * 1024
CHUNK_BLOCKS = 8


def head_ranges(width, n_seq):
    share = width // n_seq
    firsts = [j * share // HEAD_DIM for j in range(n_seq)]
    count = max(-(-(j + 1) * share // HEAD_DIM) - firsts[j] for j in range(n_seq))
    firsts = [min(f, HEADS - count) for f in firsts]
    return share, firsts, count


def attention_kernel(heads, q_rows, packed_ref, seg_row_ref, seg_col_ref, out_ref):
    total = packed_ref.shape[0]
    span = heads * HEAD_DIM
    scale = 1.0 / math.sqrt(HEAD_DIM)
    for start in range(0, total, q_rows):
        end = start + q_rows
        q_place = start + lax.broadcasted_iota(jnp.int32, (q_rows, end), 0)
        k_place = lax.broadcasted_iota(jnp.int32, (q_rows, end), 1)
        visible = (seg_col_ref[start:end, :] == seg_row_ref[:, :end]) & (k_place <= q_place)
        parts = []
        for h in range(heads):
            a = h * HEAD_DIM
            q = packed_ref[start:end, a : a + HEAD_DIM]
            k = packed_ref[:end, span + a : span + a + HEAD_DIM]
            v = packed_ref[:end, 2 * span + a : 2 * span + a + HEAD_DIM]
            s = lax.dot_general(q, k, (((1,), (1,)), ((), ())), preferred_element_type=jnp.float32)
            s = jnp.where(visible, s * scale, -1e30)
            top = jnp.max(s, axis=1, keepdims=True)
            p = jnp.exp(s - top)
            denominator = jnp.sum(p, axis=1, keepdims=True)
            o = jnp.dot(p.astype(jnp.bfloat16), v, preferred_element_type=jnp.float32)
            parts.append((o / denominator).astype(jnp.bfloat16))
        out_ref[start:end, :] = jnp.concatenate(parts, axis=1)


def attention(packed, segments, heads):
    total = packed.shape[0]
    span = heads * HEAD_DIM
    return pl.pallas_call(
        functools.partial(attention_kernel, heads, 128),
        out_shape=jax.ShapeDtypeStruct((total, span), jnp.bfloat16),
        compiler_params=pltpu.CompilerParams(vmem_limit_bytes=24 * MIB),
        cost_estimate=pl.CostEstimate(
            flops=4 * total * total * span, bytes_accessed=8 * total * span, transcendentals=total * total * heads
        ),
    )(packed, segments[None, :], segments[:, None])


def dot_t(a, b):
    return lax.dot_general(a, b, (((1,), (1,)), ((), ())), preferred_element_type=jnp.float32)


def expert_kernel(
    local, rows, tokens, first_ref, x_ref, tgt_ref, gates_ref, wg_ref, wu_ref, wd_ref, out_ref, kept_ref
):
    le = pl.program_id(0)
    chunk = pl.program_id(1)

    def selection(which):
        base = (first_ref[0] + which) * CAP
        row_id = lax.broadcasted_iota(jnp.int32, (rows, tokens), 0)
        block = lax.broadcasted_iota(jnp.int32, (1, tokens), 1) // 64
        picks, weights = None, None
        for j in range(2):
            slot = tgt_ref[0, j : j + 1, :] - base
            place = jnp.where((slot >= 0) & (slot < CAP), block * CAP + slot, -1)
            hit = row_id == place
            gate = jnp.where(hit, gates_ref[0, j : j + 1, :], 0.0)
            picks = hit if picks is None else picks | hit
            weights = gate if weights is None else weights + gate
        return picks.astype(jnp.float32).astype(jnp.bfloat16), jnp.sum(weights, axis=1, keepdims=True)

    pick, weight = selection(le)
    chosen = jnp.dot(pick, x_ref[...], preferred_element_type=jnp.float32).astype(jnp.bfloat16)
    gate = dot_t(chosen, wg_ref[0])
    upper = dot_t(chosen, wu_ref[0])
    hidden = (gate / (1.0 + jnp.exp(-gate)) * upper).astype(jnp.bfloat16)
    y = jnp.dot(hidden, wd_ref[0], preferred_element_type=jnp.float32)
    y = (y * weight).astype(jnp.bfloat16)

    if local > 1:

        @pl.when(le < local - 1)
        def _():
            kept_ref[le, chunk] = y

    @pl.when(le == local - 1)
    def _():
        total = lax.dot_general(pick, y, (((0,), (0,)), ((), ())), preferred_element_type=jnp.float32)
        for other in range(local - 1):
            pick_o, _ = selection(other)
            total += lax.dot_general(
                pick_o, kept_ref[other, chunk], (((0,), (0,)), ((), ())), preferred_element_type=jnp.float32
            )
        out_ref[...] = total.astype(jnp.bfloat16)


def experts(x, tgt, gates, w_gate, w_up, w_down, first):
    local, hidden, width = w_gate.shape
    chunks, _, tokens = tgt.shape
    rows = tokens // 64 * CAP
    last = local - 1
    return pl.pallas_call(
        functools.partial(expert_kernel, local, rows, tokens),
        out_shape=jax.ShapeDtypeStruct(x.shape, jnp.bfloat16),
        grid=(local, chunks),
        in_specs=[
            pl.BlockSpec(memory_space=pltpu.SMEM),
            pl.BlockSpec((tokens, width), lambda e, c: (c, 0)),
            pl.BlockSpec((1, 2, tokens), lambda e, c: (c, 0, 0)),
            pl.BlockSpec((1, 2, tokens), lambda e, c: (c, 0, 0)),
            pl.BlockSpec((1, hidden, width), lambda e, c: (e, 0, 0)),
            pl.BlockSpec((1, hidden, width), lambda e, c: (e, 0, 0)),
            pl.BlockSpec((1, hidden, width), lambda e, c: (e, 0, 0)),
        ],
        out_specs=pl.BlockSpec((tokens, width), lambda e, c: (jnp.where(e == last, c, 0), 0)),
        scratch_shapes=[pltpu.VMEM((max(last, 1), chunks if last else 1, rows, width), jnp.bfloat16)],
        compiler_params=pltpu.CompilerParams(vmem_limit_bytes=58 * MIB),
        cost_estimate=pl.CostEstimate(
            flops=6 * local * chunks * rows * width * hidden,
            bytes_accessed=6 * local * width * hidden + 6 * chunks * tokens * width,
            transcendentals=local * chunks * rows * hidden,
        ),
    )(first, x, tgt, gates, w_gate, w_up, w_down)


def pack_kernel(firsts, span, q_ref, kv_ref, out_ref):
    keys, values = kv_ref[:, 0, :], kv_ref[:, 1, :]
    for j, first in enumerate(firsts):
        lanes = slice(first * HEAD_DIM, first * HEAD_DIM + span)
        out_ref[j] = jnp.concatenate([q_ref[:, lanes], keys[:, lanes], values[:, lanes]], axis=1)


def pack_heads(query, key_value, firsts, span):
    rows_dev = query.shape[0]
    n_seq = len(firsts)
    return pl.pallas_call(
        functools.partial(pack_kernel, firsts, span),
        out_shape=jax.ShapeDtypeStruct((n_seq, rows_dev, 3 * span), jnp.bfloat16),
        compiler_params=pltpu.CompilerParams(vmem_limit_bytes=12 * MIB),
        cost_estimate=pl.CostEstimate(flops=0, bytes_accessed=12 * n_seq * rows_dev * span, transcendentals=0),
    )(query, key_value)


def norm_kernel(share, offsets, context_ref, residual_ref, gain_ref, facts_ref, stream_ref, piece_ref):
    n_seq, _, _ = context_ref.shape
    width = residual_ref.shape[1]
    parts = [context_ref[j][:, offsets[j] : offsets[j] + share] for j in range(n_seq)]
    context = jnp.concatenate(parts, axis=1).astype(jnp.float32)
    stream = residual_ref[...].astype(jnp.float32) + context
    stream_ref[...] = stream
    mean = jnp.mean(stream * stream, axis=1, keepdims=True)
    normed = stream * lax.rsqrt(mean + 1e-05) * gain_ref[...].astype(jnp.float32)
    piece_ref[:, :width] = normed.astype(jnp.bfloat16)
    facts = facts_ref[...]
    lane = lax.broadcasted_iota(jnp.int32, facts.shape, 1)
    high = facts.astype(jnp.bfloat16).astype(jnp.float32)
    middle = (facts - high).astype(jnp.bfloat16).astype(jnp.float32)
    low = facts - high - middle
    own = jnp.where(lane < 4, high, jnp.where(lane < 6, middle, low))
    piece_ref[:, width:] = own.astype(jnp.bfloat16)


def norm_tokens(context, residual, gain, facts, share, offsets):
    rows_dev, width = residual.shape
    return pl.pallas_call(
        functools.partial(norm_kernel, share, offsets),
        out_shape=(
            jax.ShapeDtypeStruct((rows_dev, width), jnp.float32),
            jax.ShapeDtypeStruct((rows_dev, width + facts.shape[1]), jnp.bfloat16),
        ),
        compiler_params=pltpu.CompilerParams(vmem_limit_bytes=12 * MIB),
        cost_estimate=pl.CostEstimate(
            flops=10 * rows_dev * width, bytes_accessed=10 * rows_dev * width, transcendentals=rows_dev
        ),
    )(context, residual, gain[None, :], facts)


def pick_pages_kernel(per_device, first_lane, order_ref, packed_ref, late_ref, out_ref):
    del late_ref
    for j in range(out_ref.shape[0]):
        for i in range(per_device):
            rows = pl.ds(pl.multiple_of(order_ref[j * per_device + i] * PAGE, PAGE), PAGE)
            out_ref[j, i * PAGE : (i + 1) * PAGE, :] = packed_ref[rows, first_lane:]


def pick_pages(packed, order, late, n_seq, span):
    rows = packed.shape[0] // n_seq
    vmem = pl.BlockSpec(memory_space=pltpu.VMEM)
    return pl.pallas_call(
        functools.partial(pick_pages_kernel, rows // PAGE, span),
        out_shape=jax.ShapeDtypeStruct((n_seq, rows, 2 * span), jnp.bfloat16),
        in_specs=[pl.BlockSpec(memory_space=pltpu.SMEM), vmem, pl.BlockSpec(memory_space=pl.ANY)],
        compiler_params=pltpu.CompilerParams(vmem_limit_bytes=8 * MIB),
        cost_estimate=pl.CostEstimate(flops=0, bytes_accessed=10 * packed.shape[0] * span, transcendentals=0),
    )(order, packed, late)


def join_pages_kernel(share, offsets, span, pages_ref, behind_ref, out_ref, ended_ref):
    del behind_ref
    ended_ref[...] = jnp.zeros_like(ended_ref)
    width = share * len(offsets)
    for part in range(2):
        parts = [
            pages_ref[j][:, part * span + offsets[j] : part * span + offsets[j] + share]
            for j in range(len(offsets))
        ]
        out_ref[:, part * width : (part + 1) * width] = jnp.concatenate(parts, axis=1)


def join_pages(pages, share, offsets, span, behind):
    n_seq, rows, _ = pages.shape
    return pl.pallas_call(
        functools.partial(join_pages_kernel, share, offsets, span),
        out_shape=(
            jax.ShapeDtypeStruct((rows, 2 * share * n_seq), jnp.bfloat16),
            jax.ShapeDtypeStruct((8, 128), jnp.float32),
        ),
        in_specs=[pl.BlockSpec(memory_space=pltpu.VMEM), pl.BlockSpec(memory_space=pl.ANY)],
        compiler_params=pltpu.CompilerParams(vmem_limit_bytes=12 * MIB),
        cost_estimate=pl.CostEstimate(flops=0, bytes_accessed=8 * rows * n_seq * span, transcendentals=0),
    )(pages, behind)


def places_of(slots, base, shift):
    place = -1
    for slot in slots:
        slot = slot.astype(jnp.int32) - base
        place = jnp.where((slot >= 0) & (slot < CAP), shift + slot, place)
    return place


def hold_kernel(*refs):
    del refs


def hold(a, waits):
    anywhere = pl.BlockSpec(memory_space=pl.ANY)
    return pl.pallas_call(
        hold_kernel,
        out_shape=jax.ShapeDtypeStruct(a.shape, a.dtype),
        in_specs=[anywhere] * (1 + len(waits)),
        out_specs=anywhere,
        input_output_aliases={0: 0},
        compiler_params=pltpu.CompilerParams(vmem_limit_bytes=MIB),
        cost_estimate=pl.CostEstimate(flops=0, bytes_accessed=0, transcendentals=0),
    )(a, *waits)


def facts_by_lane(x):
    unit = lax.broadcasted_iota(jnp.int32, (8, 128), 0) == lax.broadcasted_iota(jnp.int32, (8, 128), 1)
    return dot_t(unit.astype(jnp.float32).astype(jnp.bfloat16), x)


def select_kernel(local, rows_dev, count, bases_ref, *refs):
    piece_refs, (own_ref, sib_ref, facts_ref) = refs[:count], refs[-3:]
    width = own_ref.shape[2]
    tokens, rows = 4 * rows_dev, 4 * CAP
    shift = lax.broadcasted_iota(jnp.int32, (1, tokens), 1) // rows_dev * CAP
    row_id = lax.broadcasted_iota(jnp.int32, (rows, tokens), 0)
    for g in range(len(piece_refs) // 4):
        x = jnp.concatenate([p[...] for p in piece_refs[4 * g : 4 * g + 4]], axis=0)
        facts_ref[g * tokens : (g + 1) * tokens, :] = x[:, width:]
        facts = facts_by_lane(x[:, width:])
        picks = []
        for core in range(2):
            for e in range(local):
                base = (bases_ref[core] + e) * CAP
                hit = row_id == places_of([facts[j : j + 1] for j in range(2)], base, shift)
                picks.append(hit.astype(jnp.float32))
        picks = jnp.concatenate(picks, axis=0).astype(jnp.bfloat16)
        chosen = jnp.dot(picks, x[:, :width], preferred_element_type=jnp.float32).astype(jnp.bfloat16)
        for e in range(local):
            own_ref[e, g * rows : (g + 1) * rows, :] = chosen[e * rows : (e + 1) * rows]
            sib_ref[e, g * rows : (g + 1) * rows, :] = chosen[(local + e) * rows : (local + e + 1) * rows]


def select_rows(pieces, bases, local, waits=()):
    rows_dev, wide = pieces[0].shape
    width = wide - 128
    rows = len(pieces) * CAP
    out = jax.ShapeDtypeStruct((local, rows, width), jnp.bfloat16)
    vmem = pl.BlockSpec(memory_space=pltpu.VMEM)
    return pl.pallas_call(
        functools.partial(select_kernel, local, rows_dev, len(pieces)),
        out_shape=(out, out, jax.ShapeDtypeStruct((len(pieces) * rows_dev, 128), jnp.bfloat16)),
        in_specs=[pl.BlockSpec(memory_space=pltpu.SMEM)]
        + [vmem] * len(pieces)
        + [pl.BlockSpec(memory_space=pl.ANY)] * len(waits),
        out_specs=(vmem, vmem, vmem),
        compiler_params=pltpu.CompilerParams(vmem_limit_bytes=20 * MIB),
        cost_estimate=pl.CostEstimate(
            flops=16 * local * CAP * rows_dev * len(pieces) * width,
            bytes_accessed=2 * len(pieces) * rows_dev * wide + 4 * local * rows * width,
            transcendentals=0,
        ),
    )(bases, *pieces, *waits)


def rows_kernel(local, waits, own_ref, got_ref, wg_hbm, wu_hbm, wd_hbm, *rest):
    y_own_ref, y_sib_ref, ended_ref, wg, wu, wd, weight_sem = rest[waits:]
    ended_ref[...] = jnp.zeros_like(ended_ref)
    half = got_ref.shape[1]
    copies = [
        pltpu.make_async_copy(source.at[e], target.at[e], weight_sem.at[3 * e + i])
        for e in range(local)
        for i, (source, target) in enumerate(((wg_hbm, wg), (wu_hbm, wu), (wd_hbm, wd)))
    ]
    for copy in copies[:2]:
        copy.start()

    def arrived(number):
        copies[number].wait()
        if number + 2 < len(copies):
            copies[number + 2].start()

    for e in range(local):
        rows = jnp.concatenate([own_ref[e], got_ref[e]], axis=0).T
        arrived(3 * e)
        gate = jnp.dot(wg[e], rows, preferred_element_type=jnp.float32)
        arrived(3 * e + 1)
        upper = jnp.dot(wu[e], rows, preferred_element_type=jnp.float32)
        hidden = (gate / (1.0 + jnp.exp(-gate)) * upper).T.astype(jnp.bfloat16)
        arrived(3 * e + 2)
        y = jnp.dot(hidden, wd[e], preferred_element_type=jnp.float32).astype(jnp.bfloat16)
        y_own_ref[e] = y[:half]
        y_sib_ref[e] = y[half:]


def expert_rows(own, got, w_gate, w_up, w_down, waits):
    local, hidden, width = w_gate.shape
    rows = 2 * own.shape[1]
    out = jax.ShapeDtypeStruct(own.shape, jnp.bfloat16)
    vmem = pl.BlockSpec(memory_space=pltpu.VMEM)
    weights = pltpu.VMEM((local, hidden, width), jnp.bfloat16)
    return pl.pallas_call(
        functools.partial(rows_kernel, local, len(waits)),
        out_shape=(out, out, jax.ShapeDtypeStruct((8, 128), jnp.float32)),
        in_specs=[vmem, vmem]
        + [pl.BlockSpec(memory_space=pl.ANY)] * (3 + len(waits)),
        out_specs=(vmem, vmem, vmem),
        scratch_shapes=[
            weights,
            weights,
            weights,
            pltpu.SemaphoreType.DMA((3 * local,)),
        ],
        compiler_params=pltpu.CompilerParams(vmem_limit_bytes=44 * MIB),
        cost_estimate=pl.CostEstimate(
            flops=6 * local * rows * width * hidden,
            bytes_accessed=6 * local * width * hidden + 4 * local * rows * width,
            transcendentals=local * rows * hidden,
        ),
    )(own, got, w_gate, w_up, w_down, *waits)


def put_kernel(local, rows_dev, planes, waits, bases_ref, y_own_ref, y_got_ref, facts_ref, *rest):
    kept_ref, *send_refs, ended_ref = rest[waits:]
    ended_ref[...] = jnp.zeros_like(ended_ref)
    tokens, rows = 4 * rows_dev, 4 * CAP
    total = 2 * local * rows
    shift = lax.broadcasted_iota(jnp.int32, (tokens, 1), 0) // rows_dev * CAP
    lane = lax.broadcasted_iota(jnp.int32, (tokens, total), 1)
    for g in range(planes):
        facts = facts_ref[g * tokens : (g + 1) * tokens, :].astype(jnp.float32)
        high, middle = jnp.zeros((tokens, total), jnp.float32), jnp.zeros((tokens, total), jnp.float32)
        for j in range(2):
            slot = facts[:, j : j + 1].astype(jnp.int32)
            place = jnp.full((tokens, 1), -1, jnp.int32)
            for core in range(2):
                for e in range(local):
                    near = slot - (bases_ref[core] + e) * CAP
                    here = shift + near + (core * local + e) * rows
                    place = jnp.where((near >= 0) & (near < CAP), here, place)
            hit = lane == place
            high = jnp.where(hit, facts[:, 2 + j : 3 + j], high)
            middle = jnp.where(hit, facts[:, 4 + j : 5 + j], middle)
        here = slice(g * rows, (g + 1) * rows)
        y = jnp.concatenate([ref[e, here, :] for ref in (y_own_ref, y_got_ref) for e in range(local)], axis=0)
        out = jnp.dot(high.astype(jnp.bfloat16), y, preferred_element_type=jnp.float32)
        out += jnp.dot(middle.astype(jnp.bfloat16), y, preferred_element_type=jnp.float32)
        out = out.astype(jnp.bfloat16)
        kept_ref[g * tokens // 2 : (g + 1) * tokens // 2, :] = out[: tokens // 2]
        send_refs[g][...] = out[tokens // 2 :]


def put_rows(y_own, y_got, facts, bases, rows_dev, waits):
    local, _, width = y_own.shape
    tokens = facts.shape[0]
    planes = tokens // (4 * rows_dev)
    vmem = pl.BlockSpec(memory_space=pltpu.VMEM)
    shape = lambda n: jax.ShapeDtypeStruct((n, width), jnp.bfloat16)
    out = pl.pallas_call(
        functools.partial(put_kernel, local, rows_dev, planes, len(waits)),
        out_shape=(shape(2 * planes * rows_dev),)
        + (shape(2 * rows_dev),) * planes
        + (jax.ShapeDtypeStruct((8, 128), jnp.float32),),
        in_specs=[pl.BlockSpec(memory_space=pltpu.SMEM), vmem, vmem, vmem]
        + [pl.BlockSpec(memory_space=pl.ANY)] * len(waits),
        out_specs=(vmem,) * (2 + planes),
        compiler_params=pltpu.CompilerParams(vmem_limit_bytes=20 * MIB),
        cost_estimate=pl.CostEstimate(
            flops=16 * local * CAP * tokens * width,
            bytes_accessed=8 * local * tokens * width,
            transcendentals=0,
        ),
    )(bases, y_own, y_got, facts, *waits)
    return out[0], out[1:-1], out[-1]


def swap(a, axis, size, distance):
    return lax.ppermute(a, axis, [(i, i ^ distance) for i in range(size)])


def fold_kernel(groups, count, waits, keep_ref, *rest):
    got_refs, (kept_ref, *send_refs) = rest[:count], rest[count + waits :]
    part = keep_ref.shape[0] // (2 * groups)
    span = got_refs[0].shape[0]
    for i in range(2 * groups):
        start = i * part
        got = got_refs[start // span][start % span : start % span + part, :]
        total = keep_ref[start : start + part, :].astype(jnp.float32) + got.astype(jnp.float32)
        total = total.astype(jnp.bfloat16)
        if i % 2 == 0:
            kept_ref[i // 2 * part : (i // 2 + 1) * part, :] = total
        else:
            send_refs[i // 2][...] = total


def fold(keep, gots, groups, waits=()):
    rows, width = keep.shape
    part = rows // (2 * groups)
    vmem = pl.BlockSpec(memory_space=pltpu.VMEM)
    shape = lambda n: jax.ShapeDtypeStruct((n, width), jnp.bfloat16)
    out = pl.pallas_call(
        functools.partial(fold_kernel, groups, len(gots), len(waits)),
        out_shape=(shape(groups * part),) + (shape(part),) * groups,
        in_specs=[vmem] * (1 + len(gots)) + [pl.BlockSpec(memory_space=pl.ANY)] * len(waits),
        out_specs=(vmem,) * (1 + groups),
        compiler_params=pltpu.CompilerParams(vmem_limit_bytes=10 * MIB),
        cost_estimate=pl.CostEstimate(flops=rows * width, bytes_accessed=6 * rows * width, transcendentals=0),
    )(keep, *gots, *waits)
    return out[0], out[1:]


def exchange_experts(piece, w_gate, w_up, w_down, n_seq, n_exp, late_work):
    x = lambda a: swap(a, "seq", n_seq, 1)
    y = lambda a: swap(a, "exp", n_exp, 2)
    core = lambda a: swap(a, "exp", n_exp, 1)
    z = lambda a, k: swap(a, "seq", n_seq, 2 * k)
    local = w_gate.shape[0]
    me = lax.axis_index("exp").astype(jnp.int32)
    bases = jnp.stack([me, me ^ 1]) * local
    starts = [piece, z(piece, 1), z(piece, 2)]
    ways = [("xy", "yx")[k % 2] for k in range(4)]
    over = {"x": x, "y": y}
    single = [[over[way](starts[k]) for way in ways[k]] for k in range(2)]
    starts[2] = hold(starts[2], single[0] + single[1])
    single.append([over[way](starts[2]) for way in ways[2]])

    def both(k):
        return over[ways[k][1]](single[k][0])

    double = [both(0), both(1)]
    starts.append(hold(z(starts[2], 1), double))
    single.append([over[way](starts[3]) for way in ways[3]])
    double += [both(2), both(3)]

    def gather(k):
        near = []
        for i in (k, k + 1):
            by_f, by_g = single[i]
            near += [starts[i], by_g, by_f, double[i]]
        return near

    near_b, near_a = gather(0), gather(2)
    own_a, sib_a, facts_a = select_rows(near_a, bases, local)
    got_a = core(sib_a)
    pages, fill = late_work(facts_a)
    own_b, sib_b, facts_b = select_rows(near_b, bases, local, [pages])
    got_b = core(sib_b)
    own_a, sib_a, ended = expert_rows(own_a, got_a, w_gate, w_up, w_down, [facts_b, pages])
    cache, filled = fill(ended)
    got_a = core(sib_a)
    own_b, sib_b, ended = expert_rows(own_b, got_b, w_gate, w_up, w_down, [filled])
    got_b = core(sib_b)
    keep_a, (fx_a, fy_a), _ = put_rows(own_a, got_a, facts_a, bases, piece.shape[0], [ended])
    keep_a, (gy_a, gx_a) = fold(keep_a, [x(fx_a), y(fy_a)], 2)
    keep_b, (fx_b, fy_b), put_b = put_rows(own_b, got_b, facts_b, bases, piece.shape[0], [gy_a])
    gy_a, gx_a = y(gy_a), x(gx_a)
    fx_b, fy_b = hold(fx_b, [gy_a, gx_a]), hold(fy_b, [gy_a, gx_a])
    keep_a, (z_a,) = fold(keep_a, [gy_a, gx_a], 1, [put_b])
    over_z = (keep_a.astype(jnp.float32) + z(z_a, 1).astype(jnp.float32)).astype(jnp.bfloat16)
    keep_b, (gy_b, gx_b) = fold(keep_b, [x(fx_b), y(fy_b)], 2, [over_z])
    back_a = z(over_z, 2)
    keep_b, (z_b,) = fold(keep_b, [y(gy_b), x(gx_b)], 1, [back_a])
    mine = keep_b.astype(jnp.float32) + z(z_b, 1).astype(jnp.float32)
    return mine + back_a.astype(jnp.float32), cache


def body(
    n_seq,
    n_exp,
    query,
    key_value,
    residual,
    norm_gain,
    segment_ids,
    routes,
    gate_weights,
    page_table,
    w_gate,
    w_up,
    w_down,
):
    rows_dev, width = query.shape[1:]
    everyone = ("exp", "seq")
    group = segment_ids.shape[1]
    share, firsts, heads = head_ranges(width, n_seq)
    span = heads * HEAD_DIM

    flat = routes[0].reshape(rows_dev * 2)
    onehot = (flat[:, None] == jnp.arange(EXPERTS, dtype=jnp.int32)[None, :]).astype(jnp.int32)
    before = jnp.cumsum(onehot, axis=0) - onehot
    target = (flat * CAP + jnp.sum(before * onehot, axis=1)).reshape(rows_dev, 2).astype(jnp.float32)


    packed = pack_heads(query[0], key_value[0], firsts, span)
    packed = lax.all_to_all(packed, "seq", split_axis=0, concat_axis=0, tiled=True)
    packed = packed.reshape(group, 3 * span)
    context = attention(packed, segment_ids[0], heads)
    context = lax.all_to_all(
        context.reshape(n_seq, rows_dev, span), "seq", split_axis=0, concat_axis=0, tiled=True
    )
    offsets = [j * share - firsts[j] * HEAD_DIM for j in range(n_seq)]

    first = (lax.axis_index("exp") * (EXPERTS // n_exp)).astype(jnp.int32).reshape(1)
    w_gate, w_up = jnp.swapaxes(w_gate, 1, 2), jnp.swapaxes(w_up, 1, 2)
    gates = gate_weights[0]
    facts = jnp.concatenate([target, gates, gates, gates], axis=1)
    facts = jnp.pad(facts, ((0, 0), (0, 128 - facts.shape[1])))
    stream, piece = norm_tokens(context, residual[0], norm_gain, facts, share, offsets)

    slots = jnp.arange(group // PAGE, dtype=jnp.int32)
    order = jnp.sum(jnp.where(page_table[0][None, :] == slots[:, None], slots[None, :], 0), axis=1)

    def fill_cache(late):
        pages = pick_pages(packed, order, late, n_seq, span)
        sent = lax.all_to_all(pages, "seq", split_axis=0, concat_axis=0, tiled=True)
        return pages, lambda behind: join_pages(sent, share, offsets, span, behind)

    if (n_seq, n_exp) == (8, 4):
        mixture, cache = exchange_experts(piece, w_gate, w_up, w_down, n_seq, n_exp, fill_cache)
    else:
        cache, _ = fill_cache(piece)[1](piece)
        blocks = n_seq * n_exp
        everything = lax.all_gather(piece, everyone, axis=0, tiled=True)
        facts = everything[:, width : width + 8].astype(jnp.float32)
        facts = facts.reshape(blocks // CHUNK_BLOCKS, CHUNK_BLOCKS * rows_dev, 8).transpose(0, 2, 1)
        gates = facts[:, 2:4] + facts[:, 4:6] + facts[:, 6:8]
        partial = experts(
            everything[:, :width], facts[:, :2].astype(jnp.int32), gates, w_gate, w_up, w_down, first
        )
        mixture = lax.psum_scatter(partial, everyone, scatter_dimension=0, tiled=True).astype(jnp.float32)
    layer_out = (stream + mixture).astype(jnp.bfloat16)
    return (layer_out[None], cache.reshape(1, rows_dev // PAGE, PAGE, 2 * width))


def solution(mesh):
    in_specs = (
        P("exp", "seq", None),
        P("exp", "seq", None, None),
        P("exp", "seq", None),
        P(),
        P("exp", None),
        P("exp", "seq", None),
        P("exp", "seq", None),
        P("exp", None),
        P("exp", None, "seq"),
        P("exp", None, "seq"),
        P("exp", "seq", None),
    )
    out_specs = (P("exp", "seq", None), P("exp", "seq", None, None))
    run = functools.partial(body, mesh.shape["seq"], mesh.shape["exp"])
    return jax.shard_map(run, mesh=mesh, in_specs=in_specs, out_specs=out_specs, check_vma=False)
```

```python
import functools
import math

import jax
import jax.numpy as jnp
from jax import lax
from jax.experimental import pallas as pl
from jax.experimental.pallas import tpu as pltpu
from jax.sharding import PartitionSpec as P

HEADS = 36
HEAD_DIM = 64
EXPERTS = 8
PAGE = 16
CAP = 24
MIB = 1024 * 1024
CHUNK_BLOCKS = 8


def head_ranges(width, n_seq):
    share = width // n_seq
    firsts = [j * share // HEAD_DIM for j in range(n_seq)]
    count = max(-(-(j + 1) * share // HEAD_DIM) - firsts[j] for j in range(n_seq))
    firsts = [min(f, HEADS - count) for f in firsts]
    return share, firsts, count


def attention_kernel(heads, q_rows, packed_ref, seg_row_ref, seg_col_ref, out_ref):
    total = packed_ref.shape[0]
    span = heads * HEAD_DIM
    scale = jnp.bfloat16(1.0 / math.sqrt(HEAD_DIM))
    for start in range(0, total, q_rows):
        end = start + q_rows
        q_place = start + lax.broadcasted_iota(jnp.int32, (q_rows, end), 0)
        k_place = lax.broadcasted_iota(jnp.int32, (q_rows, end), 1)
        visible = (seg_col_ref[start:end, :] == seg_row_ref[:, :end]) & (k_place <= q_place)
        parts = []
        for h in range(heads):
            a = h * HEAD_DIM
            q = packed_ref[start:end, a : a + HEAD_DIM] * scale
            k = packed_ref[:end, span + a : span + a + HEAD_DIM]
            v = packed_ref[:end, 2 * span + a : 2 * span + a + HEAD_DIM]
            s = lax.dot_general(q, k, (((1,), (1,)), ((), ())), preferred_element_type=jnp.float32)
            s = jnp.where(visible, s, -1e30)
            top = jnp.max(s, axis=1, keepdims=True)
            p = jnp.exp(s - top)
            denominator = jnp.sum(p, axis=1, keepdims=True)
            o = jnp.dot(p.astype(jnp.bfloat16), v, preferred_element_type=jnp.float32)
            parts.append((o / denominator).astype(jnp.bfloat16))
        out_ref[start:end, :] = jnp.concatenate(parts, axis=1)


def attention(packed, segments, heads):
    total = packed.shape[0]
    span = heads * HEAD_DIM
    return pl.pallas_call(
        functools.partial(attention_kernel, heads, 128),
        out_shape=jax.ShapeDtypeStruct((total, span), jnp.bfloat16),
        compiler_params=pltpu.CompilerParams(vmem_limit_bytes=24 * MIB),
        cost_estimate=pl.CostEstimate(
            flops=4 * total * total * span, bytes_accessed=8 * total * span, transcendentals=total * total * heads
        ),
    )(packed, segments[None, :], segments[:, None])


def dot_t(a, b):
    return lax.dot_general(a, b, (((1,), (1,)), ((), ())), preferred_element_type=jnp.float32)


def expert_kernel(
    local, rows, tokens, first_ref, x_ref, tgt_ref, gates_ref, wg_ref, wu_ref, wd_ref, out_ref, kept_ref
):
    le = pl.program_id(0)
    chunk = pl.program_id(1)

    def selection(which):
        base = (first_ref[0] + which) * CAP
        row_id = lax.broadcasted_iota(jnp.int32, (rows, tokens), 0)
        block = lax.broadcasted_iota(jnp.int32, (1, tokens), 1) // 64
        picks, weights = None, None
        for j in range(2):
            slot = tgt_ref[0, j : j + 1, :] - base
            place = jnp.where((slot >= 0) & (slot < CAP), block * CAP + slot, -1)
            hit = row_id == place
            gate = jnp.where(hit, gates_ref[0, j : j + 1, :], 0.0)
            picks = hit if picks is None else picks | hit
            weights = gate if weights is None else weights + gate
        return picks.astype(jnp.float32).astype(jnp.bfloat16), jnp.sum(weights, axis=1, keepdims=True)

    pick, weight = selection(le)
    chosen = jnp.dot(pick, x_ref[...], preferred_element_type=jnp.float32).astype(jnp.bfloat16)
    gate = dot_t(chosen, wg_ref[0])
    upper = dot_t(chosen, wu_ref[0])
    hidden = (gate / (1.0 + jnp.exp(-gate)) * upper).astype(jnp.bfloat16)
    y = jnp.dot(hidden, wd_ref[0], preferred_element_type=jnp.float32)
    y = (y * weight).astype(jnp.bfloat16)

    if local > 1:

        @pl.when(le < local - 1)
        def _():
            kept_ref[le, chunk] = y

    @pl.when(le == local - 1)
    def _():
        total = lax.dot_general(pick, y, (((0,), (0,)), ((), ())), preferred_element_type=jnp.float32)
        for other in range(local - 1):
            pick_o, _ = selection(other)
            total += lax.dot_general(
                pick_o, kept_ref[other, chunk], (((0,), (0,)), ((), ())), preferred_element_type=jnp.float32
            )
        out_ref[...] = total.astype(jnp.bfloat16)


def experts(x, tgt, gates, w_gate, w_up, w_down, first):
    local, hidden, width = w_gate.shape
    chunks, _, tokens = tgt.shape
    rows = tokens // 64 * CAP
    last = local - 1
    return pl.pallas_call(
        functools.partial(expert_kernel, local, rows, tokens),
        out_shape=jax.ShapeDtypeStruct(x.shape, jnp.bfloat16),
        grid=(local, chunks),
        in_specs=[
            pl.BlockSpec(memory_space=pltpu.SMEM),
            pl.BlockSpec((tokens, width), lambda e, c: (c, 0)),
            pl.BlockSpec((1, 2, tokens), lambda e, c: (c, 0, 0)),
            pl.BlockSpec((1, 2, tokens), lambda e, c: (c, 0, 0)),
            pl.BlockSpec((1, hidden, width), lambda e, c: (e, 0, 0)),
            pl.BlockSpec((1, hidden, width), lambda e, c: (e, 0, 0)),
            pl.BlockSpec((1, hidden, width), lambda e, c: (e, 0, 0)),
        ],
        out_specs=pl.BlockSpec((tokens, width), lambda e, c: (jnp.where(e == last, c, 0), 0)),
        scratch_shapes=[pltpu.VMEM((max(last, 1), chunks if last else 1, rows, width), jnp.bfloat16)],
        compiler_params=pltpu.CompilerParams(vmem_limit_bytes=58 * MIB),
        cost_estimate=pl.CostEstimate(
            flops=6 * local * chunks * rows * width * hidden,
            bytes_accessed=6 * local * width * hidden + 6 * chunks * tokens * width,
            transcendentals=local * chunks * rows * hidden,
        ),
    )(first, x, tgt, gates, w_gate, w_up, w_down)


def pack_kernel(firsts, span, q_ref, k_ref, v_ref, out_ref):
    for j, first in enumerate(firsts):
        lanes = slice(first * HEAD_DIM, first * HEAD_DIM + span)
        out_ref[j] = jnp.concatenate([r[:, lanes] for r in (q_ref, k_ref, v_ref)], axis=1)


def pack_heads(query, keys, values, firsts, span):
    rows_dev = query.shape[0]
    n_seq = len(firsts)
    return pl.pallas_call(
        functools.partial(pack_kernel, firsts, span),
        out_shape=jax.ShapeDtypeStruct((n_seq, rows_dev, 3 * span), jnp.bfloat16),
        compiler_params=pltpu.CompilerParams(vmem_limit_bytes=12 * MIB),
        cost_estimate=pl.CostEstimate(flops=0, bytes_accessed=12 * n_seq * rows_dev * span, transcendentals=0),
    )(query, keys, values)


def norm_kernel(share, offsets, context_ref, residual_ref, gain_ref, facts_ref, stream_ref, piece_ref):
    n_seq, _, _ = context_ref.shape
    width = residual_ref.shape[1]
    parts = [context_ref[j][:, offsets[j] : offsets[j] + share] for j in range(n_seq)]
    context = jnp.concatenate(parts, axis=1).astype(jnp.float32)
    stream = residual_ref[...].astype(jnp.float32) + context
    stream_ref[...] = stream
    mean = jnp.mean(stream * stream, axis=1, keepdims=True)
    normed = stream * lax.rsqrt(mean + 1e-05) * gain_ref[...].astype(jnp.float32)
    piece_ref[:, :width] = normed.astype(jnp.bfloat16)
    facts = facts_ref[...]
    lane = lax.broadcasted_iota(jnp.int32, facts.shape, 1)
    high = facts.astype(jnp.bfloat16).astype(jnp.float32)
    middle = (facts - high).astype(jnp.bfloat16).astype(jnp.float32)
    low = facts - high - middle
    own = jnp.where(lane < 4, high, jnp.where(lane < 6, middle, low))
    piece_ref[:, width:] = own.astype(jnp.bfloat16)


def norm_tokens(context, residual, gain, facts, share, offsets):
    rows_dev, width = residual.shape
    return pl.pallas_call(
        functools.partial(norm_kernel, share, offsets),
        out_shape=(
            jax.ShapeDtypeStruct((rows_dev, width), jnp.float32),
            jax.ShapeDtypeStruct((rows_dev, width + facts.shape[1]), jnp.bfloat16),
        ),
        compiler_params=pltpu.CompilerParams(vmem_limit_bytes=12 * MIB),
        cost_estimate=pl.CostEstimate(
            flops=10 * rows_dev * width, bytes_accessed=10 * rows_dev * width, transcendentals=rows_dev
        ),
    )(context, residual, gain[None, :], facts)


def pick_pages_kernel(per_device, first_lane, order_ref, packed_ref, late_ref, out_ref):
    del late_ref
    for j in range(out_ref.shape[0]):
        for i in range(per_device):
            rows = pl.ds(pl.multiple_of(order_ref[j * per_device + i] * PAGE, PAGE), PAGE)
            out_ref[j, i * PAGE : (i + 1) * PAGE, :] = packed_ref[rows, first_lane:]


def pick_pages(packed, order, late, n_seq, span):
    rows = packed.shape[0] // n_seq
    vmem = pl.BlockSpec(memory_space=pltpu.VMEM)
    return pl.pallas_call(
        functools.partial(pick_pages_kernel, rows // PAGE, span),
        out_shape=jax.ShapeDtypeStruct((n_seq, rows, 2 * span), jnp.bfloat16),
        in_specs=[pl.BlockSpec(memory_space=pltpu.SMEM), vmem, pl.BlockSpec(memory_space=pl.ANY)],
        compiler_params=pltpu.CompilerParams(vmem_limit_bytes=8 * MIB),
        cost_estimate=pl.CostEstimate(flops=0, bytes_accessed=10 * packed.shape[0] * span, transcendentals=0),
    )(order, packed, late)


def join_pages_kernel(share, offsets, span, pages_ref, behind_ref, out_ref, ended_ref):
    del behind_ref
    ended_ref[...] = jnp.zeros_like(ended_ref)
    width = share * len(offsets)
    for part in range(2):
        parts = [
            pages_ref[j][:, part * span + offsets[j] : part * span + offsets[j] + share]
            for j in range(len(offsets))
        ]
        out_ref[:, part * width : (part + 1) * width] = jnp.concatenate(parts, axis=1)


def join_pages(pages, share, offsets, span, behind):
    n_seq, rows, _ = pages.shape
    return pl.pallas_call(
        functools.partial(join_pages_kernel, share, offsets, span),
        out_shape=(
            jax.ShapeDtypeStruct((rows, 2 * share * n_seq), jnp.bfloat16),
            jax.ShapeDtypeStruct((8, 128), jnp.float32),
        ),
        in_specs=[pl.BlockSpec(memory_space=pltpu.VMEM), pl.BlockSpec(memory_space=pl.ANY)],
        compiler_params=pltpu.CompilerParams(vmem_limit_bytes=12 * MIB),
        cost_estimate=pl.CostEstimate(flops=0, bytes_accessed=8 * rows * n_seq * span, transcendentals=0),
    )(pages, behind)


def places_of(slots, base, shift):
    place = -1
    for slot in slots:
        slot = slot.astype(jnp.int32) - base
        place = jnp.where((slot >= 0) & (slot < CAP), shift + slot, place)
    return place


def hold_kernel(*refs):
    del refs


def hold(a, waits):
    anywhere = pl.BlockSpec(memory_space=pl.ANY)
    return pl.pallas_call(
        hold_kernel,
        out_shape=jax.ShapeDtypeStruct(a.shape, a.dtype),
        in_specs=[anywhere] * (1 + len(waits)),
        out_specs=anywhere,
        input_output_aliases={0: 0},
        compiler_params=pltpu.CompilerParams(vmem_limit_bytes=MIB),
        cost_estimate=pl.CostEstimate(flops=0, bytes_accessed=0, transcendentals=0),
    )(a, *waits)


def facts_by_lane(x):
    unit = lax.broadcasted_iota(jnp.int32, (8, 128), 0) == lax.broadcasted_iota(jnp.int32, (8, 128), 1)
    return dot_t(unit.astype(jnp.float32).astype(jnp.bfloat16), x)


def select_kernel(local, rows_dev, count, bases_ref, *refs):
    piece_refs, (own_ref, sib_ref, facts_ref) = refs[:count], refs[-3:]
    width = own_ref.shape[2]
    tokens, rows = 4 * rows_dev, 4 * CAP
    shift = lax.broadcasted_iota(jnp.int32, (1, tokens), 1) // rows_dev * CAP
    row_id = lax.broadcasted_iota(jnp.int32, (rows, tokens), 0)
    for g in range(len(piece_refs) // 4):
        x = jnp.concatenate([p[...] for p in piece_refs[4 * g : 4 * g + 4]], axis=0)
        facts_ref[g * tokens : (g + 1) * tokens, :] = x[:, width:]
        facts = facts_by_lane(x[:, width:])
        picks = []
        for core in range(2):
            for e in range(local):
                base = (bases_ref[core] + e) * CAP
                hit = row_id == places_of([facts[j : j + 1] for j in range(2)], base, shift)
                picks.append(hit.astype(jnp.float32))
        picks = jnp.concatenate(picks, axis=0).astype(jnp.bfloat16)
        chosen = jnp.dot(picks, x[:, :width], preferred_element_type=jnp.float32).astype(jnp.bfloat16)
        for e in range(local):
            own_ref[e, g * rows : (g + 1) * rows, :] = chosen[e * rows : (e + 1) * rows]
            sib_ref[e, g * rows : (g + 1) * rows, :] = chosen[(local + e) * rows : (local + e + 1) * rows]


def select_rows(pieces, bases, local, waits=()):
    rows_dev, wide = pieces[0].shape
    width = wide - 128
    rows = len(pieces) * CAP
    out = jax.ShapeDtypeStruct((local, rows, width), jnp.bfloat16)
    vmem = pl.BlockSpec(memory_space=pltpu.VMEM)
    return pl.pallas_call(
        functools.partial(select_kernel, local, rows_dev, len(pieces)),
        out_shape=(out, out, jax.ShapeDtypeStruct((len(pieces) * rows_dev, 128), jnp.bfloat16)),
        in_specs=[pl.BlockSpec(memory_space=pltpu.SMEM)]
        + [vmem] * len(pieces)
        + [pl.BlockSpec(memory_space=pl.ANY)] * len(waits),
        out_specs=(vmem, vmem, vmem),
        compiler_params=pltpu.CompilerParams(vmem_limit_bytes=20 * MIB),
        cost_estimate=pl.CostEstimate(
            flops=16 * local * CAP * rows_dev * len(pieces) * width,
            bytes_accessed=2 * len(pieces) * rows_dev * wide + 4 * local * rows * width,
            transcendentals=0,
        ),
    )(bases, *pieces, *waits)


def rows_kernel(local, waits, own_ref, got_ref, wg_hbm, wu_hbm, wd_hbm, *rest):
    y_own_ref, y_sib_ref, ended_ref, wg, wu, wd, weight_sem = rest[waits:]
    ended_ref[...] = jnp.zeros_like(ended_ref)
    half = got_ref.shape[1]
    copies = [
        [
            pltpu.make_async_copy(source.at[e], target.at[e], weight_sem.at[3 * e + i])
            for i, (source, target) in enumerate(((wg_hbm, wg), (wu_hbm, wu), (wd_hbm, wd)))
        ]
        for e in range(local)
    ]
    for group in copies:
        for copy in group:
            copy.start()
    for e in range(local):
        rows = jnp.concatenate([own_ref[e], got_ref[e]], axis=0)
        copies[e][0].wait()
        gate = dot_t(rows, wg[e])
        copies[e][1].wait()
        upper = dot_t(rows, wu[e])
        hidden = (gate / (1.0 + jnp.exp(-gate)) * upper).astype(jnp.bfloat16)
        copies[e][2].wait()
        y = jnp.dot(hidden, wd[e], preferred_element_type=jnp.float32).astype(jnp.bfloat16)
        y_own_ref[e] = y[:half]
        y_sib_ref[e] = y[half:]


def expert_rows(own, got, w_gate, w_up, w_down, waits):
    local, hidden, width = w_gate.shape
    rows = 2 * own.shape[1]
    out = jax.ShapeDtypeStruct(own.shape, jnp.bfloat16)
    vmem = pl.BlockSpec(memory_space=pltpu.VMEM)
    weights = pltpu.VMEM((local, hidden, width), jnp.bfloat16)
    return pl.pallas_call(
        functools.partial(rows_kernel, local, len(waits)),
        out_shape=(out, out, jax.ShapeDtypeStruct((8, 128), jnp.float32)),
        in_specs=[vmem, vmem]
        + [pl.BlockSpec(memory_space=pl.ANY)] * (3 + len(waits)),
        out_specs=(vmem, vmem, vmem),
        scratch_shapes=[
            weights,
            weights,
            weights,
            pltpu.SemaphoreType.DMA((3 * local,)),
        ],
        compiler_params=pltpu.CompilerParams(vmem_limit_bytes=44 * MIB),
        cost_estimate=pl.CostEstimate(
            flops=6 * local * rows * width * hidden,
            bytes_accessed=6 * local * width * hidden + 4 * local * rows * width,
            transcendentals=local * rows * hidden,
        ),
    )(own, got, w_gate, w_up, w_down, *waits)


def put_kernel(local, rows_dev, planes, waits, bases_ref, y_own_ref, y_got_ref, facts_ref, *rest):
    kept_ref, *send_refs, ended_ref = rest[waits:]
    ended_ref[...] = jnp.zeros_like(ended_ref)
    tokens, rows = 4 * rows_dev, 4 * CAP
    total = 2 * local * rows
    shift_lane = lax.broadcasted_iota(jnp.int32, (1, tokens), 1) // rows_dev * CAP
    shift_row = lax.broadcasted_iota(jnp.int32, (tokens, 1), 0) // rows_dev * CAP
    row_id = lax.broadcasted_iota(jnp.int32, (rows, tokens), 0)
    lane = lax.broadcasted_iota(jnp.int32, (tokens, total), 1)
    for g in range(planes):
        facts = facts_ref[g * tokens : (g + 1) * tokens, :]
        by_lane = facts_by_lane(facts)
        by_row = facts.astype(jnp.float32)
        here = slice(g * rows, (g + 1) * rows)
        weighed, put = [], None
        for core, y_ref in enumerate((y_own_ref, y_got_ref)):
            for e in range(local):
                base = (bases_ref[core] + e) * CAP
                weight = jnp.zeros((rows, tokens), jnp.float32)
                for j in range(2):
                    hit = row_id == places_of([by_lane[j : j + 1]], base, shift_lane)
                    gate = by_lane[2 + j : 3 + j] + by_lane[4 + j : 5 + j] + by_lane[6 + j : 7 + j]
                    weight = weight + jnp.where(hit, gate, 0.0)
                weight = jnp.sum(weight, axis=1, keepdims=True)
                weighed.append((y_ref[e, here, :].astype(jnp.float32) * weight).astype(jnp.bfloat16))
                first = (core * local + e) * rows
                hit = lane == places_of([by_row[:, j : j + 1] for j in range(2)], base, shift_row + first)
                put = hit if put is None else put | hit
        put = put.astype(jnp.float32).astype(jnp.bfloat16)
        out = jnp.dot(put, jnp.concatenate(weighed, axis=0), preferred_element_type=jnp.float32)
        out = out.astype(jnp.bfloat16)
        kept_ref[g * tokens // 2 : (g + 1) * tokens // 2, :] = out[: tokens // 2]
        send_refs[g][...] = out[tokens // 2 :]


def put_rows(y_own, y_got, facts, bases, rows_dev, waits):
    local, _, width = y_own.shape
    tokens = facts.shape[0]
    planes = tokens // (4 * rows_dev)
    vmem = pl.BlockSpec(memory_space=pltpu.VMEM)
    shape = lambda n: jax.ShapeDtypeStruct((n, width), jnp.bfloat16)
    out = pl.pallas_call(
        functools.partial(put_kernel, local, rows_dev, planes, len(waits)),
        out_shape=(shape(2 * planes * rows_dev),)
        + (shape(2 * rows_dev),) * planes
        + (jax.ShapeDtypeStruct((8, 128), jnp.float32),),
        in_specs=[pl.BlockSpec(memory_space=pltpu.SMEM), vmem, vmem, vmem]
        + [pl.BlockSpec(memory_space=pl.ANY)] * len(waits),
        out_specs=(vmem,) * (2 + planes),
        compiler_params=pltpu.CompilerParams(vmem_limit_bytes=20 * MIB),
        cost_estimate=pl.CostEstimate(
            flops=16 * local * CAP * tokens * width,
            bytes_accessed=8 * local * tokens * width,
            transcendentals=0,
        ),
    )(bases, y_own, y_got, facts, *waits)
    return out[0], out[1:-1], out[-1]


def swap(a, axis, size, distance):
    return lax.ppermute(a, axis, [(i, i ^ distance) for i in range(size)])


def fold_kernel(groups, count, waits, keep_ref, *rest):
    got_refs, (kept_ref, *send_refs) = rest[:count], rest[count + waits :]
    part = keep_ref.shape[0] // (2 * groups)
    span = got_refs[0].shape[0]
    for i in range(2 * groups):
        start = i * part
        got = got_refs[start // span][start % span : start % span + part, :]
        total = keep_ref[start : start + part, :].astype(jnp.float32) + got.astype(jnp.float32)
        total = total.astype(jnp.bfloat16)
        if i % 2 == 0:
            kept_ref[i // 2 * part : (i // 2 + 1) * part, :] = total
        else:
            send_refs[i // 2][...] = total


def fold(keep, gots, groups, waits=()):
    rows, width = keep.shape
    part = rows // (2 * groups)
    vmem = pl.BlockSpec(memory_space=pltpu.VMEM)
    shape = lambda n: jax.ShapeDtypeStruct((n, width), jnp.bfloat16)
    out = pl.pallas_call(
        functools.partial(fold_kernel, groups, len(gots), len(waits)),
        out_shape=(shape(groups * part),) + (shape(part),) * groups,
        in_specs=[vmem] * (1 + len(gots)) + [pl.BlockSpec(memory_space=pl.ANY)] * len(waits),
        out_specs=(vmem,) * (1 + groups),
        compiler_params=pltpu.CompilerParams(vmem_limit_bytes=10 * MIB),
        cost_estimate=pl.CostEstimate(flops=rows * width, bytes_accessed=6 * rows * width, transcendentals=0),
    )(keep, *gots, *waits)
    return out[0], out[1:]


def exchange_experts(piece, w_gate, w_up, w_down, n_seq, n_exp, late_work):
    x = lambda a: swap(a, "seq", n_seq, 1)
    y = lambda a: swap(a, "exp", n_exp, 2)
    core = lambda a: swap(a, "exp", n_exp, 1)
    z = lambda a, k: swap(a, "seq", n_seq, 2 * k)
    local = w_gate.shape[0]
    me = lax.axis_index("exp").astype(jnp.int32)
    bases = jnp.stack([me, me ^ 1]) * local
    starts = [piece, z(piece, 1), z(piece, 2)]
    ways = [("xy", "yx")[k % 2] for k in range(4)]
    over = {"x": x, "y": y}
    single = [[over[way](starts[k]) for way in ways[k]] for k in range(2)]
    starts[2] = hold(starts[2], single[0] + single[1])
    single.append([over[way](starts[2]) for way in ways[2]])

    def both(k):
        return over[ways[k][1]](single[k][0])

    double = [both(0), both(1)]
    starts.append(hold(z(starts[2], 1), double))
    single.append([over[way](starts[3]) for way in ways[3]])
    double += [both(2), both(3)]

    def gather(k):
        near = []
        for i in (k, k + 1):
            by_f, by_g = single[i]
            near += [starts[i], by_g, by_f, double[i]]
        return near

    near_b, near_a = gather(0), gather(2)
    own_a, sib_a, facts_a = select_rows(near_a, bases, local)
    got_a = core(sib_a)
    pages, fill = late_work(facts_a)
    own_b, sib_b, facts_b = select_rows(near_b, bases, local, [pages])
    got_b = core(sib_b)
    own_a, sib_a, ended = expert_rows(own_a, got_a, w_gate, w_up, w_down, [facts_b, pages])
    cache, filled = fill(ended)
    got_a = core(sib_a)
    own_b, sib_b, ended = expert_rows(own_b, got_b, w_gate, w_up, w_down, [ended])
    got_b = core(sib_b)
    keep_a, (fx_a, fy_a), _ = put_rows(own_a, got_a, facts_a, bases, piece.shape[0], [ended])
    keep_a, (gy_a, gx_a) = fold(keep_a, [x(fx_a), y(fy_a)], 2, [filled])
    keep_b, (fx_b, fy_b), put_b = put_rows(own_b, got_b, facts_b, bases, piece.shape[0], [gy_a])
    gy_a, gx_a = y(gy_a), x(gx_a)
    fx_b, fy_b = hold(fx_b, [gy_a, gx_a]), hold(fy_b, [gy_a, gx_a])
    keep_a, (z_a,) = fold(keep_a, [gy_a, gx_a], 1, [put_b])
    over_z = (keep_a.astype(jnp.float32) + z(z_a, 1).astype(jnp.float32)).astype(jnp.bfloat16)
    keep_b, (gy_b, gx_b) = fold(keep_b, [x(fx_b), y(fy_b)], 2, [over_z])
    back_a = z(over_z, 2)
    keep_b, (z_b,) = fold(keep_b, [y(gy_b), x(gx_b)], 1, [back_a])
    mine = keep_b.astype(jnp.float32) + z(z_b, 1).astype(jnp.float32)
    return mine + back_a.astype(jnp.float32), cache


def body(
    n_seq,
    n_exp,
    query,
    key_value,
    residual,
    norm_gain,
    segment_ids,
    routes,
    gate_weights,
    page_table,
    w_gate,
    w_up,
    w_down,
):
    rows_dev, width = query.shape[1:]
    everyone = ("exp", "seq")
    group = segment_ids.shape[1]
    share, firsts, heads = head_ranges(width, n_seq)
    span = heads * HEAD_DIM

    flat = routes[0].reshape(rows_dev * 2)
    onehot = (flat[:, None] == jnp.arange(EXPERTS, dtype=jnp.int32)[None, :]).astype(jnp.int32)
    before = jnp.cumsum(onehot, axis=0) - onehot
    target = (flat * CAP + jnp.sum(before * onehot, axis=1)).reshape(rows_dev, 2).astype(jnp.float32)

    keys, values = key_value[0, :, 0], key_value[0, :, 1]

    packed = pack_heads(query[0], keys, values, firsts, span)
    packed = lax.all_to_all(packed, "seq", split_axis=0, concat_axis=0, tiled=True)
    packed = packed.reshape(group, 3 * span)
    context = attention(packed, segment_ids[0], heads)
    context = lax.all_to_all(
        context.reshape(n_seq, rows_dev, span), "seq", split_axis=0, concat_axis=0, tiled=True
    )
    offsets = [j * share - firsts[j] * HEAD_DIM for j in range(n_seq)]

    first = (lax.axis_index("exp") * (EXPERTS // n_exp)).astype(jnp.int32).reshape(1)
    w_gate, w_up = jnp.swapaxes(w_gate, 1, 2), jnp.swapaxes(w_up, 1, 2)
    gates = gate_weights[0]
    facts = jnp.concatenate([target, gates, gates, gates], axis=1)
    facts = jnp.pad(facts, ((0, 0), (0, 128 - facts.shape[1])))
    stream, piece = norm_tokens(context, residual[0], norm_gain, facts, share, offsets)

    slots = jnp.arange(group // PAGE, dtype=jnp.int32)
    order = jnp.sum(jnp.where(page_table[0][None, :] == slots[:, None], slots[None, :], 0), axis=1)

    def fill_cache(late):
        pages = pick_pages(packed, order, late, n_seq, span)
        sent = lax.all_to_all(pages, "seq", split_axis=0, concat_axis=0, tiled=True)
        return pages, lambda behind: join_pages(sent, share, offsets, span, behind)

    if (n_seq, n_exp) == (8, 4):
        mixture, cache = exchange_experts(piece, w_gate, w_up, w_down, n_seq, n_exp, fill_cache)
    else:
        cache, _ = fill_cache(piece)[1](piece)
        blocks = n_seq * n_exp
        everything = lax.all_gather(piece, everyone, axis=0, tiled=True)
        facts = everything[:, width : width + 8].astype(jnp.float32)
        facts = facts.reshape(blocks // CHUNK_BLOCKS, CHUNK_BLOCKS * rows_dev, 8).transpose(0, 2, 1)
        gates = facts[:, 2:4] + facts[:, 4:6] + facts[:, 6:8]
        partial = experts(
            everything[:, :width], facts[:, :2].astype(jnp.int32), gates, w_gate, w_up, w_down, first
        )
        mixture = lax.psum_scatter(partial, everyone, scatter_dimension=0, tiled=True).astype(jnp.float32)
    layer_out = (stream + mixture).astype(jnp.bfloat16)
    return (layer_out[None], cache.reshape(1, rows_dev // PAGE, PAGE, 2 * width))


def solution(mesh):
    in_specs = (
        P("exp", "seq", None),
        P("exp", "seq", None, None),
        P("exp", "seq", None),
        P(),
        P("exp", None),
        P("exp", "seq", None),
        P("exp", "seq", None),
        P("exp", None),
        P("exp", None, "seq"),
        P("exp", None, "seq"),
        P("exp", "seq", None),
    )
    out_specs = (P("exp", "seq", None), P("exp", "seq", None, None))
    run = functools.partial(body, mesh.shape["seq"], mesh.shape["exp"])
    return jax.shard_map(run, mesh=mesh, in_specs=in_specs, out_specs=out_specs, check_vma=False)
```
